32 devices in a mesh: dp: 4 (over x, core), fsdp: 4 (over z), ctx: 2 (over y).
Axes of the slice: x: 2, y: 2, z: 4, core: 2. Of those that a mesh axis runs over, the one named last changes fastest.
Arguments:
- x_in: bfloat16 [16, 1024, 2048], P(('dp', 'fsdp'), 'ctx'), may hold values from -6 to 6
- span_order: int32 [16, 2], P(('dp', 'fsdp')), may hold values from 0 to 1, each once within a row
- attn_gain: bfloat16 [2048], P(('fsdp', 'ctx')), may hold values from 0.25 to 1.75
- w_qkv: bfloat16 [2048, 3072], P(('fsdp', 'ctx')), may hold values from -0.125 to 0.125
- w_out: bfloat16 [2048, 2048], P(('fsdp', 'ctx')), may hold values from -1 to 1
- ffn_gain: bfloat16 [2048], P(('fsdp', 'ctx')), may hold values from 0.25 to 1.75
- w_gate_up: bfloat16 [2048, 16384], P(('fsdp', 'ctx')), may hold values from -0.125 to 0.125
- w_down: bfloat16 [2048, 8192], P(('fsdp', 'ctx')), may hold values from -0.0625 to 0.0625
- cotangent: bfloat16 [16, 1024, 2048], P(('dp', 'fsdp'), 'ctx'), may hold values from -6 to 6
Outputs:
- y_out: bfloat16 [16, 1024, 2048], P(('dp', 'fsdp'), 'ctx')
- grad_input: float32 [16, 1024, 2048], P(('dp', 'fsdp'), 'ctx')
- grad_attn_gain: float32 [2048], P(('fsdp', 'ctx'))
- grad_qkv: float32 [2048, 3072], P(('fsdp', 'ctx'))
- grad_out: float32 [2048, 2048], P(('fsdp', 'ctx'))
- grad_ffn_gain: float32 [2048], P(('fsdp', 'ctx'))
- grad_gate_up: float32 [2048, 16384], P(('fsdp', 'ctx'))
- grad_down: float32 [2048, 8192], P(('fsdp', 'ctx'))
The draws below stay inside these ranges and needn't reach their ends.
Inputs may be any that keep to these rules, and one draw needn't show every extreme that they name: Each row is a permutation; device c of ctx holds positions span_order[s, c] * 512 to span_order[s, c] * 512 + 511 of sequence s.
All inputs are finite; a program needn't handle non-finite values.
Results may differ from the reference program's by a relative error of at most 0.02.
Values may be sent and summed in bfloat16 or wider, within the bound.
A program may use at most 832 MiB of HBM per device.

```python
import math
import jax
import jax.numpy as jnp
from jax import lax

D = 2048
HEADS = 32
KV_HEADS = 8
HD = 64
FF = 8192
SPAN = 512
LEN = 1024
SEQUENCES = 16
QKV = 3072
N_CTX = 2


def raised(entries, rng, source, target, blocks, factor):
    owner, partner = [(jnp.arange(entries.shape[dim]) // (entries.shape[dim] // blocks)).reshape([-1 if axis == dim else 1 for axis in range(entries.ndim)]) for dim in (source, target)]
    chosen = jax.random.permutation(rng, blocks)[partner]
    strong = (owner == chosen) | (owner == (partner + blocks // 2) % blocks)
    return jnp.where(strong, factor * entries, entries)


def steps_of(key, dims, pieces, least, top_value):
    def one(dim, shards_of):
        draws = jax.random.uniform(jax.random.fold_in(jax.random.fold_in(key, 6), dim), (shards_of,), jnp.float32, least / len(pieces), top_value / len(pieces))
        return jnp.repeat(jnp.exp(draws), dims[dim] // shards_of).reshape((-1,) + (1,) * (len(dims) - dim - 1))

    level = one(*pieces[0])
    for cut in pieces[1:]:
        level = level * one(*cut)
    return level


def noise(key, shape, scale, most, shards=(), kind=jnp.bfloat16):
    drawn = jax.random.normal(key, shape, jnp.float32) * scale
    if len(shards) > 0:
        drawn = steps_of(key, shape, shards, -0.22, 0.18) * drawn
    return jnp.clip(drawn, min=-most, max=most).astype(kind)


def heavy_noise(own_key, dims, width, reach, pieces, heavy, kind=jnp.bfloat16):
    array = width * jax.random.normal(own_key, dims, jnp.float32)
    if pieces:
        array = array * steps_of(own_key, dims, pieces, -0.22, 0.18)
    return jnp.clip(raised(array, jax.random.fold_in(own_key, 3), *heavy), -reach, reach).astype(kind)


def setup_inputs(seed: int = 0) -> dict:
    key_of = jax.random.split(jax.random.key(seed), 10)
    x_in = noise(key_of[0], (SEQUENCES, LEN, D), 1.0, 6.0, ((0, 16), (1, 2)))
    span_order = jax.vmap(lambda own: jax.random.permutation(own, N_CTX))(jax.random.split(key_of[1], SEQUENCES)).reshape((SEQUENCES, N_CTX)).astype(jnp.int32)
    attn_gain = jnp.clip(1.0 + 0.15 * jax.random.normal(key_of[2], (D,), jnp.float32), 0.25, 1.75).astype(jnp.bfloat16)
    w_qkv = noise(key_of[3], (D, QKV), D ** -0.5, 0.125, ((0, 8),))
    w_out = noise(key_of[4], (D, D), (HD // 2) ** -0.5, 1.0, ((0, 8),))
    ffn_gain = jnp.clip(1.0 + 0.15 * jax.random.normal(key_of[5], (D,), jnp.float32), 0.25, 1.75).astype(jnp.bfloat16)
    w_gate_up = noise(key_of[6], (D, 2 * FF), D ** -0.5, 0.125, ((0, 8),))
    w_down = noise(key_of[7], (D, FF), FF ** -0.5, 0.0625, ((0, 8),))
    cotangent = heavy_noise(key_of[8], (SEQUENCES, LEN, D), 1.0, 6.0, ((0, 16), (1, 2)), (1, 2, 2, 2.0))
    return dict(x_in=x_in, span_order=span_order, attn_gain=attn_gain, w_qkv=w_qkv, w_out=w_out, ffn_gain=ffn_gain, w_gate_up=w_gate_up, w_down=w_down, cotangent=cotangent)


EPS = 1e-05

@jax.custom_vjp
def low(v):
    return lax.optimization_barrier(v.astype(jnp.bfloat16)).astype(jnp.float32)

@jax.custom_vjp
def low_back(v):
    return v

def low_keep(v):
    return (low(v), None)

def low_pass(kept, grad):
    return (grad,)

def back_keep(v):
    return (v, None)

def back_low(kept, grad):
    return (low(grad),)
low.defvjp(low_keep, low_pass)
low_back.defvjp(back_keep, back_low)

def rotate(tensor, positions):
    half = tensor.shape[-1] // 2
    freq = jnp.exp(jnp.arange(half, dtype=jnp.float32) * (-math.log(500000.0) / half))
    angle = positions[:, None] * freq[None, :]
    cosine = jnp.concatenate([jnp.cos(angle), jnp.cos(angle)], -1)[:, None, :]
    sine = jnp.concatenate([jnp.sin(angle), jnp.sin(angle)], -1)[:, None, :]
    turned = jnp.concatenate([-tensor[..., half:], tensor[..., :half]], -1)
    return tensor * cosine + turned * sine

def normalize(rows, gain):
    return rows * lax.rsqrt(lax.optimization_barrier(jnp.mean(rows * rows, -1, keepdims=True)) + EPS) * gain

def matmul(left, right):
    return jnp.dot(left, right, precision=lax.Precision.HIGHEST)

def attend(query, keys, values, causal):
    length = query.shape[0]
    ratio = HEADS // KV_HEADS
    grouped = jnp.transpose(query.reshape(length, KV_HEADS, ratio, HD), (1, 0, 2, 3))
    key_heads = jnp.transpose(keys, (1, 0, 2))
    value_heads = jnp.transpose(values, (1, 0, 2))

    def one_group(operands):
        qhead, khead, vhead = operands
        scores = low_back(jnp.einsum('crd,ld->rcl', qhead, khead, precision=lax.Precision.HIGHEST) * HD ** (-0.5))
        scores = jnp.where(causal[None], scores, -1e+30)
        peak = lax.optimization_barrier(jnp.max(scores, -1, keepdims=True))
        expd = jnp.exp(scores - peak)
        probs = expd / lax.optimization_barrier(jnp.sum(expd, -1, keepdims=True))
        result = jnp.einsum('rcl,ld->crd', low(probs), vhead, precision=lax.Precision.HIGHEST)
        return low_back(low(result))
    results = lax.map(jax.checkpoint(one_group), (grouped, key_heads, value_heads))
    return jnp.transpose(results, (1, 0, 2, 3)).reshape(length, HEADS * HD)

def layer(tokens, positions, causal, attn_gain, w_qkv, w_out, ffn_gain, w_gate_up, w_down):
    qwidth = HEADS * HD
    kvwidth = KV_HEADS * HD
    length = tokens.shape[0]
    normed_one = low(normalize(tokens, attn_gain))
    qkv = low_back(matmul(normed_one, w_qkv))
    query = low(rotate(qkv[:, :qwidth].reshape(length, HEADS, HD), positions))
    keys = low(rotate(qkv[:, qwidth:qwidth + kvwidth].reshape(length, KV_HEADS, HD), positions))
    values = low(qkv[:, qwidth + kvwidth:]).reshape(length, KV_HEADS, HD)
    mixed = attend(query, keys, values, causal)
    hidden_one = tokens + low_back(matmul(mixed, w_out))
    normed_two = low(normalize(hidden_one, ffn_gain))
    gate_up = low_back(matmul(normed_two, w_gate_up))
    inner = low(jax.nn.silu(gate_up[:, :FF]) * gate_up[:, FF:])
    return hidden_one + jnp.dot(inner, w_down.T, precision=lax.Precision.HIGHEST)

def reference(x_in, span_order, attn_gain, w_qkv, w_out, ffn_gain, w_gate_up, w_down, cotangent):
    offsets = jnp.arange(SPAN, dtype=jnp.int32)
    positions = (span_order[:, :, None] * SPAN + offsets[None, None, :]).reshape(SEQUENCES, LEN).astype(jnp.int32)
    params = tuple((w.astype(jnp.float32) for w in (attn_gain, w_qkv, w_out, ffn_gain, w_gate_up, w_down)))
    checked = jax.checkpoint(layer)

    def forward(tokens, *weights):

        def step(carry, inputs):
            seq_tokens, seq_pos = inputs
            causal = seq_pos[:, None] >= seq_pos[None, :]
            return (carry, checked(seq_tokens, seq_pos.astype(jnp.float32), causal, *weights))
        _, outs = lax.scan(step, jnp.zeros((), jnp.float32), (tokens, positions))
        return outs
    outs, pull = jax.vjp(forward, x_in.astype(jnp.float32), *params)
    grads = pull(cotangent.astype(jnp.float32))
    return (outs.astype(jnp.bfloat16), grads[0], grads[1], grads[2], grads[3], grads[4], grads[5], grads[6])
```

```python
import math

import jax
import jax.numpy as jnp
from jax import lax
from jax.experimental import pallas as pl
from jax.experimental.pallas import tpu as pltpu
from jax.sharding import PartitionSpec as P

HEADS = 32
KV_HEADS = 8
HD = 64
EPS = 1e-05
SUBS = 4

BF = jnp.bfloat16
F32 = jnp.float32
GRID = ("fsdp", "ctx")


def matmul(left, right):
    return jnp.dot(left, right, preferred_element_type=F32)


def matmul_rows(left, right):
    return lax.dot_general(left, right, (((1,), (1,)), ((), ())), preferred_element_type=F32)


def matmul_tokens(left, right):
    return lax.dot_general(left, right, (((0,), (0,)), ((), ())), preferred_element_type=F32)


def rope_tables(positions):
    half = HD // 2
    freq = jnp.exp(jnp.arange(half, dtype=F32) * (-math.log(500000.0) / half))
    angle = positions[:, None] * freq[None, :]
    cosine, sine = jnp.cos(angle), jnp.sin(angle)
    zero = jnp.zeros_like(sine)
    return (
        jnp.concatenate([cosine] * 4, -1),
        jnp.concatenate([-sine, zero] * 2, -1),
        jnp.concatenate([zero, sine] * 2, -1),
    )


def inv_rms(rows):
    return lax.rsqrt(jnp.mean(rows * rows, -1, keepdims=True) + EPS)


def norm_back(rows, scale, gain, grad):
    unit = rows * scale
    pulled = grad * gain[None, :]
    inner = jnp.mean(pulled * unit, -1, keepdims=True)
    return scale * (pulled - unit * inner), jnp.sum(grad * unit, 0)


MIB = 1 << 20
ANY = pl.BlockSpec(memory_space=pl.ANY)
WHOLE = pl.BlockSpec(memory_space=pltpu.VMEM)


def cost(flops, moved, exps=0):
    return pl.CostEstimate(flops=int(flops), bytes_accessed=int(moved), transcendentals=int(exps))


def params(mib):
    return pltpu.CompilerParams(vmem_limit_bytes=mib * MIB)


def dot_nn(a, b):
    return lax.dot_general(a, b, (((1,), (0,)), ((), ())), preferred_element_type=F32)


def dot_nt(a, b):
    return lax.dot_general(a, b, (((1,), (1,)), ((), ())), preferred_element_type=F32)


def dot_tn(a, b):
    return lax.dot_general(a, b, (((0,), (0,)), ((), ())), preferred_element_type=F32)


def reorder(array, places, axis=1, deps=()):
    count = places.shape[0]
    if axis == 1 and (array.shape[1] // count) % 128 != 0:
        size = array.shape[1] // count
        blocks = [lax.dynamic_slice_in_dim(array, places[s] * size, size, 1) for s in range(count)]
        return jnp.concatenate(blocks, 1)
    if axis == 1:
        shape = (array.shape[0], array.shape[1] // count)
        took = lambda s, where: (0, where[s])
        gave = lambda s, where: (0, s)
    else:
        shape = (array.shape[0] // count, array.shape[1])
        took = lambda s, where: (where[s], 0)
        gave = lambda s, where: (s, 0)

    def kernel(where, source, *rest):
        rest[-1][...] = source[...]

    return pl.pallas_call(
        kernel,
        grid_spec=pltpu.PrefetchScalarGridSpec(
            num_scalar_prefetch=1,
            grid=(count,),
            in_specs=[pl.BlockSpec(shape, took)] + [ANY] * len(deps),
            out_specs=pl.BlockSpec(shape, gave),
        ),
        out_shape=jax.ShapeDtypeStruct(array.shape, array.dtype),
        compiler_params=params(16),
        cost_estimate=cost(0, 2 * array.size * array.dtype.itemsize),
    )(places, array, *deps)


def turn(piece, cosine, sine_low, sine_high):
    return (
        piece * cosine
        + pltpu.roll(piece, 128 - HD // 2, axis=1) * sine_low
        + pltpu.roll(piece, HD // 2, axis=1) * sine_high
    )


def head_of(block, group):
    odd = (group // 2) % 2 == 1
    return jnp.where(odd, block[:, HD:], block[:, :HD])


def causal_tile(size):
    key = lax.broadcasted_iota(jnp.int32, (size, size), 0)
    query = lax.broadcasted_iota(jnp.int32, (size, size), 1)
    return key <= query


def scores_of(key, key_far, query, seen, mask, span):
    tile = query.shape[0]
    own = dot_nt(key, query)
    if key.shape[0] > tile:
        last = key.shape[0] - tile
        own = jnp.concatenate([own[:last], jnp.where(mask, own[last:], -1e30)], 0)
    else:
        own = jnp.where(mask, own, -1e30)
    far = dot_nt(key_far, query)
    far = [jnp.where(seen[k], far[k * span : (k + 1) * span], -1e30) for k in range(len(seen))]
    return own, (far[0] if len(far) == 1 else jnp.concatenate(far, 0))


def place_grads(pieces, columns, sub, ffwidth):
    rows = pieces[0].shape[0]
    count = len(pieces)

    def kernel(*refs):
        where = refs[0]
        sources = refs[1 : 1 + count]
        gu_ref, down_ref, took, gave, in_sems, out_sems = refs[1 + count :]

        def read(k):
            return pltpu.make_async_copy(sources[k], took.at[k % 2], in_sems.at[k % 2])

        def writes(k):
            at = pl.multiple_of(where[k], 128)
            here = gave.at[k % 2]
            return (
                pltpu.make_async_copy(
                    here.at[:, pl.ds(0, sub)], gu_ref.at[:, pl.ds(at, sub)], out_sems.at[k % 2, 0]
                ),
                pltpu.make_async_copy(
                    here.at[:, pl.ds(sub, sub)], gu_ref.at[:, pl.ds(at + ffwidth, sub)], out_sems.at[k % 2, 1]
                ),
                pltpu.make_async_copy(
                    here.at[:, pl.ds(2 * sub, sub)], down_ref.at[:, pl.ds(at, sub)], out_sems.at[k % 2, 2]
                ),
            )

        read(0).start()
        for k in range(count):
            if k + 1 < count:
                read(k + 1).start()
            read(k).wait()
            if k >= 2:
                for copy in writes(k - 2):
                    copy.wait()
            gave[k % 2] = took[k % 2].astype(F32)
            for copy in writes(k):
                copy.start()
        for k in range(max(0, count - 2), count):
            for copy in writes(k):
                copy.wait()

    return pl.pallas_call(
        kernel,
        in_specs=[pl.BlockSpec(memory_space=pltpu.SMEM)] + [ANY] * count,
        out_specs=[ANY, ANY],
        out_shape=[
            jax.ShapeDtypeStruct((rows, 2 * ffwidth), F32),
            jax.ShapeDtypeStruct((rows, ffwidth), F32),
        ],
        scratch_shapes=[
            pltpu.VMEM((2, rows, 3 * sub), BF),
            pltpu.VMEM((2, rows, 3 * sub), F32),
            pltpu.SemaphoreType.DMA((2,)),
            pltpu.SemaphoreType.DMA((2, 3)),
        ],
        compiler_params=params(32),
        cost_estimate=cost(0, rows * ffwidth * 18),
    )(columns, *pieces)


MESH = pl.DeviceIdType.MESH


def ring_place(n_fsdp):
    f, c = lax.axis_index("fsdp"), lax.axis_index("ctx")

    def device(place):
        row, k = place // n_fsdp, place % n_fsdp
        return {"fsdp": k + (row % 2) * (n_fsdp - 1 - 2 * k), "ctx": row}

    return c * n_fsdp + f + (c % 2) * (n_fsdp - 1 - 2 * f), device


def slot_lanes(ref, block, rows):
    if rows % 128 == 0:
        return ref[:, pl.ds(pl.multiple_of(block * rows, 128), rows)].astype(F32)
    share = 128 // rows
    wide = ref[:, pl.ds(pl.multiple_of(block // share * 128, 128), 128)].astype(F32)
    part = wide[:, :rows]
    for k in range(1, share):
        part = jnp.where(block % share == k, wide[:, k * rows : (k + 1) * rows], part)
    return part


def team_place(size, me, bit):
    return me + bit - 2 * bit * ((me // bit) % 2)


def greet(partners):
    barrier = pltpu.get_barrier_semaphore()
    for partner in partners:
        pl.semaphore_signal(barrier, inc=1, device_id=partner, device_id_type=MESH)
    pl.semaphore_wait(barrier, len(partners))


def own_columns(size, w_gate_up, w_down, first):
    ffwidth = w_down.shape[1]
    ffq = ffwidth // size
    sub = ffq // SUBS
    out = []
    for way in range(2):
        at = lax.axis_index("dp") * ffq + (first + way) * sub
        out.append(
            [
                (w_gate_up.at[:, pl.ds(pl.multiple_of(at, 128), sub)], 0),
                (w_gate_up.at[:, pl.ds(pl.multiple_of(at + ffwidth, 128), sub)], sub),
                (w_down.at[:, pl.ds(pl.multiple_of(at, 128), sub)], 2 * sub),
            ]
        )
    return out


class RingGather:
    def __init__(self, sizes, own, out, own_v, own_sem, store_sem, send, recv):
        self.n = sizes[1] * sizes[2]
        self.rows = own_v.shape[1]
        self.own, self.out, self.own_v = own, out, own_v
        self.own_sem, self.store_sem, self.send, self.recv = own_sem, store_sem, send, recv
        place, device = ring_place(sizes[1])
        self.partners = [device((place + 1) % self.n), device((place + self.n - 1) % self.n)]

    def rows_of(self, way, t):
        slot = t if way == 0 else (self.n - t) % self.n
        return pl.ds(slot * self.rows, self.rows)

    def loads(self, way):
        width = self.own_v.shape[2] // 3
        return [
            pltpu.make_async_copy(
                source, self.own_v.at[way, :, pl.ds(place, width)], self.own_sem.at[way, place // width]
            )
            for source, place in self.own[way]
        ]

    def store(self, way):
        return pltpu.make_async_copy(
            self.own_v.at[way], self.out[way].at[pl.ds(0, self.rows)], self.store_sem.at[way]
        )

    def ring(self, way, t, first=False):
        source = self.own_v.at[way] if first else self.out[way].at[self.rows_of(way, t - 1)]
        return pltpu.make_async_remote_copy(
            src_ref=source,
            dst_ref=self.out[way].at[self.rows_of(way, t)],
            send_sem=self.send.at[way, t],
            recv_sem=self.recv.at[way, t],
            device_id=self.partners[way],
            device_id_type=MESH,
        )

    def arrived(self, way, t):
        target = self.out[way].at[self.rows_of(way, t)]
        return pltpu.make_async_remote_copy(
            src_ref=target,
            dst_ref=target,
            send_sem=self.send.at[way, t],
            recv_sem=self.recv.at[way, t],
            device_id=self.partners[way],
            device_id_type=MESH,
        )

    def first(self):
        for way in range(2):
            for copy in self.loads(way):
                copy.start()
        for way in range(2):
            for copy in self.loads(way):
                copy.wait()
            self.ring(way, 1, True).start()
            self.store(way).start()

    def tick(self, t):
        for way in range(2):
            self.arrived(way, t - 1).wait_recv()
            self.ring(way, t).start()

    def last(self):
        for way in range(2):
            self.arrived(way, self.n - 1).wait_recv()
            self.store(way).wait()
            self.ring(way, 1, True).wait_send()
            for t in range(2, self.n):
                self.ring(way, t).wait_send()


def gather_scratch(n, rows, wide):
    dma = pltpu.SemaphoreType.DMA
    return [pltpu.VMEM((2, rows, wide), BF), dma((2, 3)), dma((2,)), dma((2, n)), dma((2, n))]


class RingReduce:
    def __init__(self, sizes, parts, out, land, own_v, land_v, send_v, own_sem, land_sem, out_sem, send, recv):
        self.n = sizes[1] * sizes[2]
        self.rows = out[0].shape[0]
        self.parts, self.out, self.land = parts, out, land
        self.own_v, self.land_v, self.send_v = own_v, land_v, send_v
        self.own_sem, self.land_sem, self.out_sem = own_sem, land_sem, out_sem
        self.send, self.recv = send, recv
        place, device = ring_place(sizes[1])
        self.partners = [device((place + 1) % self.n), device((place + self.n - 1) % self.n)]

    def load_own(self, way, t):
        slot = t % self.n if way == 0 else self.n - t
        return pltpu.make_async_copy(
            self.parts[way].at[pl.ds(slot * self.rows, self.rows)],
            self.own_v.at[way, t % 2],
            self.own_sem.at[way, t % 2],
        )

    def load_land(self, way, t):
        return pltpu.make_async_copy(self.land.at[way, t - 1], self.land_v.at[way], self.land_sem.at[way])

    def ring(self, way, t):
        return pltpu.make_async_remote_copy(
            src_ref=self.send_v.at[way, t % 2],
            dst_ref=self.land.at[way, t - 1],
            send_sem=self.send.at[way, t],
            recv_sem=self.recv.at[way, t],
            device_id=self.partners[way],
            device_id_type=MESH,
        )

    def save(self, way):
        return pltpu.make_async_copy(self.own_v.at[way, self.n % 2], self.out[way], self.out_sem.at[way])

    def first(self):
        for way in range(2):
            self.load_own(way, 1).start()
            self.load_own(way, 2).start()
        for way in range(2):
            self.load_own(way, 1).wait()
            self.send_v[way, 1] = self.own_v[way, 1]
            self.ring(way, 1).start()

    def tick(self, t):
        for way in range(2):
            self.ring(way, t - 1).wait_recv()
            self.load_land(way, t - 1).start()
            self.load_own(way, t + 1).start()
        for way in range(2):
            self.load_own(way, t).wait()
            self.load_land(way, t - 1).wait()

            @pl.when(t >= 3)
            def _():
                self.ring(way, t - 2).wait_send()

            total = self.own_v[way, t % 2].astype(F32) + self.land_v[way].astype(F32)
            self.send_v[way, t % 2] = total.astype(BF)
            self.ring(way, t).start()

    def last(self):
        n = self.n
        for way in range(2):
            self.ring(way, n - 1).wait_recv()
            self.load_land(way, n - 1).start()
        for way in range(2):
            self.load_own(way, n).wait()
            self.load_land(way, n - 1).wait()
            total = self.own_v[way, n % 2].astype(F32) + self.land_v[way].astype(F32)
            self.own_v[way, n % 2] = total.astype(BF)
            self.save(way).start()
        for way in range(2):
            self.ring(way, n - 2).wait_send()
            self.ring(way, n - 1).wait_send()
            self.save(way).wait()


class RingReduceNear(RingReduce):
    def __init__(self, sizes, parts, out, land, own_v, own_sem, out_sem, send, recv):
        RingReduce.__init__(self, sizes, parts, out, land, own_v, None, None, own_sem, None, out_sem, send, recv)

    def ring(self, way, t, first=False):
        return pltpu.make_async_remote_copy(
            src_ref=self.own_v.at[way, 1] if first else self.land.at[way, t - 2],
            dst_ref=self.land.at[way, t - 1],
            send_sem=self.send.at[way, t],
            recv_sem=self.recv.at[way, t],
            device_id=self.partners[way],
            device_id_type=MESH,
        )

    def arrived(self, way, t):
        target = self.land.at[way, t - 1]
        return pltpu.make_async_remote_copy(
            src_ref=target,
            dst_ref=target,
            send_sem=self.send.at[way, t],
            recv_sem=self.recv.at[way, t],
            device_id=self.partners[way],
            device_id_type=MESH,
        )

    def first(self):
        for way in range(2):
            self.load_own(way, 1).start()
            self.load_own(way, 2).start()
        for way in range(2):
            self.load_own(way, 1).wait()
            self.ring(way, 1, True).start()

    def tick(self, t):
        for way in range(2):
            self.arrived(way, t - 1).wait_recv()
            self.load_own(way, t).wait()
            total = self.own_v[way, t % 2].astype(F32) + self.land[way, t - 2].astype(F32)
            self.land[way, t - 2] = total.astype(BF)
            self.ring(way, t).start()

            @pl.when(t == 2)
            def _():
                self.ring(way, 1, True).wait_send()

            self.load_own(way, t + 1).start()

    def last(self):
        n = self.n
        for way in range(2):
            self.arrived(way, n - 1).wait_recv()
            self.load_own(way, n).wait()
            total = self.own_v[way, n % 2].astype(F32) + self.land[way, n - 2].astype(F32)
            self.own_v[way, n % 2] = total.astype(BF)
            self.save(way).start()
        for way in range(2):
            for t in range(2, n):
                self.ring(way, t).wait_send()
            self.save(way).wait()


def near_scratch(n, rows, wide):
    dma = pltpu.SemaphoreType.DMA
    return [
        pltpu.VMEM((2, n - 1, rows, wide), BF),
        pltpu.VMEM((2, 2, rows, wide), BF),
        dma((2, 2)),
        dma((2,)),
        dma((2, n)),
        dma((2, n)),
    ]


class TeamSpread:
    def __init__(self, size, own, others, send, recv):
        self.own, self.others, self.send, self.recv = own, others, send, recv
        self.count = len(own)
        me = lax.axis_index("dp")
        self.stages = []
        held, bit = 1, size // 2
        while bit:
            partner = {"dp": me + bit - 2 * bit * ((me // bit) % 2)}
            self.stages.append((held, partner))
            held, bit = 2 * held, bit // 2

    def partners(self):
        return [partner for _, partner in self.stages]

    def copies(self, stage):
        held, partner = self.stages[stage]
        for k in range(self.count):
            for b in range(held):
                yield pltpu.make_async_remote_copy(
                    src_ref=self.own[k] if b == 0 else self.others[k][b - 1],
                    dst_ref=self.others[k][held + b - 1],
                    send_sem=self.send.at[k, held + b - 1],
                    recv_sem=self.recv.at[k, held + b - 1],
                    device_id=partner,
                    device_id_type=MESH,
                )

    def start(self, stage):
        if stage < len(self.stages):
            for copy in self.copies(stage):
                copy.start()

    def arrive(self, stage):
        if stage < len(self.stages):
            for copy in self.copies(stage):
                copy.wait_recv()

    def last(self):
        for stage in range(len(self.stages)):
            for copy in self.copies(stage):
                copy.wait_send()


def spread_scratch(count, size):
    return [pltpu.SemaphoreType.DMA((count, size)), pltpu.SemaphoreType.DMA((count, size))]


def reduce_scratch(n, rows, wide):
    dma = pltpu.SemaphoreType.DMA
    return [
        pltpu.VMEM((2, 2, rows, wide), BF),
        pltpu.VMEM((2, rows, wide), BF),
        pltpu.VMEM((2, 2, rows, wide), BF),
        dma((2, 2)),
        dma((2,)),
        dma((2,)),
        dma((2, n)),
        dma((2, n)),
    ]


def feed_forward(sizes, xs, dys, weights, before, ring_parts, reducing, ident):
    n_dp, n_fsdp, n_ctx = sizes
    n = n_fsdp * n_ctx
    team, (span, width) = len(xs), xs[0].shape
    rows, wide = width // n, weights[0][0].shape[1]
    sub = wide // 3
    pieces = [piece for group in weights for piece in group]
    counts = [len(group) for group in weights]
    tile = min(span, 256)
    per = span // tile
    steps = team * per
    part = max(rows, 128)
    half = width // 2
    gsteps = width // part
    total = 2 * steps + gsteps
    inside = team // 2 if reducing and team > 2 else 0
    carried = [] if before is None else [b[0] for b in before] + [b[1] for b in before]
    backwards = reducing

    def kernel(*refs):
        refs = list(refs)

        def take(count):
            out = refs[:count]
            del refs[:count]
            return out

        x_refs, dy_refs, piece_refs = take(team), take(team), take(len(pieces))
        old_y, old_dn = take(len(carried) // 2), take(len(carried) // 2)
        part_refs = take(2)
        y_refs, dn_refs, grad_refs, ring_outs = take(team), take(team), take(2), take(2)
        if reducing:
            (land,) = take(1)
            near = take(max(1, inside))
            (far,) = take(1)
        wgu, wd, xb, dyb, yb, dnb, dgu, inner, xg, dyg, gout = take(11)
        w_sems, x_sems, y_sems, g_sems, gout_sems = take(5)
        if carried:
            cb, c_sems = take(2)
        if reducing:
            swap_send, swap_recv, face_send, face_recv = take(4)
            ring = RingReduce(sizes, part_refs, ring_outs, land, *refs)
        else:
            ring = RingGather(sizes, own_columns(n_dp, *part_refs, SUBS // 2), ring_outs, *refs)
        me = lax.axis_index("dp")
        sibling = {"dp": me + 1 - 2 * (me % 2)}
        bit = team // 2
        facing = {"dp": me + bit - 2 * bit * ((me // bit) % 2)}

        k = 0
        w_copies = []
        for b, count in enumerate(counts):
            at = 0
            for ref in piece_refs[k : k + count]:
                high = ref.shape[0]
                w_copies += [
                    pltpu.make_async_copy(
                        ref.at[:, pl.ds(0, 2 * sub)],
                        wgu.at[pl.ds(at, high), pl.ds(b * 2 * sub, 2 * sub)],
                        w_sems.at[2 * k],
                    ),
                    pltpu.make_async_copy(
                        ref.at[:, pl.ds(2 * sub, sub)],
                        wd.at[pl.ds(at, high), pl.ds(b * sub, sub)],
                        w_sems.at[2 * k + 1],
                    ),
                ]
                at += high
                k += 1
        for copy in w_copies:
            copy.start()

        def block_of(i):
            return team - 1 - i // per if backwards else i // per

        def loads(m, i):
            rows_here = pl.ds((i % per) * tile, tile)
            return [
                pltpu.make_async_copy(x_refs[m].at[rows_here], xb.at[i % 2], x_sems.at[0, i % 2]),
                pltpu.make_async_copy(dy_refs[m].at[rows_here], dyb.at[i % 2], x_sems.at[1, i % 2]),
            ]

        def more(m, i):
            if not carried:
                return []
            rows_here = pl.ds((i % per) * tile, tile)
            out = [
                pltpu.make_async_copy(old_y[m].at[rows_here], cb.at[0], c_sems.at[0]),
                pltpu.make_async_copy(old_dn[m].at[rows_here], cb.at[1], c_sems.at[1]),
            ]
            if m < inside:
                out.append(pltpu.make_async_copy(near[m].at[rows_here], cb.at[2], c_sems.at[2]))
            return out

        def writes(m, i):
            rows_here = pl.ds((i % per) * tile, tile)
            return [
                pltpu.make_async_copy(yb, y_refs[m].at[rows_here], y_sems.at[0]),
                pltpu.make_async_copy(dnb, dn_refs[m].at[rows_here], y_sems.at[1]),
            ]

        def on_block(i, act):
            for m in range(team):

                @pl.when(block_of(i) == m)
                def _():
                    act(m)

        def swap(m):
            return pltpu.make_async_remote_copy(
                src_ref=dn_refs[m],
                dst_ref=near[m - inside],
                send_sem=swap_send.at[m - inside],
                recv_sem=swap_recv.at[m - inside],
                device_id=sibling,
                device_id_type=MESH,
            )

        def face():
            return pltpu.make_async_remote_copy(
                src_ref=dn_refs[1],
                dst_ref=far,
                send_sem=face_send,
                recv_sem=face_recv,
                device_id=facing,
                device_id_type=MESH,
            )

        def go(copies):
            for copy in copies:
                copy.start()

        def end(copies):
            for copy in copies:
                copy.wait()

        def ticks(lo, hi):
            lax.fori_loop(2 + lo * (n - 2) // total, 2 + hi * (n - 2) // total, lambda t, c: (ring.tick(t), c)[1], 0)

        on_block(0, lambda m: go(loads(m, 0)))
        partners = list(ring.partners)
        if inside:
            partners.append(sibling)
        if reducing and team > 1:
            partners.append(facing)
        greet(partners)
        ring.first()
        for copy in w_copies:
            copy.wait()

        def forward(i, carry):
            @pl.when(i + 1 < steps)
            def _():
                on_block(i + 1, lambda m: go(loads(m, i + 1)))

            @pl.when(i == steps - 1)
            def _():
                go(sides(0))

            if inside:
                @pl.when(i % per == 0)
                def _():
                    on_block(i, lambda m: swap(m + inside).wait_recv() if m < inside else None)

            on_block(i, lambda m: go(more(m, i)))
            ticks(2 * i, 2 * i + 2)
            end(loads(0, i))
            here = pl.ds(pl.multiple_of(i * tile, tile), tile)
            for b in range(2):
                gate_up = dot_nn(xb[i % 2], wgu[:, b * 2 * sub : (b + 1) * 2 * sub])
                d_inner = dot_nn(dyb[i % 2], wd[:, b * sub : (b + 1) * sub])
                gate, up = gate_up[:, :sub], gate_up[:, sub:]
                sig = 1.0 / (1.0 + jnp.exp(-gate))
                act = gate * sig
                inner[here, b * sub : (b + 1) * sub] = (act * up).astype(BF)
                dgu[here, b * 2 * sub : b * 2 * sub + sub] = (
                    d_inner * up * (sig + act * (1.0 - sig))
                ).astype(BF)
                dgu[here, b * 2 * sub + sub : (b + 1) * 2 * sub] = (d_inner * act).astype(BF)
            drained = (i > 0) & (i % per != 0) if reducing else i > 0

            @pl.when(drained)
            def _():
                end(writes(0, i))

            if carried:
                on_block(i, lambda m: end(more(m, i)))
            for at in range(0, width, half):
                lanes = slice(at, at + half)
                y = dot_nt(inner[here, :], wd[lanes, :])
                if carried:
                    y = y + cb[0, :, lanes].astype(F32)
                yb[:, lanes] = y.astype(BF)
                dn = dot_nt(dgu[here, :], wgu[lanes, :])
                if carried:
                    dn = dn + cb[1, :, lanes].astype(F32)
                if inside:
                    dn = dn + jnp.where(block_of(i) < inside, cb[2, :, lanes].astype(F32), 0.0)
                dnb[:, lanes] = dn.astype(BF)
            on_block(i, lambda m: go(writes(m, i)))
            if reducing and team > 1:

                @pl.when(i % per == per - 1)
                def _():
                    def sent(m):
                        if m >= 1:
                            end(writes(m, i))
                            go([swap(m)] if inside and m >= inside else [face()])

                    on_block(i, sent)

            return carry

        def sides(g):
            cols = pl.ds(g * part, part) if isinstance(g, int) else pl.ds(pl.multiple_of(g * part, part), part)
            out = []
            for k in range(team):
                m = team - 1 - k if backwards else k
                at = pl.ds(k * span, span)
                out += [
                    pltpu.make_async_copy(x_refs[m].at[:, cols], xg.at[g % 2, at], g_sems.at[0, g % 2, k]),
                    pltpu.make_async_copy(dy_refs[m].at[:, cols], dyg.at[g % 2, at], g_sems.at[1, g % 2, k]),
                ]
            return out

        def keep(g):
            at = pl.ds(pl.multiple_of(g * part, part), part)
            return [pltpu.make_async_copy(gout.at[b], grad_refs[b].at[at], gout_sems.at[b]) for b in range(2)]

        def outer(g, carry):
            @pl.when(g + 1 < gsteps)
            def _():
                go(sides(g + 1))

            ticks(2 * steps + g, 2 * steps + g + 1)
            end(sides(g))

            @pl.when(g > 0)
            def _():
                end(keep(g))

            for b in range(2):
                up_down = dot_tn(xg[g % 2], dgu[:, b * 2 * sub : (b + 1) * 2 * sub])
                gout[b, :, : 2 * sub] = up_down.astype(BF)
                down = dot_tn(dyg[g % 2], inner[:, b * sub : (b + 1) * sub])
                gout[b, :, 2 * sub :] = down.astype(BF)
            go(keep(g))
            return carry

        lax.fori_loop(0, steps, forward, 0)
        lax.fori_loop(0, gsteps, outer, 0)
        end(writes(0, 0))
        end(keep(0))
        ring.last()
        if reducing and team > 1:
            for m in range(inside, team) if inside else []:
                swap(m).wait_send()
            face().wait_recv()
            face().wait_send()

    shape = lambda a, b: jax.ShapeDtypeStruct((a, b), BF)
    outs = [shape(span, width)] * (2 * team) + [shape(width, wide)] * 2
    if reducing:
        outs += [shape(rows, wide)] * 2 + [jax.ShapeDtypeStruct((2, n - 1, rows, wide), BF)]
        outs += [shape(span, width)] * (max(1, inside) + 1)
    else:
        outs += [shape(width, wide)] * 2
    dma = pltpu.SemaphoreType.DMA
    scratch = [
        pltpu.VMEM((width, 4 * sub), BF),
        pltpu.VMEM((width, 2 * sub), BF),
        pltpu.VMEM((2, tile, width), BF),
        pltpu.VMEM((2, tile, width), BF),
        pltpu.VMEM((tile, width), BF),
        pltpu.VMEM((tile, width), BF),
        pltpu.VMEM((team * span, 4 * sub), BF),
        pltpu.VMEM((team * span, 2 * sub), BF),
        pltpu.VMEM((2, team * span, part), BF),
        pltpu.VMEM((2, team * span, part), BF),
        pltpu.VMEM((2, part, wide), BF),
        dma((2 * len(pieces),)),
        dma((2, 2)),
        dma((2,)),
        dma((2, 2, team)),
        dma((2,)),
    ]
    if carried:
        scratch += [pltpu.VMEM((3 if inside else 2, tile, width), BF), dma((3,))]
    if reducing:
        scratch += [dma((max(1, inside),)), dma((max(1, inside),)), dma(()), dma(())]
        scratch += reduce_scratch(n, rows, wide)
    else:
        scratch += gather_scratch(n, rows, wide)
    operands = list(xs) + list(dys) + pieces + carried + list(ring_parts)
    out = pl.pallas_call(
        kernel,
        in_specs=[ANY] * len(operands),
        out_specs=[ANY] * len(outs),
        out_shape=outs,
        scratch_shapes=scratch,
        compiler_params=pltpu.CompilerParams(
            collective_id=ident, has_side_effects=True, vmem_limit_bytes=56 * MIB
        ),
        cost_estimate=cost(18 * team * span * width * 2 * sub, 40 * MIB),
    )(*operands)
    y, dn, grads, ringed = out[:team], out[team : 2 * team], out[2 * team : 2 * team + 2], out[2 * team + 2 :]
    if reducing:
        return y, (dn[0], ringed[-1]) if team > 1 else (dn[0],), grads, ringed[:2]
    return y, dn, grads, ringed[:2]


def attend_forward(sizes, x, qkv, kv_far, seen, w_out, gains, dy, w_gate_up, w_down):
    n_dp, n_fsdp, n_ctx = sizes
    n = n_fsdp * n_ctx
    span, width = x.shape
    rows = width // n
    far = kv_far.shape[0]
    blocks = far // span
    qwidth, kvwidth = HEADS * HD, KV_HEADS * HD
    near, kvpairs = qwidth // 128, kvwidth // 128
    pairs = HEADS // 2
    tile = min(span, 256)
    wide = 3 * (w_down.shape[1] // n_dp // SUBS)
    early = max(0, 3 * (n - 2) // 7)
    others = n_dp - 1
    chunk = min(512, width)

    def kernel(seen_ref, q_ref, k_ref, v_ref, kf_ref, vf_ref, x_ref, gains_ref, *refs):
        refs = list(refs)

        def take(count):
            out = refs[:count]
            del refs[:count]
            return out

        wo_ref, dy_ref, gu_ref, down_ref = take(4)
        lse_ref, attn_out, hidden_out, normed_out = take(4)
        x_blocks, dy_blocks, ring_outs = take(others), take(others), take(2)
        attn_v, wo_v, hidden_v, normed_v, load_sem, save_sems = take(6)
        dy_send, dy_recv, x_send, x_recv = take(4)
        ring = RingGather(sizes, own_columns(n_dp, gu_ref, down_ref, 0), ring_outs, *refs)
        dy_spread = TeamSpread(n_dp, [dy_ref], [dy_blocks], dy_send, dy_recv)
        x_spread = TeamSpread(n_dp, [normed_v], [x_blocks], x_send, x_recv)
        group = pl.program_id(0)
        mask = causal_tile(tile)
        flags = [seen_ref[k] == 1 for k in range(blocks)]
        load = pltpu.make_async_copy(wo_ref, wo_v, load_sem)

        @pl.when(group == 0)
        def _():
            greet(ring.partners + dy_spread.partners())
            ring.first()
            dy_spread.start(0)
            load.start()

        lax.fori_loop(
            2 + group * early // pairs,
            2 + (group + 1) * early // pairs,
            lambda t, c: (ring.tick(t), c)[1],
            0,
        )
        key, value = head_of(k_ref[...], group), head_of(v_ref[...], group)
        key_far, value_far = head_of(kf_ref[...], group), head_of(vf_ref[...], group)
        value_t = value.astype(F32).T.astype(BF)
        value_far_t = value_far.astype(F32).T.astype(BF)
        for head in range(2):
            down = pl.ds(pl.multiple_of(group * 128 + head * HD, HD), HD)
            for at in range(0, span, tile):
                end = at + tile
                q = q_ref[at:end, head * HD : (head + 1) * HD]
                own, other = scores_of(key[:end], key_far, q, flags, mask, span)
                peak = jnp.maximum(jnp.max(own, 0, keepdims=True), jnp.max(other, 0, keepdims=True))
                own = jnp.exp(own - peak)
                other = jnp.exp(other - peak)
                total = jnp.sum(own, 0, keepdims=True) + jnp.sum(other, 0, keepdims=True)
                scale = 1.0 / total
                result = dot_nn(value_t[:, :end], (own * scale).astype(BF)) + dot_nn(
                    value_far_t, (other * scale).astype(BF)
                )
                attn_v[down, at:end] = result.astype(BF)
                lse_ref[0, head : head + 1, at:end] = peak + jnp.log(total)

        @pl.when(group == pairs - 1)
        def _():
            saves = [
                pltpu.make_async_copy(a, b, save_sems.at[k])
                for k, (a, b) in enumerate([(attn_v, attn_out), (hidden_v, hidden_out), (normed_v, normed_out)])
            ]
            saves[0].start()
            load.wait()
            square = jnp.zeros((span, 1), F32)
            for at in range(0, width, chunk):
                lanes = slice(at, at + chunk)
                hidden = x_ref[:, lanes].astype(F32) + dot_tn(attn_v[...], wo_v[:, lanes])
                hidden_v[:, lanes] = hidden
                square = square + jnp.sum(hidden * hidden, -1, keepdims=True)
            scale = lax.rsqrt(square / width + EPS)
            place, device = ring_place(n_fsdp)
            for slot in range(n):
                there = device((place + n - slot) % n)
                part = slot_lanes(hidden_v, there["fsdp"] * n_ctx + there["ctx"], rows)
                normed = part * scale * gains_ref[slot, 1:2, :].astype(F32)
                normed_v[:, slot * rows : (slot + 1) * rows] = normed.astype(BF)
            x_spread.start(0)
            saves[1].start()
            saves[2].start()
            dy_spread.arrive(0)
            dy_spread.start(1)
            middle = max(2 + early, n - 2)
            for t in range(2 + early, middle):
                ring.tick(t)
            x_spread.arrive(0)
            x_spread.start(1)
            for t in range(middle, n):
                ring.tick(t)
            dy_spread.arrive(1)
            x_spread.arrive(1)
            ring.last()
            dy_spread.last()
            x_spread.last()
            for copy in saves:
                copy.wait()

    pair = lambda high, shift: pl.BlockSpec((high, 128), lambda i: (0, i // 4 + shift))
    dma = pltpu.SemaphoreType.DMA
    block = jax.ShapeDtypeStruct((span, width), BF)
    out = pl.pallas_call(
        kernel,
        grid=(pairs,),
        in_specs=[
            pl.BlockSpec(memory_space=pltpu.SMEM),
            pl.BlockSpec((span, 128), lambda i: (0, i)),
            pair(span, near),
            pair(span, near + kvpairs),
            pair(far, 0),
            pair(far, kvpairs),
            pl.BlockSpec((span, width), lambda i: (0, 0)),
            pl.BlockSpec(gains.shape, lambda i: (0, 0, 0)),
        ]
        + [ANY] * 4,
        out_specs=[pl.BlockSpec((1, 8, span), lambda i: (i, 0, 0))] + [ANY] * (5 + 2 * others),
        out_shape=[
            jax.ShapeDtypeStruct((pairs, 8, span), F32),
            jax.ShapeDtypeStruct((qwidth, span), BF),
            jax.ShapeDtypeStruct((span, width), F32),
        ]
        + [block] * (1 + 2 * others)
        + [jax.ShapeDtypeStruct((width, wide), BF)] * 2,
        scratch_shapes=[
            pltpu.VMEM((qwidth, span), BF),
            pltpu.VMEM((qwidth, width), BF),
            pltpu.VMEM((span, width), F32),
            pltpu.VMEM((span, width), BF),
            dma(()),
            dma((3,)),
        ]
        + spread_scratch(1, n_dp)
        + spread_scratch(1, n_dp)
        + gather_scratch(n, rows, wide),
        compiler_params=pltpu.CompilerParams(
            collective_id=5, has_side_effects=True, vmem_limit_bytes=48 * MIB
        ),
        cost_estimate=cost(pairs * 2 * span * (span + far) * 128 * 4, 30 * MIB),
    )(seen, qkv, qkv, qkv, kv_far, kv_far, x, gains, w_out, dy, w_gate_up, w_down)
    lse, attn, hidden, normed = out[:4]
    return attn, lse, hidden, normed, out[4 : 4 + others], out[4 + others : 4 + 2 * others], out[4 + 2 * others :]


def attend_backward(sizes, qkv, kv_far, d_attn, lse, seen, tables, attn_t, d_proj, normed, ring_parts, sums, ident):
    n_dp, n_fsdp, n_ctx = sizes
    n = n_fsdp * n_ctx
    span, far = qkv.shape[0], kv_far.shape[0]
    blocks = far // span
    qwidth, kvwidth = HEADS * HD, KV_HEADS * HD
    near, kvpairs = qwidth // 128, kvwidth // 128
    pairs = HEADS // 2
    tile = min(span, 256)
    rows, wide = ring_parts[0].shape[0] // n, ring_parts[0].shape[1]
    early = 4 * (n - 2) // 7
    width = normed.shape[1]
    qkvwidth = qwidth + 2 * kvwidth
    part = max(rows, 128)
    others = n_dp - 1

    def kernel(seen_ref, q_ref, k_ref, v_ref, kf_ref, vf_ref, d_ref, lse_ref, cos_ref, low_ref, high_ref, *refs):
        refs = list(refs)

        def take(count):
            out = refs[:count]
            del refs[:count]
            return out

        attn_ref, proj_ref, normed_ref = take(3)
        parts, own_sums = take(2), take(2)
        dqkv_out, go_out, gq_out = take(3)
        ring_outs, blocks_out = take(2), take(2 * others)
        dqkv_v, dkv, dkv_far, give, got, save_sem, kv_send, kv_recv = take(8)
        attn_v, proj_v, normed_v, stage, load_sems, stage_sems = take(6)
        spread_send, spread_recv = take(2)
        ring = RingReduceNear(sizes, parts, ring_outs, *refs)
        spread = TeamSpread(
            n_dp, own_sums, [blocks_out[k * others : (k + 1) * others] for k in range(2)], spread_send, spread_recv
        )
        loads = [
            pltpu.make_async_copy(a, b, load_sems.at[k])
            for k, (a, b) in enumerate([(attn_ref, attn_v), (proj_ref, proj_v), (normed_ref, normed_v)])
        ]

        def product(out, cols, make):
            def write(g):
                return pltpu.make_async_copy(
                    stage.at[g % 2, :, pl.ds(0, cols)],
                    out.at[pl.ds(pl.multiple_of(g * part, part), part)],
                    stage_sems.at[g % 2],
                )

            def body(g, carry):
                @pl.when(g >= 2)
                def _():
                    write(g - 2).wait()

                stage[g % 2, :, :cols] = make(pl.ds(pl.multiple_of(g * part, part), part)).astype(BF)
                write(g).start()
                return carry

            count = width // part
            lax.fori_loop(0, count, body, 0)
            for g in range(max(0, count - 2), count):
                write(g).wait()

        ctx = lax.axis_index("ctx")
        group = pl.program_id(0)
        mask = causal_tile(tile)
        flags = [seen_ref[k] == 1 for k in range(blocks)]
        key, value = head_of(k_ref[...], group), head_of(v_ref[...], group)
        key_far, value_far = head_of(kf_ref[...], group), head_of(vf_ref[...], group)
        key_t = key.astype(F32).T.astype(BF)
        key_far_t = key_far.astype(F32).T.astype(BF)
        odd = (group // 2) % 2 == 1
        cosine, low, high = cos_ref[...], -low_ref[...], -high_ref[...]

        @pl.when(group == 0)
        def _():
            greet(ring.partners + [{"ctx": (ctx + k) % n_ctx} for k in range(1, n_ctx)] + spread.partners())
            ring.first()
            spread.start(0)
            for copy in loads:
                copy.start()
            dkv[...] = jnp.zeros_like(dkv)
            dkv_far[...] = jnp.zeros_like(dkv_far)

        @pl.when(group == pairs - 4)
        def _():
            spread.arrive(0)
            spread.start(1)

        lax.fori_loop(
            2 + group * early // pairs,
            2 + (group + 1) * early // pairs,
            lambda t, c: (ring.tick(t), c)[1],
            0,
        )

        def put(ref, size, shift, add):
            zero = jnp.zeros_like(add)
            lanes = pl.ds(pl.multiple_of(group // 4 * 128 + shift, 128), 128)
            ref[0:size, lanes] += jnp.concatenate([jnp.where(odd, zero, add), jnp.where(odd, add, zero)], 1)

        for at in range(0, span, tile):
            end = at + tile
            turned = []
            for head in range(2):
                lanes = slice(head * HD, (head + 1) * HD)
                q = q_ref[at:end, lanes]
                d = d_ref[at:end, lanes]
                own, other = scores_of(key[:end], key_far, q, flags, mask, span)
                base = lse_ref[0, head : head + 1, at:end]
                own = jnp.exp(own - base)
                other = jnp.exp(other - base)
                d_own = dot_nt(value[:end], d)
                d_other = dot_nt(value_far, d)
                delta = jnp.sum(own * d_own, 0, keepdims=True) + jnp.sum(other * d_other, 0, keepdims=True)
                ds_own = (own * (d_own - delta)).astype(BF)
                ds_other = (other * (d_other - delta)).astype(BF)
                put(dkv, end, kvwidth, dot_nn(own.astype(BF), d))
                put(dkv_far, far, kvwidth, dot_nn(other.astype(BF), d))
                put(dkv, end, 0, dot_nn(ds_own, q))
                put(dkv_far, far, 0, dot_nn(ds_other, q))
                turned.append(dot_nn(key_t[:, :end], ds_own) + dot_nn(key_far_t, ds_other))
            d_query = jnp.concatenate(turned, 0).T * HD**-0.5
            dqkv_v[at:end, pl.ds(pl.multiple_of(group * 128, 128), 128)] = turn(
                d_query, cosine[at:end], low[at:end], high[at:end]
            ).astype(BF)

        @pl.when(group == pairs - 1)
        def _():
            give[...] = dkv_far[...].astype(BF)

            def back(k):
                return pltpu.make_async_remote_copy(
                    src_ref=give.at[pl.ds((k - 1) * span, span)],
                    dst_ref=got.at[k - 1],
                    send_sem=kv_send.at[k],
                    recv_sem=kv_recv.at[k],
                    device_id={"ctx": (ctx + k) % n_ctx},
                    device_id_type=MESH,
                )

            for k in range(1, n_ctx):
                back(k).start()
            middle = (2 + early + n) // 2
            for t in range(2 + early, middle):
                ring.tick(t)
            for copy in loads:
                copy.wait()
            product(go_out, qwidth, lambda at: dot_nn(attn_v[at, :], proj_v[...]))
            for k in range(1, n_ctx):
                back(k).wait_recv()
            for at in range(0, 2 * kvwidth, 128):
                piece = dkv[:, at : at + 128]
                for k in range(1, n_ctx):
                    piece = piece + got[k - 1, :, at : at + 128].astype(F32)
                if at < kvwidth:
                    piece = turn(piece, cosine, low, high)
                dqkv_v[:, qwidth + at : qwidth + at + 128] = piece.astype(BF)
            save = pltpu.make_async_copy(dqkv_v, dqkv_out, save_sem)
            save.start()
            for t in range(middle, n - 1):
                ring.tick(t)
            product(gq_out, qkvwidth, lambda at: dot_tn(normed_v[:, at], dqkv_v[...]))
            ring.tick(n - 1)
            spread.arrive(1)
            ring.last()
            spread.last()
            for k in range(1, n_ctx):
                back(k).wait_send()
            save.wait()

    pair = lambda high, shift: pl.BlockSpec((high, 128), lambda i: (0, i // 4 + shift))
    wide_block = pl.BlockSpec((span, 128), lambda i: (0, i))
    table = pl.BlockSpec((span, 128), lambda i: (0, 0))
    dma = pltpu.SemaphoreType.DMA
    out = pl.pallas_call(
        kernel,
        grid=(pairs,),
        in_specs=[
            pl.BlockSpec(memory_space=pltpu.SMEM),
            wide_block,
            pair(span, near),
            pair(span, near + kvpairs),
            pair(far, 0),
            pair(far, kvpairs),
            wide_block,
            pl.BlockSpec((1, 8, span), lambda i: (i, 0, 0)),
            table,
            table,
            table,
        ]
        + [ANY] * 7,
        out_specs=[ANY] * (5 + 2 * others),
        out_shape=[
            jax.ShapeDtypeStruct((span, qkvwidth), BF),
            jax.ShapeDtypeStruct((width, qwidth), BF),
            jax.ShapeDtypeStruct((width, qkvwidth), BF),
        ]
        + [jax.ShapeDtypeStruct((rows, wide), BF)] * (2 + 2 * others),
        scratch_shapes=[
            pltpu.VMEM((span, qwidth + 2 * kvwidth), BF),
            pltpu.VMEM((span, 2 * kvwidth), F32),
            pltpu.VMEM((far, 2 * kvwidth), F32),
            pltpu.VMEM((far, 2 * kvwidth), BF),
            pltpu.VMEM((n_ctx - 1, span, 2 * kvwidth), BF),
            dma(()),
            dma((n_ctx,)),
            dma((n_ctx,)),
            pltpu.VMEM(attn_t.shape, BF),
            pltpu.VMEM(d_proj.shape, BF),
            pltpu.VMEM(normed.shape, BF),
            pltpu.VMEM((2, part, max(qwidth, qkvwidth)), BF),
            dma((3,)),
            dma((2,)),
        ]
        + spread_scratch(2, n_dp)
        + near_scratch(n, rows, wide),
        compiler_params=pltpu.CompilerParams(
            collective_id=ident, has_side_effects=True, vmem_limit_bytes=40 * MIB
        ),
        cost_estimate=cost(pairs * 2 * span * (span + far) * 128 * 10, 30 * MIB),
    )(seen, qkv, qkv, qkv, kv_far, kv_far, d_attn, lse, *tables, attn_t, d_proj, normed, *ring_parts, *sums)
    return out[0], out[1], out[2], out[3:5], [out[5 + k * others : 5 + (k + 1) * others] for k in range(2)]


def opening(sizes, x, w_qkv, w_out, gains, tables):
    n_dp, n_fsdp, n_ctx = sizes
    n = n_fsdp * n_ctx
    span, width = x.shape
    rows = width // n
    share, half = w_qkv.shape[1] // n_dp, w_out.shape[1] // 2
    qwidth, kvwidth = HEADS * HD, KV_HEADS * HD
    qkvwidth = qwidth + 2 * kvwidth
    chunk = share // 2 if share % 256 == 0 else share
    across_x = n_dp > 2

    def kernel(x_ref, wq_ref, wo_ref, g_ref, cos_ref, low_ref, high_ref, *refs):
        refs = list(refs)

        def take(count):
            out = refs[:count]
            del refs[:count]
            return out

        qkv_out, far_out, xs_out, wq_out, wo_out, gains_out = take(6)
        qkv_v, far_v, xs_v = take(3)
        wq_v = take(n_dp)
        om_v, oo_v, gains_v = take(3)
        load_sems, save_sems, wq_sems, wo_sems = take(4)
        send, recv, x_send, x_recv, c_send, c_recv, o_send, o_recv = take(8)
        gain_send, gain_recv, kv_send, kv_recv = take(4)
        me = lax.axis_index("dp")
        core = me % 2
        sibling = {"dp": team_place(n_dp, me, 1)}
        facing = {"dp": team_place(n_dp, me, n_dp // 2)}
        bases = [me, team_place(n_dp, me, n_dp // 2)] if across_x else [me]
        bases = [b * share for b in bases + [team_place(n_dp, b, 1) for b in bases]]
        held = n_dp // 2
        place, device = ring_place(n_fsdp)
        ahead, behind = device((place + 1) % n), device((place + n - 1) % n)
        mine = (wq_v[0], om_v)
        widths = (share, half)

        def block_of(slot):
            there = device((place + n - slot) % n)
            return there["fsdp"] * n_ctx + there["ctx"]

        loads = [
            pltpu.make_async_copy(
                ref.at[:, pl.ds(pl.multiple_of(at, 128), w)], mine[k].at[pl.ds(0, rows)], load_sems.at[k]
            )
            for k, (ref, at, w) in enumerate(((wq_ref, me * share, share), (wo_ref, core * half, half)))
        ] + [pltpu.make_async_copy(g_ref, gains_v.at[0], load_sems.at[2])]
        for copy in loads:
            copy.start()
        ctx = lax.axis_index("ctx")
        greet(
            [ahead, behind, sibling]
            + ([facing] if across_x else [])
            + [{"ctx": (ctx + k) % n_ctx} for k in range(1, n_ctx)]
        )

        def lanes(k, way):
            return pl.ds(way * (widths[k] // 2), widths[k] // 2)

        def remote(source, target, send_sem, recv_sem, partner):
            return pltpu.make_async_remote_copy(
                src_ref=source,
                dst_ref=target,
                send_sem=send_sem,
                recv_sem=recv_sem,
                device_id=partner,
                device_id_type=MESH,
            )

        def step(k, way, t):
            here = t - 1 if way == 0 else (n - t + 1) % n
            there = t if way == 0 else n - t
            return remote(
                mine[k].at[pl.ds(here * rows, rows), lanes(k, way)],
                mine[k].at[pl.ds(there * rows, rows), lanes(k, way)],
                send.at[k, way, t],
                recv.at[k, way, t],
                ahead if way == 0 else behind,
            )

        def over_x(way, slot):
            at = (pl.ds(slot * rows, rows), lanes(0, way))
            return remote(wq_v[0].at[at], wq_v[1].at[at], x_send.at[way, slot], x_recv.at[way, slot], facing)

        def over_core(b, way, slot):
            at = (pl.ds(slot * rows, rows), lanes(0, way))
            return remote(
                wq_v[b].at[at], wq_v[held + b].at[at], c_send.at[b, way, slot], c_recv.at[b, way, slot], sibling
            )

        def out_over(way, slot):
            at = (pl.ds(slot * rows, rows), lanes(1, way))
            return remote(om_v.at[at], oo_v.at[at], o_send.at[way, slot], o_recv.at[way, slot], sibling)

        def gain_step(t):
            return remote(gains_v.at[t - 1], gains_v.at[t], gain_send.at[t], gain_recv.at[t], ahead)

        def kv_step(k):
            return remote(
                qkv_v.at[:, pl.ds(qwidth, 2 * kvwidth)],
                far_v.at[pl.ds((k - 1) * span, span)],
                kv_send.at[k],
                kv_recv.at[k],
                {"ctx": (ctx + n_ctx - k) % n_ctx},
            )

        def give(way, slot):
            if across_x:
                over_x(way, slot).start()
            over_core(0, way, slot).start()

        f32 = x_ref[...].astype(F32)
        scale = lax.rsqrt(jnp.mean(f32 * f32, -1, keepdims=True) + EPS)

        def normalize(slot):
            part = slot_lanes(x_ref, block_of(slot), rows)
            xs_v[:, slot * rows : (slot + 1) * rows] = (
                part * scale * gains_v[slot, 0:1, :].astype(F32)
            ).astype(BF)

        loads[0].wait()
        loads[2].wait()
        gain_step(1).start()
        for way in range(2):
            step(0, way, 1).start()
        loads[1].wait()
        for way in range(2):
            give(way, 0)
        normalize(0)
        for t in range(1, n):
            gain_step(t).wait_recv()
            if t < n - 1:
                gain_step(t + 1).start()
            for way in range(2):
                step(0, way, t).wait_recv()
                if t < n - 1:
                    step(0, way, t + 1).start()
                give(way, t if way == 0 else n - t)
            normalize(t)

        for way in range(2):
            step(1, way, 1).start()
            out_over(way, 0).start()

        def out_tick(t):
            for way in range(2):
                step(1, way, t).wait_recv()
                if t < n - 1:
                    step(1, way, t + 1).start()
                out_over(way, t if way == 0 else n - t).start()

        order = [(way, 0) for way in range(2)]
        for t in range(1, n):
            order += [(0, t), (1, n - t)]
        cosine, low, high = cos_ref[...], low_ref[...], high_ref[...]

        def form(b, at):
            value = dot_nn(xs_v[...], wq_v[b][:, at : at + chunk])
            for part in range(0, chunk, 128):
                piece = value[:, part : part + 128]
                here = bases[b] + at + part
                piece = jnp.where(here >= qwidth + kvwidth, piece, turn(piece, cosine, low, high))
                piece = piece * jnp.where(here < qwidth, HD**-0.5, 1.0)
                qkv_v[:, pl.ds(pl.multiple_of(here, 128), 128)] = piece.astype(BF)

        def save_share(b):
            return [
                pltpu.make_async_copy(
                    wq_v[b].at[pl.ds(slot * rows, rows)],
                    wq_out.at[
                        pl.ds(pl.multiple_of(block_of(slot) * rows, rows), rows),
                        pl.ds(pl.multiple_of(bases[b], 128), share),
                    ],
                    wq_sems.at[b, slot],
                )
                for slot in range(n)
            ]

        def save_half(k):
            whose = core if k == 0 else 1 - core
            return [
                pltpu.make_async_copy(
                    (om_v, oo_v)[k].at[pl.ds(slot * rows, rows)],
                    wo_out.at[
                        pl.ds(pl.multiple_of(block_of(slot) * rows, rows), rows),
                        pl.ds(pl.multiple_of(whose * half, 128), half),
                    ],
                    wo_sems.at[k, slot],
                )
                for slot in range(n)
            ]

        def go(copies):
            for copy in copies:
                copy.start()

        jobs = [lambda at=at: form(0, at) for at in range(0, share, chunk)]
        jobs.append(lambda: go(save_share(0)))

        def core_shares(b):
            for way, slot in order:
                over_core(b, way, slot).wait_recv()
            go(save_share(held + b))

        jobs.append(lambda: core_shares(0))
        jobs += [lambda at=at: form(held, at) for at in range(0, share, chunk)]
        if across_x:

            def relay(way, slot):
                over_x(way, slot).wait_recv()
                over_core(1, way, slot).start()

            jobs += [lambda w=way, k=slot: relay(w, k) for way, slot in order]
            jobs.append(lambda: go(save_share(1)))
            jobs += [lambda at=at: form(1, at) for at in range(0, share, chunk)]
            jobs.append(lambda: core_shares(1))
            jobs += [lambda at=at: form(held + 1, at) for at in range(0, share, chunk)]
        for k, job in enumerate(jobs):
            job()
            for t in range(1 + k * (n - 1) // len(jobs), 1 + (k + 1) * (n - 1) // len(jobs)):
                out_tick(t)
        for j in range(1, n_ctx):
            kv_step(j).start()
        saves = [
            pltpu.make_async_copy(a, b, save_sems.at[k])
            for k, (a, b) in enumerate([(qkv_v, qkv_out), (far_v, far_out), (xs_v, xs_out), (gains_v, gains_out)])
        ]
        for k in (0, 2, 3):
            saves[k].start()
        go(save_half(0))
        for way, slot in order:
            out_over(way, slot).wait_recv()
        go(save_half(1))
        for j in range(1, n_ctx):
            kv_step(j).wait_recv()
        saves[1].start()
        for t in range(1, n):
            gain_step(t).wait_send()
            for way in range(2):
                for k in range(2):
                    step(k, way, t).wait_send()
        for way, slot in order:
            out_over(way, slot).wait_send()
            for b in range(held):
                over_core(b, way, slot).wait_send()
            if across_x:
                over_x(way, slot).wait_send()
        for j in range(1, n_ctx):
            kv_step(j).wait_send()
        for copies in [save_share(b) for b in range(n_dp)] + [save_half(k) for k in range(2)] + [saves]:
            for copy in copies:
                copy.wait()

    dma = pltpu.SemaphoreType.DMA
    shapes = [
        (span, qkvwidth),
        ((n_ctx - 1) * span, 2 * kvwidth),
        (span, width),
        (width, qkvwidth),
        (width, 2 * half),
        (n, 16, rows),
    ]
    return pl.pallas_call(
        kernel,
        in_specs=[WHOLE, ANY, ANY, ANY, WHOLE, WHOLE, WHOLE],
        out_specs=[ANY] * 6,
        out_shape=[jax.ShapeDtypeStruct(shape, BF) for shape in shapes],
        scratch_shapes=[pltpu.VMEM(shape, BF) for shape in shapes[:3]]
        + [pltpu.VMEM((width, share), BF)] * n_dp
        + [pltpu.VMEM((width, half), BF)] * 2
        + [pltpu.VMEM((n, 16, rows), BF)]
        + [
            dma((3,)),
            dma((4,)),
            dma((n_dp, n)),
            dma((2, n)),
            dma((2, 2, n)),
            dma((2, 2, n)),
            dma((2, n)),
            dma((2, n)),
            dma((n_dp // 2, 2, n)),
            dma((n_dp // 2, 2, n)),
            dma((2, n)),
            dma((2, n)),
            dma((n,)),
            dma((n,)),
            dma((n_ctx,)),
            dma((n_ctx,)),
        ],
        compiler_params=pltpu.CompilerParams(
            collective_id=0, has_side_effects=True, vmem_limit_bytes=56 * MIB
        ),
        cost_estimate=cost(2 * span * width * qkvwidth, 4 * width * qkvwidth),
    )(x, w_qkv, w_out, gains, *tables)


def closing(sizes, fulls, slotted, sums):
    n_dp, n_fsdp, n_ctx = sizes
    n = n_fsdp * n_ctx
    rows = [f.shape[0] // n for f in fulls]
    widths = [f.shape[1] // 2 for f in fulls]
    kinds = [f.dtype for f in fulls]
    count = len(fulls)
    bits = [1 << k for k in range(1, n_dp.bit_length() - 1)]
    others = n_dp - 1

    def kernel(*refs):
        refs = list(refs)

        def take(size):
            out = refs[:size]
            del refs[:size]
            return out

        full, own_sums = take(count), take(len(sums))
        outs, blocks_out = take(count), take(len(sums) * others)
        near, land, done, extra, back = take(count), take(count), take(count), take(count), take(count)
        send, recv, pair_send, pair_recv, x_send, x_recv, end_send, end_recv = take(8)
        spread = TeamSpread(
            n_dp, own_sums, [blocks_out[k * others : (k + 1) * others] for k in range(len(sums))], *refs
        )
        me = lax.axis_index("dp")
        core = me % 2
        sibling = {"dp": me + 1 - 2 * core}
        place, device = ring_place(n_fsdp)
        ahead, behind = device((place + 1) % n), device((place + n - 1) % n)
        facing = [{"dp": me + bit - 2 * bit * ((me // bit) % 2)} for bit in bits]
        greet([ahead, behind, sibling] + facing)

        def half(g, way):
            return pl.ds(way * (widths[g] // 2), widths[g] // 2)

        def half_of(g, way, whose):
            base = whose * widths[g] + way * (widths[g] // 2)
            return pl.ds(pl.multiple_of(base, 128), widths[g] // 2)

        def at(g, slot):
            return pl.ds(slot * rows[g], rows[g])

        def source_at(g, slot):
            if slotted[g]:
                return at(g, slot)
            there = device((place + n - slot) % n)
            block = there["fsdp"] * n_ctx + there["ctx"]
            return pl.ds(pl.multiple_of(block * rows[g], rows[g]), rows[g])

        def swap(g, way, slot):
            return pltpu.make_async_remote_copy(
                src_ref=full[g].at[source_at(g, slot), half_of(g, way, 1 - core)],
                dst_ref=near[g].at[at(g, slot), half(g, way)],
                send_sem=pair_send.at[g, way, slot],
                recv_sem=pair_recv.at[g, way, slot],
                device_id=sibling,
                device_id_type=MESH,
            )

        def step(g, way, t):
            slot = t if way == 0 else n - t
            source = near[g].at[at(g, slot), half(g, way)] if t == 1 else land[g].at[way, t - 2]
            return pltpu.make_async_remote_copy(
                src_ref=source,
                dst_ref=land[g].at[way, t - 1],
                send_sem=send.at[g, way, t],
                recv_sem=recv.at[g, way, t],
                device_id=ahead if way == 0 else behind,
                device_id_type=MESH,
            )

        def face(g, k):
            return pltpu.make_async_remote_copy(
                src_ref=done[g].at[k],
                dst_ref=extra[g].at[k],
                send_sem=x_send.at[g, k],
                recv_sem=x_recv.at[g, k],
                device_id=facing[k],
                device_id_type=MESH,
            )

        def end(g):
            return pltpu.make_async_remote_copy(
                src_ref=done[g].at[len(bits)],
                dst_ref=back[g],
                send_sem=end_send.at[g],
                recv_sem=end_recv.at[g],
                device_id=sibling,
                device_id_type=MESH,
            )

        for t in list(range(1, n)) + [0]:
            for g in range(count):
                swap(g, 0, t).start()
                swap(g, 1, (n - t) % n).start()
        spread.start(0)
        for t in range(1, n):
            for g in range(count):
                for way in range(2):
                    slot = t if way == 0 else n - t
                    swap(g, way, slot).wait_recv()
                    cols = half(g, way)
                    value = full[g][source_at(g, slot), half_of(g, way, core)].astype(F32)
                    value = value + near[g][at(g, slot), cols].astype(F32)
                    if t == 1:
                        near[g][at(g, slot), cols] = value.astype(kinds[g])
                    else:
                        step(g, way, t - 1).wait_recv()
                        land[g][way, t - 2] = (value + land[g][way, t - 2].astype(F32)).astype(kinds[g])
                    step(g, way, t).start()
            if t == n - 2:
                spread.arrive(0)
                spread.start(1)
        for g in range(count):
            for way in range(2):
                swap(g, way, 0).wait_recv()
                step(g, way, n - 1).wait_recv()
                cols = half(g, way)
                value = full[g][source_at(g, 0), half_of(g, way, core)].astype(F32)
                value = value + near[g][at(g, 0), cols].astype(F32)
                done[g][0, :, cols] = (value + land[g][way, n - 2].astype(F32)).astype(kinds[g])
            if bits:
                face(g, 0).start()
        for k in range(len(bits)):
            for g in range(count):
                face(g, k).wait_recv()
                done[g][k + 1] = (done[g][k].astype(F32) + extra[g][k].astype(F32)).astype(kinds[g])
                if k + 1 < len(bits):
                    face(g, k + 1).start()
        for g in range(count):
            end(g).start()
            here = pl.ds(pl.multiple_of(core * widths[g], 128), widths[g])
            outs[g][:, here] = done[g][len(bits)].astype(F32)
        for g in range(count):
            end(g).wait_recv()
            here = pl.ds(pl.multiple_of((1 - core) * widths[g], 128), widths[g])
            outs[g][:, here] = back[g][...].astype(F32)
        spread.arrive(1)
        spread.last()
        for g in range(count):
            end(g).wait_send()
            for k in range(len(bits)):
                face(g, k).wait_send()
            for way in range(2):
                for t in range(1, n):
                    step(g, way, t).wait_send()
                for slot in range(n):
                    swap(g, way, slot).wait_send()

    dma = pltpu.SemaphoreType.DMA
    groups = list(zip(rows, widths, kinds))
    out = pl.pallas_call(
        kernel,
        in_specs=[WHOLE] * count + [ANY] * len(sums),
        out_specs=[WHOLE] * count + [ANY] * (len(sums) * others),
        out_shape=[jax.ShapeDtypeStruct((r, 2 * w), F32) for r, w, _ in groups]
        + [jax.ShapeDtypeStruct(a.shape, BF) for a in sums for _ in range(others)],
        scratch_shapes=[pltpu.VMEM((n * r, w), kind) for r, w, kind in groups]
        + [pltpu.VMEM((2, n - 1, r, w // 2), kind) for r, w, kind in groups]
        + [pltpu.VMEM((len(bits) + 1, r, w), kind) for r, w, kind in groups]
        + [pltpu.VMEM((max(1, len(bits)), r, w), kind) for r, w, kind in groups]
        + [pltpu.VMEM((r, w), kind) for r, w, kind in groups]
        + [
            dma((count, 2, n)),
            dma((count, 2, n)),
            dma((count, 2, n)),
            dma((count, 2, n)),
            dma((count, max(1, len(bits)))),
            dma((count, max(1, len(bits)))),
            dma((count,)),
            dma((count,)),
        ]
        + spread_scratch(len(sums), n_dp),
        compiler_params=pltpu.CompilerParams(
            collective_id=1, has_side_effects=True, vmem_limit_bytes=60 * MIB
        ),
        cost_estimate=cost(0, sum(12 * n * r * w for r, w, _ in groups)),
    )(*fulls, *sums)
    return out[:count], [out[count + k * others : count + (k + 1) * others] for k in range(len(sums))]


class Ring:
    def __init__(self, n_fsdp, n_ctx):
        order = []
        for c in range(n_ctx):
            rows = range(n_fsdp) if c % 2 == 0 else reversed(range(n_fsdp))
            order += [f * n_ctx + c for f in rows]
        self.order = order
        self.size = n = len(order)
        place = [0] * n
        for k, block in enumerate(order):
            place[block] = k
        self.place = place
        self.block = lax.axis_index(GRID)
        self.rank = jnp.array(place, jnp.int32)[self.block]

    def slot_blocks(self):
        slots = jnp.arange(self.size, dtype=jnp.int32)
        return jnp.array(self.order, jnp.int32)[(self.rank - slots) % self.size]

    def to_slots(self, array, axis=1, deps=()):
        return reorder(array, self.slot_blocks(), axis, deps)

    def from_slots(self, array, axis=1):
        return reorder(array, (self.rank - jnp.array(self.place, jnp.int32)) % self.size, axis)


class Team:
    def __init__(self, size):
        self.size = size
        self.rank = lax.axis_index("dp")
        self.bits = [1 << k for k in range(size.bit_length() - 1)]
        self.order = [0]
        for bit in reversed(self.bits):
            self.order = self.order + [m ^ bit for m in self.order]

    def swap(self, value, bit):
        return lax.ppermute(value, "dp", [(k, k ^ bit) for k in range(self.size)])

    def scatter(self, parts):
        for bit in self.bits:
            half = len(parts) // 2
            got = [self.swap(part.astype(BF), bit) for part in parts[half:]]
            parts = [kept + part.astype(F32) for kept, part in zip(parts[:half], got)]
        return parts[0]


def shards(sizes, x_in, span_order, attn_gain, w_qkv, w_out, ffn_gain, w_gate_up, w_down, cotangent):
    n_dp, n_fsdp, n_ctx = sizes
    ring = Ring(n_fsdp, n_ctx)
    team = Team(n_dp)
    n = ring.size
    width = x_in.shape[-1]
    rows = width // n
    tokens = x_in.reshape(-1, width)
    span = tokens.shape[0]
    rank = lax.axis_index("ctx")
    qwidth = HEADS * HD
    kvwidth = KV_HEADS * HD
    ffwidth = w_down.shape[1]
    order = span_order.reshape(-1)
    near = [(rank + k) % n_ctx for k in range(n_ctx)]
    offsets = jnp.arange(span, dtype=jnp.int32)
    query_pos = order[rank] * span + offsets
    seen = jnp.stack([order[c] < order[rank] for c in near[1:]]).astype(jnp.int32)
    tables = rope_tables(query_pos.astype(F32))

    ffq = ffwidth // n_dp
    sub = ffq // SUBS
    grad_y = cotangent.reshape(span, width)
    dy = ring.to_slots(grad_y)
    gains = jnp.concatenate([attn_gain[None], ffn_gain[None], jnp.zeros((14, rows), BF)], 0)
    qkv, kv_far, normed_one, wqkv, wout, gains = opening(sizes, tokens, w_qkv, w_out, gains, tables)
    attn_t, lse, hidden_one, normed_two, x_others, dy_others, weights_a = attend_forward(
        sizes, tokens, qkv, kv_far, seen, wout, gains, dy, w_gate_up, w_down
    )
    xs = [normed_two] + list(x_others)
    dys = [dy] + list(dy_others)
    gains = gains[:, :2][(ring.rank - jnp.array(ring.place, jnp.int32)) % n]
    gain_one = gains[:, 0].reshape(-1).astype(F32)
    gain_two = gains[:, 1].reshape(-1).astype(F32)
    inputs = tokens.astype(F32)
    scale_one = inv_rms(inputs)
    scale_two = inv_rms(hidden_one)

    y, dn, grads_a, weights_b = feed_forward(
        sizes, xs, dys, [[w] for w in weights_a], None, (w_gate_up, w_down), False, 2
    )
    y, dn, grads_b, sums_a = feed_forward(
        sizes, xs, dys, [[w] for w in weights_b], list(zip(y, dn)), grads_a, True, 3
    )

    d_normed_two = ring.from_slots(sum(part.astype(F32) for part in dn))
    d_hidden_norm, d_gain_two = norm_back(hidden_one, scale_two, gain_two, d_normed_two)
    d_hidden = grad_y.astype(F32) + d_hidden_norm
    d_proj = d_hidden.astype(BF)

    d_attn = matmul_rows(d_proj, wout).astype(BF)
    d_qkv, part_out, part_qkv, sums_b, others_a = attend_backward(
        sizes, qkv, kv_far, d_attn, lse, seen, tables, attn_t, d_proj, normed_one, grads_b, sums_a, 4
    )
    d_normed_one = matmul_rows(d_qkv, wqkv)
    d_input_norm, d_gain_one = norm_back(inputs, scale_one, gain_one, d_normed_one)
    grad_input = d_hidden + d_input_norm

    room = max(rows, 256)

    def by_slot(gain):
        blocks = gain.reshape(n, 1, rows)[ring.slot_blocks()]
        return jnp.pad(blocks, ((0, 0), (0, 7), (0, room - rows))).reshape(n * 8, room)

    part_gain = jnp.concatenate([by_slot(d_gain_one), by_slot(d_gain_two)], 1)
    (grad_qkv, grad_out, grad_gain), others_b = closing(
        sizes, (part_qkv, part_out, part_gain), (True, False, True), sums_b
    )

    placed, columns = [], []
    for q in range(SUBS):
        blocks = [sums_a[q]] + list(others_a[q]) if q < 2 else [sums_b[q - 2]] + list(others_b[q - 2])
        for m, block in zip(team.order, blocks):
            placed.append(block)
            columns.append((team.rank ^ m) * ffq + q * sub)
    grad_gate_up, grad_down = place_grads(placed, jnp.stack(columns).astype(jnp.int32), sub, ffwidth)

    y_out = hidden_one + ring.from_slots(team.scatter(y))
    return (
        y_out.astype(BF).reshape(x_in.shape),
        grad_input.reshape(x_in.shape),
        grad_gain[0, :rows],
        grad_qkv,
        grad_out,
        grad_gain[0, room : room + rows],
        grad_gate_up,
        grad_down,
    )


def solution(mesh):
    sizes = (mesh.shape["dp"], mesh.shape["fsdp"], mesh.shape["ctx"])
    tokens = P(("dp", "fsdp"), "ctx", None)
    weight = P(("fsdp", "ctx"), None)
    gain = P(("fsdp", "ctx"))

    def body(*args):
        return shards(sizes, *args)

    return jax.shard_map(
        body,
        mesh=mesh,
        in_specs=(tokens, P(("dp", "fsdp"), None), gain, weight, weight, gain, weight, weight, tokens),
        out_specs=(tokens, tokens, gain, weight, weight, gain, weight, weight),
        check_vma=False,
    )
```

```python
import math

import jax
import jax.numpy as jnp
from jax import lax
from jax.experimental import pallas as pl
from jax.experimental.pallas import tpu as pltpu
from jax.sharding import PartitionSpec as P

HEADS = 32
KV_HEADS = 8
HD = 64
EPS = 1e-05
SUBS = 4

BF = jnp.bfloat16
F32 = jnp.float32
GRID = ("fsdp", "ctx")


def matmul(left, right):
    return jnp.dot(left, right, preferred_element_type=F32)


def matmul_rows(left, right):
    return lax.dot_general(left, right, (((1,), (1,)), ((), ())), preferred_element_type=F32)


def matmul_tokens(left, right):
    return lax.dot_general(left, right, (((0,), (0,)), ((), ())), preferred_element_type=F32)


def rope_tables(positions):
    half = HD // 2
    freq = jnp.exp(jnp.arange(half, dtype=F32) * (-math.log(500000.0) / half))
    angle = positions[:, None] * freq[None, :]
    cosine, sine = jnp.cos(angle), jnp.sin(angle)
    zero = jnp.zeros_like(sine)
    return (
        jnp.concatenate([cosine] * 4, -1),
        jnp.concatenate([-sine, zero] * 2, -1),
        jnp.concatenate([zero, sine] * 2, -1),
    )


def inv_rms(rows):
    return lax.rsqrt(jnp.mean(rows * rows, -1, keepdims=True) + EPS)


def norm_back(rows, scale, gain, grad):
    unit = rows * scale
    pulled = grad * gain[None, :]
    inner = jnp.mean(pulled * unit, -1, keepdims=True)
    return scale * (pulled - unit * inner), jnp.sum(grad * unit, 0)


MIB = 1 << 20
ANY = pl.BlockSpec(memory_space=pl.ANY)
WHOLE = pl.BlockSpec(memory_space=pltpu.VMEM)


def cost(flops, moved, exps=0):
    return pl.CostEstimate(flops=int(flops), bytes_accessed=int(moved), transcendentals=int(exps))


def params(mib):
    return pltpu.CompilerParams(vmem_limit_bytes=mib * MIB)


def dot_nn(a, b):
    return lax.dot_general(a, b, (((1,), (0,)), ((), ())), preferred_element_type=F32)


def dot_nt(a, b):
    return lax.dot_general(a, b, (((1,), (1,)), ((), ())), preferred_element_type=F32)


def dot_tn(a, b):
    return lax.dot_general(a, b, (((0,), (0,)), ((), ())), preferred_element_type=F32)


def reorder(array, places, axis=1, deps=()):
    count = places.shape[0]
    if axis == 1 and (array.shape[1] // count) % 128 != 0:
        size = array.shape[1] // count
        blocks = [lax.dynamic_slice_in_dim(array, places[s] * size, size, 1) for s in range(count)]
        return jnp.concatenate(blocks, 1)
    if axis == 1:
        shape = (array.shape[0], array.shape[1] // count)
        took = lambda s, where: (0, where[s])
        gave = lambda s, where: (0, s)
    else:
        shape = (array.shape[0] // count, array.shape[1])
        took = lambda s, where: (where[s], 0)
        gave = lambda s, where: (s, 0)

    def kernel(where, source, *rest):
        rest[-1][...] = source[...]

    return pl.pallas_call(
        kernel,
        grid_spec=pltpu.PrefetchScalarGridSpec(
            num_scalar_prefetch=1,
            grid=(count,),
            in_specs=[pl.BlockSpec(shape, took)] + [ANY] * len(deps),
            out_specs=pl.BlockSpec(shape, gave),
        ),
        out_shape=jax.ShapeDtypeStruct(array.shape, array.dtype),
        compiler_params=params(16),
        cost_estimate=cost(0, 2 * array.size * array.dtype.itemsize),
    )(places, array, *deps)


def turn(piece, cosine, sine_low, sine_high):
    return (
        piece * cosine
        + pltpu.roll(piece, 128 - HD // 2, axis=1) * sine_low
        + pltpu.roll(piece, HD // 2, axis=1) * sine_high
    )


def head_of(block, group):
    odd = (group // 2) % 2 == 1
    return jnp.where(odd, block[:, HD:], block[:, :HD])


def causal_tile(size):
    key = lax.broadcasted_iota(jnp.int32, (size, size), 0)
    query = lax.broadcasted_iota(jnp.int32, (size, size), 1)
    return key <= query


def scores_of(key, key_far, query, seen, mask, span):
    tile = query.shape[0]
    own = dot_nt(key, query)
    if key.shape[0] > tile:
        last = key.shape[0] - tile
        own = jnp.concatenate([own[:last], jnp.where(mask, own[last:], -1e30)], 0)
    else:
        own = jnp.where(mask, own, -1e30)
    far = dot_nt(key_far, query)
    far = [jnp.where(seen[k], far[k * span : (k + 1) * span], -1e30) for k in range(len(seen))]
    return own, (far[0] if len(far) == 1 else jnp.concatenate(far, 0))


def place_grads(pieces, columns, sub, ffwidth):
    rows = pieces[0].shape[0]
    count = len(pieces)

    def kernel(*refs):
        where = refs[0]
        sources = refs[1 : 1 + count]
        gu_ref, down_ref, took, gave, in_sems, out_sems = refs[1 + count :]

        def read(k):
            return pltpu.make_async_copy(sources[k], took.at[k % 2], in_sems.at[k % 2])

        def writes(k):
            at = pl.multiple_of(where[k], 128)
            here = gave.at[k % 2]
            return (
                pltpu.make_async_copy(
                    here.at[:, pl.ds(0, sub)], gu_ref.at[:, pl.ds(at, sub)], out_sems.at[k % 2, 0]
                ),
                pltpu.make_async_copy(
                    here.at[:, pl.ds(sub, sub)], gu_ref.at[:, pl.ds(at + ffwidth, sub)], out_sems.at[k % 2, 1]
                ),
                pltpu.make_async_copy(
                    here.at[:, pl.ds(2 * sub, sub)], down_ref.at[:, pl.ds(at, sub)], out_sems.at[k % 2, 2]
                ),
            )

        read(0).start()
        for k in range(count):
            if k + 1 < count:
                read(k + 1).start()
            read(k).wait()
            if k >= 2:
                for copy in writes(k - 2):
                    copy.wait()
            gave[k % 2] = took[k % 2].astype(F32)
            for copy in writes(k):
                copy.start()
        for k in range(max(0, count - 2), count):
            for copy in writes(k):
                copy.wait()

    return pl.pallas_call(
        kernel,
        in_specs=[pl.BlockSpec(memory_space=pltpu.SMEM)] + [ANY] * count,
        out_specs=[ANY, ANY],
        out_shape=[
            jax.ShapeDtypeStruct((rows, 2 * ffwidth), F32),
            jax.ShapeDtypeStruct((rows, ffwidth), F32),
        ],
        scratch_shapes=[
            pltpu.VMEM((2, rows, 3 * sub), BF),
            pltpu.VMEM((2, rows, 3 * sub), F32),
            pltpu.SemaphoreType.DMA((2,)),
            pltpu.SemaphoreType.DMA((2, 3)),
        ],
        compiler_params=params(60),
        cost_estimate=cost(0, rows * ffwidth * 18),
    )(columns, *pieces)


MESH = pl.DeviceIdType.MESH


def ring_place(n_fsdp):
    f, c = lax.axis_index("fsdp"), lax.axis_index("ctx")

    def device(place):
        row, k = place // n_fsdp, place % n_fsdp
        return {"fsdp": k + (row % 2) * (n_fsdp - 1 - 2 * k), "ctx": row}

    return c * n_fsdp + f + (c % 2) * (n_fsdp - 1 - 2 * f), device


def slot_lanes(ref, block, rows):
    if rows % 128 == 0:
        return ref[:, pl.ds(pl.multiple_of(block * rows, 128), rows)].astype(F32)
    share = 128 // rows
    wide = ref[:, pl.ds(pl.multiple_of(block // share * 128, 128), 128)].astype(F32)
    part = wide[:, :rows]
    for k in range(1, share):
        part = jnp.where(block % share == k, wide[:, k * rows : (k + 1) * rows], part)
    return part


def team_place(size, me, bit):
    return me + bit - 2 * bit * ((me // bit) % 2)


def greet(partners):
    barrier = pltpu.get_barrier_semaphore()
    for partner in partners:
        pl.semaphore_signal(barrier, inc=1, device_id=partner, device_id_type=MESH)
    pl.semaphore_wait(barrier, len(partners))


def own_columns(size, w_gate_up, w_down, first):
    ffwidth = w_down.shape[1]
    ffq = ffwidth // size
    sub = ffq // SUBS
    out = []
    for way in range(2):
        at = lax.axis_index("dp") * ffq + (first + way) * sub
        out.append(
            [
                (w_gate_up.at[:, pl.ds(pl.multiple_of(at, 128), sub)], 0),
                (w_gate_up.at[:, pl.ds(pl.multiple_of(at + ffwidth, 128), sub)], sub),
                (w_down.at[:, pl.ds(pl.multiple_of(at, 128), sub)], 2 * sub),
            ]
        )
    return out


class RingGather:
    def __init__(self, sizes, own, out, own_v, own_sem, store_sem, send, recv):
        self.n = sizes[1] * sizes[2]
        self.rows = own_v.shape[1]
        self.own, self.out, self.own_v = own, out, own_v
        self.own_sem, self.store_sem, self.send, self.recv = own_sem, store_sem, send, recv
        place, device = ring_place(sizes[1])
        self.partners = [device((place + 1) % self.n), device((place + self.n - 1) % self.n)]

    def rows_of(self, way, t):
        slot = t if way == 0 else (self.n - t) % self.n
        return pl.ds(slot * self.rows, self.rows)

    def loads(self, way):
        width = self.own_v.shape[2] // 3
        return [
            pltpu.make_async_copy(
                source, self.own_v.at[way, :, pl.ds(place, width)], self.own_sem.at[way, place // width]
            )
            for source, place in self.own[way]
        ]

    def store(self, way):
        return pltpu.make_async_copy(
            self.own_v.at[way], self.out[way].at[pl.ds(0, self.rows)], self.store_sem.at[way]
        )

    def ring(self, way, t, first=False):
        source = self.own_v.at[way] if first else self.out[way].at[self.rows_of(way, t - 1)]
        return pltpu.make_async_remote_copy(
            src_ref=source,
            dst_ref=self.out[way].at[self.rows_of(way, t)],
            send_sem=self.send.at[way, t],
            recv_sem=self.recv.at[way, t],
            device_id=self.partners[way],
            device_id_type=MESH,
        )

    def arrived(self, way, t):
        target = self.out[way].at[self.rows_of(way, t)]
        return pltpu.make_async_remote_copy(
            src_ref=target,
            dst_ref=target,
            send_sem=self.send.at[way, t],
            recv_sem=self.recv.at[way, t],
            device_id=self.partners[way],
            device_id_type=MESH,
        )

    def first(self):
        for way in range(2):
            for copy in self.loads(way):
                copy.start()
        for way in range(2):
            for copy in self.loads(way):
                copy.wait()
            self.ring(way, 1, True).start()
            self.store(way).start()

    def tick(self, t):
        for way in range(2):
            self.arrived(way, t - 1).wait_recv()
            self.ring(way, t).start()

    def last(self):
        for way in range(2):
            self.arrived(way, self.n - 1).wait_recv()
            self.store(way).wait()
            self.ring(way, 1, True).wait_send()
            for t in range(2, self.n):
                self.ring(way, t).wait_send()


def gather_scratch(n, rows, wide):
    dma = pltpu.SemaphoreType.DMA
    return [pltpu.VMEM((2, rows, wide), BF), dma((2, 3)), dma((2,)), dma((2, n)), dma((2, n))]


class RingReduce:
    def __init__(self, sizes, parts, out, land, own_v, own_sem, out_sem, send, recv, staged=None):
        self.n = sizes[1] * sizes[2]
        self.rows, self.wide = out[0].shape
        self.parts, self.out, self.land, self.own_v = parts, out, land, own_v
        self.own_sem, self.out_sem, self.send, self.recv = own_sem, out_sem, send, recv
        self.staged = staged
        place, device = ring_place(sizes[1])
        self.partners = [device((place + 1) % self.n), device((place + self.n - 1) % self.n)]

    def lanes(self, h):
        return pl.ds(pl.multiple_of(h * (self.wide // 2), 128), self.wide // 2)

    def load_own(self, way, t):
        slot = t % self.n if way == 0 else self.n - t
        return pltpu.make_async_copy(
            self.parts[way].at[pl.ds(slot * self.rows, self.rows)],
            self.own_v.at[way, t % 3],
            self.own_sem.at[way, t % 3],
        )

    def ring(self, source, way, t, h):
        return pltpu.make_async_remote_copy(
            src_ref=source,
            dst_ref=self.land.at[way, h, t - 1],
            send_sem=self.send.at[way, h, t],
            recv_sem=self.recv.at[way, h, t],
            device_id=self.partners[way],
            device_id_type=MESH,
        )

    def arrived(self, way, t, h):
        return self.ring(self.land.at[way, h, t - 1], way, t, h)

    def start(self, way, h):
        return self.ring(self.own_v.at[way, 1, :, self.lanes(h)], way, 1, h)

    def source(self, way, t, h):
        if self.staged:
            return self.staged[1].at[way, h]
        return self.land.at[way, h, t - 2]

    def fetch(self, way, t, h):
        return pltpu.make_async_copy(
            self.land.at[way, h, t - 1], self.staged[0].at[way], self.staged[2].at[way]
        )

    def save(self, way):
        return pltpu.make_async_copy(self.own_v.at[way, self.n % 3], self.out[way], self.out_sem.at[way])

    def first(self):
        for way in range(2):
            self.load_own(way, 1).start()
            self.load_own(way, 2).start()
        for way in range(2):
            self.load_own(way, 1).wait()
            for h in range(2):
                self.start(way, h).start()

    def total(self, way, t, h):
        brought = self.staged[0][way] if self.staged else self.land[way, h, t - 2]
        return self.own_v[way, t % 3, :, self.lanes(h)].astype(F32) + brought.astype(F32)

    def step(self, u):
        t, h = u // 2, u % 2
        for way in range(2):
            self.arrived(way, t - 1, h).wait_recv()
            if self.staged:
                self.fetch(way, t - 1, h).start()

            @pl.when(h == 0)
            def _():
                self.load_own(way, t).wait()

                @pl.when(t == 3)
                def _():
                    for half in range(2):
                        self.start(way, half).wait_send()

                self.load_own(way, t + 1).start()

        for way in range(2):
            if self.staged:
                self.fetch(way, t - 1, h).wait()

                @pl.when(t >= 3)
                def _():
                    self.ring(self.source(way, t - 1, h), way, t - 1, h).wait_send()

                self.staged[1][way, h] = self.total(way, t, h).astype(BF)
            else:
                self.land[way, h, t - 2] = self.total(way, t, h).astype(BF)
            self.ring(self.source(way, t, h), way, t, h).start()

    def last(self):
        n = self.n
        for way in range(2):
            self.load_own(way, n).wait()
            for h in range(2):
                self.arrived(way, n - 1, h).wait_recv()
                if self.staged:
                    self.fetch(way, n - 1, h).start()
                    self.fetch(way, n - 1, h).wait()
                half = self.wide // 2
                total = self.total(way, n, h).astype(BF)
                self.own_v[way, n % 3, :, h * half : (h + 1) * half] = total
            self.save(way).start()
        for way in range(2):
            for h in range(2):
                for t in range(n - 1 if self.staged else 2, n):
                    self.ring(self.source(way, t, h), way, t, h).wait_send()
            self.save(way).wait()


def reduce_scratch(n, rows, wide, near):
    dma = pltpu.SemaphoreType.DMA
    land = [pltpu.VMEM((2, 2, n - 1, rows, wide // 2), BF)] if near else []
    stage = [pltpu.VMEM((2, rows, wide // 2), BF), pltpu.VMEM((2, 2, rows, wide // 2), BF), dma((2,))]
    return (
        land
        + [pltpu.VMEM((2, 3, rows, wide), BF), dma((2, 3)), dma((2,)), dma((2, 2, n)), dma((2, 2, n))]
        + ([] if near else stage)
    )


class TeamSpread:
    def __init__(self, size, own, others, send, recv):
        self.own, self.others, self.send, self.recv = own, others, send, recv
        self.count = len(own)
        me = lax.axis_index("dp")
        self.stages = []
        held, bit = 1, size // 2
        while bit:
            partner = {"dp": me + bit - 2 * bit * ((me // bit) % 2)}
            self.stages.append((held, partner))
            held, bit = 2 * held, bit // 2

    def partners(self):
        return [partner for _, partner in self.stages]

    def copies(self, stage):
        held, partner = self.stages[stage]
        for k in range(self.count):
            for b in range(held):
                yield pltpu.make_async_remote_copy(
                    src_ref=self.own[k] if b == 0 else self.others[k][b - 1],
                    dst_ref=self.others[k][held + b - 1],
                    send_sem=self.send.at[k, held + b - 1],
                    recv_sem=self.recv.at[k, held + b - 1],
                    device_id=partner,
                    device_id_type=MESH,
                )

    def start(self, stage):
        if stage < len(self.stages):
            for copy in self.copies(stage):
                copy.start()

    def arrive(self, stage):
        if stage < len(self.stages):
            for copy in self.copies(stage):
                copy.wait_recv()

    def last(self):
        for stage in range(len(self.stages)):
            for copy in self.copies(stage):
                copy.wait_send()


def spread_scratch(count, size):
    return [pltpu.SemaphoreType.DMA((count, size)), pltpu.SemaphoreType.DMA((count, size))]


def feed_forward(sizes, xs, dys, weights, before, ring_parts, reducing, ident):
    n_dp, n_fsdp, n_ctx = sizes
    n = n_fsdp * n_ctx
    team, (span, width) = len(xs), xs[0].shape
    rows, wide = width // n, weights[0][0].shape[1]
    sub = wide // 3
    pieces = [piece for group in weights for piece in group]
    counts = [len(group) for group in weights]
    tile = min(span, 256)
    per = span // tile
    steps = team * per
    part = max(rows, 128)
    half = width // 2
    gsteps = width // part
    total = 2 * steps + gsteps
    inside = team // 2 if reducing and team > 2 else 0
    carried = [] if before is None else [b[0] for b in before] + [b[1] for b in before]
    backwards = reducing

    def kernel(*refs):
        refs = list(refs)

        def take(count):
            out = refs[:count]
            del refs[:count]
            return out

        x_refs, dy_refs, piece_refs = take(team), take(team), take(len(pieces))
        old_y, old_dn = take(len(carried) // 2), take(len(carried) // 2)
        part_refs = take(2)
        y_refs, dn_refs, grad_refs, ring_outs = take(team), take(team), take(2), take(2)
        if reducing:
            (land,) = take(1)
            near = take(max(1, inside))
            (far,) = take(1)
        wgu, wd, xb, dyb, yb, dnb, dgu, inner, xg, dyg, gout = take(11)
        w_sems, x_sems, y_sems, g_sems, gout_sems = take(5)
        if carried:
            cb, c_sems = take(2)
        if reducing:
            swap_send, swap_recv, face_send, face_recv = take(4)
            ring = RingReduce(sizes, part_refs, ring_outs, land, *refs[:5], staged=refs[5:])
        else:
            ring = RingGather(sizes, own_columns(n_dp, *part_refs, SUBS // 2), ring_outs, *refs)
        me = lax.axis_index("dp")
        sibling = {"dp": me + 1 - 2 * (me % 2)}
        bit = team // 2
        facing = {"dp": me + bit - 2 * bit * ((me // bit) % 2)}

        k = 0
        w_copies = []
        for b, count in enumerate(counts):
            at = 0
            for ref in piece_refs[k : k + count]:
                high = ref.shape[0]
                w_copies += [
                    pltpu.make_async_copy(
                        ref.at[:, pl.ds(0, 2 * sub)],
                        wgu.at[pl.ds(at, high), pl.ds(b * 2 * sub, 2 * sub)],
                        w_sems.at[2 * k],
                    ),
                    pltpu.make_async_copy(
                        ref.at[:, pl.ds(2 * sub, sub)],
                        wd.at[pl.ds(at, high), pl.ds(b * sub, sub)],
                        w_sems.at[2 * k + 1],
                    ),
                ]
                at += high
                k += 1
        for copy in w_copies:
            copy.start()

        def block_of(i):
            return team - 1 - i // per if backwards else i // per

        def loads(m, i):
            rows_here = pl.ds((i % per) * tile, tile)
            return [
                pltpu.make_async_copy(x_refs[m].at[rows_here], xb.at[i % 2], x_sems.at[0, i % 2]),
                pltpu.make_async_copy(dy_refs[m].at[rows_here], dyb.at[i % 2], x_sems.at[1, i % 2]),
            ]

        def more(m, i):
            if not carried:
                return []
            rows_here = pl.ds((i % per) * tile, tile)
            out = [
                pltpu.make_async_copy(old_y[m].at[rows_here], cb.at[0], c_sems.at[0]),
                pltpu.make_async_copy(old_dn[m].at[rows_here], cb.at[1], c_sems.at[1]),
            ]
            if m < inside:
                out.append(pltpu.make_async_copy(near[m].at[rows_here], cb.at[2], c_sems.at[2]))
            return out

        def writes(m, i):
            rows_here = pl.ds((i % per) * tile, tile)
            return [
                pltpu.make_async_copy(yb, y_refs[m].at[rows_here], y_sems.at[0]),
                pltpu.make_async_copy(dnb, dn_refs[m].at[rows_here], y_sems.at[1]),
            ]

        def on_block(i, act):
            for m in range(team):

                @pl.when(block_of(i) == m)
                def _():
                    act(m)

        def swap(m):
            return pltpu.make_async_remote_copy(
                src_ref=dn_refs[m],
                dst_ref=near[m - inside],
                send_sem=swap_send.at[m - inside],
                recv_sem=swap_recv.at[m - inside],
                device_id=sibling,
                device_id_type=MESH,
            )

        def face():
            return pltpu.make_async_remote_copy(
                src_ref=dn_refs[1],
                dst_ref=far,
                send_sem=face_send,
                recv_sem=face_recv,
                device_id=facing,
                device_id_type=MESH,
            )

        def go(copies):
            for copy in copies:
                copy.start()

        def end(copies):
            for copy in copies:
                copy.wait()

        def ticks(lo, hi):
            if reducing:
                count, base, act = 2 * (n - 2), 4, ring.step
            else:
                count, base, act = n - 2, 2, ring.tick
            lax.fori_loop(
                base + lo * count // total, base + hi * count // total, lambda t, c: (act(t), c)[1], 0
            )

        on_block(0, lambda m: go(loads(m, 0)))
        partners = list(ring.partners)
        if inside:
            partners.append(sibling)
        if reducing and team > 1:
            partners.append(facing)
        greet(partners)
        ring.first()
        for copy in w_copies:
            copy.wait()

        def forward(i, carry):
            @pl.when(i + 1 < steps)
            def _():
                on_block(i + 1, lambda m: go(loads(m, i + 1)))

            @pl.when(i == steps - 1)
            def _():
                go(sides(0))

            if inside:
                @pl.when(i % per == 0)
                def _():
                    on_block(i, lambda m: swap(m + inside).wait_recv() if m < inside else None)

            on_block(i, lambda m: go(more(m, i)))
            ticks(2 * i, 2 * i + 2)
            end(loads(0, i))
            here = pl.ds(pl.multiple_of(i * tile, tile), tile)
            for b in range(2):
                gate_up = dot_nn(xb[i % 2], wgu[:, b * 2 * sub : (b + 1) * 2 * sub])
                d_inner = dot_nn(dyb[i % 2], wd[:, b * sub : (b + 1) * sub])
                gate, up = gate_up[:, :sub], gate_up[:, sub:]
                sig = 1.0 / (1.0 + jnp.exp(-gate))
                act = gate * sig
                inner[here, b * sub : (b + 1) * sub] = (act * up).astype(BF)
                dgu[here, b * 2 * sub : b * 2 * sub + sub] = (
                    d_inner * up * (sig + act * (1.0 - sig))
                ).astype(BF)
                dgu[here, b * 2 * sub + sub : (b + 1) * 2 * sub] = (d_inner * act).astype(BF)
            drained = (i > 0) & (i % per != 0) if reducing else i > 0

            @pl.when(drained)
            def _():
                end(writes(0, i))

            if carried:
                on_block(i, lambda m: end(more(m, i)))
            for at in range(0, width, half):
                lanes = slice(at, at + half)
                y = dot_nt(inner[here, :], wd[lanes, :])
                if carried:
                    y = y + cb[0, :, lanes].astype(F32)
                yb[:, lanes] = y.astype(BF)
                dn = dot_nt(dgu[here, :], wgu[lanes, :])
                if carried:
                    dn = dn + cb[1, :, lanes].astype(F32)
                if inside:
                    dn = dn + jnp.where(block_of(i) < inside, cb[2, :, lanes].astype(F32), 0.0)
                dnb[:, lanes] = dn.astype(BF)
            on_block(i, lambda m: go(writes(m, i)))
            if reducing and team > 1:

                @pl.when(i % per == per - 1)
                def _():
                    def sent(m):
                        if m >= 1:
                            end(writes(m, i))
                            go([swap(m)] if inside and m >= inside else [face()])

                    on_block(i, sent)

            return carry

        def sides(g):
            cols = pl.ds(g * part, part) if isinstance(g, int) else pl.ds(pl.multiple_of(g * part, part), part)
            out = []
            for k in range(team):
                m = team - 1 - k if backwards else k
                at = pl.ds(k * span, span)
                out += [
                    pltpu.make_async_copy(x_refs[m].at[:, cols], xg.at[g % 2, at], g_sems.at[0, g % 2, k]),
                    pltpu.make_async_copy(dy_refs[m].at[:, cols], dyg.at[g % 2, at], g_sems.at[1, g % 2, k]),
                ]
            return out

        def keep(g):
            at = pl.ds(pl.multiple_of(g * part, part), part)
            return [pltpu.make_async_copy(gout.at[b], grad_refs[b].at[at], gout_sems.at[b]) for b in range(2)]

        def outer(g, carry):
            @pl.when(g + 1 < gsteps)
            def _():
                go(sides(g + 1))

            ticks(2 * steps + g, 2 * steps + g + 1)
            end(sides(g))

            @pl.when(g > 0)
            def _():
                end(keep(g))

            for b in range(2):
                up_down = dot_tn(xg[g % 2], dgu[:, b * 2 * sub : (b + 1) * 2 * sub])
                gout[b, :, : 2 * sub] = up_down.astype(BF)
                down = dot_tn(dyg[g % 2], inner[:, b * sub : (b + 1) * sub])
                gout[b, :, 2 * sub :] = down.astype(BF)
            go(keep(g))
            return carry

        lax.fori_loop(0, steps, forward, 0)
        lax.fori_loop(0, gsteps, outer, 0)
        end(writes(0, 0))
        end(keep(0))
        ring.last()
        if reducing and team > 1:
            for m in range(inside, team) if inside else []:
                swap(m).wait_send()
            face().wait_recv()
            face().wait_send()

    shape = lambda a, b: jax.ShapeDtypeStruct((a, b), BF)
    outs = [shape(span, width)] * (2 * team) + [shape(width, wide)] * 2
    if reducing:
        outs += [shape(rows, wide)] * 2 + [jax.ShapeDtypeStruct((2, 2, n - 1, rows, wide // 2), BF)]
        outs += [shape(span, width)] * (max(1, inside) + 1)
    else:
        outs += [shape(width, wide)] * 2
    dma = pltpu.SemaphoreType.DMA
    scratch = [
        pltpu.VMEM((width, 4 * sub), BF),
        pltpu.VMEM((width, 2 * sub), BF),
        pltpu.VMEM((2, tile, width), BF),
        pltpu.VMEM((2, tile, width), BF),
        pltpu.VMEM((tile, width), BF),
        pltpu.VMEM((tile, width), BF),
        pltpu.VMEM((team * span, 4 * sub), BF),
        pltpu.VMEM((team * span, 2 * sub), BF),
        pltpu.VMEM((2, team * span, part), BF),
        pltpu.VMEM((2, team * span, part), BF),
        pltpu.VMEM((2, part, wide), BF),
        dma((2 * len(pieces),)),
        dma((2, 2)),
        dma((2,)),
        dma((2, 2, team)),
        dma((2,)),
    ]
    if carried:
        scratch += [pltpu.VMEM((3 if inside else 2, tile, width), BF), dma((3,))]
    if reducing:
        scratch += [dma((max(1, inside),)), dma((max(1, inside),)), dma(()), dma(())]
        scratch += reduce_scratch(n, rows, wide, False)
    else:
        scratch += gather_scratch(n, rows, wide)
    operands = list(xs) + list(dys) + pieces + carried + list(ring_parts)
    out = pl.pallas_call(
        kernel,
        in_specs=[ANY] * len(operands),
        out_specs=[ANY] * len(outs),
        out_shape=outs,
        scratch_shapes=scratch,
        compiler_params=pltpu.CompilerParams(
            collective_id=ident, has_side_effects=True, vmem_limit_bytes=56 * MIB
        ),
        cost_estimate=cost(18 * team * span * width * 2 * sub, 40 * MIB),
    )(*operands)
    y, dn, grads, ringed = out[:team], out[team : 2 * team], out[2 * team : 2 * team + 2], out[2 * team + 2 :]
    if reducing:
        return y, (dn[0], ringed[-1]) if team > 1 else (dn[0],), grads, ringed[:2]
    return y, dn, grads, ringed[:2]


def attend_forward(sizes, x, qkv, kv_far, seen, w_out, gains, dy, w_gate_up, w_down):
    n_dp, n_fsdp, n_ctx = sizes
    n = n_fsdp * n_ctx
    span, width = x.shape
    rows = width // n
    far = kv_far.shape[0]
    blocks = far // span
    qwidth, kvwidth = HEADS * HD, KV_HEADS * HD
    near, kvpairs = qwidth // 128, kvwidth // 128
    pairs = HEADS // 2
    tile = min(span, 256)
    wide = 3 * (w_down.shape[1] // n_dp // SUBS)
    early = max(0, 3 * (n - 2) // 7)
    others = n_dp - 1
    chunk = min(512, width)

    def kernel(seen_ref, q_ref, k_ref, v_ref, kf_ref, vf_ref, x_ref, gains_ref, *refs):
        refs = list(refs)

        def take(count):
            out = refs[:count]
            del refs[:count]
            return out

        wo_ref, dy_ref, gu_ref, down_ref = take(4)
        lse_ref, attn_out, hidden_out, normed_out = take(4)
        x_blocks, dy_blocks, ring_outs = take(others), take(others), take(2)
        attn_v, wo_v, hidden_v, normed_v, load_sem, save_sems = take(6)
        dy_send, dy_recv, x_send, x_recv = take(4)
        ring = RingGather(sizes, own_columns(n_dp, gu_ref, down_ref, 0), ring_outs, *refs)
        dy_spread = TeamSpread(n_dp, [dy_ref], [dy_blocks], dy_send, dy_recv)
        x_spread = TeamSpread(n_dp, [normed_v], [x_blocks], x_send, x_recv)
        group = pl.program_id(0)
        mask = causal_tile(tile)
        flags = [seen_ref[k] == 1 for k in range(blocks)]
        load = pltpu.make_async_copy(wo_ref, wo_v, load_sem)

        @pl.when(group == 0)
        def _():
            greet(ring.partners + dy_spread.partners())
            ring.first()
            dy_spread.start(0)
            load.start()

        lax.fori_loop(
            2 + group * early // pairs,
            2 + (group + 1) * early // pairs,
            lambda t, c: (ring.tick(t), c)[1],
            0,
        )
        key, value = head_of(k_ref[...], group), head_of(v_ref[...], group)
        key_far, value_far = head_of(kf_ref[...], group), head_of(vf_ref[...], group)
        value_t = value.astype(F32).T.astype(BF)
        value_far_t = value_far.astype(F32).T.astype(BF)
        for head in range(2):
            down = pl.ds(pl.multiple_of(group * 128 + head * HD, HD), HD)
            for at in range(0, span, tile):
                end = at + tile
                q = q_ref[at:end, head * HD : (head + 1) * HD]
                own, other = scores_of(key[:end], key_far, q, flags, mask, span)
                peak = jnp.maximum(jnp.max(own, 0, keepdims=True), jnp.max(other, 0, keepdims=True))
                own = jnp.exp(own - peak)
                other = jnp.exp(other - peak)
                total = jnp.sum(own, 0, keepdims=True) + jnp.sum(other, 0, keepdims=True)
                scale = 1.0 / total
                result = dot_nn(value_t[:, :end], (own * scale).astype(BF)) + dot_nn(
                    value_far_t, (other * scale).astype(BF)
                )
                attn_v[down, at:end] = result.astype(BF)
                lse_ref[0, head : head + 1, at:end] = peak + jnp.log(total)

        @pl.when(group == pairs - 1)
        def _():
            saves = [
                pltpu.make_async_copy(a, b, save_sems.at[k])
                for k, (a, b) in enumerate([(attn_v, attn_out), (hidden_v, hidden_out), (normed_v, normed_out)])
            ]
            saves[0].start()
            load.wait()
            square = jnp.zeros((span, 1), F32)
            for at in range(0, width, chunk):
                lanes = slice(at, at + chunk)
                hidden = x_ref[:, lanes].astype(F32) + dot_tn(attn_v[...], wo_v[:, lanes])
                hidden_v[:, lanes] = hidden
                square = square + jnp.sum(hidden * hidden, -1, keepdims=True)
            scale = lax.rsqrt(square / width + EPS)
            place, device = ring_place(n_fsdp)
            for slot in range(n):
                there = device((place + n - slot) % n)
                part = slot_lanes(hidden_v, there["fsdp"] * n_ctx + there["ctx"], rows)
                normed = part * scale * gains_ref[slot, 1:2, :].astype(F32)
                normed_v[:, slot * rows : (slot + 1) * rows] = normed.astype(BF)
            x_spread.start(0)
            saves[1].start()
            saves[2].start()
            dy_spread.arrive(0)
            dy_spread.start(1)
            middle = max(2 + early, n - 2)
            for t in range(2 + early, middle):
                ring.tick(t)
            x_spread.arrive(0)
            x_spread.start(1)
            for t in range(middle, n):
                ring.tick(t)
            dy_spread.arrive(1)
            x_spread.arrive(1)
            ring.last()
            dy_spread.last()
            x_spread.last()
            for copy in saves:
                copy.wait()

    pair = lambda high, shift: pl.BlockSpec((high, 128), lambda i: (0, i // 4 + shift))
    dma = pltpu.SemaphoreType.DMA
    block = jax.ShapeDtypeStruct((span, width), BF)
    out = pl.pallas_call(
        kernel,
        grid=(pairs,),
        in_specs=[
            pl.BlockSpec(memory_space=pltpu.SMEM),
            pl.BlockSpec((span, 128), lambda i: (0, i)),
            pair(span, near),
            pair(span, near + kvpairs),
            pair(far, 0),
            pair(far, kvpairs),
            pl.BlockSpec((span, width), lambda i: (0, 0)),
            pl.BlockSpec(gains.shape, lambda i: (0, 0, 0)),
        ]
        + [ANY] * 4,
        out_specs=[pl.BlockSpec((1, 8, span), lambda i: (i, 0, 0))] + [ANY] * (5 + 2 * others),
        out_shape=[
            jax.ShapeDtypeStruct((pairs, 8, span), F32),
            jax.ShapeDtypeStruct((qwidth, span), BF),
            jax.ShapeDtypeStruct((span, width), F32),
        ]
        + [block] * (1 + 2 * others)
        + [jax.ShapeDtypeStruct((width, wide), BF)] * 2,
        scratch_shapes=[
            pltpu.VMEM((qwidth, span), BF),
            pltpu.VMEM((qwidth, width), BF),
            pltpu.VMEM((span, width), F32),
            pltpu.VMEM((span, width), BF),
            dma(()),
            dma((3,)),
        ]
        + spread_scratch(1, n_dp)
        + spread_scratch(1, n_dp)
        + gather_scratch(n, rows, wide),
        compiler_params=pltpu.CompilerParams(
            collective_id=5, has_side_effects=True, vmem_limit_bytes=58 * MIB
        ),
        cost_estimate=cost(pairs * 2 * span * (span + far) * 128 * 4, 30 * MIB),
    )(seen, qkv, qkv, qkv, kv_far, kv_far, x, gains, w_out, dy, w_gate_up, w_down)
    lse, attn, hidden, normed = out[:4]
    return attn, lse, hidden, normed, out[4 : 4 + others], out[4 + others : 4 + 2 * others], out[4 + 2 * others :]


def attend_backward(sizes, qkv, kv_far, d_attn, lse, seen, tables, attn_t, d_proj, normed, ring_parts, sums, ident):
    n_dp, n_fsdp, n_ctx = sizes
    n = n_fsdp * n_ctx
    span, far = qkv.shape[0], kv_far.shape[0]
    blocks = far // span
    qwidth, kvwidth = HEADS * HD, KV_HEADS * HD
    near, kvpairs = qwidth // 128, kvwidth // 128
    pairs = HEADS // 2
    tile = min(span, 256)
    rows, wide = ring_parts[0].shape[0] // n, ring_parts[0].shape[1]
    early = 4 + 8 * (n - 2) // 6
    width = normed.shape[1]
    qkvwidth = qwidth + 2 * kvwidth
    part = max(rows, 128)
    others = n_dp - 1

    def kernel(seen_ref, q_ref, k_ref, v_ref, kf_ref, vf_ref, d_ref, lse_ref, cos_ref, low_ref, high_ref, *refs):
        refs = list(refs)

        def take(count):
            out = refs[:count]
            del refs[:count]
            return out

        attn_ref, proj_ref, normed_ref = take(3)
        parts, own_sums = take(2), take(2)
        dqkv_out, go_out, gq_out = take(3)
        ring_outs, blocks_out = take(2), take(2 * others)
        dqkv_v, dkv, dkv_far, give, got, save_sem, kv_send, kv_recv = take(8)
        attn_v, proj_v, normed_v, stage, load_sems, stage_sems = take(6)
        spread_send, spread_recv = take(2)
        ring = RingReduce(sizes, parts, ring_outs, *refs)
        spread = TeamSpread(
            n_dp, own_sums, [blocks_out[k * others : (k + 1) * others] for k in range(2)], spread_send, spread_recv
        )
        loads = [
            pltpu.make_async_copy(a, b, load_sems.at[k])
            for k, (a, b) in enumerate([(attn_ref, attn_v), (proj_ref, proj_v), (normed_ref, normed_v)])
        ]

        def product(out, cols, make):
            def write(g):
                return pltpu.make_async_copy(
                    stage.at[g % 2, :, pl.ds(0, cols)],
                    out.at[pl.ds(pl.multiple_of(g * part, part), part)],
                    stage_sems.at[g % 2],
                )

            def body(g, carry):
                @pl.when(g >= 2)
                def _():
                    write(g - 2).wait()

                stage[g % 2, :, :cols] = make(pl.ds(pl.multiple_of(g * part, part), part)).astype(BF)
                write(g).start()
                return carry

            count = width // part
            lax.fori_loop(0, count, body, 0)
            for g in range(max(0, count - 2), count):
                write(g).wait()

        ctx = lax.axis_index("ctx")
        group = pl.program_id(0)
        mask = causal_tile(tile)
        flags = [seen_ref[k] == 1 for k in range(blocks)]
        key, value = head_of(k_ref[...], group), head_of(v_ref[...], group)
        key_far, value_far = head_of(kf_ref[...], group), head_of(vf_ref[...], group)
        key_t = key.astype(F32).T.astype(BF)
        key_far_t = key_far.astype(F32).T.astype(BF)
        odd = (group // 2) % 2 == 1
        cosine, low, high = cos_ref[...], -low_ref[...], -high_ref[...]

        @pl.when(group == 0)
        def _():
            greet(ring.partners + [{"ctx": (ctx + k) % n_ctx} for k in range(1, n_ctx)] + spread.partners())
            ring.first()
            spread.start(0)
            for copy in loads:
                copy.start()
            dkv[...] = jnp.zeros_like(dkv)
            dkv_far[...] = jnp.zeros_like(dkv_far)

        @pl.when(group == pairs - 4)
        def _():
            spread.arrive(0)
            spread.start(1)

        lax.fori_loop(
            4 + group * (early - 4) // pairs,
            4 + (group + 1) * (early - 4) // pairs,
            lambda u, c: (ring.step(u), c)[1],
            0,
        )

        def put(ref, size, shift, add):
            zero = jnp.zeros_like(add)
            lanes = pl.ds(pl.multiple_of(group // 4 * 128 + shift, 128), 128)
            ref[0:size, lanes] += jnp.concatenate([jnp.where(odd, zero, add), jnp.where(odd, add, zero)], 1)

        for at in range(0, span, tile):
            end = at + tile
            turned = []
            for head in range(2):
                lanes = slice(head * HD, (head + 1) * HD)
                q = q_ref[at:end, lanes]
                d = d_ref[at:end, lanes]
                own, other = scores_of(key[:end], key_far, q, flags, mask, span)
                base = lse_ref[0, head : head + 1, at:end]
                own = jnp.exp(own - base)
                other = jnp.exp(other - base)
                d_own = dot_nt(value[:end], d)
                d_other = dot_nt(value_far, d)
                delta = jnp.sum(own * d_own, 0, keepdims=True) + jnp.sum(other * d_other, 0, keepdims=True)
                ds_own = (own * (d_own - delta)).astype(BF)
                ds_other = (other * (d_other - delta)).astype(BF)
                put(dkv, end, kvwidth, dot_nn(own.astype(BF), d))
                put(dkv_far, far, kvwidth, dot_nn(other.astype(BF), d))
                put(dkv, end, 0, dot_nn(ds_own, q))
                put(dkv_far, far, 0, dot_nn(ds_other, q))
                turned.append(dot_nn(key_t[:, :end], ds_own) + dot_nn(key_far_t, ds_other))
            d_query = jnp.concatenate(turned, 0).T * HD**-0.5
            dqkv_v[at:end, pl.ds(pl.multiple_of(group * 128, 128), 128)] = turn(
                d_query, cosine[at:end], low[at:end], high[at:end]
            ).astype(BF)

        @pl.when(group == pairs - 1)
        def _():
            give[...] = dkv_far[...].astype(BF)

            def back(k):
                return pltpu.make_async_remote_copy(
                    src_ref=give.at[pl.ds((k - 1) * span, span)],
                    dst_ref=got.at[k - 1],
                    send_sem=kv_send.at[k],
                    recv_sem=kv_recv.at[k],
                    device_id={"ctx": (ctx + k) % n_ctx},
                    device_id_type=MESH,
                )

            for k in range(1, n_ctx):
                back(k).start()
            for copy in loads:
                copy.wait()
            ring.step(early)
            product(go_out, qwidth, lambda at: dot_nn(attn_v[at, :], proj_v[...]))
            ring.step(early + 1)
            for k in range(1, n_ctx):
                back(k).wait_recv()
            for at in range(0, 2 * kvwidth, 128):
                piece = dkv[:, at : at + 128]
                for k in range(1, n_ctx):
                    piece = piece + got[k - 1, :, at : at + 128].astype(F32)
                if at < kvwidth:
                    piece = turn(piece, cosine, low, high)
                dqkv_v[:, qwidth + at : qwidth + at + 128] = piece.astype(BF)
            save = pltpu.make_async_copy(dqkv_v, dqkv_out, save_sem)
            save.start()
            lax.fori_loop(early + 2, 2 * n - 1, lambda u, c: (ring.step(u), c)[1], 0)
            product(gq_out, qkvwidth, lambda at: dot_tn(normed_v[:, at], dqkv_v[...]))
            if early + 2 < 2 * n:
                ring.step(2 * n - 1)
            spread.arrive(1)
            ring.last()
            spread.last()
            for k in range(1, n_ctx):
                back(k).wait_send()
            save.wait()

    pair = lambda high, shift: pl.BlockSpec((high, 128), lambda i: (0, i // 4 + shift))
    wide_block = pl.BlockSpec((span, 128), lambda i: (0, i))
    table = pl.BlockSpec((span, 128), lambda i: (0, 0))
    dma = pltpu.SemaphoreType.DMA
    out = pl.pallas_call(
        kernel,
        grid=(pairs,),
        in_specs=[
            pl.BlockSpec(memory_space=pltpu.SMEM),
            wide_block,
            pair(span, near),
            pair(span, near + kvpairs),
            pair(far, 0),
            pair(far, kvpairs),
            wide_block,
            pl.BlockSpec((1, 8, span), lambda i: (i, 0, 0)),
            table,
            table,
            table,
        ]
        + [ANY] * 7,
        out_specs=[ANY] * (5 + 2 * others),
        out_shape=[
            jax.ShapeDtypeStruct((span, qkvwidth), BF),
            jax.ShapeDtypeStruct((width, qwidth), BF),
            jax.ShapeDtypeStruct((width, qkvwidth), BF),
        ]
        + [jax.ShapeDtypeStruct((rows, wide), BF)] * (2 + 2 * others),
        scratch_shapes=[
            pltpu.VMEM((span, qwidth + 2 * kvwidth), BF),
            pltpu.VMEM((span, 2 * kvwidth), F32),
            pltpu.VMEM((far, 2 * kvwidth), F32),
            pltpu.VMEM((far, 2 * kvwidth), BF),
            pltpu.VMEM((n_ctx - 1, span, 2 * kvwidth), BF),
            dma(()),
            dma((n_ctx,)),
            dma((n_ctx,)),
            pltpu.VMEM(attn_t.shape, BF),
            pltpu.VMEM(d_proj.shape, BF),
            pltpu.VMEM(normed.shape, BF),
            pltpu.VMEM((2, part, max(qwidth, qkvwidth)), BF),
            dma((3,)),
            dma((2,)),
        ]
        + spread_scratch(2, n_dp)
        + reduce_scratch(n, rows, wide, True),
        compiler_params=pltpu.CompilerParams(
            collective_id=ident, has_side_effects=True, vmem_limit_bytes=58 * MIB
        ),
        cost_estimate=cost(pairs * 2 * span * (span + far) * 128 * 10, 30 * MIB),
    )(seen, qkv, qkv, qkv, kv_far, kv_far, d_attn, lse, *tables, attn_t, d_proj, normed, *ring_parts, *sums)
    return out[0], out[1], out[2], out[3:5], [out[5 + k * others : 5 + (k + 1) * others] for k in range(2)]


def opening(sizes, x, w_qkv, w_out, gains, tables):
    n_dp, n_fsdp, n_ctx = sizes
    n = n_fsdp * n_ctx
    span, width = x.shape
    rows = width // n
    share, half = w_qkv.shape[1] // n_dp, w_out.shape[1] // 2
    qwidth, kvwidth = HEADS * HD, KV_HEADS * HD
    qkvwidth = qwidth + 2 * kvwidth
    chunk = share // 2 if share % 256 == 0 else share
    across_x = n_dp > 2

    def kernel(x_ref, wq_ref, wo_ref, g_ref, cos_ref, low_ref, high_ref, *refs):
        refs = list(refs)

        def take(count):
            out = refs[:count]
            del refs[:count]
            return out

        qkv_out, far_out, xs_out, wq_out, wo_out, gains_out = take(6)
        qkv_v, far_v, xs_v = take(3)
        wq_v = take(n_dp)
        om_v, oo_v, gains_v = take(3)
        load_sems, save_sems, wq_sems, wo_sems = take(4)
        send, recv, x_send, x_recv, c_send, c_recv, o_send, o_recv = take(8)
        gain_send, gain_recv, kv_send, kv_recv = take(4)
        me = lax.axis_index("dp")
        core = me % 2
        sibling = {"dp": team_place(n_dp, me, 1)}
        facing = {"dp": team_place(n_dp, me, n_dp // 2)}
        bases = [me, team_place(n_dp, me, n_dp // 2)] if across_x else [me]
        bases = [b * share for b in bases + [team_place(n_dp, b, 1) for b in bases]]
        held = n_dp // 2
        place, device = ring_place(n_fsdp)
        ahead, behind = device((place + 1) % n), device((place + n - 1) % n)
        mine = (wq_v[0], om_v)
        widths = (share, half)

        def block_of(slot):
            there = device((place + n - slot) % n)
            return there["fsdp"] * n_ctx + there["ctx"]

        loads = [
            pltpu.make_async_copy(
                ref.at[:, pl.ds(pl.multiple_of(at, 128), w)], mine[k].at[pl.ds(0, rows)], load_sems.at[k]
            )
            for k, (ref, at, w) in enumerate(((wq_ref, me * share, share), (wo_ref, core * half, half)))
        ] + [pltpu.make_async_copy(g_ref, gains_v.at[0], load_sems.at[2])]
        for copy in loads:
            copy.start()
        ctx = lax.axis_index("ctx")
        greet(
            [ahead, behind, sibling]
            + ([facing] if across_x else [])
            + [{"ctx": (ctx + k) % n_ctx} for k in range(1, n_ctx)]
        )

        def lanes(k, way):
            return pl.ds(way * (widths[k] // 2), widths[k] // 2)

        def remote(source, target, send_sem, recv_sem, partner):
            return pltpu.make_async_remote_copy(
                src_ref=source,
                dst_ref=target,
                send_sem=send_sem,
                recv_sem=recv_sem,
                device_id=partner,
                device_id_type=MESH,
            )

        def step(k, way, t):
            here = t - 1 if way == 0 else (n - t + 1) % n
            there = t if way == 0 else n - t
            return remote(
                mine[k].at[pl.ds(here * rows, rows), lanes(k, way)],
                mine[k].at[pl.ds(there * rows, rows), lanes(k, way)],
                send.at[k, way, t],
                recv.at[k, way, t],
                ahead if way == 0 else behind,
            )

        def over_x(way, slot):
            at = (pl.ds(slot * rows, rows), lanes(0, way))
            return remote(wq_v[0].at[at], wq_v[1].at[at], x_send.at[way, slot], x_recv.at[way, slot], facing)

        def over_core(b, way, slot):
            at = (pl.ds(slot * rows, rows), lanes(0, way))
            return remote(
                wq_v[b].at[at], wq_v[held + b].at[at], c_send.at[b, way, slot], c_recv.at[b, way, slot], sibling
            )

        def out_over(way, slot):
            at = (pl.ds(slot * rows, rows), lanes(1, way))
            return remote(om_v.at[at], oo_v.at[at], o_send.at[way, slot], o_recv.at[way, slot], sibling)

        def gain_step(t):
            return remote(gains_v.at[t - 1], gains_v.at[t], gain_send.at[t], gain_recv.at[t], ahead)

        def kv_step(k):
            return remote(
                qkv_v.at[:, pl.ds(qwidth, 2 * kvwidth)],
                far_v.at[pl.ds((k - 1) * span, span)],
                kv_send.at[k],
                kv_recv.at[k],
                {"ctx": (ctx + n_ctx - k) % n_ctx},
            )

        def give(way, slot):
            if across_x:
                over_x(way, slot).start()
            over_core(0, way, slot).start()

        f32 = x_ref[...].astype(F32)
        scale = lax.rsqrt(jnp.mean(f32 * f32, -1, keepdims=True) + EPS)

        def normalize(slot):
            part = slot_lanes(x_ref, block_of(slot), rows)
            xs_v[:, slot * rows : (slot + 1) * rows] = (
                part * scale * gains_v[slot, 0:1, :].astype(F32)
            ).astype(BF)

        loads[0].wait()
        loads[2].wait()
        gain_step(1).start()
        for way in range(2):
            step(0, way, 1).start()
        loads[1].wait()
        for way in range(2):
            give(way, 0)
        normalize(0)
        for t in range(1, n):
            gain_step(t).wait_recv()
            if t < n - 1:
                gain_step(t + 1).start()
            for way in range(2):
                step(0, way, t).wait_recv()
                if t < n - 1:
                    step(0, way, t + 1).start()
                give(way, t if way == 0 else n - t)
            normalize(t)

        for way in range(2):
            step(1, way, 1).start()
            out_over(way, 0).start()

        def out_tick(t):
            for way in range(2):
                step(1, way, t).wait_recv()
                if t < n - 1:
                    step(1, way, t + 1).start()
                out_over(way, t if way == 0 else n - t).start()

        order = [(way, 0) for way in range(2)]
        for t in range(1, n):
            order += [(0, t), (1, n - t)]
        cosine, low, high = cos_ref[...], low_ref[...], high_ref[...]

        def form(b, at):
            value = dot_nn(xs_v[...], wq_v[b][:, at : at + chunk])
            for part in range(0, chunk, 128):
                piece = value[:, part : part + 128]
                here = bases[b] + at + part
                piece = jnp.where(here >= qwidth + kvwidth, piece, turn(piece, cosine, low, high))
                piece = piece * jnp.where(here < qwidth, HD**-0.5, 1.0)
                qkv_v[:, pl.ds(pl.multiple_of(here, 128), 128)] = piece.astype(BF)

        def save_share(b):
            return [
                pltpu.make_async_copy(
                    wq_v[b].at[pl.ds(slot * rows, rows)],
                    wq_out.at[
                        pl.ds(pl.multiple_of(block_of(slot) * rows, rows), rows),
                        pl.ds(pl.multiple_of(bases[b], 128), share),
                    ],
                    wq_sems.at[b, slot],
                )
                for slot in range(n)
            ]

        def save_half(k):
            whose = core if k == 0 else 1 - core
            return [
                pltpu.make_async_copy(
                    (om_v, oo_v)[k].at[pl.ds(slot * rows, rows)],
                    wo_out.at[
                        pl.ds(pl.multiple_of(block_of(slot) * rows, rows), rows),
                        pl.ds(pl.multiple_of(whose * half, 128), half),
                    ],
                    wo_sems.at[k, slot],
                )
                for slot in range(n)
            ]

        def go(copies):
            for copy in copies:
                copy.start()

        jobs = [lambda at=at: form(0, at) for at in range(0, share, chunk)]
        jobs.append(lambda: go(save_share(0)))

        def core_shares(b):
            for way, slot in order:
                over_core(b, way, slot).wait_recv()
            go(save_share(held + b))

        jobs.append(lambda: core_shares(0))
        jobs += [lambda at=at: form(held, at) for at in range(0, share, chunk)]
        if across_x:

            def relay(way, slot):
                over_x(way, slot).wait_recv()
                over_core(1, way, slot).start()

            jobs += [lambda w=way, k=slot: relay(w, k) for way, slot in order]
            jobs.append(lambda: go(save_share(1)))
            jobs += [lambda at=at: form(1, at) for at in range(0, share, chunk)]
            jobs.append(lambda: core_shares(1))
            jobs += [lambda at=at: form(held + 1, at) for at in range(0, share, chunk)]
        for k, job in enumerate(jobs):
            job()
            for t in range(1 + k * (n - 1) // len(jobs), 1 + (k + 1) * (n - 1) // len(jobs)):
                out_tick(t)
        for j in range(1, n_ctx):
            kv_step(j).start()
        saves = [
            pltpu.make_async_copy(a, b, save_sems.at[k])
            for k, (a, b) in enumerate([(qkv_v, qkv_out), (far_v, far_out), (xs_v, xs_out), (gains_v, gains_out)])
        ]
        for k in (0, 2, 3):
            saves[k].start()
        go(save_half(0))
        for way, slot in order:
            out_over(way, slot).wait_recv()
        go(save_half(1))
        for j in range(1, n_ctx):
            kv_step(j).wait_recv()
        saves[1].start()
        for t in range(1, n):
            gain_step(t).wait_send()
            for way in range(2):
                for k in range(2):
                    step(k, way, t).wait_send()
        for way, slot in order:
            out_over(way, slot).wait_send()
            for b in range(held):
                over_core(b, way, slot).wait_send()
            if across_x:
                over_x(way, slot).wait_send()
        for j in range(1, n_ctx):
            kv_step(j).wait_send()
        for copies in [save_share(b) for b in range(n_dp)] + [save_half(k) for k in range(2)] + [saves]:
            for copy in copies:
                copy.wait()

    dma = pltpu.SemaphoreType.DMA
    shapes = [
        (span, qkvwidth),
        ((n_ctx - 1) * span, 2 * kvwidth),
        (span, width),
        (width, qkvwidth),
        (width, 2 * half),
        (n, 16, rows),
    ]
    return pl.pallas_call(
        kernel,
        in_specs=[WHOLE, ANY, ANY, ANY, WHOLE, WHOLE, WHOLE],
        out_specs=[ANY] * 6,
        out_shape=[jax.ShapeDtypeStruct(shape, BF) for shape in shapes],
        scratch_shapes=[pltpu.VMEM(shape, BF) for shape in shapes[:3]]
        + [pltpu.VMEM((width, share), BF)] * n_dp
        + [pltpu.VMEM((width, half), BF)] * 2
        + [pltpu.VMEM((n, 16, rows), BF)]
        + [
            dma((3,)),
            dma((4,)),
            dma((n_dp, n)),
            dma((2, n)),
            dma((2, 2, n)),
            dma((2, 2, n)),
            dma((2, n)),
            dma((2, n)),
            dma((n_dp // 2, 2, n)),
            dma((n_dp // 2, 2, n)),
            dma((2, n)),
            dma((2, n)),
            dma((n,)),
            dma((n,)),
            dma((n_ctx,)),
            dma((n_ctx,)),
        ],
        compiler_params=pltpu.CompilerParams(
            collective_id=0, has_side_effects=True, vmem_limit_bytes=56 * MIB
        ),
        cost_estimate=cost(2 * span * width * qkvwidth, 4 * width * qkvwidth),
    )(x, w_qkv, w_out, gains, *tables)


def closing(sizes, fulls, slotted, sums):
    n_dp, n_fsdp, n_ctx = sizes
    n = n_fsdp * n_ctx
    rows = [f.shape[0] // n for f in fulls]
    widths = [f.shape[1] // 2 for f in fulls]
    kinds = [f.dtype for f in fulls]
    count = len(fulls)
    bits = [1 << k for k in range(1, n_dp.bit_length() - 1)]
    others = n_dp - 1

    def kernel(*refs):
        refs = list(refs)

        def take(size):
            out = refs[:size]
            del refs[:size]
            return out

        full, own_sums = take(count), take(len(sums))
        outs, blocks_out = take(count), take(len(sums) * others)
        near, land, done, extra, back = take(count), take(count), take(count), take(count), take(count)
        own = take(count)
        (own_sems,) = take(1)
        send, recv, pair_send, pair_recv, x_send, x_recv, end_send, end_recv = take(8)
        spread = TeamSpread(
            n_dp, own_sums, [blocks_out[k * others : (k + 1) * others] for k in range(len(sums))], *refs
        )
        me = lax.axis_index("dp")
        core = me % 2
        sibling = {"dp": me + 1 - 2 * core}
        place, device = ring_place(n_fsdp)
        ahead, behind = device((place + 1) % n), device((place + n - 1) % n)
        facing = [{"dp": me + bit - 2 * bit * ((me // bit) % 2)} for bit in bits]
        greet([ahead, behind, sibling] + facing)

        def half(g, way):
            return pl.ds(way * (widths[g] // 2), widths[g] // 2)

        def half_of(g, way, whose):
            base = whose * widths[g] + way * (widths[g] // 2)
            return pl.ds(pl.multiple_of(base, 128), widths[g] // 2)

        def at(g, slot):
            return pl.ds(slot * rows[g], rows[g])

        def source_at(g, slot):
            if slotted[g]:
                return at(g, slot)
            there = device((place + n - slot) % n)
            block = there["fsdp"] * n_ctx + there["ctx"]
            return pl.ds(pl.multiple_of(block * rows[g], rows[g]), rows[g])

        def swap(g, way, slot):
            return pltpu.make_async_remote_copy(
                src_ref=full[g].at[source_at(g, slot), half_of(g, way, 1 - core)],
                dst_ref=near[g].at[at(g, slot), half(g, way)],
                send_sem=pair_send.at[g, way, slot],
                recv_sem=pair_recv.at[g, way, slot],
                device_id=sibling,
                device_id_type=MESH,
            )

        def step(g, way, t):
            slot = t if way == 0 else n - t
            source = near[g].at[at(g, slot), half(g, way)] if t == 1 else land[g].at[way, t - 2]
            return pltpu.make_async_remote_copy(
                src_ref=source,
                dst_ref=land[g].at[way, t - 1],
                send_sem=send.at[g, way, t],
                recv_sem=recv.at[g, way, t],
                device_id=ahead if way == 0 else behind,
                device_id_type=MESH,
            )

        def face(g, k):
            return pltpu.make_async_remote_copy(
                src_ref=done[g].at[k],
                dst_ref=extra[g].at[k],
                send_sem=x_send.at[g, k],
                recv_sem=x_recv.at[g, k],
                device_id=facing[k],
                device_id_type=MESH,
            )

        def end(g):
            return pltpu.make_async_remote_copy(
                src_ref=done[g].at[len(bits)],
                dst_ref=back[g],
                send_sem=end_send.at[g],
                recv_sem=end_recv.at[g],
                device_id=sibling,
                device_id_type=MESH,
            )

        def own_load(g, way, t):
            slot = t % n if way == 0 else n - t
            return pltpu.make_async_copy(
                full[g].at[source_at(g, slot), half_of(g, way, core)],
                own[g].at[way, t % 2],
                own_sems.at[g, way, t % 2],
            )

        def both(g, way, t, slot):
            own_load(g, way, t).wait()
            swap(g, way, slot).wait_recv()
            return own[g][way, t % 2].astype(F32) + near[g][at(g, slot), half(g, way)].astype(F32)

        def forward(g, t):
            for way in range(2):
                slot = t if way == 0 else n - t
                value = both(g, way, t, slot)
                if t == 1:
                    near[g][at(g, slot), half(g, way)] = value.astype(kinds[g])
                else:
                    step(g, way, t - 1).wait_recv()
                    land[g][way, t - 2] = (value + land[g][way, t - 2].astype(F32)).astype(kinds[g])
                step(g, way, t).start()
                own_load(g, way, t + 1).start()

        def finish(g):
            for way in range(2):
                value = both(g, way, n, 0)
                step(g, way, n - 1).wait_recv()
                done[g][0, :, half(g, way)] = (value + land[g][way, n - 2].astype(F32)).astype(kinds[g])
            if bits:
                face(g, 0).start()

        rest = list(range(1, count))
        for g in range(count):
            for way in range(2):
                own_load(g, way, 1).start()
        for t in range(1, n + 1):
            for g in rest + [0]:
                swap(g, 0, t % n).start()
                swap(g, 1, n - t).start()
        spread.start(0)
        for t in range(1, n):
            for g in rest:
                forward(g, t)
            if t >= 2:
                forward(0, t - 1)
        spread.arrive(0)
        spread.start(1)
        for g in rest:
            finish(g)
        forward(0, n - 1)
        finish(0)
        for k in range(len(bits)):
            for g in range(count):
                face(g, k).wait_recv()
                done[g][k + 1] = (done[g][k].astype(F32) + extra[g][k].astype(F32)).astype(kinds[g])
                if k + 1 < len(bits):
                    face(g, k + 1).start()
        for g in range(count):
            end(g).start()
            here = pl.ds(pl.multiple_of(core * widths[g], 128), widths[g])
            outs[g][:, here] = done[g][len(bits)].astype(F32)
        for g in range(count):
            end(g).wait_recv()
            here = pl.ds(pl.multiple_of((1 - core) * widths[g], 128), widths[g])
            outs[g][:, here] = back[g][...].astype(F32)
        spread.arrive(1)
        spread.last()
        for g in range(count):
            end(g).wait_send()
            for k in range(len(bits)):
                face(g, k).wait_send()
            for way in range(2):
                for t in range(1, n):
                    step(g, way, t).wait_send()
                for slot in range(n):
                    swap(g, way, slot).wait_send()

    dma = pltpu.SemaphoreType.DMA
    groups = list(zip(rows, widths, kinds))
    out = pl.pallas_call(
        kernel,
        in_specs=[ANY] * (count + len(sums)),
        out_specs=[WHOLE] * count + [ANY] * (len(sums) * others),
        out_shape=[jax.ShapeDtypeStruct((r, 2 * w), F32) for r, w, _ in groups]
        + [jax.ShapeDtypeStruct(a.shape, BF) for a in sums for _ in range(others)],
        scratch_shapes=[pltpu.VMEM((n * r, w), kind) for r, w, kind in groups]
        + [pltpu.VMEM((2, n - 1, r, w // 2), kind) for r, w, kind in groups]
        + [pltpu.VMEM((len(bits) + 1, r, w), kind) for r, w, kind in groups]
        + [pltpu.VMEM((max(1, len(bits)), r, w), kind) for r, w, kind in groups]
        + [pltpu.VMEM((r, w), kind) for r, w, kind in groups]
        + [pltpu.VMEM((2, 2, r, w // 2), kind) for r, w, kind in groups]
        + [
            dma((count, 2, 2)),
            dma((count, 2, n)),
            dma((count, 2, n)),
            dma((count, 2, n)),
            dma((count, 2, n)),
            dma((count, max(1, len(bits)))),
            dma((count, max(1, len(bits)))),
            dma((count,)),
            dma((count,)),
        ]
        + spread_scratch(len(sums), n_dp),
        compiler_params=pltpu.CompilerParams(
            collective_id=1, has_side_effects=True, vmem_limit_bytes=60 * MIB
        ),
        cost_estimate=cost(0, sum(12 * n * r * w for r, w, _ in groups)),
    )(*fulls, *sums)
    return out[:count], [out[count + k * others : count + (k + 1) * others] for k in range(len(sums))]


class Ring:
    def __init__(self, n_fsdp, n_ctx):
        order = []
        for c in range(n_ctx):
            rows = range(n_fsdp) if c % 2 == 0 else reversed(range(n_fsdp))
            order += [f * n_ctx + c for f in rows]
        self.order = order
        self.size = n = len(order)
        place = [0] * n
        for k, block in enumerate(order):
            place[block] = k
        self.place = place
        self.block = lax.axis_index(GRID)
        self.rank = jnp.array(place, jnp.int32)[self.block]

    def slot_blocks(self):
        slots = jnp.arange(self.size, dtype=jnp.int32)
        return jnp.array(self.order, jnp.int32)[(self.rank - slots) % self.size]

    def to_slots(self, array, axis=1, deps=()):
        return reorder(array, self.slot_blocks(), axis, deps)

    def from_slots(self, array, axis=1):
        return reorder(array, (self.rank - jnp.array(self.place, jnp.int32)) % self.size, axis)


class Team:
    def __init__(self, size):
        self.size = size
        self.rank = lax.axis_index("dp")
        self.bits = [1 << k for k in range(size.bit_length() - 1)]
        self.order = [0]
        for bit in reversed(self.bits):
            self.order = self.order + [m ^ bit for m in self.order]

    def swap(self, value, bit):
        return lax.ppermute(value, "dp", [(k, k ^ bit) for k in range(self.size)])

    def scatter(self, parts):
        for bit in self.bits:
            half = len(parts) // 2
            got = [self.swap(part.astype(BF), bit) for part in parts[half:]]
            parts = [kept + part.astype(F32) for kept, part in zip(parts[:half], got)]
        return parts[0]


def shards(sizes, x_in, span_order, attn_gain, w_qkv, w_out, ffn_gain, w_gate_up, w_down, cotangent):
    n_dp, n_fsdp, n_ctx = sizes
    ring = Ring(n_fsdp, n_ctx)
    team = Team(n_dp)
    n = ring.size
    width = x_in.shape[-1]
    rows = width // n
    tokens = x_in.reshape(-1, width)
    span = tokens.shape[0]
    rank = lax.axis_index("ctx")
    qwidth = HEADS * HD
    kvwidth = KV_HEADS * HD
    ffwidth = w_down.shape[1]
    order = span_order.reshape(-1)
    near = [(rank + k) % n_ctx for k in range(n_ctx)]
    offsets = jnp.arange(span, dtype=jnp.int32)
    query_pos = order[rank] * span + offsets
    seen = jnp.stack([order[c] < order[rank] for c in near[1:]]).astype(jnp.int32)
    tables = rope_tables(query_pos.astype(F32))

    ffq = ffwidth // n_dp
    sub = ffq // SUBS
    grad_y = cotangent.reshape(span, width)
    dy = ring.to_slots(grad_y)
    gains = jnp.concatenate([attn_gain[None], ffn_gain[None], jnp.zeros((14, rows), BF)], 0)
    qkv, kv_far, normed_one, wqkv, wout, gains = opening(sizes, tokens, w_qkv, w_out, gains, tables)
    attn_t, lse, hidden_one, normed_two, x_others, dy_others, weights_a = attend_forward(
        sizes, tokens, qkv, kv_far, seen, wout, gains, dy, w_gate_up, w_down
    )
    xs = [normed_two] + list(x_others)
    dys = [dy] + list(dy_others)
    gains = gains[:, :2][(ring.rank - jnp.array(ring.place, jnp.int32)) % n]
    gain_one = gains[:, 0].reshape(-1).astype(F32)
    gain_two = gains[:, 1].reshape(-1).astype(F32)
    inputs = tokens.astype(F32)
    scale_one = inv_rms(inputs)
    scale_two = inv_rms(hidden_one)

    y, dn, grads_a, weights_b = feed_forward(
        sizes, xs, dys, [[w] for w in weights_a], None, (w_gate_up, w_down), False, 2
    )
    y, dn, grads_b, sums_a = feed_forward(
        sizes, xs, dys, [[w] for w in weights_b], list(zip(y, dn)), grads_a, True, 3
    )

    d_normed_two = ring.from_slots(sum(part.astype(F32) for part in dn))
    d_hidden_norm, d_gain_two = norm_back(hidden_one, scale_two, gain_two, d_normed_two)
    d_hidden = grad_y.astype(F32) + d_hidden_norm
    d_proj = d_hidden.astype(BF)

    d_attn = matmul_rows(d_proj, wout).astype(BF)
    d_qkv, part_out, part_qkv, sums_b, others_a = attend_backward(
        sizes, qkv, kv_far, d_attn, lse, seen, tables, attn_t, d_proj, normed_one, grads_b, sums_a, 4
    )
    d_normed_one = matmul_rows(d_qkv, wqkv)
    d_input_norm, d_gain_one = norm_back(inputs, scale_one, gain_one, d_normed_one)
    grad_input = d_hidden + d_input_norm

    room = max(rows, 256)

    def by_slot(gain):
        blocks = gain.reshape(n, 1, rows)[ring.slot_blocks()]
        return jnp.pad(blocks, ((0, 0), (0, 7), (0, room - rows))).reshape(n * 8, room)

    part_gain = jnp.concatenate([by_slot(d_gain_one), by_slot(d_gain_two)], 1)
    (grad_qkv, grad_out, grad_gain), others_b = closing(
        sizes, (part_qkv, part_out, part_gain), (True, False, True), sums_b
    )

    placed, columns = [], []
    for q in range(SUBS):
        blocks = [sums_a[q]] + list(others_a[q]) if q < 2 else [sums_b[q - 2]] + list(others_b[q - 2])
        for m, block in zip(team.order, blocks):
            placed.append(block)
            columns.append((team.rank ^ m) * ffq + q * sub)
    grad_gate_up, grad_down = place_grads(placed, jnp.stack(columns).astype(jnp.int32), sub, ffwidth)

    y_out = hidden_one + ring.from_slots(team.scatter(y))
    return (
        y_out.astype(BF).reshape(x_in.shape),
        grad_input.reshape(x_in.shape),
        grad_gain[0, :rows],
        grad_qkv,
        grad_out,
        grad_gain[0, room : room + rows],
        grad_gate_up,
        grad_down,
    )


def solution(mesh):
    sizes = (mesh.shape["dp"], mesh.shape["fsdp"], mesh.shape["ctx"])
    tokens = P(("dp", "fsdp"), "ctx", None)
    weight = P(("fsdp", "ctx"), None)
    gain = P(("fsdp", "ctx"))

    def body(*args):
        return shards(sizes, *args)

    return jax.shard_map(
        body,
        mesh=mesh,
        in_specs=(tokens, P(("dp", "fsdp"), None), gain, weight, weight, gain, weight, weight, tokens),
        out_specs=(tokens, tokens, gain, weight, weight, gain, weight, weight),
        check_vma=False,
    )
```

```python
import math

import jax
import jax.numpy as jnp
from jax import lax
from jax.experimental import pallas as pl
from jax.experimental.pallas import tpu as pltpu
from jax.sharding import PartitionSpec as P

HEADS = 32
KV_HEADS = 8
HD = 64
EPS = 1e-05
SUBS = 4

BF = jnp.bfloat16
F32 = jnp.float32
GRID = ("fsdp", "ctx")


def matmul(left, right):
    return jnp.dot(left, right, preferred_element_type=F32)


def matmul_rows(left, right):
    return lax.dot_general(left, right, (((1,), (1,)), ((), ())), preferred_element_type=F32)


def matmul_tokens(left, right):
    return lax.dot_general(left, right, (((0,), (0,)), ((), ())), preferred_element_type=F32)


def rope_tables(positions):
    half = HD // 2
    freq = jnp.exp(jnp.arange(half, dtype=F32) * (-math.log(500000.0) / half))
    angle = positions[:, None] * freq[None, :]
    cosine, sine = jnp.cos(angle), jnp.sin(angle)
    zero = jnp.zeros_like(sine)
    return (
        jnp.concatenate([cosine] * 4, -1),
        jnp.concatenate([-sine, zero] * 2, -1),
        jnp.concatenate([zero, sine] * 2, -1),
    )


def inv_rms(rows):
    return lax.rsqrt(jnp.mean(rows * rows, -1, keepdims=True) + EPS)


def norm_back(rows, scale, gain, grad):
    unit = rows * scale
    pulled = grad * gain[None, :]
    inner = jnp.mean(pulled * unit, -1, keepdims=True)
    return scale * (pulled - unit * inner), jnp.sum(grad * unit, 0)


MIB = 1 << 20
ANY = pl.BlockSpec(memory_space=pl.ANY)
WHOLE = pl.BlockSpec(memory_space=pltpu.VMEM)


def cost(flops, moved, exps=0):
    return pl.CostEstimate(flops=int(flops), bytes_accessed=int(moved), transcendentals=int(exps))


def params(mib):
    return pltpu.CompilerParams(vmem_limit_bytes=mib * MIB)


def dot_nn(a, b):
    return lax.dot_general(a, b, (((1,), (0,)), ((), ())), preferred_element_type=F32)


def dot_nt(a, b):
    return lax.dot_general(a, b, (((1,), (1,)), ((), ())), preferred_element_type=F32)


def dot_tn(a, b):
    return lax.dot_general(a, b, (((0,), (0,)), ((), ())), preferred_element_type=F32)


def reorder(array, places, axis=1, deps=()):
    count = places.shape[0]
    if axis == 1 and (array.shape[1] // count) % 128 != 0:
        size = array.shape[1] // count
        blocks = [lax.dynamic_slice_in_dim(array, places[s] * size, size, 1) for s in range(count)]
        return jnp.concatenate(blocks, 1)
    if axis == 1:
        shape = (array.shape[0], array.shape[1] // count)
        took = lambda s, where: (0, where[s])
        gave = lambda s, where: (0, s)
    else:
        shape = (array.shape[0] // count, array.shape[1])
        took = lambda s, where: (where[s], 0)
        gave = lambda s, where: (s, 0)

    def kernel(where, source, *rest):
        rest[-1][...] = source[...]

    return pl.pallas_call(
        kernel,
        grid_spec=pltpu.PrefetchScalarGridSpec(
            num_scalar_prefetch=1,
            grid=(count,),
            in_specs=[pl.BlockSpec(shape, took)] + [ANY] * len(deps),
            out_specs=pl.BlockSpec(shape, gave),
        ),
        out_shape=jax.ShapeDtypeStruct(array.shape, array.dtype),
        compiler_params=params(16),
        cost_estimate=cost(0, 2 * array.size * array.dtype.itemsize),
    )(places, array, *deps)


def turn(piece, cosine, sine_low, sine_high):
    return (
        piece * cosine
        + pltpu.roll(piece, 128 - HD // 2, axis=1) * sine_low
        + pltpu.roll(piece, HD // 2, axis=1) * sine_high
    )


def head_of(block, group):
    odd = (group // 2) % 2 == 1
    return jnp.where(odd, block[:, HD:], block[:, :HD])


def causal_tile(size):
    key = lax.broadcasted_iota(jnp.int32, (size, size), 0)
    query = lax.broadcasted_iota(jnp.int32, (size, size), 1)
    return key <= query


def scores_of(key, key_far, query, seen, mask, span):
    tile = query.shape[0]
    own = dot_nt(key, query)
    if key.shape[0] > tile:
        last = key.shape[0] - tile
        own = jnp.concatenate([own[:last], jnp.where(mask, own[last:], -1e30)], 0)
    else:
        own = jnp.where(mask, own, -1e30)
    far = dot_nt(key_far, query)
    far = [jnp.where(seen[k], far[k * span : (k + 1) * span], -1e30) for k in range(len(seen))]
    return own, (far[0] if len(far) == 1 else jnp.concatenate(far, 0))


def place_grads(pieces, columns, sub, ffwidth):
    rows = pieces[0].shape[0]
    count = len(pieces)

    def kernel(*refs):
        where = refs[0]
        sources = refs[1 : 1 + count]
        gu_ref, down_ref, took, gave, in_sems, out_sems = refs[1 + count :]

        def read(k):
            return pltpu.make_async_copy(sources[k], took.at[k % 2], in_sems.at[k % 2])

        def writes(k):
            at = pl.multiple_of(where[k], 128)
            here = gave.at[k % 2]
            return (
                pltpu.make_async_copy(
                    here.at[:, pl.ds(0, sub)], gu_ref.at[:, pl.ds(at, sub)], out_sems.at[k % 2, 0]
                ),
                pltpu.make_async_copy(
                    here.at[:, pl.ds(sub, sub)], gu_ref.at[:, pl.ds(at + ffwidth, sub)], out_sems.at[k % 2, 1]
                ),
                pltpu.make_async_copy(
                    here.at[:, pl.ds(2 * sub, sub)], down_ref.at[:, pl.ds(at, sub)], out_sems.at[k % 2, 2]
                ),
            )

        read(0).start()
        for k in range(count):
            if k + 1 < count:
                read(k + 1).start()
            read(k).wait()
            if k >= 2:
                for copy in writes(k - 2):
                    copy.wait()
            gave[k % 2] = took[k % 2].astype(F32)
            for copy in writes(k):
                copy.start()
        for k in range(max(0, count - 2), count):
            for copy in writes(k):
                copy.wait()

    return pl.pallas_call(
        kernel,
        in_specs=[pl.BlockSpec(memory_space=pltpu.SMEM)] + [ANY] * count,
        out_specs=[ANY, ANY],
        out_shape=[
            jax.ShapeDtypeStruct((rows, 2 * ffwidth), F32),
            jax.ShapeDtypeStruct((rows, ffwidth), F32),
        ],
        scratch_shapes=[
            pltpu.VMEM((2, rows, 3 * sub), BF),
            pltpu.VMEM((2, rows, 3 * sub), F32),
            pltpu.SemaphoreType.DMA((2,)),
            pltpu.SemaphoreType.DMA((2, 3)),
        ],
        compiler_params=params(60),
        cost_estimate=cost(0, rows * ffwidth * 18),
    )(columns, *pieces)


MESH = pl.DeviceIdType.MESH


def ring_place(n_fsdp):
    f, c = lax.axis_index("fsdp"), lax.axis_index("ctx")

    def device(place):
        row, k = place // n_fsdp, place % n_fsdp
        return {"fsdp": k + (row % 2) * (n_fsdp - 1 - 2 * k), "ctx": row}

    return c * n_fsdp + f + (c % 2) * (n_fsdp - 1 - 2 * f), device


def slot_lanes(ref, block, rows):
    if rows % 128 == 0:
        return ref[:, pl.ds(pl.multiple_of(block * rows, 128), rows)].astype(F32)
    share = 128 // rows
    wide = ref[:, pl.ds(pl.multiple_of(block // share * 128, 128), 128)].astype(F32)
    part = wide[:, :rows]
    for k in range(1, share):
        part = jnp.where(block % share == k, wide[:, k * rows : (k + 1) * rows], part)
    return part


def team_place(size, me, bit):
    return me + bit - 2 * bit * ((me // bit) % 2)


def greet(partners):
    barrier = pltpu.get_barrier_semaphore()
    for partner in partners:
        pl.semaphore_signal(barrier, inc=1, device_id=partner, device_id_type=MESH)
    pl.semaphore_wait(barrier, len(partners))


def own_columns(size, w_gate_up, w_down, first):
    ffwidth = w_down.shape[1]
    ffq = ffwidth // size
    sub = ffq // SUBS
    out = []
    for way in range(2):
        at = lax.axis_index("dp") * ffq + (first + way) * sub
        out.append(
            [
                (w_gate_up.at[:, pl.ds(pl.multiple_of(at, 128), sub)], 0),
                (w_gate_up.at[:, pl.ds(pl.multiple_of(at + ffwidth, 128), sub)], sub),
                (w_down.at[:, pl.ds(pl.multiple_of(at, 128), sub)], 2 * sub),
            ]
        )
    return out


class RingGather:
    def __init__(self, sizes, own, out, own_v, own_sem, store_sem, send, recv):
        self.n = sizes[1] * sizes[2]
        self.rows = own_v.shape[1]
        self.own, self.out, self.own_v = own, out, own_v
        self.own_sem, self.store_sem, self.send, self.recv = own_sem, store_sem, send, recv
        place, device = ring_place(sizes[1])
        self.partners = [device((place + 1) % self.n), device((place + self.n - 1) % self.n)]

    def rows_of(self, way, t):
        slot = t if way == 0 else (self.n - t) % self.n
        return pl.ds(slot * self.rows, self.rows)

    def loads(self, way):
        width = self.own_v.shape[2] // 3
        return [
            pltpu.make_async_copy(
                source, self.own_v.at[way, :, pl.ds(place, width)], self.own_sem.at[way, place // width]
            )
            for source, place in self.own[way]
        ]

    def store(self, way):
        return pltpu.make_async_copy(
            self.own_v.at[way], self.out[way].at[pl.ds(0, self.rows)], self.store_sem.at[way]
        )

    def ring(self, way, t, first=False):
        source = self.own_v.at[way] if first else self.out[way].at[self.rows_of(way, t - 1)]
        return pltpu.make_async_remote_copy(
            src_ref=source,
            dst_ref=self.out[way].at[self.rows_of(way, t)],
            send_sem=self.send.at[way, t],
            recv_sem=self.recv.at[way, t],
            device_id=self.partners[way],
            device_id_type=MESH,
        )

    def arrived(self, way, t):
        target = self.out[way].at[self.rows_of(way, t)]
        return pltpu.make_async_remote_copy(
            src_ref=target,
            dst_ref=target,
            send_sem=self.send.at[way, t],
            recv_sem=self.recv.at[way, t],
            device_id=self.partners[way],
            device_id_type=MESH,
        )

    def first(self):
        for way in range(2):
            for copy in self.loads(way):
                copy.start()
        for way in range(2):
            for copy in self.loads(way):
                copy.wait()
            self.ring(way, 1, True).start()
            self.store(way).start()

    def tick(self, t):
        for way in range(2):
            self.arrived(way, t - 1).wait_recv()
            self.ring(way, t).start()

    def last(self):
        for way in range(2):
            self.arrived(way, self.n - 1).wait_recv()
            self.store(way).wait()
            self.ring(way, 1, True).wait_send()
            for t in range(2, self.n):
                self.ring(way, t).wait_send()


def gather_scratch(n, rows, wide):
    dma = pltpu.SemaphoreType.DMA
    return [pltpu.VMEM((2, rows, wide), BF), dma((2, 3)), dma((2,)), dma((2, n)), dma((2, n))]


class RingReduce:
    def __init__(self, sizes, parts, out, land, own_v, own_sem, out_sem, send, recv):
        self.n = sizes[1] * sizes[2]
        self.rows, self.wide = out[0].shape
        self.parts, self.out, self.land, self.own_v = parts, out, land, own_v
        self.own_sem, self.out_sem, self.send, self.recv = own_sem, out_sem, send, recv
        place, device = ring_place(sizes[1])
        self.partners = [device((place + 1) % self.n), device((place + self.n - 1) % self.n)]

    def lanes(self, h):
        return pl.ds(pl.multiple_of(h * (self.wide // 2), 128), self.wide // 2)

    def load_own(self, way, t):
        slot = t % self.n if way == 0 else self.n - t
        return pltpu.make_async_copy(
            self.parts[way].at[pl.ds(slot * self.rows, self.rows)],
            self.own_v.at[way, t % 3],
            self.own_sem.at[way, t % 3],
        )

    def ring(self, source, way, t, h):
        return pltpu.make_async_remote_copy(
            src_ref=source,
            dst_ref=self.land.at[way, h, t - 1],
            send_sem=self.send.at[way, h, t],
            recv_sem=self.recv.at[way, h, t],
            device_id=self.partners[way],
            device_id_type=MESH,
        )

    def arrived(self, way, t, h):
        return self.ring(self.land.at[way, h, t - 1], way, t, h)

    def start(self, way, h):
        return self.ring(self.own_v.at[way, 1, :, self.lanes(h)], way, 1, h)

    def forward(self, way, t, h):
        return self.ring(self.land.at[way, h, t - 2], way, t, h)

    def save(self, way):
        return pltpu.make_async_copy(self.own_v.at[way, self.n % 3], self.out[way], self.out_sem.at[way])

    def first(self):
        for way in range(2):
            self.load_own(way, 1).start()
            self.load_own(way, 2).start()
        for way in range(2):
            self.load_own(way, 1).wait()
            for h in range(2):
                self.start(way, h).start()

    def total(self, way, t, h):
        return self.own_v[way, t % 3, :, self.lanes(h)].astype(F32) + self.land[way, h, t - 2].astype(F32)

    def step(self, u):
        t, h = u // 2, u % 2
        for way in range(2):
            self.arrived(way, t - 1, h).wait_recv()

            @pl.when(h == 0)
            def _():
                self.load_own(way, t).wait()

                @pl.when(t == 3)
                def _():
                    for half in range(2):
                        self.start(way, half).wait_send()

                self.load_own(way, t + 1).start()

            self.land[way, h, t - 2] = self.total(way, t, h).astype(BF)
            self.forward(way, t, h).start()

    def last(self):
        n = self.n
        for way in range(2):
            self.load_own(way, n).wait()
            for h in range(2):
                self.arrived(way, n - 1, h).wait_recv()
                half = self.wide // 2
                total = self.total(way, n, h).astype(BF)
                self.own_v[way, n % 3, :, h * half : (h + 1) * half] = total
            self.save(way).start()
        for way in range(2):
            for h in range(2):
                for t in range(2, n):
                    self.forward(way, t, h).wait_send()
            self.save(way).wait()


def reduce_scratch(n, rows, wide):
    dma = pltpu.SemaphoreType.DMA
    return [
        pltpu.VMEM((2, 2, n - 1, rows, wide // 2), BF),
        pltpu.VMEM((2, 3, rows, wide), BF),
        dma((2, 3)),
        dma((2,)),
        dma((2, 2, n)),
        dma((2, 2, n)),
    ]


class TeamSpread:
    def __init__(self, size, own, others, send, recv):
        self.own, self.others, self.send, self.recv = own, others, send, recv
        self.count = len(own)
        me = lax.axis_index("dp")
        self.stages = []
        held, bit = 1, size // 2
        while bit:
            partner = {"dp": me + bit - 2 * bit * ((me // bit) % 2)}
            self.stages.append((held, partner))
            held, bit = 2 * held, bit // 2

    def partners(self):
        return [partner for _, partner in self.stages]

    def copies(self, stage):
        held, partner = self.stages[stage]
        for k in range(self.count):
            for b in range(held):
                yield pltpu.make_async_remote_copy(
                    src_ref=self.own[k] if b == 0 else self.others[k][b - 1],
                    dst_ref=self.others[k][held + b - 1],
                    send_sem=self.send.at[k, held + b - 1],
                    recv_sem=self.recv.at[k, held + b - 1],
                    device_id=partner,
                    device_id_type=MESH,
                )

    def start(self, stage):
        if stage < len(self.stages):
            for copy in self.copies(stage):
                copy.start()

    def arrive(self, stage):
        if stage < len(self.stages):
            for copy in self.copies(stage):
                copy.wait_recv()

    def last(self):
        for stage in range(len(self.stages)):
            for copy in self.copies(stage):
                copy.wait_send()


def spread_scratch(count, size):
    return [pltpu.SemaphoreType.DMA((count, size)), pltpu.SemaphoreType.DMA((count, size))]


def feed_forward(sizes, xs, dys, weights, before, ring_parts, reducing, ident):
    n_dp, n_fsdp, n_ctx = sizes
    n = n_fsdp * n_ctx
    team, (span, width) = len(xs), xs[0].shape
    rows, wide = width // n, weights[0][0].shape[1]
    sub = wide // 3
    pieces = [piece for group in weights for piece in group]
    counts = [len(group) for group in weights]
    tile = min(span, 256)
    per = span // tile
    steps = team * per
    part = max(rows, 128)
    half = width // 2
    gsteps = width // part
    total = 2 * steps + gsteps
    inside = team // 2 if reducing and team > 2 else 0
    carried = [] if before is None else [b[0] for b in before] + [b[1] for b in before]
    backwards = reducing

    def kernel(*refs):
        refs = list(refs)

        def take(count):
            out = refs[:count]
            del refs[:count]
            return out

        x_refs, dy_refs, piece_refs = take(team), take(team), take(len(pieces))
        old_y, old_dn = take(len(carried) // 2), take(len(carried) // 2)
        part_refs = take(2)
        y_refs, dn_refs, grad_refs, ring_outs = take(team), take(team), take(2), take(2)
        if reducing:
            near = take(max(1, inside))
            (far,) = take(1)
        wgu, wd, xb, dyb, yb, dnb, dgu, inner, xg, dyg, gout = take(11)
        w_sems, x_sems, y_sems, g_sems, gout_sems = take(5)
        if carried:
            cb, c_sems = take(2)
        if reducing:
            swap_send, swap_recv, face_send, face_recv = take(4)
            ring = RingReduce(sizes, part_refs, ring_outs, *refs)
        else:
            ring = RingGather(sizes, own_columns(n_dp, *part_refs, SUBS // 2), ring_outs, *refs)
        me = lax.axis_index("dp")
        sibling = {"dp": me + 1 - 2 * (me % 2)}
        bit = team // 2
        facing = {"dp": me + bit - 2 * bit * ((me // bit) % 2)}

        k = 0
        w_copies = []
        for b, count in enumerate(counts):
            at = 0
            for ref in piece_refs[k : k + count]:
                high = ref.shape[0]
                w_copies += [
                    pltpu.make_async_copy(
                        ref.at[:, pl.ds(0, 2 * sub)],
                        wgu.at[pl.ds(at, high), pl.ds(b * 2 * sub, 2 * sub)],
                        w_sems.at[2 * k],
                    ),
                    pltpu.make_async_copy(
                        ref.at[:, pl.ds(2 * sub, sub)],
                        wd.at[pl.ds(at, high), pl.ds(b * sub, sub)],
                        w_sems.at[2 * k + 1],
                    ),
                ]
                at += high
                k += 1
        for copy in w_copies:
            copy.start()

        def block_of(i):
            return team - 1 - i // per if backwards else i // per

        def loads(m, i):
            rows_here = pl.ds((i % per) * tile, tile)
            return [
                pltpu.make_async_copy(x_refs[m].at[rows_here], xb.at[i % 2], x_sems.at[0, i % 2]),
                pltpu.make_async_copy(dy_refs[m].at[rows_here], dyb.at[i % 2], x_sems.at[1, i % 2]),
            ]

        def more(m, i):
            if not carried:
                return []
            rows_here = pl.ds((i % per) * tile, tile)
            out = [
                pltpu.make_async_copy(old_y[m].at[rows_here], yb, c_sems.at[0]),
                pltpu.make_async_copy(old_dn[m].at[rows_here], dnb, c_sems.at[1]),
            ]
            if m < inside:
                out.append(pltpu.make_async_copy(near[m].at[rows_here], cb, c_sems.at[2]))
            return out

        def writes(m, i):
            rows_here = pl.ds((i % per) * tile, tile)
            return [
                pltpu.make_async_copy(yb, y_refs[m].at[rows_here], y_sems.at[0]),
                pltpu.make_async_copy(dnb, dn_refs[m].at[rows_here], y_sems.at[1]),
            ]

        def on_block(i, act):
            for m in range(team):

                @pl.when(block_of(i) == m)
                def _():
                    act(m)

        def swap(m):
            return pltpu.make_async_remote_copy(
                src_ref=dn_refs[m],
                dst_ref=near[m - inside],
                send_sem=swap_send.at[m - inside],
                recv_sem=swap_recv.at[m - inside],
                device_id=sibling,
                device_id_type=MESH,
            )

        def face():
            return pltpu.make_async_remote_copy(
                src_ref=dn_refs[1],
                dst_ref=far,
                send_sem=face_send,
                recv_sem=face_recv,
                device_id=facing,
                device_id_type=MESH,
            )

        def go(copies):
            for copy in copies:
                copy.start()

        def end(copies):
            for copy in copies:
                copy.wait()

        def ticks(lo, hi):
            if reducing:
                count, base, act = 2 * (n - 2), 4, ring.step
            else:
                count, base, act = n - 2, 2, ring.tick
            lax.fori_loop(
                base + lo * count // total, base + hi * count // total, lambda t, c: (act(t), c)[1], 0
            )

        on_block(0, lambda m: go(loads(m, 0)))
        partners = list(ring.partners)
        if inside:
            partners.append(sibling)
        if reducing and team > 1:
            partners.append(facing)
        greet(partners)
        ring.first()
        for copy in w_copies:
            copy.wait()

        def forward(i, carry):
            @pl.when(i + 1 < steps)
            def _():
                on_block(i + 1, lambda m: go(loads(m, i + 1)))

            @pl.when(i == steps - 1)
            def _():
                go(sides(0))

            if inside:
                @pl.when(i % per == 0)
                def _():
                    on_block(i, lambda m: swap(m + inside).wait_recv() if m < inside else None)

            ticks(2 * i, 2 * i + 2)
            end(loads(0, i))
            here = pl.ds(pl.multiple_of(i * tile, tile), tile)
            if carried:
                drained = (i > 0) & (i % per != 0) if reducing else i > 0

                @pl.when(drained)
                def _():
                    end(writes(0, i))

                on_block(i, lambda m: go(more(m, i)))
            for b in range(2):
                gate_up = dot_nn(xb[i % 2], wgu[:, b * 2 * sub : (b + 1) * 2 * sub])
                d_inner = dot_nn(dyb[i % 2], wd[:, b * sub : (b + 1) * sub])
                gate, up = gate_up[:, :sub], gate_up[:, sub:]
                sig = 1.0 / (1.0 + jnp.exp(-gate))
                act = gate * sig
                inner[here, b * sub : (b + 1) * sub] = (act * up).astype(BF)
                dgu[here, b * 2 * sub : b * 2 * sub + sub] = (
                    d_inner * up * (sig + act * (1.0 - sig))
                ).astype(BF)
                dgu[here, b * 2 * sub + sub : (b + 1) * 2 * sub] = (d_inner * act).astype(BF)
            if not carried:

                @pl.when(i > 0)
                def _():
                    end(writes(0, i))

            else:
                on_block(i, lambda m: end(more(m, i)))
            for at in range(0, width, half):
                lanes = slice(at, at + half)
                y = dot_nt(inner[here, :], wd[lanes, :])
                if carried:
                    y = y + yb[:, lanes].astype(F32)
                yb[:, lanes] = y.astype(BF)
                dn = dot_nt(dgu[here, :], wgu[lanes, :])
                if carried:
                    dn = dn + dnb[:, lanes].astype(F32)
                if inside:
                    dn = dn + jnp.where(block_of(i) < inside, cb[:, lanes].astype(F32), 0.0)
                dnb[:, lanes] = dn.astype(BF)
            on_block(i, lambda m: go(writes(m, i)))
            if reducing and team > 1:

                @pl.when(i % per == per - 1)
                def _():
                    def sent(m):
                        if m >= 1:
                            end(writes(m, i))
                            go([swap(m)] if inside and m >= inside else [face()])

                    on_block(i, sent)

            return carry

        def sides(g):
            cols = pl.ds(g * part, part) if isinstance(g, int) else pl.ds(pl.multiple_of(g * part, part), part)
            out = []
            for k in range(team):
                m = team - 1 - k if backwards else k
                at = pl.ds(k * span, span)
                out += [
                    pltpu.make_async_copy(x_refs[m].at[:, cols], xg.at[g % 2, at], g_sems.at[0, g % 2, k]),
                    pltpu.make_async_copy(dy_refs[m].at[:, cols], dyg.at[g % 2, at], g_sems.at[1, g % 2, k]),
                ]
            return out

        def keep(g):
            at = pl.ds(pl.multiple_of(g * part, part), part)
            return [pltpu.make_async_copy(gout.at[b], grad_refs[b].at[at], gout_sems.at[b]) for b in range(2)]

        def outer(g, carry):
            @pl.when(g + 1 < gsteps)
            def _():
                go(sides(g + 1))

            ticks(2 * steps + g, 2 * steps + g + 1)
            end(sides(g))

            @pl.when(g > 0)
            def _():
                end(keep(g))

            for b in range(2):
                up_down = dot_tn(xg[g % 2], dgu[:, b * 2 * sub : (b + 1) * 2 * sub])
                gout[b, :, : 2 * sub] = up_down.astype(BF)
                down = dot_tn(dyg[g % 2], inner[:, b * sub : (b + 1) * sub])
                gout[b, :, 2 * sub :] = down.astype(BF)
            go(keep(g))
            return carry

        lax.fori_loop(0, steps, forward, 0)
        lax.fori_loop(0, gsteps, outer, 0)
        end(writes(0, 0))
        end(keep(0))
        ring.last()
        if reducing and team > 1:
            for m in range(inside, team) if inside else []:
                swap(m).wait_send()
            face().wait_recv()
            face().wait_send()

    shape = lambda a, b: jax.ShapeDtypeStruct((a, b), BF)
    outs = [shape(span, width)] * (2 * team) + [shape(width, wide)] * 2
    if reducing:
        outs += [shape(rows, wide)] * 2
        outs += [shape(span, width)] * (max(1, inside) + 1)
    else:
        outs += [shape(width, wide)] * 2
    dma = pltpu.SemaphoreType.DMA
    scratch = [
        pltpu.VMEM((width, 4 * sub), BF),
        pltpu.VMEM((width, 2 * sub), BF),
        pltpu.VMEM((2, tile, width), BF),
        pltpu.VMEM((2, tile, width), BF),
        pltpu.VMEM((tile, width), BF),
        pltpu.VMEM((tile, width), BF),
        pltpu.VMEM((team * span, 4 * sub), BF),
        pltpu.VMEM((team * span, 2 * sub), BF),
        pltpu.VMEM((2, team * span, part), BF),
        pltpu.VMEM((2, team * span, part), BF),
        pltpu.VMEM((2, part, wide), BF),
        dma((2 * len(pieces),)),
        dma((2, 2)),
        dma((2,)),
        dma((2, 2, team)),
        dma((2,)),
    ]
    if carried:
        scratch += [pltpu.VMEM((tile, width) if inside else (16, 128), BF), dma((3,))]
    if reducing:
        scratch += [dma((max(1, inside),)), dma((max(1, inside),)), dma(()), dma(())]
        scratch += reduce_scratch(n, rows, wide)
    else:
        scratch += gather_scratch(n, rows, wide)
    operands = list(xs) + list(dys) + pieces + carried + list(ring_parts)
    out = pl.pallas_call(
        kernel,
        in_specs=[ANY] * len(operands),
        out_specs=[ANY] * len(outs),
        out_shape=outs,
        scratch_shapes=scratch,
        compiler_params=pltpu.CompilerParams(
            collective_id=ident, has_side_effects=True, vmem_limit_bytes=60 * MIB
        ),
        cost_estimate=cost(18 * team * span * width * 2 * sub, 40 * MIB),
    )(*operands)
    y, dn, grads, ringed = out[:team], out[team : 2 * team], out[2 * team : 2 * team + 2], out[2 * team + 2 :]
    if reducing:
        return y, (dn[0], ringed[-1]) if team > 1 else (dn[0],), grads, ringed[:2]
    return y, dn, grads, ringed[:2]


def attend_forward(sizes, x, qkv, kv_far, seen, w_out, gains, dy, w_gate_up, w_down):
    n_dp, n_fsdp, n_ctx = sizes
    n = n_fsdp * n_ctx
    span, width = x.shape
    rows = width // n
    far = kv_far.shape[0]
    blocks = far // span
    qwidth, kvwidth = HEADS * HD, KV_HEADS * HD
    near, kvpairs = qwidth // 128, kvwidth // 128
    pairs = HEADS // 2
    tile = min(span, 256)
    wide = 3 * (w_down.shape[1] // n_dp // SUBS)
    early = max(0, 3 * (n - 2) // 7)
    others = n_dp - 1
    chunk = min(512, width)

    def kernel(seen_ref, q_ref, k_ref, v_ref, kf_ref, vf_ref, x_ref, gains_ref, *refs):
        refs = list(refs)

        def take(count):
            out = refs[:count]
            del refs[:count]
            return out

        wo_ref, dy_ref, gu_ref, down_ref = take(4)
        lse_ref, attn_out, hidden_out, normed_out = take(4)
        x_blocks, dy_blocks, ring_outs = take(others), take(others), take(2)
        attn_v, wo_v, hidden_v, normed_v, load_sem, save_sems = take(6)
        dy_send, dy_recv, x_send, x_recv = take(4)
        ring = RingGather(sizes, own_columns(n_dp, gu_ref, down_ref, 0), ring_outs, *refs)
        dy_spread = TeamSpread(n_dp, [dy_ref], [dy_blocks], dy_send, dy_recv)
        x_spread = TeamSpread(n_dp, [normed_v], [x_blocks], x_send, x_recv)
        group = pl.program_id(0)
        mask = causal_tile(tile)
        flags = [seen_ref[k] == 1 for k in range(blocks)]
        load = pltpu.make_async_copy(wo_ref, wo_v, load_sem)

        @pl.when(group == 0)
        def _():
            greet(ring.partners + dy_spread.partners())
            ring.first()
            dy_spread.start(0)
            load.start()

        lax.fori_loop(
            2 + group * early // pairs,
            2 + (group + 1) * early // pairs,
            lambda t, c: (ring.tick(t), c)[1],
            0,
        )
        key, value = head_of(k_ref[...], group), head_of(v_ref[...], group)
        key_far, value_far = head_of(kf_ref[...], group), head_of(vf_ref[...], group)
        value_t = value.astype(F32).T.astype(BF)
        value_far_t = value_far.astype(F32).T.astype(BF)
        for head in range(2):
            down = pl.ds(pl.multiple_of(group * 128 + head * HD, HD), HD)
            for at in range(0, span, tile):
                end = at + tile
                q = q_ref[at:end, head * HD : (head + 1) * HD]
                own, other = scores_of(key[:end], key_far, q, flags, mask, span)
                peak = jnp.maximum(jnp.max(own, 0, keepdims=True), jnp.max(other, 0, keepdims=True))
                own = jnp.exp(own - peak)
                other = jnp.exp(other - peak)
                total = jnp.sum(own, 0, keepdims=True) + jnp.sum(other, 0, keepdims=True)
                scale = 1.0 / total
                result = dot_nn(value_t[:, :end], (own * scale).astype(BF)) + dot_nn(
                    value_far_t, (other * scale).astype(BF)
                )
                attn_v[down, at:end] = result.astype(BF)
                lse_ref[0, head : head + 1, at:end] = peak + jnp.log(total)

        @pl.when(group == pairs - 1)
        def _():
            saves = [
                pltpu.make_async_copy(a, b, save_sems.at[k])
                for k, (a, b) in enumerate([(attn_v, attn_out), (hidden_v, hidden_out), (normed_v, normed_out)])
            ]
            saves[0].start()
            load.wait()
            square = jnp.zeros((span, 1), F32)
            for at in range(0, width, chunk):
                lanes = slice(at, at + chunk)
                hidden = x_ref[:, lanes].astype(F32) + dot_tn(attn_v[...], wo_v[:, lanes])
                hidden_v[:, lanes] = hidden
                square = square + jnp.sum(hidden * hidden, -1, keepdims=True)
            scale = lax.rsqrt(square / width + EPS)
            place, device = ring_place(n_fsdp)
            for slot in range(n):
                there = device((place + n - slot) % n)
                part = slot_lanes(hidden_v, there["fsdp"] * n_ctx + there["ctx"], rows)
                normed = part * scale * gains_ref[slot, 1:2, :].astype(F32)
                normed_v[:, slot * rows : (slot + 1) * rows] = normed.astype(BF)
            x_spread.start(0)
            saves[1].start()
            saves[2].start()
            dy_spread.arrive(0)
            dy_spread.start(1)
            middle = max(2 + early, n - 2)
            for t in range(2 + early, middle):
                ring.tick(t)
            x_spread.arrive(0)
            x_spread.start(1)
            for t in range(middle, n):
                ring.tick(t)
            dy_spread.arrive(1)
            x_spread.arrive(1)
            ring.last()
            dy_spread.last()
            x_spread.last()
            for copy in saves:
                copy.wait()

    pair = lambda high, shift: pl.BlockSpec((high, 128), lambda i: (0, i // 4 + shift))
    dma = pltpu.SemaphoreType.DMA
    block = jax.ShapeDtypeStruct((span, width), BF)
    out = pl.pallas_call(
        kernel,
        grid=(pairs,),
        in_specs=[
            pl.BlockSpec(memory_space=pltpu.SMEM),
            pl.BlockSpec((span, 128), lambda i: (0, i)),
            pair(span, near),
            pair(span, near + kvpairs),
            pair(far, 0),
            pair(far, kvpairs),
            pl.BlockSpec((span, width), lambda i: (0, 0)),
            pl.BlockSpec(gains.shape, lambda i: (0, 0, 0)),
        ]
        + [ANY] * 4,
        out_specs=[pl.BlockSpec((1, 8, span), lambda i: (i, 0, 0))] + [ANY] * (5 + 2 * others),
        out_shape=[
            jax.ShapeDtypeStruct((pairs, 8, span), F32),
            jax.ShapeDtypeStruct((qwidth, span), BF),
            jax.ShapeDtypeStruct((span, width), F32),
        ]
        + [block] * (1 + 2 * others)
        + [jax.ShapeDtypeStruct((width, wide), BF)] * 2,
        scratch_shapes=[
            pltpu.VMEM((qwidth, span), BF),
            pltpu.VMEM((qwidth, width), BF),
            pltpu.VMEM((span, width), F32),
            pltpu.VMEM((span, width), BF),
            dma(()),
            dma((3,)),
        ]
        + spread_scratch(1, n_dp)
        + spread_scratch(1, n_dp)
        + gather_scratch(n, rows, wide),
        compiler_params=pltpu.CompilerParams(
            collective_id=5, has_side_effects=True, vmem_limit_bytes=58 * MIB
        ),
        cost_estimate=cost(pairs * 2 * span * (span + far) * 128 * 4, 30 * MIB),
    )(seen, qkv, qkv, qkv, kv_far, kv_far, x, gains, w_out, dy, w_gate_up, w_down)
    lse, attn, hidden, normed = out[:4]
    return attn, lse, hidden, normed, out[4 : 4 + others], out[4 + others : 4 + 2 * others], out[4 + 2 * others :]


def attend_backward(sizes, qkv, kv_far, d_attn, lse, seen, tables, attn_t, d_proj, normed, ring_parts, sums, ident):
    n_dp, n_fsdp, n_ctx = sizes
    n = n_fsdp * n_ctx
    span, far = qkv.shape[0], kv_far.shape[0]
    blocks = far // span
    qwidth, kvwidth = HEADS * HD, KV_HEADS * HD
    near, kvpairs = qwidth // 128, kvwidth // 128
    pairs = HEADS // 2
    tile = min(span, 256)
    rows, wide = ring_parts[0].shape[0] // n, ring_parts[0].shape[1]
    early = 4 + 8 * (n - 2) // 6
    width = normed.shape[1]
    qkvwidth = qwidth + 2 * kvwidth
    part = max(rows, 128)
    others = n_dp - 1

    def kernel(seen_ref, q_ref, k_ref, v_ref, kf_ref, vf_ref, d_ref, lse_ref, cos_ref, low_ref, high_ref, *refs):
        refs = list(refs)

        def take(count):
            out = refs[:count]
            del refs[:count]
            return out

        attn_ref, proj_ref, normed_ref = take(3)
        parts, own_sums = take(2), take(2)
        dqkv_out, go_out, gq_out = take(3)
        ring_outs, blocks_out = take(2), take(2 * others)
        dqkv_v, dkv, dkv_far, give, got, save_sem, kv_send, kv_recv = take(8)
        attn_v, proj_v, normed_v, stage, load_sems, stage_sems = take(6)
        spread_send, spread_recv = take(2)
        ring = RingReduce(sizes, parts, ring_outs, *refs)
        spread = TeamSpread(
            n_dp, own_sums, [blocks_out[k * others : (k + 1) * others] for k in range(2)], spread_send, spread_recv
        )
        loads = [
            pltpu.make_async_copy(a, b, load_sems.at[k])
            for k, (a, b) in enumerate([(attn_ref, attn_v), (proj_ref, proj_v), (normed_ref, normed_v)])
        ]

        def product(out, cols, make):
            def write(g):
                return pltpu.make_async_copy(
                    stage.at[g % 2, :, pl.ds(0, cols)],
                    out.at[pl.ds(pl.multiple_of(g * part, part), part)],
                    stage_sems.at[g % 2],
                )

            def body(g, carry):
                @pl.when(g >= 2)
                def _():
                    write(g - 2).wait()

                stage[g % 2, :, :cols] = make(pl.ds(pl.multiple_of(g * part, part), part)).astype(BF)
                write(g).start()
                return carry

            count = width // part
            lax.fori_loop(0, count, body, 0)
            for g in range(max(0, count - 2), count):
                write(g).wait()

        ctx = lax.axis_index("ctx")
        group = pl.program_id(0)
        mask = causal_tile(tile)
        flags = [seen_ref[k] == 1 for k in range(blocks)]
        key, value = head_of(k_ref[...], group), head_of(v_ref[...], group)
        key_far, value_far = head_of(kf_ref[...], group), head_of(vf_ref[...], group)
        key_t = key.astype(F32).T.astype(BF)
        key_far_t = key_far.astype(F32).T.astype(BF)
        odd = (group // 2) % 2 == 1
        cosine, low, high = cos_ref[...], -low_ref[...], -high_ref[...]

        @pl.when(group == 0)
        def _():
            greet(ring.partners + [{"ctx": (ctx + k) % n_ctx} for k in range(1, n_ctx)] + spread.partners())
            ring.first()
            spread.start(0)
            for copy in loads:
                copy.start()
            dkv[...] = jnp.zeros_like(dkv)
            dkv_far[...] = jnp.zeros_like(dkv_far)

        @pl.when(group == pairs - 4)
        def _():
            spread.arrive(0)
            spread.start(1)

        lax.fori_loop(
            4 + group * (early - 4) // pairs,
            4 + (group + 1) * (early - 4) // pairs,
            lambda u, c: (ring.step(u), c)[1],
            0,
        )

        def put(ref, size, shift, add):
            zero = jnp.zeros_like(add)
            lanes = pl.ds(pl.multiple_of(group // 4 * 128 + shift, 128), 128)
            ref[0:size, lanes] += jnp.concatenate([jnp.where(odd, zero, add), jnp.where(odd, add, zero)], 1)

        for at in range(0, span, tile):
            end = at + tile
            turned = []
            for head in range(2):
                lanes = slice(head * HD, (head + 1) * HD)
                q = q_ref[at:end, lanes]
                d = d_ref[at:end, lanes]
                own, other = scores_of(key[:end], key_far, q, flags, mask, span)
                base = lse_ref[0, head : head + 1, at:end]
                own = jnp.exp(own - base)
                other = jnp.exp(other - base)
                d_own = dot_nt(value[:end], d)
                d_other = dot_nt(value_far, d)
                delta = jnp.sum(own * d_own, 0, keepdims=True) + jnp.sum(other * d_other, 0, keepdims=True)
                ds_own = (own * (d_own - delta)).astype(BF)
                ds_other = (other * (d_other - delta)).astype(BF)
                put(dkv, end, kvwidth, dot_nn(own.astype(BF), d))
                put(dkv_far, far, kvwidth, dot_nn(other.astype(BF), d))
                put(dkv, end, 0, dot_nn(ds_own, q))
                put(dkv_far, far, 0, dot_nn(ds_other, q))
                turned.append(dot_nn(key_t[:, :end], ds_own) + dot_nn(key_far_t, ds_other))
            d_query = jnp.concatenate(turned, 0).T * HD**-0.5
            dqkv_v[at:end, pl.ds(pl.multiple_of(group * 128, 128), 128)] = turn(
                d_query, cosine[at:end], low[at:end], high[at:end]
            ).astype(BF)

        @pl.when(group == pairs - 1)
        def _():
            give[...] = dkv_far[...].astype(BF)

            def back(k):
                return pltpu.make_async_remote_copy(
                    src_ref=give.at[pl.ds((k - 1) * span, span)],
                    dst_ref=got.at[k - 1],
                    send_sem=kv_send.at[k],
                    recv_sem=kv_recv.at[k],
                    device_id={"ctx": (ctx + k) % n_ctx},
                    device_id_type=MESH,
                )

            for k in range(1, n_ctx):
                back(k).start()
            for copy in loads:
                copy.wait()
            ring.step(early)
            product(go_out, qwidth, lambda at: dot_nn(attn_v[at, :], proj_v[...]))
            ring.step(early + 1)
            for k in range(1, n_ctx):
                back(k).wait_recv()
            for at in range(0, 2 * kvwidth, 128):
                piece = dkv[:, at : at + 128]
                for k in range(1, n_ctx):
                    piece = piece + got[k - 1, :, at : at + 128].astype(F32)
                if at < kvwidth:
                    piece = turn(piece, cosine, low, high)
                dqkv_v[:, qwidth + at : qwidth + at + 128] = piece.astype(BF)
            save = pltpu.make_async_copy(dqkv_v, dqkv_out, save_sem)
            save.start()
            lax.fori_loop(early + 2, 2 * n - 1, lambda u, c: (ring.step(u), c)[1], 0)
            product(gq_out, qkvwidth, lambda at: dot_tn(normed_v[:, at], dqkv_v[...]))
            if early + 2 < 2 * n:
                ring.step(2 * n - 1)
            spread.arrive(1)
            ring.last()
            spread.last()
            for k in range(1, n_ctx):
                back(k).wait_send()
            save.wait()

    pair = lambda high, shift: pl.BlockSpec((high, 128), lambda i: (0, i // 4 + shift))
    wide_block = pl.BlockSpec((span, 128), lambda i: (0, i))
    table = pl.BlockSpec((span, 128), lambda i: (0, 0))
    dma = pltpu.SemaphoreType.DMA
    out = pl.pallas_call(
        kernel,
        grid=(pairs,),
        in_specs=[
            pl.BlockSpec(memory_space=pltpu.SMEM),
            wide_block,
            pair(span, near),
            pair(span, near + kvpairs),
            pair(far, 0),
            pair(far, kvpairs),
            wide_block,
            pl.BlockSpec((1, 8, span), lambda i: (i, 0, 0)),
            table,
            table,
            table,
        ]
        + [ANY] * 7,
        out_specs=[ANY] * (5 + 2 * others),
        out_shape=[
            jax.ShapeDtypeStruct((span, qkvwidth), BF),
            jax.ShapeDtypeStruct((width, qwidth), BF),
            jax.ShapeDtypeStruct((width, qkvwidth), BF),
        ]
        + [jax.ShapeDtypeStruct((rows, wide), BF)] * (2 + 2 * others),
        scratch_shapes=[
            pltpu.VMEM((span, qwidth + 2 * kvwidth), BF),
            pltpu.VMEM((span, 2 * kvwidth), F32),
            pltpu.VMEM((far, 2 * kvwidth), F32),
            pltpu.VMEM((far, 2 * kvwidth), BF),
            pltpu.VMEM((n_ctx - 1, span, 2 * kvwidth), BF),
            dma(()),
            dma((n_ctx,)),
            dma((n_ctx,)),
            pltpu.VMEM(attn_t.shape, BF),
            pltpu.VMEM(d_proj.shape, BF),
            pltpu.VMEM(normed.shape, BF),
            pltpu.VMEM((2, part, max(qwidth, qkvwidth)), BF),
            dma((3,)),
            dma((2,)),
        ]
        + spread_scratch(2, n_dp)
        + reduce_scratch(n, rows, wide),
        compiler_params=pltpu.CompilerParams(
            collective_id=ident, has_side_effects=True, vmem_limit_bytes=58 * MIB
        ),
        cost_estimate=cost(pairs * 2 * span * (span + far) * 128 * 10, 30 * MIB),
    )(seen, qkv, qkv, qkv, kv_far, kv_far, d_attn, lse, *tables, attn_t, d_proj, normed, *ring_parts, *sums)
    return out[0], out[1], out[2], out[3:5], [out[5 + k * others : 5 + (k + 1) * others] for k in range(2)]


def opening(sizes, x, dy, w_qkv, w_out, gains, tables):
    n_dp, n_fsdp, n_ctx = sizes
    n = n_fsdp * n_ctx
    span, width = x.shape
    rows = width // n
    share, half = w_qkv.shape[1] // n_dp, w_out.shape[1] // 2
    qwidth, kvwidth = HEADS * HD, KV_HEADS * HD
    qkvwidth = qwidth + 2 * kvwidth
    chunk = share // 2 if share % 256 == 0 else share
    across_x = n_dp > 2

    def kernel(x_ref, dy_ref, wq_ref, wo_ref, g_ref, cos_ref, low_ref, high_ref, *refs):
        refs = list(refs)

        def take(count):
            out = refs[:count]
            del refs[:count]
            return out

        qkv_out, far_out, xs_out, wq_out, wo_out, gains_out, dy_out = take(7)
        qkv_v, far_v, xs_v, dy_v = take(4)
        wq_v = take(n_dp)
        om_v, oo_v, gains_v = take(3)
        load_sems, save_sems, wq_sems, wo_sems = take(4)
        send, recv, x_send, x_recv, c_send, c_recv, o_send, o_recv = take(8)
        gain_send, gain_recv, kv_send, kv_recv = take(4)
        me = lax.axis_index("dp")
        core = me % 2
        sibling = {"dp": team_place(n_dp, me, 1)}
        facing = {"dp": team_place(n_dp, me, n_dp // 2)}
        bases = [me, team_place(n_dp, me, n_dp // 2)] if across_x else [me]
        bases = [b * share for b in bases + [team_place(n_dp, b, 1) for b in bases]]
        held = n_dp // 2
        place, device = ring_place(n_fsdp)
        ahead, behind = device((place + 1) % n), device((place + n - 1) % n)
        mine = (wq_v[0], om_v)
        widths = (share, half)

        def block_of(slot):
            there = device((place + n - slot) % n)
            return there["fsdp"] * n_ctx + there["ctx"]

        loads = [
            pltpu.make_async_copy(
                ref.at[:, pl.ds(pl.multiple_of(at, 128), w)], mine[k].at[pl.ds(0, rows)], load_sems.at[k]
            )
            for k, (ref, at, w) in enumerate(((wq_ref, me * share, share), (wo_ref, core * half, half)))
        ] + [pltpu.make_async_copy(g_ref, gains_v.at[0], load_sems.at[2])]
        for copy in loads:
            copy.start()
        ctx = lax.axis_index("ctx")
        greet(
            [ahead, behind, sibling]
            + ([facing] if across_x else [])
            + [{"ctx": (ctx + k) % n_ctx} for k in range(1, n_ctx)]
        )

        def lanes(k, way):
            return pl.ds(way * (widths[k] // 2), widths[k] // 2)

        def remote(source, target, send_sem, recv_sem, partner):
            return pltpu.make_async_remote_copy(
                src_ref=source,
                dst_ref=target,
                send_sem=send_sem,
                recv_sem=recv_sem,
                device_id=partner,
                device_id_type=MESH,
            )

        def step(k, way, t):
            here = t - 1 if way == 0 else (n - t + 1) % n
            there = t if way == 0 else n - t
            return remote(
                mine[k].at[pl.ds(here * rows, rows), lanes(k, way)],
                mine[k].at[pl.ds(there * rows, rows), lanes(k, way)],
                send.at[k, way, t],
                recv.at[k, way, t],
                ahead if way == 0 else behind,
            )

        def over_x(way, slot):
            at = (pl.ds(slot * rows, rows), lanes(0, way))
            return remote(wq_v[0].at[at], wq_v[1].at[at], x_send.at[way, slot], x_recv.at[way, slot], facing)

        def over_core(b, way, slot):
            at = (pl.ds(slot * rows, rows), lanes(0, way))
            return remote(
                wq_v[b].at[at], wq_v[held + b].at[at], c_send.at[b, way, slot], c_recv.at[b, way, slot], sibling
            )

        def out_over(way, slot):
            at = (pl.ds(slot * rows, rows), lanes(1, way))
            return remote(om_v.at[at], oo_v.at[at], o_send.at[way, slot], o_recv.at[way, slot], sibling)

        def gain_step(t):
            return remote(gains_v.at[t - 1], gains_v.at[t], gain_send.at[t], gain_recv.at[t], ahead)

        def kv_step(k):
            return remote(
                qkv_v.at[:, pl.ds(qwidth, 2 * kvwidth)],
                far_v.at[pl.ds((k - 1) * span, span)],
                kv_send.at[k],
                kv_recv.at[k],
                {"ctx": (ctx + n_ctx - k) % n_ctx},
            )

        def give(way, slot):
            if across_x:
                over_x(way, slot).start()
            over_core(0, way, slot).start()

        f32 = x_ref[...].astype(F32)
        scale = lax.rsqrt(jnp.mean(f32 * f32, -1, keepdims=True) + EPS)

        def normalize(slot):
            part = slot_lanes(x_ref, block_of(slot), rows)
            xs_v[:, slot * rows : (slot + 1) * rows] = (
                part * scale * gains_v[slot, 0:1, :].astype(F32)
            ).astype(BF)
            dy_v[:, slot * rows : (slot + 1) * rows] = slot_lanes(dy_ref, block_of(slot), rows).astype(BF)

        loads[0].wait()
        loads[2].wait()
        gain_step(1).start()
        for way in range(2):
            step(0, way, 1).start()
        loads[1].wait()
        for way in range(2):
            give(way, 0)
        normalize(0)
        for t in range(1, n):
            gain_step(t).wait_recv()
            if t < n - 1:
                gain_step(t + 1).start()
            for way in range(2):
                step(0, way, t).wait_recv()
                if t < n - 1:
                    step(0, way, t + 1).start()
                give(way, t if way == 0 else n - t)
            normalize(t)

        for way in range(2):
            step(1, way, 1).start()
            out_over(way, 0).start()

        def out_tick(t):
            for way in range(2):
                step(1, way, t).wait_recv()
                if t < n - 1:
                    step(1, way, t + 1).start()
                out_over(way, t if way == 0 else n - t).start()

        order = [(way, 0) for way in range(2)]
        for t in range(1, n):
            order += [(0, t), (1, n - t)]
        cosine, low, high = cos_ref[...], low_ref[...], high_ref[...]

        def form(b, at):
            value = dot_nn(xs_v[...], wq_v[b][:, at : at + chunk])
            for part in range(0, chunk, 128):
                piece = value[:, part : part + 128]
                here = bases[b] + at + part
                piece = jnp.where(here >= qwidth + kvwidth, piece, turn(piece, cosine, low, high))
                piece = piece * jnp.where(here < qwidth, HD**-0.5, 1.0)
                qkv_v[:, pl.ds(pl.multiple_of(here, 128), 128)] = piece.astype(BF)

        def save_share(b):
            return [
                pltpu.make_async_copy(
                    wq_v[b].at[pl.ds(slot * rows, rows)],
                    wq_out.at[
                        pl.ds(pl.multiple_of(block_of(slot) * rows, rows), rows),
                        pl.ds(pl.multiple_of(bases[b], 128), share),
                    ],
                    wq_sems.at[b, slot],
                )
                for slot in range(n)
            ]

        def save_half(k):
            whose = core if k == 0 else 1 - core
            return [
                pltpu.make_async_copy(
                    (om_v, oo_v)[k].at[pl.ds(slot * rows, rows)],
                    wo_out.at[
                        pl.ds(pl.multiple_of(block_of(slot) * rows, rows), rows),
                        pl.ds(pl.multiple_of(whose * half, 128), half),
                    ],
                    wo_sems.at[k, slot],
                )
                for slot in range(n)
            ]

        def go(copies):
            for copy in copies:
                copy.start()

        jobs = [lambda at=at: form(0, at) for at in range(0, share, chunk)]
        jobs.append(lambda: go(save_share(0)))

        def core_shares(b):
            for way, slot in order:
                over_core(b, way, slot).wait_recv()
            go(save_share(held + b))

        jobs.append(lambda: core_shares(0))
        jobs += [lambda at=at: form(held, at) for at in range(0, share, chunk)]
        if across_x:

            def relay(way, slot):
                over_x(way, slot).wait_recv()
                over_core(1, way, slot).start()

            jobs += [lambda w=way, k=slot: relay(w, k) for way, slot in order]
            jobs.append(lambda: go(save_share(1)))
            jobs += [lambda at=at: form(1, at) for at in range(0, share, chunk)]
            jobs.append(lambda: core_shares(1))
            jobs += [lambda at=at: form(held + 1, at) for at in range(0, share, chunk)]
        for k, job in enumerate(jobs):
            job()
            for t in range(1 + k * (n - 1) // len(jobs), 1 + (k + 1) * (n - 1) // len(jobs)):
                out_tick(t)
        for j in range(1, n_ctx):
            kv_step(j).start()
        saves = [
            pltpu.make_async_copy(a, b, save_sems.at[k])
            for k, (a, b) in enumerate(
                [(qkv_v, qkv_out), (far_v, far_out), (xs_v, xs_out), (gains_v, gains_out), (dy_v, dy_out)]
            )
        ]
        for k in (0, 2, 3, 4):
            saves[k].start()
        go(save_half(0))
        for way, slot in order:
            out_over(way, slot).wait_recv()
        go(save_half(1))
        for j in range(1, n_ctx):
            kv_step(j).wait_recv()
        saves[1].start()
        for t in range(1, n):
            gain_step(t).wait_send()
            for way in range(2):
                for k in range(2):
                    step(k, way, t).wait_send()
        for way, slot in order:
            out_over(way, slot).wait_send()
            for b in range(held):
                over_core(b, way, slot).wait_send()
            if across_x:
                over_x(way, slot).wait_send()
        for j in range(1, n_ctx):
            kv_step(j).wait_send()
        for copies in [save_share(b) for b in range(n_dp)] + [save_half(k) for k in range(2)] + [saves]:
            for copy in copies:
                copy.wait()

    dma = pltpu.SemaphoreType.DMA
    shapes = [
        (span, qkvwidth),
        ((n_ctx - 1) * span, 2 * kvwidth),
        (span, width),
        (width, qkvwidth),
        (width, 2 * half),
        (n, 16, rows),
        (span, width),
    ]
    return pl.pallas_call(
        kernel,
        in_specs=[WHOLE, WHOLE, ANY, ANY, ANY, WHOLE, WHOLE, WHOLE],
        out_specs=[ANY] * 7,
        out_shape=[jax.ShapeDtypeStruct(shape, BF) for shape in shapes],
        scratch_shapes=[pltpu.VMEM(shape, BF) for shape in shapes[:3] + shapes[6:]]
        + [pltpu.VMEM((width, share), BF)] * n_dp
        + [pltpu.VMEM((width, half), BF)] * 2
        + [pltpu.VMEM((n, 16, rows), BF)]
        + [
            dma((3,)),
            dma((5,)),
            dma((n_dp, n)),
            dma((2, n)),
            dma((2, 2, n)),
            dma((2, 2, n)),
            dma((2, n)),
            dma((2, n)),
            dma((n_dp // 2, 2, n)),
            dma((n_dp // 2, 2, n)),
            dma((2, n)),
            dma((2, n)),
            dma((n,)),
            dma((n,)),
            dma((n_ctx,)),
            dma((n_ctx,)),
        ],
        compiler_params=pltpu.CompilerParams(
            collective_id=0, has_side_effects=True, vmem_limit_bytes=56 * MIB
        ),
        cost_estimate=cost(2 * span * width * qkvwidth, 4 * width * qkvwidth),
    )(x, dy, w_qkv, w_out, gains, *tables)


def closing(sizes, fulls, slotted, sums, d_qkv, w_qkv, x, gain, d_gain):
    n_dp, n_fsdp, n_ctx = sizes
    n = n_fsdp * n_ctx
    span, width = x.shape
    mine = width // n
    rows = [f.shape[0] // n for f in fulls] + [8]
    widths = [f.shape[1] // 2 for f in fulls] + [max(mine, 256)]
    kinds = [f.dtype for f in fulls] + [F32]
    count = len(fulls) + 1
    chunk = min(512, width)
    parts = width // chunk
    bits = [1 << k for k in range(1, n_dp.bit_length() - 1)]
    others = n_dp - 1

    def kernel(*refs):
        refs = list(refs)

        def take(size):
            out = refs[:size]
            del refs[:size]
            return out

        full, own_sums = take(count - 1), take(len(sums))
        dq_ref, w_ref, x_ref, gain_ref, d_gain_ref = take(5)
        outs, blocks_out, (input_out,) = take(count), take(len(sums) * others), take(1)
        gain_v, both_v, d_v, w_v, dn_v, w_sem, d_sem, dn_sem = take(8)
        full = full + [gain_v]
        near, land, done, extra, back = take(count), take(count), take(count), take(count), take(count)
        own = take(count)
        (own_sems,) = take(1)
        send, recv, pair_send, pair_recv, x_send, x_recv, end_send, end_recv = take(8)
        spread = TeamSpread(
            n_dp, own_sums, [blocks_out[k * others : (k + 1) * others] for k in range(len(sums))], *refs
        )
        me = lax.axis_index("dp")
        core = me % 2
        sibling = {"dp": me + 1 - 2 * core}
        place, device = ring_place(n_fsdp)
        ahead, behind = device((place + 1) % n), device((place + n - 1) % n)
        facing = [{"dp": me + bit - 2 * bit * ((me // bit) % 2)} for bit in bits]
        greet([ahead, behind, sibling] + facing)

        def half(g, way):
            return pl.ds(way * (widths[g] // 2), widths[g] // 2)

        def half_of(g, way, whose):
            base = whose * widths[g] + way * (widths[g] // 2)
            return pl.ds(pl.multiple_of(base, 128), widths[g] // 2)

        def at(g, slot):
            return pl.ds(slot * rows[g], rows[g])

        def source_at(g, slot):
            if slotted[g]:
                return at(g, slot)
            there = device((place + n - slot) % n)
            block = there["fsdp"] * n_ctx + there["ctx"]
            return pl.ds(pl.multiple_of(block * rows[g], rows[g]), rows[g])

        def swap(g, way, slot):
            return pltpu.make_async_remote_copy(
                src_ref=full[g].at[source_at(g, slot), half_of(g, way, 1 - core)],
                dst_ref=near[g].at[at(g, slot), half(g, way)],
                send_sem=pair_send.at[g, way, slot],
                recv_sem=pair_recv.at[g, way, slot],
                device_id=sibling,
                device_id_type=MESH,
            )

        def step(g, way, t):
            slot = t if way == 0 else n - t
            source = near[g].at[at(g, slot), half(g, way)] if t == 1 else land[g].at[way, t - 2]
            return pltpu.make_async_remote_copy(
                src_ref=source,
                dst_ref=land[g].at[way, t - 1],
                send_sem=send.at[g, way, t],
                recv_sem=recv.at[g, way, t],
                device_id=ahead if way == 0 else behind,
                device_id_type=MESH,
            )

        def face(g, k):
            return pltpu.make_async_remote_copy(
                src_ref=done[g].at[k],
                dst_ref=extra[g].at[k],
                send_sem=x_send.at[g, k],
                recv_sem=x_recv.at[g, k],
                device_id=facing[k],
                device_id_type=MESH,
            )

        def end(g):
            return pltpu.make_async_remote_copy(
                src_ref=done[g].at[len(bits)],
                dst_ref=back[g],
                send_sem=end_send.at[g],
                recv_sem=end_recv.at[g],
                device_id=sibling,
                device_id_type=MESH,
            )

        def own_load(g, way, t):
            slot = t % n if way == 0 else n - t
            return pltpu.make_async_copy(
                full[g].at[source_at(g, slot), half_of(g, way, core)],
                own[g].at[way, t % 2],
                own_sems.at[g, way, t % 2],
            )

        def both(g, way, t, slot):
            own_load(g, way, t).wait()
            swap(g, way, slot).wait_recv()
            return own[g][way, t % 2].astype(F32) + near[g][at(g, slot), half(g, way)].astype(F32)

        def forward(g, t):
            for way in range(2):
                slot = t if way == 0 else n - t
                value = both(g, way, t, slot)
                if t == 1:
                    near[g][at(g, slot), half(g, way)] = value.astype(kinds[g])
                else:
                    step(g, way, t - 1).wait_recv()
                    land[g][way, t - 2] = (value + land[g][way, t - 2].astype(F32)).astype(kinds[g])
                step(g, way, t).start()
                own_load(g, way, t + 1).start()

        def finish(g):
            for way in range(2):
                value = both(g, way, n, 0)
                step(g, way, n - 1).wait_recv()
                done[g][0, :, half(g, way)] = (value + land[g][way, n - 2].astype(F32)).astype(kinds[g])
            if bits:
                face(g, 0).start()

        w_load = pltpu.make_async_copy(w_ref, w_v, w_sem)
        d_load = pltpu.make_async_copy(dq_ref, d_v, d_sem)
        dn_save = pltpu.make_async_copy(dn_v, input_out, dn_sem)

        def begin(g):
            for way in range(2):
                own_load(g, way, 1).start()

        def swaps(g, t):
            swap(g, 0, t % n).start()
            swap(g, 1, n - t).start()

        def product(k):
            lanes = slice(k * chunk, (k + 1) * chunk)
            dn_v[:, lanes] = dot_nt(d_v[...], w_v[lanes, :])

        def norm():
            square = jnp.zeros((span, 1), F32)
            for k in range(parts):
                value = x_ref[:, k * chunk : (k + 1) * chunk].astype(F32)
                square = square + jnp.sum(value * value, -1, keepdims=True)
            scale = lax.rsqrt(square / width + EPS)
            inner = jnp.zeros((span, 1), F32)
            for k in range(parts):
                lanes = slice(k * chunk, (k + 1) * chunk)
                unit = x_ref[:, lanes].astype(F32) * scale
                product = dn_v[:, lanes] * unit
                both_v[1:2, lanes] = jnp.sum(product, 0, keepdims=True)
                inner = inner + jnp.sum(product * gain_ref[0:1, lanes], -1, keepdims=True)
            inner = inner / width
            for k in range(parts):
                lanes = slice(k * chunk, (k + 1) * chunk)
                unit = x_ref[:, lanes].astype(F32) * scale
                dn_v[:, lanes] = scale * (dn_v[:, lanes] * gain_ref[0:1, lanes] - unit * inner)
            dn_save.start()
            gain_v[...] = jnp.zeros_like(gain_v)
            both_v[0:1, :] = d_gain_ref[0:1, :]
            both_v[2:8, :] = jnp.zeros((6, width), F32)
            for slot in range(n):
                there = device((place + n - slot) % n)
                pair = slot_lanes(both_v, there["fsdp"] * n_ctx + there["ctx"], mine)
                gain_v[slot * 8 : slot * 8 + 1, :mine] = pair[1:2]
                gain_v[slot * 8 : slot * 8 + 1, widths[-1] : widths[-1] + mine] = pair[0:1]

        rest, gains = list(range(1, count - 1)), count - 1
        d_load.start()
        w_load.start()
        for g in range(count - 1):
            begin(g)
        for t in range(1, n + 1):
            for g in rest + [0]:
                swaps(g, t)
        spread.start(0)
        jobs = [(lambda k=k: product(k)) for k in range(parts)] + [norm]
        for t in range(1, n):
            for g in rest:
                forward(g, t)
            if t >= 2:
                forward(0, t - 1)
            if t == 1:
                d_load.wait()
                w_load.wait()
            for k in range((t - 1) * len(jobs) // (n - 1), t * len(jobs) // (n - 1)):
                jobs[k]()
        begin(gains)
        for t in range(1, n + 1):
            swaps(gains, t)
        for g in rest:
            finish(g)
        spread.arrive(0)
        spread.start(1)
        forward(0, n - 1)
        for t in range(1, n):
            forward(gains, t)
        finish(0)
        finish(gains)
        for k in range(len(bits)):
            for g in range(count):
                face(g, k).wait_recv()
                done[g][k + 1] = (done[g][k].astype(F32) + extra[g][k].astype(F32)).astype(kinds[g])
                if k + 1 < len(bits):
                    face(g, k + 1).start()
        for g in range(count):
            end(g).start()
            here = pl.ds(pl.multiple_of(core * widths[g], 128), widths[g])
            outs[g][:, here] = done[g][len(bits)].astype(F32)
        for g in range(count):
            end(g).wait_recv()
            here = pl.ds(pl.multiple_of((1 - core) * widths[g], 128), widths[g])
            outs[g][:, here] = back[g][...].astype(F32)
        spread.arrive(1)
        spread.last()
        dn_save.wait()
        for g in range(count):
            end(g).wait_send()
            for k in range(len(bits)):
                face(g, k).wait_send()
            for way in range(2):
                for t in range(1, n):
                    step(g, way, t).wait_send()
                for slot in range(n):
                    swap(g, way, slot).wait_send()

    dma = pltpu.SemaphoreType.DMA
    groups = list(zip(rows, widths, kinds))
    out = pl.pallas_call(
        kernel,
        in_specs=[ANY] * (count - 1 + len(sums) + 2) + [WHOLE] * 3,
        out_specs=[WHOLE] * count + [ANY] * (len(sums) * others + 1),
        out_shape=[jax.ShapeDtypeStruct((r, 2 * w), F32) for r, w, _ in groups]
        + [jax.ShapeDtypeStruct(a.shape, BF) for a in sums for _ in range(others)]
        + [jax.ShapeDtypeStruct((span, width), F32)],
        scratch_shapes=[
            pltpu.VMEM((n * 8, 2 * widths[-1]), F32),
            pltpu.VMEM((8, width), F32),
            pltpu.VMEM(d_qkv.shape, BF),
            pltpu.VMEM(w_qkv.shape, BF),
            pltpu.VMEM((span, width), F32),
            dma(()),
            dma(()),
            dma(()),
        ]
        + [pltpu.VMEM((n * r, w), kind) for r, w, kind in groups]
        + [pltpu.VMEM((2, n - 1, r, w // 2), kind) for r, w, kind in groups]
        + [pltpu.VMEM((len(bits) + 1, r, w), kind) for r, w, kind in groups]
        + [pltpu.VMEM((max(1, len(bits)), r, w), kind) for r, w, kind in groups]
        + [pltpu.VMEM((r, w), kind) for r, w, kind in groups]
        + [pltpu.VMEM((2, 2, r, w // 2), kind) for r, w, kind in groups]
        + [
            dma((count, 2, 2)),
            dma((count, 2, n)),
            dma((count, 2, n)),
            dma((count, 2, n)),
            dma((count, 2, n)),
            dma((count, max(1, len(bits)))),
            dma((count, max(1, len(bits)))),
            dma((count,)),
            dma((count,)),
        ]
        + spread_scratch(len(sums), n_dp),
        compiler_params=pltpu.CompilerParams(
            collective_id=1, has_side_effects=True, vmem_limit_bytes=58 * MIB
        ),
        cost_estimate=cost(0, sum(12 * n * r * w for r, w, _ in groups)),
    )(*fulls, *sums, d_qkv, w_qkv, x, gain, d_gain)
    blocks = [out[count + k * others : count + (k + 1) * others] for k in range(len(sums))]
    return out[:count], blocks, out[-1]


class Ring:
    def __init__(self, n_fsdp, n_ctx):
        order = []
        for c in range(n_ctx):
            rows = range(n_fsdp) if c % 2 == 0 else reversed(range(n_fsdp))
            order += [f * n_ctx + c for f in rows]
        self.order = order
        self.size = n = len(order)
        place = [0] * n
        for k, block in enumerate(order):
            place[block] = k
        self.place = place
        self.block = lax.axis_index(GRID)
        self.rank = jnp.array(place, jnp.int32)[self.block]

    def slot_blocks(self):
        slots = jnp.arange(self.size, dtype=jnp.int32)
        return jnp.array(self.order, jnp.int32)[(self.rank - slots) % self.size]

    def to_slots(self, array, axis=1, deps=()):
        return reorder(array, self.slot_blocks(), axis, deps)

    def from_slots(self, array, axis=1):
        return reorder(array, (self.rank - jnp.array(self.place, jnp.int32)) % self.size, axis)


class Team:
    def __init__(self, size):
        self.size = size
        self.rank = lax.axis_index("dp")
        self.bits = [1 << k for k in range(size.bit_length() - 1)]
        self.order = [0]
        for bit in reversed(self.bits):
            self.order = self.order + [m ^ bit for m in self.order]

    def swap(self, value, bit):
        return lax.ppermute(value, "dp", [(k, k ^ bit) for k in range(self.size)])

    def scatter(self, parts):
        for bit in self.bits:
            half = len(parts) // 2
            got = [self.swap(part.astype(BF), bit) for part in parts[half:]]
            parts = [kept + part.astype(F32) for kept, part in zip(parts[:half], got)]
        return parts[0]


def shards(sizes, x_in, span_order, attn_gain, w_qkv, w_out, ffn_gain, w_gate_up, w_down, cotangent):
    n_dp, n_fsdp, n_ctx = sizes
    ring = Ring(n_fsdp, n_ctx)
    team = Team(n_dp)
    n = ring.size
    width = x_in.shape[-1]
    rows = width // n
    tokens = x_in.reshape(-1, width)
    span = tokens.shape[0]
    rank = lax.axis_index("ctx")
    qwidth = HEADS * HD
    kvwidth = KV_HEADS * HD
    ffwidth = w_down.shape[1]
    order = span_order.reshape(-1)
    near = [(rank + k) % n_ctx for k in range(n_ctx)]
    offsets = jnp.arange(span, dtype=jnp.int32)
    query_pos = order[rank] * span + offsets
    seen = jnp.stack([order[c] < order[rank] for c in near[1:]]).astype(jnp.int32)
    tables = rope_tables(query_pos.astype(F32))

    ffq = ffwidth // n_dp
    sub = ffq // SUBS
    grad_y = cotangent.reshape(span, width)
    gains = jnp.concatenate([attn_gain[None], ffn_gain[None], jnp.zeros((14, rows), BF)], 0)
    qkv, kv_far, normed_one, wqkv, wout, gains, dy = opening(
        sizes, tokens, grad_y, w_qkv, w_out, gains, tables
    )
    attn_t, lse, hidden_one, normed_two, x_others, dy_others, weights_a = attend_forward(
        sizes, tokens, qkv, kv_far, seen, wout, gains, dy, w_gate_up, w_down
    )
    xs = [normed_two] + list(x_others)
    dys = [dy] + list(dy_others)
    gains = gains[:, :2][(ring.rank - jnp.array(ring.place, jnp.int32)) % n]
    gain_one = gains[:, 0].reshape(-1).astype(F32)
    gain_two = gains[:, 1].reshape(-1).astype(F32)
    scale_two = inv_rms(hidden_one)

    y, dn, grads_a, weights_b = feed_forward(
        sizes, xs, dys, [[w] for w in weights_a], None, (w_gate_up, w_down), False, 2
    )
    y, dn, grads_b, sums_a = feed_forward(
        sizes, xs, dys, [[w] for w in weights_b], list(zip(y, dn)), grads_a, True, 3
    )

    d_normed_two = ring.from_slots(sum(part.astype(F32) for part in dn))
    d_hidden_norm, d_gain_two = norm_back(hidden_one, scale_two, gain_two, d_normed_two)
    d_hidden = grad_y.astype(F32) + d_hidden_norm
    d_proj = d_hidden.astype(BF)

    d_attn = matmul_rows(d_proj, wout).astype(BF)
    d_qkv, part_out, part_qkv, sums_b, others_a = attend_backward(
        sizes, qkv, kv_far, d_attn, lse, seen, tables, attn_t, d_proj, normed_one, grads_b, sums_a, 4
    )
    room = max(rows, 256)
    (grad_qkv, grad_out, grad_gain), others_b, d_input_norm = closing(
        sizes,
        (part_qkv, part_out),
        (True, False, True),
        sums_b,
        d_qkv,
        wqkv,
        tokens,
        jnp.broadcast_to(gain_one[None], (8, width)),
        jnp.broadcast_to(d_gain_two[None], (8, width)),
    )
    grad_input = d_hidden + d_input_norm

    placed, columns = [], []
    for q in range(SUBS):
        blocks = [sums_a[q]] + list(others_a[q]) if q < 2 else [sums_b[q - 2]] + list(others_b[q - 2])
        for m, block in zip(team.order, blocks):
            placed.append(block)
            columns.append((team.rank ^ m) * ffq + q * sub)
    grad_gate_up, grad_down = place_grads(placed, jnp.stack(columns).astype(jnp.int32), sub, ffwidth)

    y_out = hidden_one + ring.from_slots(team.scatter(y))
    return (
        y_out.astype(BF).reshape(x_in.shape),
        grad_input.reshape(x_in.shape),
        grad_gain[0, :rows],
        grad_qkv,
        grad_out,
        grad_gain[0, room : room + rows],
        grad_gate_up,
        grad_down,
    )


def solution(mesh):
    sizes = (mesh.shape["dp"], mesh.shape["fsdp"], mesh.shape["ctx"])
    tokens = P(("dp", "fsdp"), "ctx", None)
    weight = P(("fsdp", "ctx"), None)
    gain = P(("fsdp", "ctx"))

    def body(*args):
        return shards(sizes, *args)

    return jax.shard_map(
        body,
        mesh=mesh,
        in_specs=(tokens, P(("dp", "fsdp"), None), gain, weight, weight, gain, weight, weight, tokens),
        out_specs=(tokens, tokens, gain, weight, weight, gain, weight, weight),
        check_vma=False,
    )
```

```python
import math

import jax
import jax.numpy as jnp
from jax import lax
from jax.experimental import pallas as pl
from jax.experimental.pallas import tpu as pltpu
from jax.sharding import PartitionSpec as P

HEADS = 32
KV_HEADS = 8
HD = 64
EPS = 1e-05
SUBS = 4

BF = jnp.bfloat16
F32 = jnp.float32
GRID = ("fsdp", "ctx")


def matmul(left, right):
    return jnp.dot(left, right, preferred_element_type=F32)


def matmul_rows(left, right):
    return lax.dot_general(left, right, (((1,), (1,)), ((), ())), preferred_element_type=F32)


def matmul_tokens(left, right):
    return lax.dot_general(left, right, (((0,), (0,)), ((), ())), preferred_element_type=F32)


def rope_tables(positions):
    half = HD // 2
    freq = jnp.exp(jnp.arange(half, dtype=F32) * (-math.log(500000.0) / half))
    angle = positions[:, None] * freq[None, :]
    cosine, sine = jnp.cos(angle), jnp.sin(angle)
    zero = jnp.zeros_like(sine)
    return (
        jnp.concatenate([cosine] * 4, -1),
        jnp.concatenate([-sine, zero] * 2, -1),
        jnp.concatenate([zero, sine] * 2, -1),
    )


def inv_rms(rows):
    return lax.rsqrt(jnp.mean(rows * rows, -1, keepdims=True) + EPS)


def norm_back(rows, scale, gain, grad):
    unit = rows * scale
    pulled = grad * gain[None, :]
    inner = jnp.mean(pulled * unit, -1, keepdims=True)
    return scale * (pulled - unit * inner), jnp.sum(grad * unit, 0)


MIB = 1 << 20
ANY = pl.BlockSpec(memory_space=pl.ANY)
WHOLE = pl.BlockSpec(memory_space=pltpu.VMEM)


def cost(flops, moved, exps=0):
    return pl.CostEstimate(flops=int(flops), bytes_accessed=int(moved), transcendentals=int(exps))


def params(mib):
    return pltpu.CompilerParams(vmem_limit_bytes=mib * MIB)


def dot_nn(a, b):
    return lax.dot_general(a, b, (((1,), (0,)), ((), ())), preferred_element_type=F32)


def dot_nt(a, b):
    return lax.dot_general(a, b, (((1,), (1,)), ((), ())), preferred_element_type=F32)


def dot_tn(a, b):
    return lax.dot_general(a, b, (((0,), (0,)), ((), ())), preferred_element_type=F32)


def reorder(array, places, axis=1, deps=()):
    count = places.shape[0]
    if axis == 1 and (array.shape[1] // count) % 128 != 0:
        size = array.shape[1] // count
        blocks = [lax.dynamic_slice_in_dim(array, places[s] * size, size, 1) for s in range(count)]
        return jnp.concatenate(blocks, 1)
    if axis == 1:
        shape = (array.shape[0], array.shape[1] // count)
        took = lambda s, where: (0, where[s])
        gave = lambda s, where: (0, s)
    else:
        shape = (array.shape[0] // count, array.shape[1])
        took = lambda s, where: (where[s], 0)
        gave = lambda s, where: (s, 0)

    def kernel(where, source, *rest):
        rest[-1][...] = source[...]

    return pl.pallas_call(
        kernel,
        grid_spec=pltpu.PrefetchScalarGridSpec(
            num_scalar_prefetch=1,
            grid=(count,),
            in_specs=[pl.BlockSpec(shape, took)] + [ANY] * len(deps),
            out_specs=pl.BlockSpec(shape, gave),
        ),
        out_shape=jax.ShapeDtypeStruct(array.shape, array.dtype),
        compiler_params=params(16),
        cost_estimate=cost(0, 2 * array.size * array.dtype.itemsize),
    )(places, array, *deps)


def turn(piece, cosine, sine_low, sine_high):
    return (
        piece * cosine
        + pltpu.roll(piece, 128 - HD // 2, axis=1) * sine_low
        + pltpu.roll(piece, HD // 2, axis=1) * sine_high
    )


def head_of(block, group):
    odd = (group // 2) % 2 == 1
    return jnp.where(odd, block[:, HD:], block[:, :HD])


def causal_tile(size):
    key = lax.broadcasted_iota(jnp.int32, (size, size), 0)
    query = lax.broadcasted_iota(jnp.int32, (size, size), 1)
    return key <= query


def scores_of(key, key_far, query, seen, mask, span):
    tile = query.shape[0]
    own = dot_nt(key, query)
    if key.shape[0] > tile:
        last = key.shape[0] - tile
        own = jnp.concatenate([own[:last], jnp.where(mask, own[last:], -1e30)], 0)
    else:
        own = jnp.where(mask, own, -1e30)
    far = dot_nt(key_far, query)
    far = [jnp.where(seen[k], far[k * span : (k + 1) * span], -1e30) for k in range(len(seen))]
    return own, (far[0] if len(far) == 1 else jnp.concatenate(far, 0))


def place_grads(pieces, columns, sub, ffwidth):
    rows = pieces[0].shape[0]
    count = len(pieces)

    def kernel(*refs):
        where = refs[0]
        sources = refs[1 : 1 + count]
        gu_ref, down_ref, took, gave, in_sems, out_sems = refs[1 + count :]

        def read(k):
            return pltpu.make_async_copy(sources[k], took.at[k % 2], in_sems.at[k % 2])

        def writes(k):
            at = pl.multiple_of(where[k], 128)
            here = gave.at[k % 2]
            return (
                pltpu.make_async_copy(
                    here.at[:, pl.ds(0, sub)], gu_ref.at[:, pl.ds(at, sub)], out_sems.at[k % 2, 0]
                ),
                pltpu.make_async_copy(
                    here.at[:, pl.ds(sub, sub)], gu_ref.at[:, pl.ds(at + ffwidth, sub)], out_sems.at[k % 2, 1]
                ),
                pltpu.make_async_copy(
                    here.at[:, pl.ds(2 * sub, sub)], down_ref.at[:, pl.ds(at, sub)], out_sems.at[k % 2, 2]
                ),
            )

        read(0).start()
        for k in range(count):
            if k + 1 < count:
                read(k + 1).start()
            read(k).wait()
            if k >= 2:
                for copy in writes(k - 2):
                    copy.wait()
            gave[k % 2] = took[k % 2].astype(F32)
            for copy in writes(k):
                copy.start()
        for k in range(max(0, count - 2), count):
            for copy in writes(k):
                copy.wait()

    return pl.pallas_call(
        kernel,
        in_specs=[pl.BlockSpec(memory_space=pltpu.SMEM)] + [ANY] * count,
        out_specs=[ANY, ANY],
        out_shape=[
            jax.ShapeDtypeStruct((rows, 2 * ffwidth), F32),
            jax.ShapeDtypeStruct((rows, ffwidth), F32),
        ],
        scratch_shapes=[
            pltpu.VMEM((2, rows, 3 * sub), BF),
            pltpu.VMEM((2, rows, 3 * sub), F32),
            pltpu.SemaphoreType.DMA((2,)),
            pltpu.SemaphoreType.DMA((2, 3)),
        ],
        compiler_params=params(60),
        cost_estimate=cost(0, rows * ffwidth * 18),
    )(columns, *pieces)


MESH = pl.DeviceIdType.MESH


def ring_place(n_fsdp):
    f, c = lax.axis_index("fsdp"), lax.axis_index("ctx")

    def device(place):
        row, k = place // n_fsdp, place % n_fsdp
        return {"fsdp": k + (row % 2) * (n_fsdp - 1 - 2 * k), "ctx": row}

    return c * n_fsdp + f + (c % 2) * (n_fsdp - 1 - 2 * f), device


def slot_lanes(ref, block, rows):
    if rows % 128 == 0:
        return ref[:, pl.ds(pl.multiple_of(block * rows, 128), rows)].astype(F32)
    share = 128 // rows
    wide = ref[:, pl.ds(pl.multiple_of(block // share * 128, 128), 128)].astype(F32)
    part = wide[:, :rows]
    for k in range(1, share):
        part = jnp.where(block % share == k, wide[:, k * rows : (k + 1) * rows], part)
    return part


def team_place(size, me, bit):
    return me + bit - 2 * bit * ((me // bit) % 2)


def greet(partners):
    barrier = pltpu.get_barrier_semaphore()
    for partner in partners:
        pl.semaphore_signal(barrier, inc=1, device_id=partner, device_id_type=MESH)
    pl.semaphore_wait(barrier, len(partners))


def own_columns(size, w_gate_up, w_down, first):
    ffwidth = w_down.shape[1]
    ffq = ffwidth // size
    sub = ffq // SUBS
    out = []
    for way in range(2):
        at = lax.axis_index("dp") * ffq + (first + way) * sub
        out.append(
            [
                (w_gate_up.at[:, pl.ds(pl.multiple_of(at, 128), sub)], 0),
                (w_gate_up.at[:, pl.ds(pl.multiple_of(at + ffwidth, 128), sub)], sub),
                (w_down.at[:, pl.ds(pl.multiple_of(at, 128), sub)], 2 * sub),
            ]
        )
    return out


class RingGather:
    def __init__(self, sizes, own, out, own_v, own_sem, store_sem, send, recv):
        self.n = sizes[1] * sizes[2]
        self.rows = own_v.shape[1]
        self.own, self.out, self.own_v = own, out, own_v
        self.own_sem, self.store_sem, self.send, self.recv = own_sem, store_sem, send, recv
        place, device = ring_place(sizes[1])
        self.partners = [device((place + 1) % self.n), device((place + self.n - 1) % self.n)]

    def rows_of(self, way, t):
        slot = t if way == 0 else (self.n - t) % self.n
        return pl.ds(slot * self.rows, self.rows)

    def loads(self, way):
        width = self.own_v.shape[2] // 3
        return [
            pltpu.make_async_copy(
                source, self.own_v.at[way, :, pl.ds(place, width)], self.own_sem.at[way, place // width]
            )
            for source, place in self.own[way]
        ]

    def store(self, way):
        return pltpu.make_async_copy(
            self.own_v.at[way], self.out[way].at[pl.ds(0, self.rows)], self.store_sem.at[way]
        )

    def ring(self, way, t, first=False):
        source = self.own_v.at[way] if first else self.out[way].at[self.rows_of(way, t - 1)]
        return pltpu.make_async_remote_copy(
            src_ref=source,
            dst_ref=self.out[way].at[self.rows_of(way, t)],
            send_sem=self.send.at[way, t],
            recv_sem=self.recv.at[way, t],
            device_id=self.partners[way],
            device_id_type=MESH,
        )

    def arrived(self, way, t):
        target = self.out[way].at[self.rows_of(way, t)]
        return pltpu.make_async_remote_copy(
            src_ref=target,
            dst_ref=target,
            send_sem=self.send.at[way, t],
            recv_sem=self.recv.at[way, t],
            device_id=self.partners[way],
            device_id_type=MESH,
        )

    def first(self):
        for way in range(2):
            for copy in self.loads(way):
                copy.start()
        for way in range(2):
            for copy in self.loads(way):
                copy.wait()
            self.ring(way, 1, True).start()
            self.store(way).start()

    def tick(self, t):
        for way in range(2):
            self.arrived(way, t - 1).wait_recv()
            self.ring(way, t).start()

    def last(self):
        for way in range(2):
            self.arrived(way, self.n - 1).wait_recv()
            self.store(way).wait()
            self.ring(way, 1, True).wait_send()
            for t in range(2, self.n):
                self.ring(way, t).wait_send()


def gather_scratch(n, rows, wide):
    dma = pltpu.SemaphoreType.DMA
    return [pltpu.VMEM((2, rows, wide), BF), dma((2, 3)), dma((2,)), dma((2, n)), dma((2, n))]


class RingReduce:
    def __init__(self, sizes, parts, out, land, own_v, own_sem, out_sem, send, recv):
        self.n = sizes[1] * sizes[2]
        self.rows, self.wide = out[0].shape
        self.parts, self.out, self.land, self.own_v = parts, out, land, own_v
        self.own_sem, self.out_sem, self.send, self.recv = own_sem, out_sem, send, recv
        place, device = ring_place(sizes[1])
        self.partners = [device((place + 1) % self.n), device((place + self.n - 1) % self.n)]

    def lanes(self, h):
        return pl.ds(pl.multiple_of(h * (self.wide // 2), 128), self.wide // 2)

    def load_own(self, way, t):
        slot = t % self.n if way == 0 else self.n - t
        return pltpu.make_async_copy(
            self.parts[way].at[pl.ds(slot * self.rows, self.rows)],
            self.own_v.at[way, t % 3],
            self.own_sem.at[way, t % 3],
        )

    def ring(self, source, way, t, h):
        return pltpu.make_async_remote_copy(
            src_ref=source,
            dst_ref=self.land.at[way, h, t - 1],
            send_sem=self.send.at[way, h, t],
            recv_sem=self.recv.at[way, h, t],
            device_id=self.partners[way],
            device_id_type=MESH,
        )

    def arrived(self, way, t, h):
        return self.ring(self.land.at[way, h, t - 1], way, t, h)

    def start(self, way, h):
        return self.ring(self.own_v.at[way, 1, :, self.lanes(h)], way, 1, h)

    def forward(self, way, t, h):
        return self.ring(self.land.at[way, h, t - 2], way, t, h)

    def save(self, way):
        return pltpu.make_async_copy(self.own_v.at[way, self.n % 3], self.out[way], self.out_sem.at[way])

    def first(self):
        for way in range(2):
            self.load_own(way, 1).start()
            self.load_own(way, 2).start()
        for way in range(2):
            self.load_own(way, 1).wait()
            for h in range(2):
                self.start(way, h).start()

    def total(self, way, t, h):
        return self.own_v[way, t % 3, :, self.lanes(h)].astype(F32) + self.land[way, h, t - 2].astype(F32)

    def step(self, u):
        t, h = u // 2, u % 2
        for way in range(2):
            self.arrived(way, t - 1, h).wait_recv()

            @pl.when(h == 0)
            def _():
                self.load_own(way, t).wait()

                @pl.when(t == 3)
                def _():
                    for half in range(2):
                        self.start(way, half).wait_send()

                self.load_own(way, t + 1).start()

            self.land[way, h, t - 2] = self.total(way, t, h).astype(BF)
            self.forward(way, t, h).start()

    def last(self):
        n = self.n
        for way in range(2):
            self.load_own(way, n).wait()
            for h in range(2):
                self.arrived(way, n - 1, h).wait_recv()
                half = self.wide // 2
                total = self.total(way, n, h).astype(BF)
                self.own_v[way, n % 3, :, h * half : (h + 1) * half] = total
            self.save(way).start()
        for way in range(2):
            for h in range(2):
                for t in range(2, n):
                    self.forward(way, t, h).wait_send()
            self.save(way).wait()


def reduce_scratch(n, rows, wide):
    dma = pltpu.SemaphoreType.DMA
    return [
        pltpu.VMEM((2, 2, n - 1, rows, wide // 2), BF),
        pltpu.VMEM((2, 3, rows, wide), BF),
        dma((2, 3)),
        dma((2,)),
        dma((2, 2, n)),
        dma((2, 2, n)),
    ]


class TeamSpread:
    def __init__(self, size, own, others, send, recv):
        self.own, self.others, self.send, self.recv = own, others, send, recv
        self.count = len(own)
        me = lax.axis_index("dp")
        self.stages = []
        held, bit = 1, size // 2
        while bit:
            partner = {"dp": me + bit - 2 * bit * ((me // bit) % 2)}
            self.stages.append((held, partner))
            held, bit = 2 * held, bit // 2

    def partners(self):
        return [partner for _, partner in self.stages]

    def copies(self, stage):
        held, partner = self.stages[stage]
        for k in range(self.count):
            for b in range(held):
                yield pltpu.make_async_remote_copy(
                    src_ref=self.own[k] if b == 0 else self.others[k][b - 1],
                    dst_ref=self.others[k][held + b - 1],
                    send_sem=self.send.at[k, held + b - 1],
                    recv_sem=self.recv.at[k, held + b - 1],
                    device_id=partner,
                    device_id_type=MESH,
                )

    def start(self, stage):
        if stage < len(self.stages):
            for copy in self.copies(stage):
                copy.start()

    def arrive(self, stage):
        if stage < len(self.stages):
            for copy in self.copies(stage):
                copy.wait_recv()

    def last(self):
        for stage in range(len(self.stages)):
            for copy in self.copies(stage):
                copy.wait_send()


def spread_scratch(count, size):
    return [pltpu.SemaphoreType.DMA((count, size)), pltpu.SemaphoreType.DMA((count, size))]


def feed_forward(sizes, xs, dys, weights, before, ring_parts, reducing, ident):
    n_dp, n_fsdp, n_ctx = sizes
    n = n_fsdp * n_ctx
    team, (span, width) = len(xs), xs[0].shape
    rows, wide = width // n, weights[0][0].shape[1]
    sub = wide // 3
    pieces = [piece for group in weights for piece in group]
    counts = [len(group) for group in weights]
    tile = min(span, 256)
    per = span // tile
    steps = team * per
    part = max(rows, 128)
    half = width // 2
    gsteps = width // part
    total = 2 * steps + gsteps
    inside = team // 2 if reducing and team > 2 else 0
    carried = [] if before is None else [b[0] for b in before] + [b[1] for b in before]
    backwards = reducing

    def kernel(*refs):
        refs = list(refs)

        def take(count):
            out = refs[:count]
            del refs[:count]
            return out

        x_refs, dy_refs, piece_refs = take(team), take(team), take(len(pieces))
        old_y, old_dn = take(len(carried) // 2), take(len(carried) // 2)
        part_refs = take(2)
        y_refs, dn_refs, grad_refs, ring_outs = take(team), take(team), take(2), take(2)
        if reducing:
            near = take(max(1, inside))
            (far,) = take(1)
        wgu, wd, xb, dyb, yb, dnb, dgu, inner, xg, dyg, gout = take(11)
        w_sems, x_sems, y_sems, g_sems, gout_sems = take(5)
        if carried:
            cb, c_sems = take(2)
        if reducing:
            swap_send, swap_recv, face_send, face_recv = take(4)
            ring = RingReduce(sizes, part_refs, ring_outs, *refs)
        else:
            ring = RingGather(sizes, own_columns(n_dp, *part_refs, SUBS // 2), ring_outs, *refs)
        me = lax.axis_index("dp")
        sibling = {"dp": me + 1 - 2 * (me % 2)}
        bit = team // 2
        facing = {"dp": me + bit - 2 * bit * ((me // bit) % 2)}

        k = 0
        w_copies = []
        for b, count in enumerate(counts):
            at = 0
            for ref in piece_refs[k : k + count]:
                high = ref.shape[0]
                w_copies += [
                    pltpu.make_async_copy(
                        ref.at[:, pl.ds(0, 2 * sub)],
                        wgu.at[pl.ds(at, high), pl.ds(b * 2 * sub, 2 * sub)],
                        w_sems.at[2 * k],
                    ),
                    pltpu.make_async_copy(
                        ref.at[:, pl.ds(2 * sub, sub)],
                        wd.at[pl.ds(at, high), pl.ds(b * sub, sub)],
                        w_sems.at[2 * k + 1],
                    ),
                ]
                at += high
                k += 1
        for copy in w_copies:
            copy.start()

        def block_of(i):
            return team - 1 - i // per if backwards else i // per

        def loads(m, i):
            rows_here = pl.ds((i % per) * tile, tile)
            return [
                pltpu.make_async_copy(x_refs[m].at[rows_here], xb.at[i % 2], x_sems.at[0, i % 2]),
                pltpu.make_async_copy(dy_refs[m].at[rows_here], dyb.at[i % 2], x_sems.at[1, i % 2]),
            ]

        def more(m, i):
            if not carried:
                return []
            rows_here = pl.ds((i % per) * tile, tile)
            out = [
                pltpu.make_async_copy(old_y[m].at[rows_here], yb, c_sems.at[0]),
                pltpu.make_async_copy(old_dn[m].at[rows_here], dnb, c_sems.at[1]),
            ]
            if m < inside:
                out.append(pltpu.make_async_copy(near[m].at[rows_here], cb, c_sems.at[2]))
            return out

        def writes(m, i):
            rows_here = pl.ds((i % per) * tile, tile)
            return [
                pltpu.make_async_copy(yb, y_refs[m].at[rows_here], y_sems.at[0]),
                pltpu.make_async_copy(dnb, dn_refs[m].at[rows_here], y_sems.at[1]),
            ]

        def on_block(i, act):
            for m in range(team):

                @pl.when(block_of(i) == m)
                def _():
                    act(m)

        def swap(m):
            return pltpu.make_async_remote_copy(
                src_ref=dn_refs[m],
                dst_ref=near[m - inside],
                send_sem=swap_send.at[m - inside],
                recv_sem=swap_recv.at[m - inside],
                device_id=sibling,
                device_id_type=MESH,
            )

        def face():
            return pltpu.make_async_remote_copy(
                src_ref=dn_refs[1],
                dst_ref=far,
                send_sem=face_send,
                recv_sem=face_recv,
                device_id=facing,
                device_id_type=MESH,
            )

        def go(copies):
            for copy in copies:
                copy.start()

        def end(copies):
            for copy in copies:
                copy.wait()

        def ticks(lo, hi):
            if reducing:
                count, base, act = 2 * (n - 2), 4, ring.step
            else:
                count, base, act = n - 2, 2, ring.tick
            lax.fori_loop(
                base + lo * count // total, base + hi * count // total, lambda t, c: (act(t), c)[1], 0
            )

        on_block(0, lambda m: go(loads(m, 0)))
        partners = list(ring.partners)
        if inside:
            partners.append(sibling)
        if reducing and team > 1:
            partners.append(facing)
        greet(partners)
        ring.first()
        for copy in w_copies:
            copy.wait()

        def forward(i, carry):
            @pl.when(i + 1 < steps)
            def _():
                on_block(i + 1, lambda m: go(loads(m, i + 1)))

            @pl.when(i == steps - 1)
            def _():
                go(sides(0))

            if inside:
                @pl.when(i % per == 0)
                def _():
                    on_block(i, lambda m: swap(m + inside).wait_recv() if m < inside else None)

            ticks(2 * i, 2 * i + 2)
            end(loads(0, i))
            here = pl.ds(pl.multiple_of(i * tile, tile), tile)
            if carried:
                drained = (i > 0) & (i % per != 0) if reducing else i > 0

                @pl.when(drained)
                def _():
                    end(writes(0, i))

                on_block(i, lambda m: go(more(m, i)))
            for b in range(2):
                gate_up = dot_nn(xb[i % 2], wgu[:, b * 2 * sub : (b + 1) * 2 * sub])
                d_inner = dot_nn(dyb[i % 2], wd[:, b * sub : (b + 1) * sub])
                gate, up = gate_up[:, :sub], gate_up[:, sub:]
                sig = 1.0 / (1.0 + jnp.exp(-gate))
                act = gate * sig
                inner[here, b * sub : (b + 1) * sub] = (act * up).astype(BF)
                dgu[here, b * 2 * sub : b * 2 * sub + sub] = (
                    d_inner * up * (sig + act * (1.0 - sig))
                ).astype(BF)
                dgu[here, b * 2 * sub + sub : (b + 1) * 2 * sub] = (d_inner * act).astype(BF)
            if not carried:

                @pl.when(i > 0)
                def _():
                    end(writes(0, i))

            else:
                on_block(i, lambda m: end(more(m, i)))
            for at in range(0, width, half):
                lanes = slice(at, at + half)
                y = dot_nt(inner[here, :], wd[lanes, :])
                if carried:
                    y = y + yb[:, lanes].astype(F32)
                yb[:, lanes] = y.astype(BF)
                dn = dot_nt(dgu[here, :], wgu[lanes, :])
                if carried:
                    dn = dn + dnb[:, lanes].astype(F32)
                if inside:
                    dn = dn + jnp.where(block_of(i) < inside, cb[:, lanes].astype(F32), 0.0)
                dnb[:, lanes] = dn.astype(BF)
            on_block(i, lambda m: go(writes(m, i)))
            if reducing and team > 1:

                @pl.when(i % per == per - 1)
                def _():
                    def sent(m):
                        if m >= 1:
                            end(writes(m, i))
                            go([swap(m)] if inside and m >= inside else [face()])

                    on_block(i, sent)

            return carry

        def sides(g):
            cols = pl.ds(g * part, part) if isinstance(g, int) else pl.ds(pl.multiple_of(g * part, part), part)
            out = []
            for k in range(team):
                m = team - 1 - k if backwards else k
                at = pl.ds(k * span, span)
                out += [
                    pltpu.make_async_copy(x_refs[m].at[:, cols], xg.at[g % 2, at], g_sems.at[0, g % 2, k]),
                    pltpu.make_async_copy(dy_refs[m].at[:, cols], dyg.at[g % 2, at], g_sems.at[1, g % 2, k]),
                ]
            return out

        def keep(g):
            at = pl.ds(pl.multiple_of(g * part, part), part)
            return [pltpu.make_async_copy(gout.at[b], grad_refs[b].at[at], gout_sems.at[b]) for b in range(2)]

        def outer(g, carry):
            @pl.when(g + 1 < gsteps)
            def _():
                go(sides(g + 1))

            ticks(2 * steps + g, 2 * steps + g + 1)
            end(sides(g))

            @pl.when(g > 0)
            def _():
                end(keep(g))

            for b in range(2):
                up_down = dot_tn(xg[g % 2], dgu[:, b * 2 * sub : (b + 1) * 2 * sub])
                gout[b, :, : 2 * sub] = up_down.astype(BF)
                down = dot_tn(dyg[g % 2], inner[:, b * sub : (b + 1) * sub])
                gout[b, :, 2 * sub :] = down.astype(BF)
            go(keep(g))
            return carry

        lax.fori_loop(0, steps, forward, 0)
        lax.fori_loop(0, gsteps, outer, 0)
        end(writes(0, 0))
        end(keep(0))
        ring.last()
        if reducing and team > 1:
            for m in range(inside, team) if inside else []:
                swap(m).wait_send()
            face().wait_recv()
            face().wait_send()

    shape = lambda a, b: jax.ShapeDtypeStruct((a, b), BF)
    outs = [shape(span, width)] * (2 * team) + [shape(width, wide)] * 2
    if reducing:
        outs += [shape(rows, wide)] * 2
        outs += [shape(span, width)] * (max(1, inside) + 1)
    else:
        outs += [shape(width, wide)] * 2
    dma = pltpu.SemaphoreType.DMA
    scratch = [
        pltpu.VMEM((width, 4 * sub), BF),
        pltpu.VMEM((width, 2 * sub), BF),
        pltpu.VMEM((2, tile, width), BF),
        pltpu.VMEM((2, tile, width), BF),
        pltpu.VMEM((tile, width), BF),
        pltpu.VMEM((tile, width), BF),
        pltpu.VMEM((team * span, 4 * sub), BF),
        pltpu.VMEM((team * span, 2 * sub), BF),
        pltpu.VMEM((2, team * span, part), BF),
        pltpu.VMEM((2, team * span, part), BF),
        pltpu.VMEM((2, part, wide), BF),
        dma((2 * len(pieces),)),
        dma((2, 2)),
        dma((2,)),
        dma((2, 2, team)),
        dma((2,)),
    ]
    if carried:
        scratch += [pltpu.VMEM((tile, width) if inside else (16, 128), BF), dma((3,))]
    if reducing:
        scratch += [dma((max(1, inside),)), dma((max(1, inside),)), dma(()), dma(())]
        scratch += reduce_scratch(n, rows, wide)
    else:
        scratch += gather_scratch(n, rows, wide)
    operands = list(xs) + list(dys) + pieces + carried + list(ring_parts)
    out = pl.pallas_call(
        kernel,
        in_specs=[ANY] * len(operands),
        out_specs=[ANY] * len(outs),
        out_shape=outs,
        scratch_shapes=scratch,
        compiler_params=pltpu.CompilerParams(
            collective_id=ident, has_side_effects=True, vmem_limit_bytes=60 * MIB
        ),
        cost_estimate=cost(18 * team * span * width * 2 * sub, 40 * MIB),
    )(*operands)
    y, dn, grads, ringed = out[:team], out[team : 2 * team], out[2 * team : 2 * team + 2], out[2 * team + 2 :]
    if reducing:
        return y, (dn[0], ringed[-1]) if team > 1 else (dn[0],), grads, ringed[:2]
    return y, dn, grads, ringed[:2]


def attend_forward(sizes, x, qkv, kv_far, seen, w_out, gains, dy, w_gate_up, w_down):
    n_dp, n_fsdp, n_ctx = sizes
    n = n_fsdp * n_ctx
    span, width = x.shape
    rows = width // n
    far = kv_far.shape[0]
    blocks = far // span
    qwidth, kvwidth = HEADS * HD, KV_HEADS * HD
    near, kvpairs = qwidth // 128, kvwidth // 128
    pairs = HEADS // 2
    tile = min(span, 256)
    wide = 3 * (w_down.shape[1] // n_dp // SUBS)
    early = max(0, 3 * (n - 2) // 7)
    others = n_dp - 1
    chunk = min(512, width)

    def kernel(seen_ref, q_ref, k_ref, v_ref, kf_ref, vf_ref, x_ref, gains_ref, *refs):
        refs = list(refs)

        def take(count):
            out = refs[:count]
            del refs[:count]
            return out

        wo_ref, dy_ref, gu_ref, down_ref = take(4)
        lse_ref, attn_out, hidden_out, normed_out = take(4)
        x_blocks, dy_blocks, ring_outs = take(others), take(others), take(2)
        attn_v, wo_v, hidden_v, normed_v, load_sem, save_sems = take(6)
        dy_send, dy_recv, x_send, x_recv = take(4)
        ring = RingGather(sizes, own_columns(n_dp, gu_ref, down_ref, 0), ring_outs, *refs)
        dy_spread = TeamSpread(n_dp, [dy_ref], [dy_blocks], dy_send, dy_recv)
        x_spread = TeamSpread(n_dp, [normed_v], [x_blocks], x_send, x_recv)
        group = pl.program_id(0)
        mask = causal_tile(tile)
        flags = [seen_ref[k] == 1 for k in range(blocks)]
        load = pltpu.make_async_copy(wo_ref, wo_v, load_sem)

        @pl.when(group == 0)
        def _():
            greet(ring.partners + dy_spread.partners())
            ring.first()
            dy_spread.start(0)
            load.start()

        lax.fori_loop(
            2 + group * early // pairs,
            2 + (group + 1) * early // pairs,
            lambda t, c: (ring.tick(t), c)[1],
            0,
        )
        key, value = head_of(k_ref[...], group), head_of(v_ref[...], group)
        key_far, value_far = head_of(kf_ref[...], group), head_of(vf_ref[...], group)
        value_t = value.astype(F32).T.astype(BF)
        value_far_t = value_far.astype(F32).T.astype(BF)
        for head in range(2):
            down = pl.ds(pl.multiple_of(group * 128 + head * HD, HD), HD)
            for at in range(0, span, tile):
                end = at + tile
                q = q_ref[at:end, head * HD : (head + 1) * HD]
                own, other = scores_of(key[:end], key_far, q, flags, mask, span)
                peak = jnp.maximum(jnp.max(own, 0, keepdims=True), jnp.max(other, 0, keepdims=True))
                own = jnp.exp(own - peak)
                other = jnp.exp(other - peak)
                total = jnp.sum(own, 0, keepdims=True) + jnp.sum(other, 0, keepdims=True)
                scale = 1.0 / total
                result = dot_nn(value_t[:, :end], (own * scale).astype(BF)) + dot_nn(
                    value_far_t, (other * scale).astype(BF)
                )
                attn_v[down, at:end] = result.astype(BF)
                lse_ref[0, head : head + 1, at:end] = peak + jnp.log(total)

        @pl.when(group == pairs - 1)
        def _():
            saves = [
                pltpu.make_async_copy(a, b, save_sems.at[k])
                for k, (a, b) in enumerate([(attn_v, attn_out), (hidden_v, hidden_out), (normed_v, normed_out)])
            ]
            saves[0].start()
            load.wait()
            square = jnp.zeros((span, 1), F32)
            for at in range(0, width, chunk):
                lanes = slice(at, at + chunk)
                hidden = x_ref[:, lanes].astype(F32) + dot_tn(attn_v[...], wo_v[:, lanes])
                hidden_v[:, lanes] = hidden
                square = square + jnp.sum(hidden * hidden, -1, keepdims=True)
            scale = lax.rsqrt(square / width + EPS)
            place, device = ring_place(n_fsdp)
            for slot in range(n):
                there = device((place + n - slot) % n)
                part = slot_lanes(hidden_v, there["fsdp"] * n_ctx + there["ctx"], rows)
                normed = part * scale * gains_ref[slot, 1:2, :].astype(F32)
                normed_v[:, slot * rows : (slot + 1) * rows] = normed.astype(BF)
            x_spread.start(0)
            saves[1].start()
            saves[2].start()
            dy_spread.arrive(0)
            dy_spread.start(1)
            middle = max(2 + early, n - 2)
            for t in range(2 + early, middle):
                ring.tick(t)
            x_spread.arrive(0)
            x_spread.start(1)
            for t in range(middle, n):
                ring.tick(t)
            dy_spread.arrive(1)
            x_spread.arrive(1)
            ring.last()
            dy_spread.last()
            x_spread.last()
            for copy in saves:
                copy.wait()

    pair = lambda high, shift: pl.BlockSpec((high, 128), lambda i: (0, i // 4 + shift))
    dma = pltpu.SemaphoreType.DMA
    block = jax.ShapeDtypeStruct((span, width), BF)
    out = pl.pallas_call(
        kernel,
        grid=(pairs,),
        in_specs=[
            pl.BlockSpec(memory_space=pltpu.SMEM),
            pl.BlockSpec((span, 128), lambda i: (0, i)),
            pair(span, near),
            pair(span, near + kvpairs),
            pair(far, 0),
            pair(far, kvpairs),
            pl.BlockSpec((span, width), lambda i: (0, 0)),
            pl.BlockSpec(gains.shape, lambda i: (0, 0, 0)),
        ]
        + [ANY] * 4,
        out_specs=[pl.BlockSpec((1, 8, span), lambda i: (i, 0, 0))] + [ANY] * (5 + 2 * others),
        out_shape=[
            jax.ShapeDtypeStruct((pairs, 8, span), F32),
            jax.ShapeDtypeStruct((qwidth, span), BF),
            jax.ShapeDtypeStruct((span, width), F32),
        ]
        + [block] * (1 + 2 * others)
        + [jax.ShapeDtypeStruct((width, wide), BF)] * 2,
        scratch_shapes=[
            pltpu.VMEM((qwidth, span), BF),
            pltpu.VMEM((qwidth, width), BF),
            pltpu.VMEM((span, width), F32),
            pltpu.VMEM((span, width), BF),
            dma(()),
            dma((3,)),
        ]
        + spread_scratch(1, n_dp)
        + spread_scratch(1, n_dp)
        + gather_scratch(n, rows, wide),
        compiler_params=pltpu.CompilerParams(
            collective_id=5, has_side_effects=True, vmem_limit_bytes=58 * MIB
        ),
        cost_estimate=cost(pairs * 2 * span * (span + far) * 128 * 4, 30 * MIB),
    )(seen, qkv, qkv, qkv, kv_far, kv_far, x, gains, w_out, dy, w_gate_up, w_down)
    lse, attn, hidden, normed = out[:4]
    return attn, lse, hidden, normed, out[4 : 4 + others], out[4 + others : 4 + 2 * others], out[4 + 2 * others :]


def attend_backward(sizes, qkv, kv_far, d_attn, lse, seen, tables, attn_t, d_proj, normed, ring_parts, sums, ident):
    n_dp, n_fsdp, n_ctx = sizes
    n = n_fsdp * n_ctx
    span, far = qkv.shape[0], kv_far.shape[0]
    blocks = far // span
    qwidth, kvwidth = HEADS * HD, KV_HEADS * HD
    near, kvpairs = qwidth // 128, kvwidth // 128
    pairs = HEADS // 2
    tile = min(span, 256)
    rows, wide = ring_parts[0].shape[0] // n, ring_parts[0].shape[1]
    early = 4 + 8 * (n - 2) // 6
    width = normed.shape[1]
    qkvwidth = qwidth + 2 * kvwidth
    part = max(rows, 128)
    others = n_dp - 1

    def kernel(seen_ref, q_ref, k_ref, v_ref, kf_ref, vf_ref, d_ref, lse_ref, cos_ref, low_ref, high_ref, *refs):
        refs = list(refs)

        def take(count):
            out = refs[:count]
            del refs[:count]
            return out

        attn_ref, proj_ref, normed_ref = take(3)
        parts, own_sums = take(2), take(2)
        dqkv_out, go_out, gq_out = take(3)
        ring_outs, blocks_out = take(2), take(2 * others)
        dqkv_v, dkv, dkv_far, give, got, save_sem, kv_send, kv_recv = take(8)
        attn_v, proj_v, normed_v, stage, load_sems, stage_sems = take(6)
        spread_send, spread_recv = take(2)
        ring = RingReduce(sizes, parts, ring_outs, *refs)
        spread = TeamSpread(
            n_dp, own_sums, [blocks_out[k * others : (k + 1) * others] for k in range(2)], spread_send, spread_recv
        )
        loads = [
            pltpu.make_async_copy(a, b, load_sems.at[k])
            for k, (a, b) in enumerate([(attn_ref, attn_v), (proj_ref, proj_v), (normed_ref, normed_v)])
        ]

        def product(out, cols, make):
            def write(g):
                return pltpu.make_async_copy(
                    stage.at[g % 2, :, pl.ds(0, cols)],
                    out.at[pl.ds(pl.multiple_of(g * part, part), part)],
                    stage_sems.at[g % 2],
                )

            def body(g, carry):
                @pl.when(g >= 2)
                def _():
                    write(g - 2).wait()

                stage[g % 2, :, :cols] = make(pl.ds(pl.multiple_of(g * part, part), part)).astype(BF)
                write(g).start()
                return carry

            count = width // part
            lax.fori_loop(0, count, body, 0)
            for g in range(max(0, count - 2), count):
                write(g).wait()

        ctx = lax.axis_index("ctx")
        group = pl.program_id(0)
        mask = causal_tile(tile)
        flags = [seen_ref[k] == 1 for k in range(blocks)]
        key, value = head_of(k_ref[...], group), head_of(v_ref[...], group)
        key_far, value_far = head_of(kf_ref[...], group), head_of(vf_ref[...], group)
        key_t = key.astype(F32).T.astype(BF)
        key_far_t = key_far.astype(F32).T.astype(BF)
        odd = (group // 2) % 2 == 1
        cosine, low, high = cos_ref[...], -low_ref[...], -high_ref[...]

        @pl.when(group == 0)
        def _():
            greet(ring.partners + [{"ctx": (ctx + k) % n_ctx} for k in range(1, n_ctx)] + spread.partners())
            ring.first()
            spread.start(0)
            for copy in loads:
                copy.start()
            dkv[...] = jnp.zeros_like(dkv)
            dkv_far[...] = jnp.zeros_like(dkv_far)

        lax.fori_loop(
            4 + group * (early - 4) // pairs,
            4 + (group + 1) * (early - 4) // pairs,
            lambda u, c: (ring.step(u), c)[1],
            0,
        )

        def put(ref, size, shift, add):
            zero = jnp.zeros_like(add)
            lanes = pl.ds(pl.multiple_of(group // 4 * 128 + shift, 128), 128)
            ref[0:size, lanes] += jnp.concatenate([jnp.where(odd, zero, add), jnp.where(odd, add, zero)], 1)

        for at in range(0, span, tile):
            end = at + tile
            turned = []
            for head in range(2):
                lanes = slice(head * HD, (head + 1) * HD)
                q = q_ref[at:end, lanes]
                d = d_ref[at:end, lanes]
                own, other = scores_of(key[:end], key_far, q, flags, mask, span)
                base = lse_ref[0, head : head + 1, at:end]
                own = jnp.exp(own - base)
                other = jnp.exp(other - base)
                d_own = dot_nt(value[:end], d)
                d_other = dot_nt(value_far, d)
                delta = jnp.sum(own * d_own, 0, keepdims=True) + jnp.sum(other * d_other, 0, keepdims=True)
                ds_own = (own * (d_own - delta)).astype(BF)
                ds_other = (other * (d_other - delta)).astype(BF)
                put(dkv, end, kvwidth, dot_nn(own.astype(BF), d))
                put(dkv_far, far, kvwidth, dot_nn(other.astype(BF), d))
                put(dkv, end, 0, dot_nn(ds_own, q))
                put(dkv_far, far, 0, dot_nn(ds_other, q))
                turned.append(dot_nn(key_t[:, :end], ds_own) + dot_nn(key_far_t, ds_other))
            d_query = jnp.concatenate(turned, 0).T * HD**-0.5
            dqkv_v[at:end, pl.ds(pl.multiple_of(group * 128, 128), 128)] = turn(
                d_query, cosine[at:end], low[at:end], high[at:end]
            ).astype(BF)

        @pl.when(group == pairs - 1)
        def _():
            give[...] = dkv_far[...].astype(BF)

            def back(k):
                return pltpu.make_async_remote_copy(
                    src_ref=give.at[pl.ds((k - 1) * span, span)],
                    dst_ref=got.at[k - 1],
                    send_sem=kv_send.at[k],
                    recv_sem=kv_recv.at[k],
                    device_id={"ctx": (ctx + k) % n_ctx},
                    device_id_type=MESH,
                )

            for k in range(1, n_ctx):
                back(k).start()
            for copy in loads:
                copy.wait()
            ring.step(early)
            product(go_out, qwidth, lambda at: dot_nn(attn_v[at, :], proj_v[...]))
            ring.step(early + 1)
            for k in range(1, n_ctx):
                back(k).wait_recv()
            for at in range(0, 2 * kvwidth, 128):
                piece = dkv[:, at : at + 128]
                for k in range(1, n_ctx):
                    piece = piece + got[k - 1, :, at : at + 128].astype(F32)
                if at < kvwidth:
                    piece = turn(piece, cosine, low, high)
                dqkv_v[:, qwidth + at : qwidth + at + 128] = piece.astype(BF)
            save = pltpu.make_async_copy(dqkv_v, dqkv_out, save_sem)
            save.start()
            lax.fori_loop(early + 2, 2 * n - 1, lambda u, c: (ring.step(u), c)[1], 0)
            spread.arrive(0)
            spread.start(1)
            product(gq_out, qkvwidth, lambda at: dot_tn(normed_v[:, at], dqkv_v[...]))
            if early + 2 < 2 * n:
                ring.step(2 * n - 1)
            spread.arrive(1)
            ring.last()
            spread.last()
            for k in range(1, n_ctx):
                back(k).wait_send()
            save.wait()

    pair = lambda high, shift: pl.BlockSpec((high, 128), lambda i: (0, i // 4 + shift))
    wide_block = pl.BlockSpec((span, 128), lambda i: (0, i))
    table = pl.BlockSpec((span, 128), lambda i: (0, 0))
    dma = pltpu.SemaphoreType.DMA
    out = pl.pallas_call(
        kernel,
        grid=(pairs,),
        in_specs=[
            pl.BlockSpec(memory_space=pltpu.SMEM),
            wide_block,
            pair(span, near),
            pair(span, near + kvpairs),
            pair(far, 0),
            pair(far, kvpairs),
            wide_block,
            pl.BlockSpec((1, 8, span), lambda i: (i, 0, 0)),
            table,
            table,
            table,
        ]
        + [ANY] * 7,
        out_specs=[ANY] * (5 + 2 * others),
        out_shape=[
            jax.ShapeDtypeStruct((span, qkvwidth), BF),
            jax.ShapeDtypeStruct((width, qwidth), BF),
            jax.ShapeDtypeStruct((width, qkvwidth), BF),
        ]
        + [jax.ShapeDtypeStruct((rows, wide), BF)] * (2 + 2 * others),
        scratch_shapes=[
            pltpu.VMEM((span, qwidth + 2 * kvwidth), BF),
            pltpu.VMEM((span, 2 * kvwidth), F32),
            pltpu.VMEM((far, 2 * kvwidth), F32),
            pltpu.VMEM((far, 2 * kvwidth), BF),
            pltpu.VMEM((n_ctx - 1, span, 2 * kvwidth), BF),
            dma(()),
            dma((n_ctx,)),
            dma((n_ctx,)),
            pltpu.VMEM(attn_t.shape, BF),
            pltpu.VMEM(d_proj.shape, BF),
            pltpu.VMEM(normed.shape, BF),
            pltpu.VMEM((2, part, max(qwidth, qkvwidth)), BF),
            dma((3,)),
            dma((2,)),
        ]
        + spread_scratch(2, n_dp)
        + reduce_scratch(n, rows, wide),
        compiler_params=pltpu.CompilerParams(
            collective_id=ident, has_side_effects=True, vmem_limit_bytes=58 * MIB
        ),
        cost_estimate=cost(pairs * 2 * span * (span + far) * 128 * 10, 30 * MIB),
    )(seen, qkv, qkv, qkv, kv_far, kv_far, d_attn, lse, *tables, attn_t, d_proj, normed, *ring_parts, *sums)
    return out[0], out[1], out[2], out[3:5], [out[5 + k * others : 5 + (k + 1) * others] for k in range(2)]


def opening(sizes, x, dy, w_qkv, w_out, gains, tables):
    n_dp, n_fsdp, n_ctx = sizes
    n = n_fsdp * n_ctx
    span, width = x.shape
    rows = width // n
    share, half = w_qkv.shape[1] // n_dp, w_out.shape[1] // 2
    qwidth, kvwidth = HEADS * HD, KV_HEADS * HD
    qkvwidth = qwidth + 2 * kvwidth
    chunk = share // 2 if share % 256 == 0 else share
    across_x = n_dp > 2

    def kernel(x_ref, dy_ref, wq_ref, wo_ref, g_ref, cos_ref, low_ref, high_ref, *refs):
        refs = list(refs)

        def take(count):
            out = refs[:count]
            del refs[:count]
            return out

        qkv_out, far_out, xs_out, wq_out, wo_out, gains_out, dy_out = take(7)
        qkv_v, far_v, xs_v, dy_v = take(4)
        wq_v = take(n_dp)
        om_v, oo_v, gains_v = take(3)
        load_sems, save_sems, wq_sems, wo_sems = take(4)
        send, recv, x_send, x_recv, c_send, c_recv, o_send, o_recv = take(8)
        gain_send, gain_recv, kv_send, kv_recv = take(4)
        me = lax.axis_index("dp")
        core = me % 2
        sibling = {"dp": team_place(n_dp, me, 1)}
        facing = {"dp": team_place(n_dp, me, n_dp // 2)}
        bases = [me, team_place(n_dp, me, n_dp // 2)] if across_x else [me]
        bases = [b * share for b in bases + [team_place(n_dp, b, 1) for b in bases]]
        held = n_dp // 2
        place, device = ring_place(n_fsdp)
        ahead, behind = device((place + 1) % n), device((place + n - 1) % n)
        mine = (wq_v[0], om_v)
        widths = (share, half)

        def block_of(slot):
            there = device((place + n - slot) % n)
            return there["fsdp"] * n_ctx + there["ctx"]

        loads = [
            pltpu.make_async_copy(
                ref.at[:, pl.ds(pl.multiple_of(at, 128), w)], mine[k].at[pl.ds(0, rows)], load_sems.at[k]
            )
            for k, (ref, at, w) in enumerate(((wq_ref, me * share, share), (wo_ref, core * half, half)))
        ] + [pltpu.make_async_copy(g_ref, gains_v.at[0], load_sems.at[2])]
        for copy in loads:
            copy.start()
        ctx = lax.axis_index("ctx")
        greet(
            [ahead, behind, sibling]
            + ([facing] if across_x else [])
            + [{"ctx": (ctx + k) % n_ctx} for k in range(1, n_ctx)]
        )

        def lanes(k, way):
            return pl.ds(way * (widths[k] // 2), widths[k] // 2)

        def remote(source, target, send_sem, recv_sem, partner):
            return pltpu.make_async_remote_copy(
                src_ref=source,
                dst_ref=target,
                send_sem=send_sem,
                recv_sem=recv_sem,
                device_id=partner,
                device_id_type=MESH,
            )

        def step(k, way, t):
            here = t - 1 if way == 0 else (n - t + 1) % n
            there = t if way == 0 else n - t
            return remote(
                mine[k].at[pl.ds(here * rows, rows), lanes(k, way)],
                mine[k].at[pl.ds(there * rows, rows), lanes(k, way)],
                send.at[k, way, t],
                recv.at[k, way, t],
                ahead if way == 0 else behind,
            )

        def over_x(way, slot):
            at = (pl.ds(slot * rows, rows), lanes(0, way))
            return remote(wq_v[0].at[at], wq_v[1].at[at], x_send.at[way, slot], x_recv.at[way, slot], facing)

        def over_core(b, way, slot):
            at = (pl.ds(slot * rows, rows), lanes(0, way))
            return remote(
                wq_v[b].at[at], wq_v[held + b].at[at], c_send.at[b, way, slot], c_recv.at[b, way, slot], sibling
            )

        def out_over(way, slot):
            at = (pl.ds(slot * rows, rows), lanes(1, way))
            return remote(om_v.at[at], oo_v.at[at], o_send.at[way, slot], o_recv.at[way, slot], sibling)

        def gain_step(t):
            return remote(gains_v.at[t - 1], gains_v.at[t], gain_send.at[t], gain_recv.at[t], ahead)

        def kv_step(k):
            return remote(
                qkv_v.at[:, pl.ds(qwidth, 2 * kvwidth)],
                far_v.at[pl.ds((k - 1) * span, span)],
                kv_send.at[k],
                kv_recv.at[k],
                {"ctx": (ctx + n_ctx - k) % n_ctx},
            )

        def give(way, slot):
            if across_x:
                over_x(way, slot).start()
            over_core(0, way, slot).start()

        f32 = x_ref[...].astype(F32)
        scale = lax.rsqrt(jnp.mean(f32 * f32, -1, keepdims=True) + EPS)

        def normalize(slot):
            part = slot_lanes(x_ref, block_of(slot), rows)
            xs_v[:, slot * rows : (slot + 1) * rows] = (
                part * scale * gains_v[slot, 0:1, :].astype(F32)
            ).astype(BF)
            dy_v[:, slot * rows : (slot + 1) * rows] = slot_lanes(dy_ref, block_of(slot), rows).astype(BF)

        loads[0].wait()
        loads[2].wait()
        gain_step(1).start()
        for way in range(2):
            step(0, way, 1).start()
        loads[1].wait()
        for way in range(2):
            give(way, 0)
        normalize(0)
        for t in range(1, n):
            gain_step(t).wait_recv()
            if t < n - 1:
                gain_step(t + 1).start()
            for way in range(2):
                step(0, way, t).wait_recv()
                if t < n - 1:
                    step(0, way, t + 1).start()
                give(way, t if way == 0 else n - t)
            normalize(t)

        for way in range(2):
            step(1, way, 1).start()
            out_over(way, 0).start()

        def out_tick(t):
            for way in range(2):
                step(1, way, t).wait_recv()
                if t < n - 1:
                    step(1, way, t + 1).start()
                out_over(way, t if way == 0 else n - t).start()

        order = [(way, 0) for way in range(2)]
        for t in range(1, n):
            order += [(0, t), (1, n - t)]
        cosine, low, high = cos_ref[...], low_ref[...], high_ref[...]

        def form(b, at):
            value = dot_nn(xs_v[...], wq_v[b][:, at : at + chunk])
            for part in range(0, chunk, 128):
                piece = value[:, part : part + 128]
                here = bases[b] + at + part
                piece = jnp.where(here >= qwidth + kvwidth, piece, turn(piece, cosine, low, high))
                piece = piece * jnp.where(here < qwidth, HD**-0.5, 1.0)
                qkv_v[:, pl.ds(pl.multiple_of(here, 128), 128)] = piece.astype(BF)

        def save_share(b):
            return [
                pltpu.make_async_copy(
                    wq_v[b].at[pl.ds(slot * rows, rows)],
                    wq_out.at[
                        pl.ds(pl.multiple_of(block_of(slot) * rows, rows), rows),
                        pl.ds(pl.multiple_of(bases[b], 128), share),
                    ],
                    wq_sems.at[b, slot],
                )
                for slot in range(n)
            ]

        def save_half(k):
            whose = core if k == 0 else 1 - core
            return [
                pltpu.make_async_copy(
                    (om_v, oo_v)[k].at[pl.ds(slot * rows, rows)],
                    wo_out.at[
                        pl.ds(pl.multiple_of(block_of(slot) * rows, rows), rows),
                        pl.ds(pl.multiple_of(whose * half, 128), half),
                    ],
                    wo_sems.at[k, slot],
                )
                for slot in range(n)
            ]

        def go(copies):
            for copy in copies:
                copy.start()

        jobs = [lambda at=at: form(0, at) for at in range(0, share, chunk)]
        jobs.append(lambda: go(save_share(0)))

        def core_shares(b):
            for way, slot in order:
                over_core(b, way, slot).wait_recv()
            go(save_share(held + b))

        jobs.append(lambda: core_shares(0))
        jobs += [lambda at=at: form(held, at) for at in range(0, share, chunk)]
        if across_x:

            def relay(way, slot):
                over_x(way, slot).wait_recv()
                over_core(1, way, slot).start()

            jobs += [lambda w=way, k=slot: relay(w, k) for way, slot in order]
            jobs.append(lambda: go(save_share(1)))
            jobs += [lambda at=at: form(1, at) for at in range(0, share, chunk)]
            jobs.append(lambda: core_shares(1))
            jobs += [lambda at=at: form(held + 1, at) for at in range(0, share, chunk)]
        for k, job in enumerate(jobs):
            job()
            for t in range(1 + k * (n - 1) // len(jobs), 1 + (k + 1) * (n - 1) // len(jobs)):
                out_tick(t)
        for j in range(1, n_ctx):
            kv_step(j).start()
        saves = [
            pltpu.make_async_copy(a, b, save_sems.at[k])
            for k, (a, b) in enumerate(
                [(qkv_v, qkv_out), (far_v, far_out), (xs_v, xs_out), (gains_v, gains_out), (dy_v, dy_out)]
            )
        ]
        for k in (0, 2, 3, 4):
            saves[k].start()
        go(save_half(0))
        for way, slot in order:
            out_over(way, slot).wait_recv()
        go(save_half(1))
        for j in range(1, n_ctx):
            kv_step(j).wait_recv()
        saves[1].start()
        for t in range(1, n):
            gain_step(t).wait_send()
            for way in range(2):
                for k in range(2):
                    step(k, way, t).wait_send()
        for way, slot in order:
            out_over(way, slot).wait_send()
            for b in range(held):
                over_core(b, way, slot).wait_send()
            if across_x:
                over_x(way, slot).wait_send()
        for j in range(1, n_ctx):
            kv_step(j).wait_send()
        for copies in [save_share(b) for b in range(n_dp)] + [save_half(k) for k in range(2)] + [saves]:
            for copy in copies:
                copy.wait()

    dma = pltpu.SemaphoreType.DMA
    shapes = [
        (span, qkvwidth),
        ((n_ctx - 1) * span, 2 * kvwidth),
        (span, width),
        (width, qkvwidth),
        (width, 2 * half),
        (n, 16, rows),
        (span, width),
    ]
    return pl.pallas_call(
        kernel,
        in_specs=[WHOLE, WHOLE, ANY, ANY, ANY, WHOLE, WHOLE, WHOLE],
        out_specs=[ANY] * 7,
        out_shape=[jax.ShapeDtypeStruct(shape, BF) for shape in shapes],
        scratch_shapes=[pltpu.VMEM(shape, BF) for shape in shapes[:3] + shapes[6:]]
        + [pltpu.VMEM((width, share), BF)] * n_dp
        + [pltpu.VMEM((width, half), BF)] * 2
        + [pltpu.VMEM((n, 16, rows), BF)]
        + [
            dma((3,)),
            dma((5,)),
            dma((n_dp, n)),
            dma((2, n)),
            dma((2, 2, n)),
            dma((2, 2, n)),
            dma((2, n)),
            dma((2, n)),
            dma((n_dp // 2, 2, n)),
            dma((n_dp // 2, 2, n)),
            dma((2, n)),
            dma((2, n)),
            dma((n,)),
            dma((n,)),
            dma((n_ctx,)),
            dma((n_ctx,)),
        ],
        compiler_params=pltpu.CompilerParams(
            collective_id=0, has_side_effects=True, vmem_limit_bytes=56 * MIB
        ),
        cost_estimate=cost(2 * span * width * qkvwidth, 4 * width * qkvwidth),
    )(x, dy, w_qkv, w_out, gains, *tables)


def closing(sizes, part_qkv, part_out, sums, d_qkv, w_qkv, x, gain, d_gain):
    n_dp, n_fsdp, n_ctx = sizes
    n = n_fsdp * n_ctx
    span, width = x.shape
    mine = width // n
    rows, widths, kinds = [mine, 8], [part_qkv.shape[1] // 2, max(mine, 256)], [BF, F32]
    count = 2
    outwidth = part_out.shape[1]
    split = n_dp > 2
    quarter = outwidth // n_dp
    chunk = min(512, width)
    parts = width // chunk
    bits = [1 << k for k in range(1, n_dp.bit_length() - 1)]
    others = n_dp - 1

    def kernel(*refs):
        refs = list(refs)

        def take(size):
            out = refs[:size]
            del refs[:size]
            return out

        full, (out_ref,), own_sums = take(1), take(1), take(len(sums))
        dq_ref, w_ref, x_ref, gain_ref, d_gain_ref = take(5)
        outs, (wo_out,) = take(count), take(1)
        blocks_out, (input_out,) = take(len(sums) * others), take(1)
        gain_v, both_v, d_v, w_v, dn_v, w_sem, d_sem, dn_sem = take(8)
        full = full + [gain_v]
        near, land, done, extra, back = take(count), take(count), take(count), take(count), take(count)
        own = take(count)
        (own_sems,) = take(1)
        o_own, o_near, o_x, o_land, o_done = take(5)
        o_blocks = take(others)
        o_load, o_swap_send, o_swap_recv, o_x_send, o_x_recv, o_send, o_recv, o_end_send, o_end_recv = take(9)
        send, recv, pair_send, pair_recv, x_send, x_recv, end_send, end_recv = take(8)
        spread = TeamSpread(
            n_dp, own_sums, [blocks_out[k * others : (k + 1) * others] for k in range(len(sums))], *refs
        )
        me = lax.axis_index("dp")
        core = me % 2
        sibling = {"dp": me + 1 - 2 * core}
        place, device = ring_place(n_fsdp)
        ahead, behind = device((place + 1) % n), device((place + n - 1) % n)
        facing = [{"dp": me + bit - 2 * bit * ((me // bit) % 2)} for bit in bits]
        greet([ahead, behind, sibling] + facing)

        def half(g, way):
            return pl.ds(way * (widths[g] // 2), widths[g] // 2)

        def half_of(g, way, whose):
            base = whose * widths[g] + way * (widths[g] // 2)
            return pl.ds(pl.multiple_of(base, 128), widths[g] // 2)

        def at(g, slot):
            return pl.ds(slot * rows[g], rows[g])

        def swap(g, way, slot):
            return pltpu.make_async_remote_copy(
                src_ref=full[g].at[at(g, slot), half_of(g, way, 1 - core)],
                dst_ref=near[g].at[at(g, slot), half(g, way)],
                send_sem=pair_send.at[g, way, slot],
                recv_sem=pair_recv.at[g, way, slot],
                device_id=sibling,
                device_id_type=MESH,
            )

        def step(g, way, t):
            slot = t if way == 0 else n - t
            source = near[g].at[at(g, slot), half(g, way)] if t == 1 else land[g].at[way, t - 2]
            return pltpu.make_async_remote_copy(
                src_ref=source,
                dst_ref=land[g].at[way, t - 1],
                send_sem=send.at[g, way, t],
                recv_sem=recv.at[g, way, t],
                device_id=ahead if way == 0 else behind,
                device_id_type=MESH,
            )

        def face(g, k):
            return pltpu.make_async_remote_copy(
                src_ref=done[g].at[k],
                dst_ref=extra[g].at[k],
                send_sem=x_send.at[g, k],
                recv_sem=x_recv.at[g, k],
                device_id=facing[k],
                device_id_type=MESH,
            )

        def end(g):
            return pltpu.make_async_remote_copy(
                src_ref=done[g].at[len(bits)],
                dst_ref=back[g],
                send_sem=end_send.at[g],
                recv_sem=end_recv.at[g],
                device_id=sibling,
                device_id_type=MESH,
            )

        def own_load(g, way, t):
            slot = t % n if way == 0 else n - t
            return pltpu.make_async_copy(
                full[g].at[at(g, slot), half_of(g, way, core)],
                own[g].at[way, t % 2],
                own_sems.at[g, way, t % 2],
            )

        def both(g, way, t, slot):
            own_load(g, way, t).wait()
            swap(g, way, slot).wait_recv()
            return own[g][way, t % 2].astype(F32) + near[g][at(g, slot), half(g, way)].astype(F32)

        def forward(g, t):
            for way in range(2):
                slot = t if way == 0 else n - t
                value = both(g, way, t, slot)
                if t == 1:
                    near[g][at(g, slot), half(g, way)] = value.astype(kinds[g])
                else:
                    step(g, way, t - 1).wait_recv()
                    land[g][way, t - 2] = (value + land[g][way, t - 2].astype(F32)).astype(kinds[g])
                step(g, way, t).start()
                own_load(g, way, t + 1).start()

        def finish(g):
            for way in range(2):
                value = both(g, way, n, 0)
                step(g, way, n - 1).wait_recv()
                done[g][0, :, half(g, way)] = (value + land[g][way, n - 2].astype(F32)).astype(kinds[g])
            if bits:
                face(g, 0).start()

        w_load = pltpu.make_async_copy(w_ref, w_v, w_sem)
        d_load = pltpu.make_async_copy(dq_ref, d_v, d_sem)
        dn_save = pltpu.make_async_copy(dn_v, input_out, dn_sem)

        def begin(g):
            for way in range(2):
                own_load(g, way, 1).start()

        def swaps(g, t):
            swap(g, 0, t % n).start()
            swap(g, 1, n - t).start()

        def product(k):
            lanes = slice(k * chunk, (k + 1) * chunk)
            dn_v[:, lanes] = dot_nt(d_v[...], w_v[lanes, :])

        def norm():
            square = jnp.zeros((span, 1), F32)
            for k in range(parts):
                value = x_ref[:, k * chunk : (k + 1) * chunk].astype(F32)
                square = square + jnp.sum(value * value, -1, keepdims=True)
            scale = lax.rsqrt(square / width + EPS)
            inner = jnp.zeros((span, 1), F32)
            for k in range(parts):
                lanes = slice(k * chunk, (k + 1) * chunk)
                unit = x_ref[:, lanes].astype(F32) * scale
                product = dn_v[:, lanes] * unit
                both_v[1:2, lanes] = jnp.sum(product, 0, keepdims=True)
                inner = inner + jnp.sum(product * gain_ref[0:1, lanes], -1, keepdims=True)
            inner = inner / width
            for k in range(parts):
                lanes = slice(k * chunk, (k + 1) * chunk)
                unit = x_ref[:, lanes].astype(F32) * scale
                dn_v[:, lanes] = scale * (dn_v[:, lanes] * gain_ref[0:1, lanes] - unit * inner)
            dn_save.start()
            gain_v[...] = jnp.zeros_like(gain_v)
            both_v[0:1, :] = d_gain_ref[0:1, :]
            both_v[2:8, :] = jnp.zeros((6, width), F32)
            for slot in range(n):
                there = device((place + n - slot) % n)
                pair = slot_lanes(both_v, there["fsdp"] * n_ctx + there["ctx"], mine)
                gain_v[slot * 8 : slot * 8 + 1, :mine] = pair[1:2]
                gain_v[slot * 8 : slot * 8 + 1, widths[-1] : widths[-1] + mine] = pair[0:1]

        side = me // 2 if split else 0
        across = {"dp": team_place(n_dp, me, n_dp // 2)}
        ends = TeamSpread(n_dp, [o_done], [o_blocks], o_end_send, o_end_recv)

        def natural(slot):
            there = device((place + n - slot) % n)
            return pl.ds(pl.multiple_of((there["fsdp"] * n_ctx + there["ctx"]) * mine, mine), mine)

        def quarter_of(whose, which):
            return pl.ds(pl.multiple_of(whose * (outwidth // 2) + which * quarter, 128), quarter)

        def piece(which):
            return pl.ds(pl.multiple_of(which * quarter, 128), quarter)

        def o_half(way):
            return pl.ds(way * (quarter // 2), quarter // 2)

        def out_load(slot):
            return pltpu.make_async_copy(
                out_ref.at[natural(slot), pl.ds(pl.multiple_of(core * (outwidth // 2), 128), outwidth // 2)],
                o_own.at[slot],
                o_load.at[slot],
            )

        def out_swap(slot, which):
            return pltpu.make_async_remote_copy(
                src_ref=out_ref.at[natural(slot), quarter_of(1 - core, which)],
                dst_ref=o_near.at[slot, :, piece(which)],
                send_sem=o_swap_send.at[slot, which],
                recv_sem=o_swap_recv.at[slot, which],
                device_id=sibling,
                device_id_type=MESH,
            )

        def out_across(slot):
            return pltpu.make_async_remote_copy(
                src_ref=o_near.at[slot, :, piece(1 - side)],
                dst_ref=o_x.at[slot],
                send_sem=o_x_send.at[slot],
                recv_sem=o_x_recv.at[slot],
                device_id=across,
                device_id_type=MESH,
            )

        def out_step(way, t):
            slot = t if way == 0 else n - t
            return pltpu.make_async_remote_copy(
                src_ref=o_x.at[slot, :, o_half(way)] if t == 1 else o_land.at[way, t - 2],
                dst_ref=o_land.at[way, t - 1],
                send_sem=o_send.at[way, t],
                recv_sem=o_recv.at[way, t],
                device_id=ahead if way == 0 else behind,
                device_id_type=MESH,
            )

        def out_pair(slot):
            out_load(slot).wait()
            for which in range(2 if split else 1):
                out_swap(slot, which).wait_recv()
            total = o_own[slot].astype(F32) + o_near[slot].astype(F32)
            o_near[slot] = total.astype(BF)
            if split:
                out_across(slot).start()

        def out_quarter(slot):
            here = o_near[slot, :, piece(side)].astype(F32)
            if split:
                out_across(slot).wait_recv()
                here = here + o_x[slot].astype(F32)
            o_x[slot] = here.astype(BF)

        def out_forward(t):
            for slot in sorted({t, n - t}):
                if min(slot, n - slot) == t:
                    out_quarter(slot)
            for way in range(2):
                slot = t if way == 0 else n - t
                if t > 1:
                    out_step(way, t - 1).wait_recv()
                    value = o_x[slot, :, o_half(way)].astype(F32) + o_land[way, t - 2].astype(F32)
                    o_land[way, t - 2] = value.astype(BF)
                out_step(way, t).start()

        def out_finish():
            out_quarter(0)
            for way in range(2):
                out_step(way, n - 1).wait_recv()
                value = o_x[0, :, o_half(way)].astype(F32) + o_land[way, n - 2].astype(F32)
                o_done[:, o_half(way)] = value.astype(BF)
            ends.start(0)

        gains = 1
        d_load.start()
        w_load.start()
        begin(0)
        slots = []
        for t in range(1, n // 2 + 1):
            slots += [t] if 2 * t == n else [t, n - t]
        slots.append(0)
        for slot in slots:
            out_load(slot).start()
        for t in range(1, n + 1):
            swaps(0, t)
            for slot in slots[t - 1 : t]:
                for which in range(2 if split else 1):
                    out_swap(slot, which).start()
        jobs = [lambda k=k: product(k) for k in range(parts)] + [norm]

        def open_gains():
            begin(gains)
            for t in range(1, n + 1):
                swaps(gains, t)

        jobs.append(open_gains)
        half_way = n // 2
        small = []
        for t in range(1, n):
            small.append(lambda t=t: forward(gains, t))
            if t % 2 == 0 or n <= 4:
                small.append(lambda t=t: out_forward(t // 2 if n > 4 else t))
        for t in range(1, n):
            forward(0, t)
            if t == 1:
                d_load.wait()
                w_load.wait()
            if t <= half_way:
                for slot in slots[(t - 1) * n // half_way : t * n // half_way]:
                    out_pair(slot)
                for job in jobs[(t - 1) * len(jobs) // half_way : t * len(jobs) // half_way]:
                    job()
                if t == half_way:
                    spread.start(0)
            else:
                left, k = n - 1 - half_way, t - half_way - 1
                for job in small[k * len(small) // left : (k + 1) * len(small) // left]:
                    job()
        finish(0)
        for t in range((n - 1) // 2 + 1 if n > 4 else n, n):
            out_forward(t)
        finish(gains)
        out_finish()
        spread.arrive(0)
        spread.start(1)
        ends.arrive(0)
        ends.start(1)
        for k in range(len(bits)):
            for g in range(count):
                face(g, k).wait_recv()
                done[g][k + 1] = (done[g][k].astype(F32) + extra[g][k].astype(F32)).astype(kinds[g])
                if k + 1 < len(bits):
                    face(g, k + 1).start()
        for g in range(count):
            end(g).start()
            here = pl.ds(pl.multiple_of(core * widths[g], 128), widths[g])
            outs[g][:, here] = done[g][len(bits)].astype(F32)
        for g in range(count):
            end(g).wait_recv()
            here = pl.ds(pl.multiple_of((1 - core) * widths[g], 128), widths[g])
            outs[g][:, here] = back[g][...].astype(F32)
        ends.arrive(1)
        bases = [core * (outwidth // 2) + side * quarter]
        if split:
            bases.append(core * (outwidth // 2) + (1 - side) * quarter)
        bases += [b + (1 - 2 * core) * (outwidth // 2) for b in bases]
        for base, ref in zip(bases, [o_done] + list(o_blocks)):
            wo_out[:, pl.ds(pl.multiple_of(base, 128), quarter)] = ref[...].astype(F32)
        ends.last()
        for slot in range(n):
            for which in range(2 if split else 1):
                out_swap(slot, which).wait_send()
            if split:
                out_across(slot).wait_send()
        for way in range(2):
            for t in range(1, n):
                out_step(way, t).wait_send()
        spread.arrive(1)
        spread.last()
        dn_save.wait()
        for g in range(count):
            end(g).wait_send()
            for k in range(len(bits)):
                face(g, k).wait_send()
            for way in range(2):
                for t in range(1, n):
                    step(g, way, t).wait_send()
                for slot in range(n):
                    swap(g, way, slot).wait_send()

    dma = pltpu.SemaphoreType.DMA
    groups = list(zip(rows, widths, kinds))
    out = pl.pallas_call(
        kernel,
        in_specs=[ANY] * (2 + len(sums) + 2) + [WHOLE] * 3,
        out_specs=[WHOLE] * (count + 1) + [ANY] * (len(sums) * others + 1),
        out_shape=[jax.ShapeDtypeStruct((r, 2 * w), F32) for r, w, _ in groups]
        + [jax.ShapeDtypeStruct((mine, outwidth), F32)]
        + [jax.ShapeDtypeStruct(a.shape, BF) for a in sums for _ in range(others)]
        + [jax.ShapeDtypeStruct((span, width), F32)],
        scratch_shapes=[
            pltpu.VMEM((n * 8, 2 * widths[-1]), F32),
            pltpu.VMEM((8, width), F32),
            pltpu.VMEM(d_qkv.shape, BF),
            pltpu.VMEM(w_qkv.shape, BF),
            pltpu.VMEM((span, width), F32),
            dma(()),
            dma(()),
            dma(()),
        ]
        + [pltpu.VMEM((n * r, w), kind) for r, w, kind in groups]
        + [pltpu.VMEM((2, n - 1, r, w // 2), kind) for r, w, kind in groups]
        + [pltpu.VMEM((len(bits) + 1, r, w), kind) for r, w, kind in groups]
        + [pltpu.VMEM((max(1, len(bits)), r, w), kind) for r, w, kind in groups]
        + [pltpu.VMEM((r, w), kind) for r, w, kind in groups]
        + [pltpu.VMEM((2, 2, r, w // 2), kind) for r, w, kind in groups]
        + [
            dma((count, 2, 2)),
            pltpu.VMEM((n, mine, outwidth // 2), BF),
            pltpu.VMEM((n, mine, outwidth // 2), BF),
            pltpu.VMEM((n, mine, quarter), BF),
            pltpu.VMEM((2, n - 1, mine, quarter // 2), BF),
            pltpu.VMEM((mine, quarter), BF),
        ]
        + [pltpu.VMEM((mine, quarter), BF)] * others
        + [
            dma((n,)),
            dma((n, 2)),
            dma((n, 2)),
            dma((n,)),
            dma((n,)),
            dma((2, n)),
            dma((2, n)),
        ]
        + spread_scratch(1, n_dp)
        + [
            dma((count, 2, n)),
            dma((count, 2, n)),
            dma((count, 2, n)),
            dma((count, 2, n)),
            dma((count, max(1, len(bits)))),
            dma((count, max(1, len(bits)))),
            dma((count,)),
            dma((count,)),
        ]
        + spread_scratch(len(sums), n_dp),
        compiler_params=pltpu.CompilerParams(
            collective_id=1, has_side_effects=True, vmem_limit_bytes=58 * MIB
        ),
        cost_estimate=cost(0, sum(12 * n * r * w for r, w, _ in groups)),
    )(part_qkv, part_out, *sums, d_qkv, w_qkv, x, gain, d_gain)
    blocks = [out[3 + k * others : 3 + (k + 1) * others] for k in range(len(sums))]
    return out[0], out[2], out[1], blocks, out[-1]


class Ring:
    def __init__(self, n_fsdp, n_ctx):
        order = []
        for c in range(n_ctx):
            rows = range(n_fsdp) if c % 2 == 0 else reversed(range(n_fsdp))
            order += [f * n_ctx + c for f in rows]
        self.order = order
        self.size = n = len(order)
        place = [0] * n
        for k, block in enumerate(order):
            place[block] = k
        self.place = place
        self.block = lax.axis_index(GRID)
        self.rank = jnp.array(place, jnp.int32)[self.block]

    def slot_blocks(self):
        slots = jnp.arange(self.size, dtype=jnp.int32)
        return jnp.array(self.order, jnp.int32)[(self.rank - slots) % self.size]

    def to_slots(self, array, axis=1, deps=()):
        return reorder(array, self.slot_blocks(), axis, deps)

    def from_slots(self, array, axis=1):
        return reorder(array, (self.rank - jnp.array(self.place, jnp.int32)) % self.size, axis)


class Team:
    def __init__(self, size):
        self.size = size
        self.rank = lax.axis_index("dp")
        self.bits = [1 << k for k in range(size.bit_length() - 1)]
        self.order = [0]
        for bit in reversed(self.bits):
            self.order = self.order + [m ^ bit for m in self.order]

    def swap(self, value, bit):
        return lax.ppermute(value, "dp", [(k, k ^ bit) for k in range(self.size)])

    def scatter(self, parts):
        for bit in self.bits:
            half = len(parts) // 2
            got = [self.swap(part.astype(BF), bit) for part in parts[half:]]
            parts = [kept + part.astype(F32) for kept, part in zip(parts[:half], got)]
        return parts[0]


def shards(sizes, x_in, span_order, attn_gain, w_qkv, w_out, ffn_gain, w_gate_up, w_down, cotangent):
    n_dp, n_fsdp, n_ctx = sizes
    ring = Ring(n_fsdp, n_ctx)
    team = Team(n_dp)
    n = ring.size
    width = x_in.shape[-1]
    rows = width // n
    tokens = x_in.reshape(-1, width)
    span = tokens.shape[0]
    rank = lax.axis_index("ctx")
    qwidth = HEADS * HD
    kvwidth = KV_HEADS * HD
    ffwidth = w_down.shape[1]
    order = span_order.reshape(-1)
    near = [(rank + k) % n_ctx for k in range(n_ctx)]
    offsets = jnp.arange(span, dtype=jnp.int32)
    query_pos = order[rank] * span + offsets
    seen = jnp.stack([order[c] < order[rank] for c in near[1:]]).astype(jnp.int32)
    tables = rope_tables(query_pos.astype(F32))

    ffq = ffwidth // n_dp
    sub = ffq // SUBS
    grad_y = cotangent.reshape(span, width)
    gains = jnp.concatenate([attn_gain[None], ffn_gain[None], jnp.zeros((14, rows), BF)], 0)
    qkv, kv_far, normed_one, wqkv, wout, gains, dy = opening(
        sizes, tokens, grad_y, w_qkv, w_out, gains, tables
    )
    attn_t, lse, hidden_one, normed_two, x_others, dy_others, weights_a = attend_forward(
        sizes, tokens, qkv, kv_far, seen, wout, gains, dy, w_gate_up, w_down
    )
    xs = [normed_two] + list(x_others)
    dys = [dy] + list(dy_others)
    gains = gains[:, :2][(ring.rank - jnp.array(ring.place, jnp.int32)) % n]
    gain_one = gains[:, 0].reshape(-1).astype(F32)
    gain_two = gains[:, 1].reshape(-1).astype(F32)
    scale_two = inv_rms(hidden_one)

    y, dn, grads_a, weights_b = feed_forward(
        sizes, xs, dys, [[w] for w in weights_a], None, (w_gate_up, w_down), False, 2
    )
    y, dn, grads_b, sums_a = feed_forward(
        sizes, xs, dys, [[w] for w in weights_b], list(zip(y, dn)), grads_a, True, 3
    )

    d_normed_two = ring.from_slots(sum(part.astype(F32) for part in dn))
    d_hidden_norm, d_gain_two = norm_back(hidden_one, scale_two, gain_two, d_normed_two)
    d_hidden = grad_y.astype(F32) + d_hidden_norm
    d_proj = d_hidden.astype(BF)

    d_attn = matmul_rows(d_proj, wout).astype(BF)
    d_qkv, part_out, part_qkv, sums_b, others_a = attend_backward(
        sizes, qkv, kv_far, d_attn, lse, seen, tables, attn_t, d_proj, normed_one, grads_b, sums_a, 4
    )
    room = max(rows, 256)
    grad_qkv, grad_out, grad_gain, others_b, d_input_norm = closing(
        sizes,
        part_qkv,
        part_out,
        sums_b,
        d_qkv,
        wqkv,
        tokens,
        jnp.broadcast_to(gain_one[None], (8, width)),
        jnp.broadcast_to(d_gain_two[None], (8, width)),
    )
    grad_input = d_hidden + d_input_norm

    placed, columns = [], []
    for q in range(SUBS):
        blocks = [sums_a[q]] + list(others_a[q]) if q < 2 else [sums_b[q - 2]] + list(others_b[q - 2])
        for m, block in zip(team.order, blocks):
            placed.append(block)
            columns.append((team.rank ^ m) * ffq + q * sub)
    grad_gate_up, grad_down = place_grads(placed, jnp.stack(columns).astype(jnp.int32), sub, ffwidth)

    y_out = hidden_one + ring.from_slots(team.scatter(y))
    return (
        y_out.astype(BF).reshape(x_in.shape),
        grad_input.reshape(x_in.shape),
        grad_gain[0, :rows],
        grad_qkv,
        grad_out,
        grad_gain[0, room : room + rows],
        grad_gate_up,
        grad_down,
    )


def solution(mesh):
    sizes = (mesh.shape["dp"], mesh.shape["fsdp"], mesh.shape["ctx"])
    tokens = P(("dp", "fsdp"), "ctx", None)
    weight = P(("fsdp", "ctx"), None)
    gain = P(("fsdp", "ctx"))

    def body(*args):
        return shards(sizes, *args)

    return jax.shard_map(
        body,
        mesh=mesh,
        in_specs=(tokens, P(("dp", "fsdp"), None), gain, weight, weight, gain, weight, weight, tokens),
        out_specs=(tokens, tokens, gain, weight, weight, gain, weight, weight),
        check_vma=False,
    )
```

```python
import math

import jax
import jax.numpy as jnp
from jax import lax
from jax.experimental import pallas as pl
from jax.experimental.pallas import tpu as pltpu
from jax.sharding import PartitionSpec as P

HEADS = 32
KV_HEADS = 8
HD = 64
EPS = 1e-05
SUBS = 4

BF = jnp.bfloat16
F32 = jnp.float32
GRID = ("fsdp", "ctx")


def matmul(left, right):
    return jnp.dot(left, right, preferred_element_type=F32)


def matmul_rows(left, right):
    return lax.dot_general(left, right, (((1,), (1,)), ((), ())), preferred_element_type=F32)


def matmul_tokens(left, right):
    return lax.dot_general(left, right, (((0,), (0,)), ((), ())), preferred_element_type=F32)


def rope_tables(positions):
    half = HD // 2
    freq = jnp.exp(jnp.arange(half, dtype=F32) * (-math.log(500000.0) / half))
    angle = positions[:, None] * freq[None, :]
    cosine, sine = jnp.cos(angle), jnp.sin(angle)
    zero = jnp.zeros_like(sine)
    return (
        jnp.concatenate([cosine] * 4, -1),
        jnp.concatenate([-sine, zero] * 2, -1),
        jnp.concatenate([zero, sine] * 2, -1),
    )


def inv_rms(rows):
    return lax.rsqrt(jnp.mean(rows * rows, -1, keepdims=True) + EPS)


def norm_back(rows, scale, gain, grad):
    unit = rows * scale
    pulled = grad * gain[None, :]
    inner = jnp.mean(pulled * unit, -1, keepdims=True)
    return scale * (pulled - unit * inner), jnp.sum(grad * unit, 0)


MIB = 1 << 20
ANY = pl.BlockSpec(memory_space=pl.ANY)
WHOLE = pl.BlockSpec(memory_space=pltpu.VMEM)


def cost(flops, moved, exps=0):
    return pl.CostEstimate(flops=int(flops), bytes_accessed=int(moved), transcendentals=int(exps))


def params(mib):
    return pltpu.CompilerParams(vmem_limit_bytes=mib * MIB)


def dot_nn(a, b):
    return lax.dot_general(a, b, (((1,), (0,)), ((), ())), preferred_element_type=F32)


def dot_nt(a, b):
    return lax.dot_general(a, b, (((1,), (1,)), ((), ())), preferred_element_type=F32)


def dot_tn(a, b):
    return lax.dot_general(a, b, (((0,), (0,)), ((), ())), preferred_element_type=F32)


def reorder(array, places, axis=1, deps=()):
    count = places.shape[0]
    if axis == 1 and (array.shape[1] // count) % 128 != 0:
        size = array.shape[1] // count
        blocks = [lax.dynamic_slice_in_dim(array, places[s] * size, size, 1) for s in range(count)]
        return jnp.concatenate(blocks, 1)
    if axis == 1:
        shape = (array.shape[0], array.shape[1] // count)
        took = lambda s, where: (0, where[s])
        gave = lambda s, where: (0, s)
    else:
        shape = (array.shape[0] // count, array.shape[1])
        took = lambda s, where: (where[s], 0)
        gave = lambda s, where: (s, 0)

    def kernel(where, source, *rest):
        rest[-1][...] = source[...]

    return pl.pallas_call(
        kernel,
        grid_spec=pltpu.PrefetchScalarGridSpec(
            num_scalar_prefetch=1,
            grid=(count,),
            in_specs=[pl.BlockSpec(shape, took)] + [ANY] * len(deps),
            out_specs=pl.BlockSpec(shape, gave),
        ),
        out_shape=jax.ShapeDtypeStruct(array.shape, array.dtype),
        compiler_params=params(16),
        cost_estimate=cost(0, 2 * array.size * array.dtype.itemsize),
    )(places, array, *deps)


def turn(piece, cosine, sine_low, sine_high):
    return (
        piece * cosine
        + pltpu.roll(piece, 128 - HD // 2, axis=1) * sine_low
        + pltpu.roll(piece, HD // 2, axis=1) * sine_high
    )


def head_of(block, group):
    odd = (group // 2) % 2 == 1
    return jnp.where(odd, block[:, HD:], block[:, :HD])


def causal_tile(size):
    key = lax.broadcasted_iota(jnp.int32, (size, size), 0)
    query = lax.broadcasted_iota(jnp.int32, (size, size), 1)
    return key <= query


def scores_of(key, key_far, query, seen, mask, span):
    tile = query.shape[0]
    own = dot_nt(key, query)
    if key.shape[0] > tile:
        last = key.shape[0] - tile
        own = jnp.concatenate([own[:last], jnp.where(mask, own[last:], -1e30)], 0)
    else:
        own = jnp.where(mask, own, -1e30)
    far = dot_nt(key_far, query)
    far = [jnp.where(seen[k], far[k * span : (k + 1) * span], -1e30) for k in range(len(seen))]
    return own, (far[0] if len(far) == 1 else jnp.concatenate(far, 0))


def place_grads(pieces, columns, sub, ffwidth):
    rows = pieces[0].shape[0]
    count = len(pieces)

    def kernel(*refs):
        where = refs[0]
        sources = refs[1 : 1 + count]
        gu_ref, down_ref, took, gave, in_sems, out_sems = refs[1 + count :]

        def read(k):
            return pltpu.make_async_copy(sources[k], took.at[k % 2], in_sems.at[k % 2])

        def writes(k):
            at = pl.multiple_of(where[k], 128)
            here = gave.at[k % 2]
            return (
                pltpu.make_async_copy(
                    here.at[:, pl.ds(0, sub)], gu_ref.at[:, pl.ds(at, sub)], out_sems.at[k % 2, 0]
                ),
                pltpu.make_async_copy(
                    here.at[:, pl.ds(sub, sub)], gu_ref.at[:, pl.ds(at + ffwidth, sub)], out_sems.at[k % 2, 1]
                ),
                pltpu.make_async_copy(
                    here.at[:, pl.ds(2 * sub, sub)], down_ref.at[:, pl.ds(at, sub)], out_sems.at[k % 2, 2]
                ),
            )

        read(0).start()
        for k in range(count):
            if k + 1 < count:
                read(k + 1).start()
            read(k).wait()
            if k >= 2:
                for copy in writes(k - 2):
                    copy.wait()
            gave[k % 2] = took[k % 2].astype(F32)
            for copy in writes(k):
                copy.start()
        for k in range(max(0, count - 2), count):
            for copy in writes(k):
                copy.wait()

    return pl.pallas_call(
        kernel,
        in_specs=[pl.BlockSpec(memory_space=pltpu.SMEM)] + [ANY] * count,
        out_specs=[ANY, ANY],
        out_shape=[
            jax.ShapeDtypeStruct((rows, 2 * ffwidth), F32),
            jax.ShapeDtypeStruct((rows, ffwidth), F32),
        ],
        scratch_shapes=[
            pltpu.VMEM((2, rows, 3 * sub), BF),
            pltpu.VMEM((2, rows, 3 * sub), F32),
            pltpu.SemaphoreType.DMA((2,)),
            pltpu.SemaphoreType.DMA((2, 3)),
        ],
        compiler_params=params(60),
        cost_estimate=cost(0, rows * ffwidth * 18),
    )(columns, *pieces)


MESH = pl.DeviceIdType.MESH


def ring_place(n_fsdp):
    f, c = lax.axis_index("fsdp"), lax.axis_index("ctx")

    def device(place):
        row, k = place // n_fsdp, place % n_fsdp
        return {"fsdp": k + (row % 2) * (n_fsdp - 1 - 2 * k), "ctx": row}

    return c * n_fsdp + f + (c % 2) * (n_fsdp - 1 - 2 * f), device


def slot_lanes(ref, block, rows):
    if rows % 128 == 0:
        return ref[:, pl.ds(pl.multiple_of(block * rows, 128), rows)].astype(F32)
    share = 128 // rows
    wide = ref[:, pl.ds(pl.multiple_of(block // share * 128, 128), 128)].astype(F32)
    part = wide[:, :rows]
    for k in range(1, share):
        part = jnp.where(block % share == k, wide[:, k * rows : (k + 1) * rows], part)
    return part


def team_place(size, me, bit):
    return me + bit - 2 * bit * ((me // bit) % 2)


def greet(partners):
    barrier = pltpu.get_barrier_semaphore()
    for partner in partners:
        pl.semaphore_signal(barrier, inc=1, device_id=partner, device_id_type=MESH)
    pl.semaphore_wait(barrier, len(partners))


def own_columns(size, w_gate_up, w_down, first):
    ffwidth = w_down.shape[1]
    ffq = ffwidth // size
    sub = ffq // SUBS
    out = []
    for way in range(2):
        at = lax.axis_index("dp") * ffq + (first + way) * sub
        out.append(
            [
                (w_gate_up.at[:, pl.ds(pl.multiple_of(at, 128), sub)], 0),
                (w_gate_up.at[:, pl.ds(pl.multiple_of(at + ffwidth, 128), sub)], sub),
                (w_down.at[:, pl.ds(pl.multiple_of(at, 128), sub)], 2 * sub),
            ]
        )
    return out


class RingGather:
    def __init__(self, sizes, own, out, own_v, own_sem, store_sem, send, recv):
        self.n = sizes[1] * sizes[2]
        self.rows = own_v.shape[1]
        self.own, self.out, self.own_v = own, out, own_v
        self.own_sem, self.store_sem, self.send, self.recv = own_sem, store_sem, send, recv
        place, device = ring_place(sizes[1])
        self.partners = [device((place + 1) % self.n), device((place + self.n - 1) % self.n)]

    def rows_of(self, way, t):
        slot = t if way == 0 else (self.n - t) % self.n
        return pl.ds(slot * self.rows, self.rows)

    def loads(self, way):
        width = self.own_v.shape[2] // 3
        return [
            pltpu.make_async_copy(
                source, self.own_v.at[way, :, pl.ds(place, width)], self.own_sem.at[way, place // width]
            )
            for source, place in self.own[way]
        ]

    def store(self, way):
        return pltpu.make_async_copy(
            self.own_v.at[way], self.out[way].at[pl.ds(0, self.rows)], self.store_sem.at[way]
        )

    def ring(self, way, t, first=False):
        source = self.own_v.at[way] if first else self.out[way].at[self.rows_of(way, t - 1)]
        return pltpu.make_async_remote_copy(
            src_ref=source,
            dst_ref=self.out[way].at[self.rows_of(way, t)],
            send_sem=self.send.at[way, t],
            recv_sem=self.recv.at[way, t],
            device_id=self.partners[way],
            device_id_type=MESH,
        )

    def arrived(self, way, t):
        target = self.out[way].at[self.rows_of(way, t)]
        return pltpu.make_async_remote_copy(
            src_ref=target,
            dst_ref=target,
            send_sem=self.send.at[way, t],
            recv_sem=self.recv.at[way, t],
            device_id=self.partners[way],
            device_id_type=MESH,
        )

    def first(self):
        for way in range(2):
            for copy in self.loads(way):
                copy.start()
        for way in range(2):
            for copy in self.loads(way):
                copy.wait()
            self.ring(way, 1, True).start()
            self.store(way).start()

    def tick(self, t):
        for way in range(2):
            self.arrived(way, t - 1).wait_recv()
            self.ring(way, t).start()

    def last(self):
        for way in range(2):
            self.arrived(way, self.n - 1).wait_recv()
            self.store(way).wait()
            self.ring(way, 1, True).wait_send()
            for t in range(2, self.n):
                self.ring(way, t).wait_send()


def gather_scratch(n, rows, wide):
    dma = pltpu.SemaphoreType.DMA
    return [pltpu.VMEM((2, rows, wide), BF), dma((2, 3)), dma((2,)), dma((2, n)), dma((2, n))]


class RingReduce:
    def __init__(self, sizes, parts, out, land, own_v, own_sem, out_sem, send, recv):
        self.n = sizes[1] * sizes[2]
        self.rows, self.wide = out[0].shape
        self.parts, self.out, self.land, self.own_v = parts, out, land, own_v
        self.own_sem, self.out_sem, self.send, self.recv = own_sem, out_sem, send, recv
        place, device = ring_place(sizes[1])
        self.partners = [device((place + 1) % self.n), device((place + self.n - 1) % self.n)]

    def lanes(self, h):
        return pl.ds(pl.multiple_of(h * (self.wide // 2), 128), self.wide // 2)

    def load_own(self, way, t):
        slot = t % self.n if way == 0 else self.n - t
        return pltpu.make_async_copy(
            self.parts[way].at[pl.ds(slot * self.rows, self.rows)],
            self.own_v.at[way, t % 3],
            self.own_sem.at[way, t % 3],
        )

    def ring(self, source, way, t, h):
        return pltpu.make_async_remote_copy(
            src_ref=source,
            dst_ref=self.land.at[way, h, t - 1],
            send_sem=self.send.at[way, h, t],
            recv_sem=self.recv.at[way, h, t],
            device_id=self.partners[way],
            device_id_type=MESH,
        )

    def arrived(self, way, t, h):
        return self.ring(self.land.at[way, h, t - 1], way, t, h)

    def start(self, way, h):
        return self.ring(self.own_v.at[way, 1, :, self.lanes(h)], way, 1, h)

    def forward(self, way, t, h):
        return self.ring(self.land.at[way, h, t - 2], way, t, h)

    def save(self, way):
        return pltpu.make_async_copy(self.own_v.at[way, self.n % 3], self.out[way], self.out_sem.at[way])

    def first(self):
        for way in range(2):
            self.load_own(way, 1).start()
            self.load_own(way, 2).start()
        for way in range(2):
            self.load_own(way, 1).wait()
            for h in range(2):
                self.start(way, h).start()

    def total(self, way, t, h):
        return self.own_v[way, t % 3, :, self.lanes(h)].astype(F32) + self.land[way, h, t - 2].astype(F32)

    def step(self, u):
        t, h = u // 2, u % 2
        for way in range(2):
            self.arrived(way, t - 1, h).wait_recv()

            @pl.when(h == 0)
            def _():
                self.load_own(way, t).wait()

                @pl.when(t == 3)
                def _():
                    for half in range(2):
                        self.start(way, half).wait_send()

                self.load_own(way, t + 1).start()

            self.land[way, h, t - 2] = self.total(way, t, h).astype(BF)
            self.forward(way, t, h).start()

    def last(self):
        n = self.n
        for way in range(2):
            self.load_own(way, n).wait()
            for h in range(2):
                self.arrived(way, n - 1, h).wait_recv()
                half = self.wide // 2
                total = self.total(way, n, h).astype(BF)
                self.own_v[way, n % 3, :, h * half : (h + 1) * half] = total
            self.save(way).start()
        for way in range(2):
            for h in range(2):
                for t in range(2, n):
                    self.forward(way, t, h).wait_send()
            self.save(way).wait()


def reduce_scratch(n, rows, wide):
    dma = pltpu.SemaphoreType.DMA
    return [
        pltpu.VMEM((2, 2, n - 1, rows, wide // 2), BF),
        pltpu.VMEM((2, 3, rows, wide), BF),
        dma((2, 3)),
        dma((2,)),
        dma((2, 2, n)),
        dma((2, 2, n)),
    ]


class TeamSpread:
    def __init__(self, size, own, others, send, recv):
        self.own, self.others, self.send, self.recv = own, others, send, recv
        self.count = len(own)
        me = lax.axis_index("dp")
        self.stages = []
        held, bit = 1, size // 2
        while bit:
            partner = {"dp": me + bit - 2 * bit * ((me // bit) % 2)}
            self.stages.append((held, partner))
            held, bit = 2 * held, bit // 2

    def partners(self):
        return [partner for _, partner in self.stages]

    def copies(self, stage):
        held, partner = self.stages[stage]
        for k in range(self.count):
            for b in range(held):
                yield pltpu.make_async_remote_copy(
                    src_ref=self.own[k] if b == 0 else self.others[k][b - 1],
                    dst_ref=self.others[k][held + b - 1],
                    send_sem=self.send.at[k, held + b - 1],
                    recv_sem=self.recv.at[k, held + b - 1],
                    device_id=partner,
                    device_id_type=MESH,
                )

    def start(self, stage):
        for later in range(stage, len(self.stages) if stage == 0 else min(stage + 1, len(self.stages))):
            held = self.stages[later][0]
            for k, copy in enumerate(self.copies(later)):
                if (k % held == 0) == (stage == 0):
                    copy.start()

    def arrive(self, stage):
        if stage < len(self.stages):
            for copy in self.copies(stage):
                copy.wait_recv()

    def last(self):
        for stage in range(len(self.stages)):
            for copy in self.copies(stage):
                copy.wait_send()


def spread_scratch(count, size):
    return [pltpu.SemaphoreType.DMA((count, size)), pltpu.SemaphoreType.DMA((count, size))]


def feed_forward(sizes, xs, dys, weights, before, ring_parts, reducing, ident):
    n_dp, n_fsdp, n_ctx = sizes
    n = n_fsdp * n_ctx
    team, (span, width) = len(xs), xs[0].shape
    rows, wide = width // n, weights[0][0].shape[1]
    sub = wide // 3
    pieces = [piece for group in weights for piece in group]
    counts = [len(group) for group in weights]
    tile = min(span, 256)
    per = span // tile
    steps = team * per
    part = max(rows, 128)
    half = width // 2
    gsteps = width // part
    total = 2 * steps + gsteps
    inside = team // 2 if reducing and team > 2 else 0
    carried = [] if before is None else [b[0] for b in before] + [b[1] for b in before]
    backwards = reducing

    def kernel(*refs):
        refs = list(refs)

        def take(count):
            out = refs[:count]
            del refs[:count]
            return out

        x_refs, dy_refs, piece_refs = take(team), take(team), take(len(pieces))
        old_y, old_dn = take(len(carried) // 2), take(len(carried) // 2)
        part_refs = take(2)
        y_refs, dn_refs, grad_refs, ring_outs = take(team), take(team), take(2), take(2)
        if reducing:
            near = take(max(1, inside))
            (far,) = take(1)
        wgu, wd, xb, dyb, yb, dnb, dgu, inner, xg, dyg, gout = take(11)
        w_sems, x_sems, y_sems, g_sems, gout_sems = take(5)
        if carried:
            cb, c_sems = take(2)
        if reducing:
            swap_send, swap_recv, face_send, face_recv = take(4)
            ring = RingReduce(sizes, part_refs, ring_outs, *refs)
        else:
            ring = RingGather(sizes, own_columns(n_dp, *part_refs, SUBS // 2), ring_outs, *refs)
        me = lax.axis_index("dp")
        sibling = {"dp": me + 1 - 2 * (me % 2)}
        bit = team // 2
        facing = {"dp": me + bit - 2 * bit * ((me // bit) % 2)}

        k = 0
        w_copies = []
        for b, count in enumerate(counts):
            at = 0
            for ref in piece_refs[k : k + count]:
                high = ref.shape[0]
                w_copies += [
                    pltpu.make_async_copy(
                        ref.at[:, pl.ds(0, 2 * sub)],
                        wgu.at[pl.ds(at, high), pl.ds(b * 2 * sub, 2 * sub)],
                        w_sems.at[2 * k],
                    ),
                    pltpu.make_async_copy(
                        ref.at[:, pl.ds(2 * sub, sub)],
                        wd.at[pl.ds(at, high), pl.ds(b * sub, sub)],
                        w_sems.at[2 * k + 1],
                    ),
                ]
                at += high
                k += 1
        for copy in w_copies:
            copy.start()

        def block_of(i):
            return team - 1 - i // per if backwards else i // per

        def loads(m, i):
            rows_here = pl.ds((i % per) * tile, tile)
            return [
                pltpu.make_async_copy(x_refs[m].at[rows_here], xb.at[i % 2], x_sems.at[0, i % 2]),
                pltpu.make_async_copy(dy_refs[m].at[rows_here], dyb.at[i % 2], x_sems.at[1, i % 2]),
            ]

        def more(m, i):
            if not carried:
                return []
            rows_here = pl.ds((i % per) * tile, tile)
            out = [
                pltpu.make_async_copy(old_y[m].at[rows_here], yb, c_sems.at[0]),
                pltpu.make_async_copy(old_dn[m].at[rows_here], dnb, c_sems.at[1]),
            ]
            if m < inside:
                out.append(pltpu.make_async_copy(near[m].at[rows_here], cb, c_sems.at[2]))
            return out

        def writes(m, i):
            rows_here = pl.ds((i % per) * tile, tile)
            return [
                pltpu.make_async_copy(yb, y_refs[m].at[rows_here], y_sems.at[0]),
                pltpu.make_async_copy(dnb, dn_refs[m].at[rows_here], y_sems.at[1]),
            ]

        def on_block(i, act):
            for m in range(team):

                @pl.when(block_of(i) == m)
                def _():
                    act(m)

        def swap(m):
            return pltpu.make_async_remote_copy(
                src_ref=dn_refs[m],
                dst_ref=near[m - inside],
                send_sem=swap_send.at[m - inside],
                recv_sem=swap_recv.at[m - inside],
                device_id=sibling,
                device_id_type=MESH,
            )

        def face():
            return pltpu.make_async_remote_copy(
                src_ref=dn_refs[1],
                dst_ref=far,
                send_sem=face_send,
                recv_sem=face_recv,
                device_id=facing,
                device_id_type=MESH,
            )

        def go(copies):
            for copy in copies:
                copy.start()

        def end(copies):
            for copy in copies:
                copy.wait()

        def ticks(lo, hi):
            if reducing:
                count, base, act = 2 * (n - 2), 4, ring.step
            else:
                count, base, act = n - 2, 2, ring.tick
            lax.fori_loop(
                base + lo * count // total, base + hi * count // total, lambda t, c: (act(t), c)[1], 0
            )

        on_block(0, lambda m: go(loads(m, 0)))
        partners = list(ring.partners)
        if inside:
            partners.append(sibling)
        if reducing and team > 1:
            partners.append(facing)
        greet(partners)
        ring.first()
        for copy in w_copies:
            copy.wait()

        def forward(i, carry):
            @pl.when(i + 1 < steps)
            def _():
                on_block(i + 1, lambda m: go(loads(m, i + 1)))

            @pl.when(i == steps - 1)
            def _():
                go(sides(0))

            if inside:
                @pl.when(i % per == 0)
                def _():
                    on_block(i, lambda m: swap(m + inside).wait_recv() if m < inside else None)

            ticks(2 * i, 2 * i + 2)
            end(loads(0, i))
            here = pl.ds(pl.multiple_of(i * tile, tile), tile)
            if carried:
                drained = (i > 0) & (i % per != 0) if reducing else i > 0

                @pl.when(drained)
                def _():
                    end(writes(0, i))

                on_block(i, lambda m: go(more(m, i)))
            for b in range(2):
                gate_up = dot_nn(xb[i % 2], wgu[:, b * 2 * sub : (b + 1) * 2 * sub])
                d_inner = dot_nn(dyb[i % 2], wd[:, b * sub : (b + 1) * sub])
                gate, up = gate_up[:, :sub], gate_up[:, sub:]
                sig = 1.0 / (1.0 + jnp.exp(-gate))
                act = gate * sig
                inner[here, b * sub : (b + 1) * sub] = (act * up).astype(BF)
                dgu[here, b * 2 * sub : b * 2 * sub + sub] = (
                    d_inner * up * (sig + act * (1.0 - sig))
                ).astype(BF)
                dgu[here, b * 2 * sub + sub : (b + 1) * 2 * sub] = (d_inner * act).astype(BF)
            if not carried:

                @pl.when(i > 0)
                def _():
                    end(writes(0, i))

            else:
                on_block(i, lambda m: end(more(m, i)))
            for at in range(0, width, half):
                lanes = slice(at, at + half)
                y = dot_nt(inner[here, :], wd[lanes, :])
                if carried:
                    y = y + yb[:, lanes].astype(F32)
                yb[:, lanes] = y.astype(BF)
                dn = dot_nt(dgu[here, :], wgu[lanes, :])
                if carried:
                    dn = dn + dnb[:, lanes].astype(F32)
                if inside:
                    dn = dn + jnp.where(block_of(i) < inside, cb[:, lanes].astype(F32), 0.0)
                dnb[:, lanes] = dn.astype(BF)
            on_block(i, lambda m: go(writes(m, i)))
            if reducing and team > 1:

                @pl.when(i % per == per - 1)
                def _():
                    def sent(m):
                        if m >= 1:
                            end(writes(m, i))
                            go([swap(m)] if inside and m >= inside else [face()])

                    on_block(i, sent)

            return carry

        def sides(g):
            cols = pl.ds(g * part, part) if isinstance(g, int) else pl.ds(pl.multiple_of(g * part, part), part)
            out = []
            for k in range(team):
                m = team - 1 - k if backwards else k
                at = pl.ds(k * span, span)
                out += [
                    pltpu.make_async_copy(x_refs[m].at[:, cols], xg.at[g % 2, at], g_sems.at[0, g % 2, k]),
                    pltpu.make_async_copy(dy_refs[m].at[:, cols], dyg.at[g % 2, at], g_sems.at[1, g % 2, k]),
                ]
            return out

        def keep(g):
            at = pl.ds(pl.multiple_of(g * part, part), part)
            return [pltpu.make_async_copy(gout.at[b], grad_refs[b].at[at], gout_sems.at[b]) for b in range(2)]

        def outer(g, carry):
            @pl.when(g + 1 < gsteps)
            def _():
                go(sides(g + 1))

            ticks(2 * steps + g, 2 * steps + g + 1)
            end(sides(g))

            @pl.when(g > 0)
            def _():
                end(keep(g))

            for b in range(2):
                up_down = dot_tn(xg[g % 2], dgu[:, b * 2 * sub : (b + 1) * 2 * sub])
                gout[b, :, : 2 * sub] = up_down.astype(BF)
                down = dot_tn(dyg[g % 2], inner[:, b * sub : (b + 1) * sub])
                gout[b, :, 2 * sub :] = down.astype(BF)
            go(keep(g))
            return carry

        lax.fori_loop(0, steps, forward, 0)
        lax.fori_loop(0, gsteps, outer, 0)
        end(writes(0, 0))
        end(keep(0))
        ring.last()
        if reducing and team > 1:
            for m in range(inside, team) if inside else []:
                swap(m).wait_send()
            face().wait_recv()
            face().wait_send()

    shape = lambda a, b: jax.ShapeDtypeStruct((a, b), BF)
    outs = [shape(span, width)] * (2 * team) + [shape(width, wide)] * 2
    if reducing:
        outs += [shape(rows, wide)] * 2
        outs += [shape(span, width)] * (max(1, inside) + 1)
    else:
        outs += [shape(width, wide)] * 2
    dma = pltpu.SemaphoreType.DMA
    scratch = [
        pltpu.VMEM((width, 4 * sub), BF),
        pltpu.VMEM((width, 2 * sub), BF),
        pltpu.VMEM((2, tile, width), BF),
        pltpu.VMEM((2, tile, width), BF),
        pltpu.VMEM((tile, width), BF),
        pltpu.VMEM((tile, width), BF),
        pltpu.VMEM((team * span, 4 * sub), BF),
        pltpu.VMEM((team * span, 2 * sub), BF),
        pltpu.VMEM((2, team * span, part), BF),
        pltpu.VMEM((2, team * span, part), BF),
        pltpu.VMEM((2, part, wide), BF),
        dma((2 * len(pieces),)),
        dma((2, 2)),
        dma((2,)),
        dma((2, 2, team)),
        dma((2,)),
    ]
    if carried:
        scratch += [pltpu.VMEM((tile, width) if inside else (16, 128), BF), dma((3,))]
    if reducing:
        scratch += [dma((max(1, inside),)), dma((max(1, inside),)), dma(()), dma(())]
        scratch += reduce_scratch(n, rows, wide)
    else:
        scratch += gather_scratch(n, rows, wide)
    operands = list(xs) + list(dys) + pieces + carried + list(ring_parts)
    out = pl.pallas_call(
        kernel,
        in_specs=[ANY] * len(operands),
        out_specs=[ANY] * len(outs),
        out_shape=outs,
        scratch_shapes=scratch,
        compiler_params=pltpu.CompilerParams(
            collective_id=ident, has_side_effects=True, vmem_limit_bytes=60 * MIB
        ),
        cost_estimate=cost(18 * team * span * width * 2 * sub, 40 * MIB),
    )(*operands)
    y, dn, grads, ringed = out[:team], out[team : 2 * team], out[2 * team : 2 * team + 2], out[2 * team + 2 :]
    if reducing:
        return y, (dn[0], ringed[-1]) if team > 1 else (dn[0],), grads, ringed[:2]
    return y, dn, grads, ringed[:2]


def attend_forward(sizes, x, qkv, kv_far, seen, w_out, gains, dy, w_gate_up, w_down):
    n_dp, n_fsdp, n_ctx = sizes
    n = n_fsdp * n_ctx
    span, width = x.shape
    rows = width // n
    far = kv_far.shape[0]
    blocks = far // span
    qwidth, kvwidth = HEADS * HD, KV_HEADS * HD
    near, kvpairs = qwidth // 128, kvwidth // 128
    pairs = HEADS // 2
    tile = min(span, 256)
    wide = 3 * (w_down.shape[1] // n_dp // SUBS)
    early = max(0, 3 * (n - 2) // 7)
    others = n_dp - 1
    chunk = min(512, width)

    def kernel(seen_ref, q_ref, k_ref, v_ref, kf_ref, vf_ref, x_ref, gains_ref, *refs):
        refs = list(refs)

        def take(count):
            out = refs[:count]
            del refs[:count]
            return out

        wo_ref, dy_ref, gu_ref, down_ref = take(4)
        lse_ref, scale_ref, attn_out, hidden_out, normed_out = take(5)
        x_blocks, dy_blocks, ring_outs = take(others), take(others), take(2)
        attn_v, wo_v, hidden_v, normed_v, load_sem, save_sems = take(6)
        dy_send, dy_recv, x_send, x_recv = take(4)
        ring = RingGather(sizes, own_columns(n_dp, gu_ref, down_ref, 0), ring_outs, *refs)
        dy_spread = TeamSpread(n_dp, [dy_ref], [dy_blocks], dy_send, dy_recv)
        x_spread = TeamSpread(n_dp, [normed_v], [x_blocks], x_send, x_recv)
        group = pl.program_id(0)
        mask = causal_tile(tile)
        flags = [seen_ref[k] == 1 for k in range(blocks)]
        load = pltpu.make_async_copy(wo_ref, wo_v, load_sem)

        @pl.when(group == 0)
        def _():
            greet(ring.partners + dy_spread.partners())
            ring.first()
            dy_spread.start(0)
            load.start()

        lax.fori_loop(
            2 + group * early // pairs,
            2 + (group + 1) * early // pairs,
            lambda t, c: (ring.tick(t), c)[1],
            0,
        )
        key, value = head_of(k_ref[...], group), head_of(v_ref[...], group)
        key_far, value_far = head_of(kf_ref[...], group), head_of(vf_ref[...], group)
        value_t = value.astype(F32).T.astype(BF)
        value_far_t = value_far.astype(F32).T.astype(BF)
        for head in range(2):
            down = pl.ds(pl.multiple_of(group * 128 + head * HD, HD), HD)
            for at in range(0, span, tile):
                end = at + tile
                q = q_ref[at:end, head * HD : (head + 1) * HD]
                own, other = scores_of(key[:end], key_far, q, flags, mask, span)
                peak = jnp.maximum(jnp.max(own, 0, keepdims=True), jnp.max(other, 0, keepdims=True))
                own = jnp.exp(own - peak)
                other = jnp.exp(other - peak)
                total = jnp.sum(own, 0, keepdims=True) + jnp.sum(other, 0, keepdims=True)
                scale = 1.0 / total
                result = dot_nn(value_t[:, :end], (own * scale).astype(BF)) + dot_nn(
                    value_far_t, (other * scale).astype(BF)
                )
                attn_v[down, at:end] = result.astype(BF)
                lse_ref[0, head : head + 1, at:end] = peak + jnp.log(total)

        @pl.when(group == pairs - 1)
        def _():
            saves = [
                pltpu.make_async_copy(a, b, save_sems.at[k])
                for k, (a, b) in enumerate([(attn_v, attn_out), (hidden_v, hidden_out), (normed_v, normed_out)])
            ]
            saves[0].start()
            load.wait()
            square = jnp.zeros((span, 1), F32)
            for at in range(0, width, chunk):
                lanes = slice(at, at + chunk)
                hidden = x_ref[:, lanes].astype(F32) + dot_tn(attn_v[...], wo_v[:, lanes])
                hidden_v[:, lanes] = hidden
                square = square + jnp.sum(hidden * hidden, -1, keepdims=True)
            scale = lax.rsqrt(square / width + EPS)
            scale_ref[...] = jnp.broadcast_to(scale, (span, 128))
            place, device = ring_place(n_fsdp)
            for slot in range(n):
                there = device((place + n - slot) % n)
                part = slot_lanes(hidden_v, there["fsdp"] * n_ctx + there["ctx"], rows)
                normed = part * scale * gains_ref[slot, 1:2, :].astype(F32)
                normed_v[:, slot * rows : (slot + 1) * rows] = normed.astype(BF)
            x_spread.start(0)
            saves[1].start()
            saves[2].start()
            dy_spread.arrive(0)
            dy_spread.start(1)
            middle = max(2 + early, n - 2)
            for t in range(2 + early, middle):
                ring.tick(t)
            x_spread.arrive(0)
            x_spread.start(1)
            for t in range(middle, n):
                ring.tick(t)
            dy_spread.arrive(1)
            x_spread.arrive(1)
            ring.last()
            dy_spread.last()
            x_spread.last()
            for copy in saves:
                copy.wait()

    pair = lambda high, shift: pl.BlockSpec((high, 128), lambda i: (0, i // 4 + shift))
    dma = pltpu.SemaphoreType.DMA
    block = jax.ShapeDtypeStruct((span, width), BF)
    out = pl.pallas_call(
        kernel,
        grid=(pairs,),
        in_specs=[
            pl.BlockSpec(memory_space=pltpu.SMEM),
            pl.BlockSpec((span, 128), lambda i: (0, i)),
            pair(span, near),
            pair(span, near + kvpairs),
            pair(far, 0),
            pair(far, kvpairs),
            pl.BlockSpec((span, width), lambda i: (0, 0)),
            pl.BlockSpec(gains.shape, lambda i: (0, 0, 0)),
        ]
        + [ANY] * 4,
        out_specs=[pl.BlockSpec((1, 8, span), lambda i: (i, 0, 0)), pl.BlockSpec((span, 128), lambda i: (0, 0))]
        + [ANY] * (5 + 2 * others),
        out_shape=[
            jax.ShapeDtypeStruct((pairs, 8, span), F32),
            jax.ShapeDtypeStruct((span, 128), F32),
            jax.ShapeDtypeStruct((qwidth, span), BF),
            jax.ShapeDtypeStruct((span, width), F32),
        ]
        + [block] * (1 + 2 * others)
        + [jax.ShapeDtypeStruct((width, wide), BF)] * 2,
        scratch_shapes=[
            pltpu.VMEM((qwidth, span), BF),
            pltpu.VMEM((qwidth, width), BF),
            pltpu.VMEM((span, width), F32),
            pltpu.VMEM((span, width), BF),
            dma(()),
            dma((3,)),
        ]
        + spread_scratch(1, n_dp)
        + spread_scratch(1, n_dp)
        + gather_scratch(n, rows, wide),
        compiler_params=pltpu.CompilerParams(
            collective_id=5, has_side_effects=True, vmem_limit_bytes=58 * MIB
        ),
        cost_estimate=cost(pairs * 2 * span * (span + far) * 128 * 4, 30 * MIB),
    )(seen, qkv, qkv, qkv, kv_far, kv_far, x, gains, w_out, dy, w_gate_up, w_down)
    lse, scale, attn, hidden, normed = out[:5]
    blocks = out[5 : 5 + others], out[5 + others : 5 + 2 * others]
    return attn, lse, hidden, scale[:, :1], normed, *blocks, out[5 + 2 * others :]


def attend_backward(sizes, qkv, kv_far, d_attn, lse, seen, tables, attn_t, d_proj, normed, ring_parts, sums, ident):
    n_dp, n_fsdp, n_ctx = sizes
    n = n_fsdp * n_ctx
    span, far = qkv.shape[0], kv_far.shape[0]
    blocks = far // span
    qwidth, kvwidth = HEADS * HD, KV_HEADS * HD
    near, kvpairs = qwidth // 128, kvwidth // 128
    pairs = HEADS // 2
    tile = min(span, 256)
    rows, wide = ring_parts[0].shape[0] // n, ring_parts[0].shape[1]
    early = 4 + 8 * (n - 2) // 6
    width = normed.shape[1]
    qkvwidth = qwidth + 2 * kvwidth
    part = max(rows, 128)
    others = n_dp - 1

    def kernel(seen_ref, q_ref, k_ref, v_ref, kf_ref, vf_ref, d_ref, lse_ref, cos_ref, low_ref, high_ref, *refs):
        refs = list(refs)

        def take(count):
            out = refs[:count]
            del refs[:count]
            return out

        attn_ref, proj_ref, normed_ref = take(3)
        parts, own_sums = take(2), take(2)
        dqkv_out, go_out, gq_out = take(3)
        ring_outs, blocks_out = take(2), take(2 * others)
        dqkv_v, dkv, dkv_far, give, got, save_sem, kv_send, kv_recv = take(8)
        attn_v, proj_v, normed_v, stage, load_sems, stage_sems = take(6)
        spread_send, spread_recv = take(2)
        ring = RingReduce(sizes, parts, ring_outs, *refs)
        spread = TeamSpread(
            n_dp, own_sums, [blocks_out[k * others : (k + 1) * others] for k in range(2)], spread_send, spread_recv
        )
        loads = [
            pltpu.make_async_copy(a, b, load_sems.at[k])
            for k, (a, b) in enumerate([(attn_ref, attn_v), (proj_ref, proj_v), (normed_ref, normed_v)])
        ]

        def product(out, cols, make):
            def write(g):
                return pltpu.make_async_copy(
                    stage.at[g % 2, :, pl.ds(0, cols)],
                    out.at[pl.ds(pl.multiple_of(g * part, part), part)],
                    stage_sems.at[g % 2],
                )

            def body(g, carry):
                @pl.when(g >= 2)
                def _():
                    write(g - 2).wait()

                stage[g % 2, :, :cols] = make(pl.ds(pl.multiple_of(g * part, part), part)).astype(BF)
                write(g).start()
                return carry

            count = width // part
            lax.fori_loop(0, count, body, 0)
            for g in range(max(0, count - 2), count):
                write(g).wait()

        ctx = lax.axis_index("ctx")
        group = pl.program_id(0)
        mask = causal_tile(tile)
        flags = [seen_ref[k] == 1 for k in range(blocks)]
        key, value = head_of(k_ref[...], group), head_of(v_ref[...], group)
        key_far, value_far = head_of(kf_ref[...], group), head_of(vf_ref[...], group)
        key_t = key.astype(F32).T.astype(BF)
        key_far_t = key_far.astype(F32).T.astype(BF)
        odd = (group // 2) % 2 == 1
        cosine, low, high = cos_ref[...], -low_ref[...], -high_ref[...]

        @pl.when(group == 0)
        def _():
            greet(ring.partners + [{"ctx": (ctx + k) % n_ctx} for k in range(1, n_ctx)] + spread.partners())
            ring.first()
            spread.start(0)
            for copy in loads:
                copy.start()
            dkv[...] = jnp.zeros_like(dkv)
            dkv_far[...] = jnp.zeros_like(dkv_far)

        lax.fori_loop(
            4 + group * (early - 4) // pairs,
            4 + (group + 1) * (early - 4) // pairs,
            lambda u, c: (ring.step(u), c)[1],
            0,
        )

        def put(ref, size, shift, add):
            zero = jnp.zeros_like(add)
            lanes = pl.ds(pl.multiple_of(group // 4 * 128 + shift, 128), 128)
            ref[0:size, lanes] += jnp.concatenate([jnp.where(odd, zero, add), jnp.where(odd, add, zero)], 1)

        for at in range(0, span, tile):
            end = at + tile
            turned = []
            for head in range(2):
                lanes = slice(head * HD, (head + 1) * HD)
                q = q_ref[at:end, lanes]
                d = d_ref[at:end, lanes]
                own, other = scores_of(key[:end], key_far, q, flags, mask, span)
                base = lse_ref[0, head : head + 1, at:end]
                own = jnp.exp(own - base)
                other = jnp.exp(other - base)
                d_own = dot_nt(value[:end], d)
                d_other = dot_nt(value_far, d)
                delta = jnp.sum(own * d_own, 0, keepdims=True) + jnp.sum(other * d_other, 0, keepdims=True)
                ds_own = (own * (d_own - delta)).astype(BF)
                ds_other = (other * (d_other - delta)).astype(BF)
                put(dkv, end, kvwidth, dot_nn(own.astype(BF), d))
                put(dkv_far, far, kvwidth, dot_nn(other.astype(BF), d))
                put(dkv, end, 0, dot_nn(ds_own, q))
                put(dkv_far, far, 0, dot_nn(ds_other, q))
                turned.append(dot_nn(key_t[:, :end], ds_own) + dot_nn(key_far_t, ds_other))
            d_query = jnp.concatenate(turned, 0).T * HD**-0.5
            dqkv_v[at:end, pl.ds(pl.multiple_of(group * 128, 128), 128)] = turn(
                d_query, cosine[at:end], low[at:end], high[at:end]
            ).astype(BF)

        @pl.when(group == pairs - 1)
        def _():
            give[...] = dkv_far[...].astype(BF)

            def back(k):
                return pltpu.make_async_remote_copy(
                    src_ref=give.at[pl.ds((k - 1) * span, span)],
                    dst_ref=got.at[k - 1],
                    send_sem=kv_send.at[k],
                    recv_sem=kv_recv.at[k],
                    device_id={"ctx": (ctx + k) % n_ctx},
                    device_id_type=MESH,
                )

            for k in range(1, n_ctx):
                back(k).start()
            for copy in loads:
                copy.wait()
            ring.step(early)
            product(go_out, qwidth, lambda at: dot_nn(attn_v[at, :], proj_v[...]))
            ring.step(early + 1)
            for k in range(1, n_ctx):
                back(k).wait_recv()
            for at in range(0, 2 * kvwidth, 128):
                piece = dkv[:, at : at + 128]
                for k in range(1, n_ctx):
                    piece = piece + got[k - 1, :, at : at + 128].astype(F32)
                if at < kvwidth:
                    piece = turn(piece, cosine, low, high)
                dqkv_v[:, qwidth + at : qwidth + at + 128] = piece.astype(BF)
            save = pltpu.make_async_copy(dqkv_v, dqkv_out, save_sem)
            save.start()
            lax.fori_loop(early + 2, 2 * n, lambda u, c: (ring.step(u), c)[1], 0)
            spread.arrive(0)
            spread.start(1)
            product(gq_out, qkvwidth, lambda at: dot_tn(normed_v[:, at], dqkv_v[...]))
            spread.arrive(1)
            ring.last()
            spread.last()
            for k in range(1, n_ctx):
                back(k).wait_send()
            save.wait()

    pair = lambda high, shift: pl.BlockSpec((high, 128), lambda i: (0, i // 4 + shift))
    wide_block = pl.BlockSpec((span, 128), lambda i: (0, i))
    table = pl.BlockSpec((span, 128), lambda i: (0, 0))
    dma = pltpu.SemaphoreType.DMA
    out = pl.pallas_call(
        kernel,
        grid=(pairs,),
        in_specs=[
            pl.BlockSpec(memory_space=pltpu.SMEM),
            wide_block,
            pair(span, near),
            pair(span, near + kvpairs),
            pair(far, 0),
            pair(far, kvpairs),
            wide_block,
            pl.BlockSpec((1, 8, span), lambda i: (i, 0, 0)),
            table,
            table,
            table,
        ]
        + [ANY] * 7,
        out_specs=[ANY] * (5 + 2 * others),
        out_shape=[
            jax.ShapeDtypeStruct((span, qkvwidth), BF),
            jax.ShapeDtypeStruct((width, qwidth), BF),
            jax.ShapeDtypeStruct((width, qkvwidth), BF),
        ]
        + [jax.ShapeDtypeStruct((rows, wide), BF)] * (2 + 2 * others),
        scratch_shapes=[
            pltpu.VMEM((span, qwidth + 2 * kvwidth), BF),
            pltpu.VMEM((span, 2 * kvwidth), F32),
            pltpu.VMEM((far, 2 * kvwidth), F32),
            pltpu.VMEM((far, 2 * kvwidth), BF),
            pltpu.VMEM((n_ctx - 1, span, 2 * kvwidth), BF),
            dma(()),
            dma((n_ctx,)),
            dma((n_ctx,)),
            pltpu.VMEM(attn_t.shape, BF),
            pltpu.VMEM(d_proj.shape, BF),
            pltpu.VMEM(normed.shape, BF),
            pltpu.VMEM((2, part, max(qwidth, qkvwidth)), BF),
            dma((3,)),
            dma((2,)),
        ]
        + spread_scratch(2, n_dp)
        + reduce_scratch(n, rows, wide),
        compiler_params=pltpu.CompilerParams(
            collective_id=ident, has_side_effects=True, vmem_limit_bytes=58 * MIB
        ),
        cost_estimate=cost(pairs * 2 * span * (span + far) * 128 * 10, 30 * MIB),
    )(seen, qkv, qkv, qkv, kv_far, kv_far, d_attn, lse, *tables, attn_t, d_proj, normed, *ring_parts, *sums)
    return out[0], out[1], out[2], out[3:5], [out[5 + k * others : 5 + (k + 1) * others] for k in range(2)]


def opening(sizes, x, dy, w_qkv, w_out, gains, tables):
    n_dp, n_fsdp, n_ctx = sizes
    n = n_fsdp * n_ctx
    span, width = x.shape
    rows = width // n
    share, half = w_qkv.shape[1] // n_dp, w_out.shape[1] // 2
    qwidth, kvwidth = HEADS * HD, KV_HEADS * HD
    qkvwidth = qwidth + 2 * kvwidth
    chunk = share // 2 if share % 256 == 0 else share
    across_x = n_dp > 2

    def kernel(x_ref, dy_ref, wq_ref, wo_ref, g_ref, cos_ref, low_ref, high_ref, *refs):
        refs = list(refs)

        def take(count):
            out = refs[:count]
            del refs[:count]
            return out

        qkv_out, far_out, xs_out, wq_out, wo_out, gains_out, dy_out = take(7)
        qkv_v, far_v, xs_v, dy_v = take(4)
        wq_v = take(n_dp)
        om_v, oo_v, gains_v = take(3)
        load_sems, save_sems, wq_sems, wo_sems = take(4)
        send, recv, x_send, x_recv, c_send, c_recv, o_send, o_recv = take(8)
        gain_send, gain_recv, kv_send, kv_recv = take(4)
        me = lax.axis_index("dp")
        core = me % 2
        sibling = {"dp": team_place(n_dp, me, 1)}
        facing = {"dp": team_place(n_dp, me, n_dp // 2)}
        bases = [me, team_place(n_dp, me, n_dp // 2)] if across_x else [me]
        bases = [b * share for b in bases + [team_place(n_dp, b, 1) for b in bases]]
        held = n_dp // 2
        place, device = ring_place(n_fsdp)
        ahead, behind = device((place + 1) % n), device((place + n - 1) % n)
        mine = (wq_v[0], om_v)
        widths = (share, half)

        def block_of(slot):
            there = device((place + n - slot) % n)
            return there["fsdp"] * n_ctx + there["ctx"]

        loads = [
            pltpu.make_async_copy(
                ref.at[:, pl.ds(pl.multiple_of(at, 128), w)], mine[k].at[pl.ds(0, rows)], load_sems.at[k]
            )
            for k, (ref, at, w) in enumerate(((wq_ref, me * share, share), (wo_ref, core * half, half)))
        ] + [pltpu.make_async_copy(g_ref, gains_v.at[0], load_sems.at[2])]
        for copy in loads:
            copy.start()
        ctx = lax.axis_index("ctx")
        greet(
            [ahead, behind, sibling]
            + ([facing] if across_x else [])
            + [{"ctx": (ctx + k) % n_ctx} for k in range(1, n_ctx)]
        )

        def lanes(k, way):
            return pl.ds(way * (widths[k] // 2), widths[k] // 2)

        def remote(source, target, send_sem, recv_sem, partner):
            return pltpu.make_async_remote_copy(
                src_ref=source,
                dst_ref=target,
                send_sem=send_sem,
                recv_sem=recv_sem,
                device_id=partner,
                device_id_type=MESH,
            )

        def step(k, way, t):
            here = t - 1 if way == 0 else (n - t + 1) % n
            there = t if way == 0 else n - t
            return remote(
                mine[k].at[pl.ds(here * rows, rows), lanes(k, way)],
                mine[k].at[pl.ds(there * rows, rows), lanes(k, way)],
                send.at[k, way, t],
                recv.at[k, way, t],
                ahead if way == 0 else behind,
            )

        def over_x(way, slot):
            at = (pl.ds(slot * rows, rows), lanes(0, way))
            return remote(wq_v[0].at[at], wq_v[1].at[at], x_send.at[way, slot], x_recv.at[way, slot], facing)

        def over_core(b, way, slot):
            at = (pl.ds(slot * rows, rows), lanes(0, way))
            return remote(
                wq_v[b].at[at], wq_v[held + b].at[at], c_send.at[b, way, slot], c_recv.at[b, way, slot], sibling
            )

        def out_over(way, slot):
            at = (pl.ds(slot * rows, rows), lanes(1, way))
            return remote(om_v.at[at], oo_v.at[at], o_send.at[way, slot], o_recv.at[way, slot], sibling)

        def gain_step(t):
            return remote(gains_v.at[t - 1], gains_v.at[t], gain_send.at[t], gain_recv.at[t], ahead)

        def kv_step(k):
            return remote(
                qkv_v.at[:, pl.ds(qwidth, 2 * kvwidth)],
                far_v.at[pl.ds((k - 1) * span, span)],
                kv_send.at[k],
                kv_recv.at[k],
                {"ctx": (ctx + n_ctx - k) % n_ctx},
            )

        def give(way, slot):
            if across_x:
                over_x(way, slot).start()
            over_core(0, way, slot).start()

        f32 = x_ref[...].astype(F32)
        scale = lax.rsqrt(jnp.mean(f32 * f32, -1, keepdims=True) + EPS)

        def normalize(slot):
            part = slot_lanes(x_ref, block_of(slot), rows)
            xs_v[:, slot * rows : (slot + 1) * rows] = (
                part * scale * gains_v[slot, 0:1, :].astype(F32)
            ).astype(BF)
            dy_v[:, slot * rows : (slot + 1) * rows] = slot_lanes(dy_ref, block_of(slot), rows).astype(BF)

        loads[0].wait()
        loads[2].wait()
        gain_step(1).start()
        for way in range(2):
            step(0, way, 1).start()
        loads[1].wait()
        for way in range(2):
            give(way, 0)
        normalize(0)
        for t in range(1, n):
            gain_step(t).wait_recv()
            if t < n - 1:
                gain_step(t + 1).start()
            for way in range(2):
                step(0, way, t).wait_recv()
                if t < n - 1:
                    step(0, way, t + 1).start()
                give(way, t if way == 0 else n - t)
            normalize(t)

        for way in range(2):
            step(1, way, 1).start()
            out_over(way, 0).start()

        def out_tick(t):
            for way in range(2):
                step(1, way, t).wait_recv()
                if t < n - 1:
                    step(1, way, t + 1).start()
                out_over(way, t if way == 0 else n - t).start()

        order = [(way, 0) for way in range(2)]
        for t in range(1, n):
            order += [(0, t), (1, n - t)]
        cosine, low, high = cos_ref[...], low_ref[...], high_ref[...]

        def form(b, at):
            value = dot_nn(xs_v[...], wq_v[b][:, at : at + chunk])
            for part in range(0, chunk, 128):
                piece = value[:, part : part + 128]
                here = bases[b] + at + part
                piece = jnp.where(here >= qwidth + kvwidth, piece, turn(piece, cosine, low, high))
                piece = piece * jnp.where(here < qwidth, HD**-0.5, 1.0)
                qkv_v[:, pl.ds(pl.multiple_of(here, 128), 128)] = piece.astype(BF)

        def save_share(b):
            return [
                pltpu.make_async_copy(
                    wq_v[b].at[pl.ds(slot * rows, rows)],
                    wq_out.at[
                        pl.ds(pl.multiple_of(block_of(slot) * rows, rows), rows),
                        pl.ds(pl.multiple_of(bases[b], 128), share),
                    ],
                    wq_sems.at[b, slot],
                )
                for slot in range(n)
            ]

        def save_half(k):
            whose = core if k == 0 else 1 - core
            return [
                pltpu.make_async_copy(
                    (om_v, oo_v)[k].at[pl.ds(slot * rows, rows)],
                    wo_out.at[
                        pl.ds(pl.multiple_of(block_of(slot) * rows, rows), rows),
                        pl.ds(pl.multiple_of(whose * half, 128), half),
                    ],
                    wo_sems.at[k, slot],
                )
                for slot in range(n)
            ]

        def go(copies):
            for copy in copies:
                copy.start()

        jobs = [lambda at=at: form(0, at) for at in range(0, share, chunk)]
        jobs.append(lambda: go(save_share(0)))

        def core_shares(b):
            for way, slot in order:
                over_core(b, way, slot).wait_recv()
            go(save_share(held + b))

        jobs.append(lambda: core_shares(0))
        jobs += [lambda at=at: form(held, at) for at in range(0, share, chunk)]
        if across_x:

            def relay(way, slot):
                over_x(way, slot).wait_recv()
                over_core(1, way, slot).start()

            jobs += [lambda w=way, k=slot: relay(w, k) for way, slot in order]
            jobs.append(lambda: go(save_share(1)))
            jobs += [lambda at=at: form(1, at) for at in range(0, share, chunk)]
            jobs.append(lambda: core_shares(1))
            jobs += [lambda at=at: form(held + 1, at) for at in range(0, share, chunk)]
        for k, job in enumerate(jobs):
            job()
            for t in range(1 + k * (n - 1) // len(jobs), 1 + (k + 1) * (n - 1) // len(jobs)):
                out_tick(t)
        for j in range(1, n_ctx):
            kv_step(j).start()
        saves = [
            pltpu.make_async_copy(a, b, save_sems.at[k])
            for k, (a, b) in enumerate(
                [(qkv_v, qkv_out), (far_v, far_out), (xs_v, xs_out), (gains_v, gains_out), (dy_v, dy_out)]
            )
        ]
        for k in (0, 2, 3, 4):
            saves[k].start()
        go(save_half(0))
        for way, slot in order:
            out_over(way, slot).wait_recv()
        go(save_half(1))
        for j in range(1, n_ctx):
            kv_step(j).wait_recv()
        saves[1].start()
        for t in range(1, n):
            gain_step(t).wait_send()
            for way in range(2):
                for k in range(2):
                    step(k, way, t).wait_send()
        for way, slot in order:
            out_over(way, slot).wait_send()
            for b in range(held):
                over_core(b, way, slot).wait_send()
            if across_x:
                over_x(way, slot).wait_send()
        for j in range(1, n_ctx):
            kv_step(j).wait_send()
        for copies in [save_share(b) for b in range(n_dp)] + [save_half(k) for k in range(2)] + [saves]:
            for copy in copies:
                copy.wait()

    dma = pltpu.SemaphoreType.DMA
    shapes = [
        (span, qkvwidth),
        ((n_ctx - 1) * span, 2 * kvwidth),
        (span, width),
        (width, qkvwidth),
        (width, 2 * half),
        (n, 16, rows),
        (span, width),
    ]
    return pl.pallas_call(
        kernel,
        in_specs=[WHOLE, WHOLE, ANY, ANY, ANY, WHOLE, WHOLE, WHOLE],
        out_specs=[ANY] * 7,
        out_shape=[jax.ShapeDtypeStruct(shape, BF) for shape in shapes],
        scratch_shapes=[pltpu.VMEM(shape, BF) for shape in shapes[:3] + shapes[6:]]
        + [pltpu.VMEM((width, share), BF)] * n_dp
        + [pltpu.VMEM((width, half), BF)] * 2
        + [pltpu.VMEM((n, 16, rows), BF)]
        + [
            dma((3,)),
            dma((5,)),
            dma((n_dp, n)),
            dma((2, n)),
            dma((2, 2, n)),
            dma((2, 2, n)),
            dma((2, n)),
            dma((2, n)),
            dma((n_dp // 2, 2, n)),
            dma((n_dp // 2, 2, n)),
            dma((2, n)),
            dma((2, n)),
            dma((n,)),
            dma((n,)),
            dma((n_ctx,)),
            dma((n_ctx,)),
        ],
        compiler_params=pltpu.CompilerParams(
            collective_id=0, has_side_effects=True, vmem_limit_bytes=56 * MIB
        ),
        cost_estimate=cost(2 * span * width * qkvwidth, 4 * width * qkvwidth),
    )(x, dy, w_qkv, w_out, gains, *tables)


def closing(sizes, part_qkv, part_out, sums, d_qkv, w_qkv, x, gain, d_gain):
    n_dp, n_fsdp, n_ctx = sizes
    n = n_fsdp * n_ctx
    span, width = x.shape
    mine = width // n
    rows, widths, kinds = [mine, 8], [part_qkv.shape[1] // 2, max(mine, 256)], [BF, F32]
    count = 2
    outwidth = part_out.shape[1]
    split = n_dp > 2
    quarter = outwidth // n_dp
    chunk = min(512, width)
    parts = width // chunk
    bits = [1 << k for k in range(1, n_dp.bit_length() - 1)]
    others = n_dp - 1

    def kernel(*refs):
        refs = list(refs)

        def take(size):
            out = refs[:size]
            del refs[:size]
            return out

        full, (out_ref,), own_sums = take(1), take(1), take(len(sums))
        dq_ref, w_ref, x_ref, gain_ref, d_gain_ref = take(5)
        outs, (wo_out,) = take(count), take(1)
        blocks_out, (input_out,) = take(len(sums) * others), take(1)
        gain_v, both_v, d_v, w_v, dn_v, w_sem, d_sem, dn_sem = take(8)
        full = full + [gain_v]
        near, land, done, extra, back = take(count), take(count), take(count), take(count), take(count)
        own = take(count)
        (own_sems,) = take(1)
        o_own, o_near, o_x, o_land, o_done = take(5)
        o_blocks = take(others)
        o_load, o_swap_send, o_swap_recv, o_x_send, o_x_recv, o_send, o_recv, o_end_send, o_end_recv = take(9)
        send, recv, pair_send, pair_recv, x_send, x_recv, end_send, end_recv = take(8)
        spread = TeamSpread(
            n_dp, own_sums, [blocks_out[k * others : (k + 1) * others] for k in range(len(sums))], *refs
        )
        me = lax.axis_index("dp")
        core = me % 2
        sibling = {"dp": me + 1 - 2 * core}
        place, device = ring_place(n_fsdp)
        ahead, behind = device((place + 1) % n), device((place + n - 1) % n)
        facing = [{"dp": me + bit - 2 * bit * ((me // bit) % 2)} for bit in bits]
        greet([ahead, behind, sibling] + facing)

        def half(g, way):
            return pl.ds(way * (widths[g] // 2), widths[g] // 2)

        def half_of(g, way, whose):
            base = whose * widths[g] + way * (widths[g] // 2)
            return pl.ds(pl.multiple_of(base, 128), widths[g] // 2)

        def at(g, slot):
            return pl.ds(slot * rows[g], rows[g])

        def swap(g, way, slot):
            return pltpu.make_async_remote_copy(
                src_ref=full[g].at[at(g, slot), half_of(g, way, 1 - core)],
                dst_ref=near[g].at[at(g, slot), half(g, way)],
                send_sem=pair_send.at[g, way, slot],
                recv_sem=pair_recv.at[g, way, slot],
                device_id=sibling,
                device_id_type=MESH,
            )

        def step(g, way, t):
            slot = t if way == 0 else n - t
            source = near[g].at[at(g, slot), half(g, way)] if t == 1 else land[g].at[way, t - 2]
            return pltpu.make_async_remote_copy(
                src_ref=source,
                dst_ref=land[g].at[way, t - 1],
                send_sem=send.at[g, way, t],
                recv_sem=recv.at[g, way, t],
                device_id=ahead if way == 0 else behind,
                device_id_type=MESH,
            )

        def face(g, k):
            return pltpu.make_async_remote_copy(
                src_ref=done[g].at[k],
                dst_ref=extra[g].at[k],
                send_sem=x_send.at[g, k],
                recv_sem=x_recv.at[g, k],
                device_id=facing[k],
                device_id_type=MESH,
            )

        def end(g):
            return pltpu.make_async_remote_copy(
                src_ref=done[g].at[len(bits)],
                dst_ref=back[g],
                send_sem=end_send.at[g],
                recv_sem=end_recv.at[g],
                device_id=sibling,
                device_id_type=MESH,
            )

        def own_load(g, way, t):
            slot = t % n if way == 0 else n - t
            return pltpu.make_async_copy(
                full[g].at[at(g, slot), half_of(g, way, core)],
                own[g].at[way, t % 2],
                own_sems.at[g, way, t % 2],
            )

        def both(g, way, t, slot):
            own_load(g, way, t).wait()
            swap(g, way, slot).wait_recv()
            return own[g][way, t % 2].astype(F32) + near[g][at(g, slot), half(g, way)].astype(F32)

        def forward(g, t):
            for way in range(2):
                slot = t if way == 0 else n - t
                value = both(g, way, t, slot)
                if t == 1:
                    near[g][at(g, slot), half(g, way)] = value.astype(kinds[g])
                else:
                    step(g, way, t - 1).wait_recv()
                    land[g][way, t - 2] = (value + land[g][way, t - 2].astype(F32)).astype(kinds[g])
                step(g, way, t).start()
                own_load(g, way, t + 1).start()

        def finish(g):
            for way in range(2):
                value = both(g, way, n, 0)
                step(g, way, n - 1).wait_recv()
                done[g][0, :, half(g, way)] = (value + land[g][way, n - 2].astype(F32)).astype(kinds[g])
            if bits:
                face(g, 0).start()

        w_load = pltpu.make_async_copy(w_ref, w_v, w_sem)
        d_load = pltpu.make_async_copy(dq_ref, d_v, d_sem)
        dn_save = pltpu.make_async_copy(dn_v, input_out, dn_sem)

        def begin(g):
            for way in range(2):
                own_load(g, way, 1).start()

        def swaps(g, t):
            swap(g, 0, t % n).start()
            swap(g, 1, n - t).start()

        def product(k):
            lanes = slice(k * chunk, (k + 1) * chunk)
            dn_v[:, lanes] = dot_nt(d_v[...], w_v[lanes, :])

        def norm():
            square = jnp.zeros((span, 1), F32)
            for k in range(parts):
                value = x_ref[:, k * chunk : (k + 1) * chunk].astype(F32)
                square = square + jnp.sum(value * value, -1, keepdims=True)
            scale = lax.rsqrt(square / width + EPS)
            inner = jnp.zeros((span, 1), F32)
            for k in range(parts):
                lanes = slice(k * chunk, (k + 1) * chunk)
                unit = x_ref[:, lanes].astype(F32) * scale
                product = dn_v[:, lanes] * unit
                both_v[1:2, lanes] = jnp.sum(product, 0, keepdims=True)
                inner = inner + jnp.sum(product * gain_ref[0:1, lanes], -1, keepdims=True)
            inner = inner / width
            for k in range(parts):
                lanes = slice(k * chunk, (k + 1) * chunk)
                unit = x_ref[:, lanes].astype(F32) * scale
                dn_v[:, lanes] = scale * (dn_v[:, lanes] * gain_ref[0:1, lanes] - unit * inner)
            dn_save.start()
            gain_v[...] = jnp.zeros_like(gain_v)
            both_v[0:1, :] = d_gain_ref[0:1, :]
            both_v[2:8, :] = jnp.zeros((6, width), F32)
            for slot in range(n):
                there = device((place + n - slot) % n)
                pair = slot_lanes(both_v, there["fsdp"] * n_ctx + there["ctx"], mine)
                gain_v[slot * 8 : slot * 8 + 1, :mine] = pair[1:2]
                gain_v[slot * 8 : slot * 8 + 1, widths[-1] : widths[-1] + mine] = pair[0:1]

        side = me // 2 if split else 0
        across = {"dp": team_place(n_dp, me, n_dp // 2)}
        ends = TeamSpread(n_dp, [o_done], [o_blocks], o_end_send, o_end_recv)

        def natural(slot):
            there = device((place + n - slot) % n)
            return pl.ds(pl.multiple_of((there["fsdp"] * n_ctx + there["ctx"]) * mine, mine), mine)

        def quarter_of(whose, which):
            return pl.ds(pl.multiple_of(whose * (outwidth // 2) + which * quarter, 128), quarter)

        def piece(which):
            return pl.ds(pl.multiple_of(which * quarter, 128), quarter)

        def o_half(way):
            return pl.ds(way * (quarter // 2), quarter // 2)

        def out_load(slot):
            return pltpu.make_async_copy(
                out_ref.at[natural(slot), pl.ds(pl.multiple_of(core * (outwidth // 2), 128), outwidth // 2)],
                o_own.at[slot],
                o_load.at[slot],
            )

        def out_swap(slot, which):
            return pltpu.make_async_remote_copy(
                src_ref=out_ref.at[natural(slot), quarter_of(1 - core, which)],
                dst_ref=o_near.at[slot, :, piece(which)],
                send_sem=o_swap_send.at[slot, which],
                recv_sem=o_swap_recv.at[slot, which],
                device_id=sibling,
                device_id_type=MESH,
            )

        def out_across(slot):
            return pltpu.make_async_remote_copy(
                src_ref=o_near.at[slot, :, piece(1 - side)],
                dst_ref=o_x.at[slot],
                send_sem=o_x_send.at[slot],
                recv_sem=o_x_recv.at[slot],
                device_id=across,
                device_id_type=MESH,
            )

        def out_step(way, t):
            slot = t if way == 0 else n - t
            return pltpu.make_async_remote_copy(
                src_ref=o_x.at[slot, :, o_half(way)] if t == 1 else o_land.at[way, t - 2],
                dst_ref=o_land.at[way, t - 1],
                send_sem=o_send.at[way, t],
                recv_sem=o_recv.at[way, t],
                device_id=ahead if way == 0 else behind,
                device_id_type=MESH,
            )

        def out_pair(slot):
            out_load(slot).wait()
            for which in range(2 if split else 1):
                out_swap(slot, which).wait_recv()
            total = o_own[slot].astype(F32) + o_near[slot].astype(F32)
            o_near[slot] = total.astype(BF)
            if split:
                out_across(slot).start()

        def out_quarter(slot):
            here = o_near[slot, :, piece(side)].astype(F32)
            if split:
                out_across(slot).wait_recv()
                here = here + o_x[slot].astype(F32)
            o_x[slot] = here.astype(BF)

        def out_forward(t):
            for slot in sorted({t, n - t}):
                if min(slot, n - slot) == t:
                    out_quarter(slot)
            for way in range(2):
                slot = t if way == 0 else n - t
                if t > 1:
                    out_step(way, t - 1).wait_recv()
                    value = o_x[slot, :, o_half(way)].astype(F32) + o_land[way, t - 2].astype(F32)
                    o_land[way, t - 2] = value.astype(BF)
                out_step(way, t).start()

        def out_finish():
            out_quarter(0)
            for way in range(2):
                out_step(way, n - 1).wait_recv()
                value = o_x[0, :, o_half(way)].astype(F32) + o_land[way, n - 2].astype(F32)
                o_done[:, o_half(way)] = value.astype(BF)
            ends.start(0)

        gains = 1
        d_load.start()
        w_load.start()
        begin(0)
        slots = []
        for t in range(1, n // 2 + 1):
            slots += [t] if 2 * t == n else [t, n - t]
        slots.append(0)
        for slot in slots:
            out_load(slot).start()
        for t in range(1, n + 1):
            swaps(0, t)
            for slot in slots[t - 1 : t]:
                for which in range(2 if split else 1):
                    out_swap(slot, which).start()
        jobs = [lambda k=k: product(k) for k in range(parts)] + [norm]

        def open_gains():
            begin(gains)
            for t in range(1, n + 1):
                swaps(gains, t)

        jobs.append(open_gains)
        half_way = n // 2
        small = []
        for t in range(1, n):
            small.append(lambda t=t: forward(gains, t))
            if t % 2 == 0 or n <= 4:
                small.append(lambda t=t: out_forward(t // 2 if n > 4 else t))
        for t in range(1, n):
            forward(0, t)
            if t == 1:
                d_load.wait()
                w_load.wait()
            if t <= half_way:
                for slot in slots[(t - 1) * n // half_way : t * n // half_way]:
                    out_pair(slot)
                for job in jobs[(t - 1) * len(jobs) // half_way : t * len(jobs) // half_way]:
                    job()
                if t == half_way:
                    spread.start(0)
            else:
                left, k = n - 1 - half_way, t - half_way - 1
                for job in small[k * len(small) // left : (k + 1) * len(small) // left]:
                    job()
        finish(0)
        for t in range((n - 1) // 2 + 1 if n > 4 else n, n):
            out_forward(t)
        finish(gains)
        out_finish()
        spread.arrive(0)
        spread.start(1)
        ends.arrive(0)
        ends.start(1)
        for k in range(len(bits)):
            for g in range(count):
                face(g, k).wait_recv()
                done[g][k + 1] = (done[g][k].astype(F32) + extra[g][k].astype(F32)).astype(kinds[g])
                if k + 1 < len(bits):
                    face(g, k + 1).start()
        for g in range(count):
            end(g).start()
            here = pl.ds(pl.multiple_of(core * widths[g], 128), widths[g])
            outs[g][:, here] = done[g][len(bits)].astype(F32)
        for g in range(count):
            end(g).wait_recv()
            here = pl.ds(pl.multiple_of((1 - core) * widths[g], 128), widths[g])
            outs[g][:, here] = back[g][...].astype(F32)
        ends.arrive(1)
        bases = [core * (outwidth // 2) + side * quarter]
        if split:
            bases.append(core * (outwidth // 2) + (1 - side) * quarter)
        bases += [b + (1 - 2 * core) * (outwidth // 2) for b in bases]
        for base, ref in zip(bases, [o_done] + list(o_blocks)):
            wo_out[:, pl.ds(pl.multiple_of(base, 128), quarter)] = ref[...].astype(F32)
        ends.last()
        for slot in range(n):
            for which in range(2 if split else 1):
                out_swap(slot, which).wait_send()
            if split:
                out_across(slot).wait_send()
        for way in range(2):
            for t in range(1, n):
                out_step(way, t).wait_send()
        spread.arrive(1)
        spread.last()
        dn_save.wait()
        for g in range(count):
            end(g).wait_send()
            for k in range(len(bits)):
                face(g, k).wait_send()
            for way in range(2):
                for t in range(1, n):
                    step(g, way, t).wait_send()
                for slot in range(n):
                    swap(g, way, slot).wait_send()

    dma = pltpu.SemaphoreType.DMA
    groups = list(zip(rows, widths, kinds))
    out = pl.pallas_call(
        kernel,
        in_specs=[ANY] * (2 + len(sums) + 2) + [WHOLE] * 3,
        out_specs=[WHOLE] * (count + 1) + [ANY] * (len(sums) * others + 1),
        out_shape=[jax.ShapeDtypeStruct((r, 2 * w), F32) for r, w, _ in groups]
        + [jax.ShapeDtypeStruct((mine, outwidth), F32)]
        + [jax.ShapeDtypeStruct(a.shape, BF) for a in sums for _ in range(others)]
        + [jax.ShapeDtypeStruct((span, width), F32)],
        scratch_shapes=[
            pltpu.VMEM((n * 8, 2 * widths[-1]), F32),
            pltpu.VMEM((8, width), F32),
            pltpu.VMEM(d_qkv.shape, BF),
            pltpu.VMEM(w_qkv.shape, BF),
            pltpu.VMEM((span, width), F32),
            dma(()),
            dma(()),
            dma(()),
        ]
        + [pltpu.VMEM((n * r, w), kind) for r, w, kind in groups]
        + [pltpu.VMEM((2, n - 1, r, w // 2), kind) for r, w, kind in groups]
        + [pltpu.VMEM((len(bits) + 1, r, w), kind) for r, w, kind in groups]
        + [pltpu.VMEM((max(1, len(bits)), r, w), kind) for r, w, kind in groups]
        + [pltpu.VMEM((r, w), kind) for r, w, kind in groups]
        + [pltpu.VMEM((2, 2, r, w // 2), kind) for r, w, kind in groups]
        + [
            dma((count, 2, 2)),
            pltpu.VMEM((n, mine, outwidth // 2), BF),
            pltpu.VMEM((n, mine, outwidth // 2), BF),
            pltpu.VMEM((n, mine, quarter), BF),
            pltpu.VMEM((2, n - 1, mine, quarter // 2), BF),
            pltpu.VMEM((mine, quarter), BF),
        ]
        + [pltpu.VMEM((mine, quarter), BF)] * others
        + [
            dma((n,)),
            dma((n, 2)),
            dma((n, 2)),
            dma((n,)),
            dma((n,)),
            dma((2, n)),
            dma((2, n)),
        ]
        + spread_scratch(1, n_dp)
        + [
            dma((count, 2, n)),
            dma((count, 2, n)),
            dma((count, 2, n)),
            dma((count, 2, n)),
            dma((count, max(1, len(bits)))),
            dma((count, max(1, len(bits)))),
            dma((count,)),
            dma((count,)),
        ]
        + spread_scratch(len(sums), n_dp),
        compiler_params=pltpu.CompilerParams(
            collective_id=1, has_side_effects=True, vmem_limit_bytes=58 * MIB
        ),
        cost_estimate=cost(0, sum(12 * n * r * w for r, w, _ in groups)),
    )(part_qkv, part_out, *sums, d_qkv, w_qkv, x, gain, d_gain)
    blocks = [out[3 + k * others : 3 + (k + 1) * others] for k in range(len(sums))]
    return out[0], out[2], out[1], blocks, out[-1]


class Ring:
    def __init__(self, n_fsdp, n_ctx):
        order = []
        for c in range(n_ctx):
            rows = range(n_fsdp) if c % 2 == 0 else reversed(range(n_fsdp))
            order += [f * n_ctx + c for f in rows]
        self.order = order
        self.size = n = len(order)
        place = [0] * n
        for k, block in enumerate(order):
            place[block] = k
        self.place = place
        self.block = lax.axis_index(GRID)
        self.rank = jnp.array(place, jnp.int32)[self.block]

    def slot_blocks(self):
        slots = jnp.arange(self.size, dtype=jnp.int32)
        return jnp.array(self.order, jnp.int32)[(self.rank - slots) % self.size]

    def to_slots(self, array, axis=1, deps=()):
        return reorder(array, self.slot_blocks(), axis, deps)

    def from_slots(self, array, axis=1):
        return reorder(array, (self.rank - jnp.array(self.place, jnp.int32)) % self.size, axis)


class Team:
    def __init__(self, size):
        self.size = size
        self.rank = lax.axis_index("dp")
        self.bits = [1 << k for k in range(size.bit_length() - 1)]
        self.order = [0]
        for bit in reversed(self.bits):
            self.order = self.order + [m ^ bit for m in self.order]

    def swap(self, value, bit):
        return lax.ppermute(value, "dp", [(k, k ^ bit) for k in range(self.size)])

    def scatter(self, parts):
        for bit in self.bits:
            half = len(parts) // 2
            got = [self.swap(part.astype(BF), bit) for part in parts[half:]]
            parts = [kept + part.astype(F32) for kept, part in zip(parts[:half], got)]
        return parts[0]


def shards(sizes, x_in, span_order, attn_gain, w_qkv, w_out, ffn_gain, w_gate_up, w_down, cotangent):
    n_dp, n_fsdp, n_ctx = sizes
    ring = Ring(n_fsdp, n_ctx)
    team = Team(n_dp)
    n = ring.size
    width = x_in.shape[-1]
    rows = width // n
    tokens = x_in.reshape(-1, width)
    span = tokens.shape[0]
    rank = lax.axis_index("ctx")
    qwidth = HEADS * HD
    kvwidth = KV_HEADS * HD
    ffwidth = w_down.shape[1]
    order = span_order.reshape(-1)
    near = [(rank + k) % n_ctx for k in range(n_ctx)]
    offsets = jnp.arange(span, dtype=jnp.int32)
    query_pos = order[rank] * span + offsets
    seen = jnp.stack([order[c] < order[rank] for c in near[1:]]).astype(jnp.int32)
    tables = rope_tables(query_pos.astype(F32))

    ffq = ffwidth // n_dp
    sub = ffq // SUBS
    grad_y = cotangent.reshape(span, width)
    gains = jnp.concatenate([attn_gain[None], ffn_gain[None], jnp.zeros((14, rows), BF)], 0)
    qkv, kv_far, normed_one, wqkv, wout, gains, dy = opening(
        sizes, tokens, grad_y, w_qkv, w_out, gains, tables
    )
    attn_t, lse, hidden_one, scale_two, normed_two, x_others, dy_others, weights_a = attend_forward(
        sizes, tokens, qkv, kv_far, seen, wout, gains, dy, w_gate_up, w_down
    )
    xs = [normed_two] + list(x_others)
    dys = [dy] + list(dy_others)
    gains = gains[:, :2][(ring.rank - jnp.array(ring.place, jnp.int32)) % n]
    gain_one = gains[:, 0].reshape(-1).astype(F32)
    gain_two = gains[:, 1].reshape(-1).astype(F32)

    y, dn, grads_a, weights_b = feed_forward(
        sizes, xs, dys, [[w] for w in weights_a], None, (w_gate_up, w_down), False, 2
    )
    y, dn, grads_b, sums_a = feed_forward(
        sizes, xs, dys, [[w] for w in weights_b], list(zip(y, dn)), grads_a, True, 3
    )

    d_normed_two = ring.from_slots(sum(part.astype(F32) for part in dn))
    d_hidden_norm, d_gain_two = norm_back(hidden_one, scale_two, gain_two, d_normed_two)
    d_hidden = grad_y.astype(F32) + d_hidden_norm
    d_proj = d_hidden.astype(BF)

    d_attn = matmul_rows(d_proj, wout).astype(BF)
    d_qkv, part_out, part_qkv, sums_b, others_a = attend_backward(
        sizes, qkv, kv_far, d_attn, lse, seen, tables, attn_t, d_proj, normed_one, grads_b, sums_a, 4
    )
    room = max(rows, 256)
    grad_qkv, grad_out, grad_gain, others_b, d_input_norm = closing(
        sizes,
        part_qkv,
        part_out,
        sums_b,
        d_qkv,
        wqkv,
        tokens,
        jnp.broadcast_to(gain_one[None], (8, width)),
        jnp.broadcast_to(d_gain_two[None], (8, width)),
    )
    grad_input = d_hidden + d_input_norm

    placed, columns = [], []
    for q in range(SUBS):
        blocks = [sums_a[q]] + list(others_a[q]) if q < 2 else [sums_b[q - 2]] + list(others_b[q - 2])
        for m, block in zip(team.order, blocks):
            placed.append(block)
            columns.append((team.rank ^ m) * ffq + q * sub)
    grad_gate_up, grad_down = place_grads(placed, jnp.stack(columns).astype(jnp.int32), sub, ffwidth)

    y_out = hidden_one + ring.from_slots(team.scatter(y))
    return (
        y_out.astype(BF).reshape(x_in.shape),
        grad_input.reshape(x_in.shape),
        grad_gain[0, :rows],
        grad_qkv,
        grad_out,
        grad_gain[0, room : room + rows],
        grad_gate_up,
        grad_down,
    )


def solution(mesh):
    sizes = (mesh.shape["dp"], mesh.shape["fsdp"], mesh.shape["ctx"])
    tokens = P(("dp", "fsdp"), "ctx", None)
    weight = P(("fsdp", "ctx"), None)
    gain = P(("fsdp", "ctx"))

    def body(*args):
        return shards(sizes, *args)

    return jax.shard_map(
        body,
        mesh=mesh,
        in_specs=(tokens, P(("dp", "fsdp"), None), gain, weight, weight, gain, weight, weight, tokens),
        out_specs=(tokens, tokens, gain, weight, weight, gain, weight, weight),
        check_vma=False,
    )
```

```python
import math

import jax
import jax.numpy as jnp
from jax import lax
from jax.experimental import pallas as pl
from jax.experimental.pallas import tpu as pltpu
from jax.sharding import PartitionSpec as P

HEADS = 32
KV_HEADS = 8
HD = 64
EPS = 1e-05
SUBS = 4

BF = jnp.bfloat16
F32 = jnp.float32
GRID = ("fsdp", "ctx")


def matmul(left, right):
    return jnp.dot(left, right, preferred_element_type=F32)


def matmul_rows(left, right):
    return lax.dot_general(left, right, (((1,), (1,)), ((), ())), preferred_element_type=F32)


def matmul_tokens(left, right):
    return lax.dot_general(left, right, (((0,), (0,)), ((), ())), preferred_element_type=F32)


def rope_tables(positions):
    half = HD // 2
    freq = jnp.exp(jnp.arange(half, dtype=F32) * (-math.log(500000.0) / half))
    angle = positions[:, None] * freq[None, :]
    cosine, sine = jnp.cos(angle), jnp.sin(angle)
    zero = jnp.zeros_like(sine)
    return (
        jnp.concatenate([cosine] * 4, -1),
        jnp.concatenate([-sine, zero] * 2, -1),
        jnp.concatenate([zero, sine] * 2, -1),
    )


def inv_rms(rows):
    return lax.rsqrt(jnp.mean(rows * rows, -1, keepdims=True) + EPS)


def norm_back(rows, scale, gain, grad):
    unit = rows * scale
    pulled = grad * gain[None, :]
    inner = jnp.mean(pulled * unit, -1, keepdims=True)
    return scale * (pulled - unit * inner), jnp.sum(grad * unit, 0)


MIB = 1 << 20
ANY = pl.BlockSpec(memory_space=pl.ANY)
WHOLE = pl.BlockSpec(memory_space=pltpu.VMEM)


def cost(flops, moved, exps=0):
    return pl.CostEstimate(flops=int(flops), bytes_accessed=int(moved), transcendentals=int(exps))


def params(mib):
    return pltpu.CompilerParams(vmem_limit_bytes=mib * MIB)


def dot_nn(a, b):
    return lax.dot_general(a, b, (((1,), (0,)), ((), ())), preferred_element_type=F32)


def dot_nt(a, b):
    return lax.dot_general(a, b, (((1,), (1,)), ((), ())), preferred_element_type=F32)


def dot_tn(a, b):
    return lax.dot_general(a, b, (((0,), (0,)), ((), ())), preferred_element_type=F32)


def reorder(array, places, axis=1, deps=()):
    count = places.shape[0]
    if axis == 1 and (array.shape[1] // count) % 128 != 0:
        size = array.shape[1] // count
        blocks = [lax.dynamic_slice_in_dim(array, places[s] * size, size, 1) for s in range(count)]
        return jnp.concatenate(blocks, 1)
    if axis == 1:
        shape = (array.shape[0], array.shape[1] // count)
        took = lambda s, where: (0, where[s])
        gave = lambda s, where: (0, s)
    else:
        shape = (array.shape[0] // count, array.shape[1])
        took = lambda s, where: (where[s], 0)
        gave = lambda s, where: (s, 0)

    def kernel(where, source, *rest):
        rest[-1][...] = source[...]

    return pl.pallas_call(
        kernel,
        grid_spec=pltpu.PrefetchScalarGridSpec(
            num_scalar_prefetch=1,
            grid=(count,),
            in_specs=[pl.BlockSpec(shape, took)] + [ANY] * len(deps),
            out_specs=pl.BlockSpec(shape, gave),
        ),
        out_shape=jax.ShapeDtypeStruct(array.shape, array.dtype),
        compiler_params=params(16),
        cost_estimate=cost(0, 2 * array.size * array.dtype.itemsize),
    )(places, array, *deps)


def turn(piece, cosine, sine_low, sine_high):
    return (
        piece * cosine
        + pltpu.roll(piece, 128 - HD // 2, axis=1) * sine_low
        + pltpu.roll(piece, HD // 2, axis=1) * sine_high
    )


def head_of(block, group):
    odd = (group // 2) % 2 == 1
    return jnp.where(odd, block[:, HD:], block[:, :HD])


def causal_tile(size):
    key = lax.broadcasted_iota(jnp.int32, (size, size), 0)
    query = lax.broadcasted_iota(jnp.int32, (size, size), 1)
    return key <= query


def scores_of(key, key_far, query, seen, mask, span):
    tile = query.shape[0]
    own = dot_nt(key, query)
    if key.shape[0] > tile:
        last = key.shape[0] - tile
        own = jnp.concatenate([own[:last], jnp.where(mask, own[last:], -1e30)], 0)
    else:
        own = jnp.where(mask, own, -1e30)
    far = dot_nt(key_far, query)
    far = [jnp.where(seen[k], far[k * span : (k + 1) * span], -1e30) for k in range(len(seen))]
    return own, (far[0] if len(far) == 1 else jnp.concatenate(far, 0))


def place_grads(pieces, columns, sub, ffwidth):
    rows = pieces[0].shape[0]
    count = len(pieces)
    depth = 4

    def kernel(*refs):
        where = refs[0]
        sources = refs[1 : 1 + count]
        gu_ref, down_ref, took, gave, in_sems, out_sems = refs[1 + count :]

        def read(k):
            return pltpu.make_async_copy(sources[k], took.at[k % depth], in_sems.at[k % depth])

        def writes(k):
            at = pl.multiple_of(where[k], 128)
            here = gave.at[k % depth]
            return (
                pltpu.make_async_copy(
                    here.at[:, pl.ds(0, sub)], gu_ref.at[:, pl.ds(at, sub)], out_sems.at[k % depth, 0]
                ),
                pltpu.make_async_copy(
                    here.at[:, pl.ds(sub, sub)], gu_ref.at[:, pl.ds(at + ffwidth, sub)], out_sems.at[k % depth, 1]
                ),
                pltpu.make_async_copy(
                    here.at[:, pl.ds(2 * sub, sub)], down_ref.at[:, pl.ds(at, sub)], out_sems.at[k % depth, 2]
                ),
            )

        for k in range(min(depth - 1, count)):
            read(k).start()
        for k in range(count):
            if k + depth - 1 < count:
                read(k + depth - 1).start()
            read(k).wait()
            if k >= depth:
                for copy in writes(k - depth):
                    copy.wait()
            gave[k % depth] = took[k % depth].astype(F32)
            for copy in writes(k):
                copy.start()
        for k in range(max(0, count - depth), count):
            for copy in writes(k):
                copy.wait()

    return pl.pallas_call(
        kernel,
        in_specs=[pl.BlockSpec(memory_space=pltpu.SMEM)] + [ANY] * count,
        out_specs=[ANY, ANY],
        out_shape=[
            jax.ShapeDtypeStruct((rows, 2 * ffwidth), F32),
            jax.ShapeDtypeStruct((rows, ffwidth), F32),
        ],
        scratch_shapes=[
            pltpu.VMEM((depth, rows, 3 * sub), BF),
            pltpu.VMEM((depth, rows, 3 * sub), F32),
            pltpu.SemaphoreType.DMA((depth,)),
            pltpu.SemaphoreType.DMA((depth, 3)),
        ],
        compiler_params=params(60),
        cost_estimate=cost(0, rows * ffwidth * 18),
    )(columns, *pieces)


MESH = pl.DeviceIdType.MESH


def ring_place(n_fsdp):
    f, c = lax.axis_index("fsdp"), lax.axis_index("ctx")

    def device(place):
        row, k = place // n_fsdp, place % n_fsdp
        return {"fsdp": k + (row % 2) * (n_fsdp - 1 - 2 * k), "ctx": row}

    return c * n_fsdp + f + (c % 2) * (n_fsdp - 1 - 2 * f), device


def slot_lanes(ref, block, rows):
    if rows % 128 == 0:
        return ref[:, pl.ds(pl.multiple_of(block * rows, 128), rows)].astype(F32)
    share = 128 // rows
    wide = ref[:, pl.ds(pl.multiple_of(block // share * 128, 128), 128)].astype(F32)
    part = wide[:, :rows]
    for k in range(1, share):
        part = jnp.where(block % share == k, wide[:, k * rows : (k + 1) * rows], part)
    return part


def team_place(size, me, bit):
    return me + bit - 2 * bit * ((me // bit) % 2)


def greet(partners):
    barrier = pltpu.get_barrier_semaphore()
    for partner in partners:
        pl.semaphore_signal(barrier, inc=1, device_id=partner, device_id_type=MESH)
    pl.semaphore_wait(barrier, len(partners))


def own_columns(size, w_gate_up, w_down, first):
    ffwidth = w_down.shape[1]
    ffq = ffwidth // size
    sub = ffq // SUBS
    out = []
    for way in range(2):
        at = lax.axis_index("dp") * ffq + (first + way) * sub
        out.append(
            [
                (w_gate_up.at[:, pl.ds(pl.multiple_of(at, 128), sub)], 0),
                (w_gate_up.at[:, pl.ds(pl.multiple_of(at + ffwidth, 128), sub)], sub),
                (w_down.at[:, pl.ds(pl.multiple_of(at, 128), sub)], 2 * sub),
            ]
        )
    return out


class RingGather:
    def __init__(self, sizes, own, out, own_v, own_sem, store_sem, send, recv):
        self.n = sizes[1] * sizes[2]
        self.rows = own_v.shape[1]
        self.own, self.out, self.own_v = own, out, own_v
        self.own_sem, self.store_sem, self.send, self.recv = own_sem, store_sem, send, recv
        place, device = ring_place(sizes[1])
        self.partners = [device((place + 1) % self.n), device((place + self.n - 1) % self.n)]

    def rows_of(self, way, t):
        slot = t if way == 0 else (self.n - t) % self.n
        return pl.ds(slot * self.rows, self.rows)

    def loads(self, way):
        width = self.own_v.shape[2] // 3
        return [
            pltpu.make_async_copy(
                source, self.own_v.at[way, :, pl.ds(place, width)], self.own_sem.at[way, place // width]
            )
            for source, place in self.own[way]
        ]

    def store(self, way):
        return pltpu.make_async_copy(
            self.own_v.at[way], self.out[way].at[pl.ds(0, self.rows)], self.store_sem.at[way]
        )

    def ring(self, way, t, first=False):
        source = self.own_v.at[way] if first else self.out[way].at[self.rows_of(way, t - 1)]
        return pltpu.make_async_remote_copy(
            src_ref=source,
            dst_ref=self.out[way].at[self.rows_of(way, t)],
            send_sem=self.send.at[way, t],
            recv_sem=self.recv.at[way, t],
            device_id=self.partners[way],
            device_id_type=MESH,
        )

    def arrived(self, way, t):
        target = self.out[way].at[self.rows_of(way, t)]
        return pltpu.make_async_remote_copy(
            src_ref=target,
            dst_ref=target,
            send_sem=self.send.at[way, t],
            recv_sem=self.recv.at[way, t],
            device_id=self.partners[way],
            device_id_type=MESH,
        )

    def first(self):
        for way in range(2):
            for copy in self.loads(way):
                copy.start()
        for way in range(2):
            for copy in self.loads(way):
                copy.wait()
            self.ring(way, 1, True).start()
            self.store(way).start()

    def tick(self, t):
        for way in range(2):
            self.arrived(way, t - 1).wait_recv()
            self.ring(way, t).start()

    def last(self):
        for way in range(2):
            self.arrived(way, self.n - 1).wait_recv()
            self.store(way).wait()
            self.ring(way, 1, True).wait_send()
            for t in range(2, self.n):
                self.ring(way, t).wait_send()


def gather_scratch(n, rows, wide):
    dma = pltpu.SemaphoreType.DMA
    return [pltpu.VMEM((2, rows, wide), BF), dma((2, 3)), dma((2,)), dma((2, n)), dma((2, n))]


class RingReduce:
    def __init__(self, sizes, parts, out, land, own_v, own_sem, out_sem, send, recv):
        self.n = sizes[1] * sizes[2]
        self.rows, self.wide = out[0].shape
        self.parts, self.out, self.land, self.own_v = parts, out, land, own_v
        self.own_sem, self.out_sem, self.send, self.recv = own_sem, out_sem, send, recv
        place, device = ring_place(sizes[1])
        self.partners = [device((place + 1) % self.n), device((place + self.n - 1) % self.n)]

    def lanes(self, h):
        return pl.ds(pl.multiple_of(h * (self.wide // 2), 128), self.wide // 2)

    def load_own(self, way, t):
        slot = t % self.n if way == 0 else self.n - t
        return pltpu.make_async_copy(
            self.parts[way].at[pl.ds(slot * self.rows, self.rows)],
            self.own_v.at[way, t % 3],
            self.own_sem.at[way, t % 3],
        )

    def ring(self, source, way, t, h):
        return pltpu.make_async_remote_copy(
            src_ref=source,
            dst_ref=self.land.at[way, h, t - 1],
            send_sem=self.send.at[way, h, t],
            recv_sem=self.recv.at[way, h, t],
            device_id=self.partners[way],
            device_id_type=MESH,
        )

    def arrived(self, way, t, h):
        return self.ring(self.land.at[way, h, t - 1], way, t, h)

    def start(self, way, h):
        return self.ring(self.own_v.at[way, 1, :, self.lanes(h)], way, 1, h)

    def forward(self, way, t, h):
        return self.ring(self.land.at[way, h, t - 2], way, t, h)

    def save(self, way):
        return pltpu.make_async_copy(self.own_v.at[way, self.n % 3], self.out[way], self.out_sem.at[way])

    def first(self):
        for way in range(2):
            self.load_own(way, 1).start()
            self.load_own(way, 2).start()
        for way in range(2):
            self.load_own(way, 1).wait()
            for h in range(2):
                self.start(way, h).start()

    def total(self, way, t, h):
        return self.own_v[way, t % 3, :, self.lanes(h)].astype(F32) + self.land[way, h, t - 2].astype(F32)

    def step(self, u):
        t, h = u // 2, u % 2
        for way in range(2):
            self.arrived(way, t - 1, h).wait_recv()

            @pl.when(h == 0)
            def _():
                self.load_own(way, t).wait()

                @pl.when(t == 3)
                def _():
                    for half in range(2):
                        self.start(way, half).wait_send()

                self.load_own(way, t + 1).start()

            self.land[way, h, t - 2] = self.total(way, t, h).astype(BF)
            self.forward(way, t, h).start()

    def last(self):
        n = self.n
        for way in range(2):
            self.load_own(way, n).wait()
            for h in range(2):
                self.arrived(way, n - 1, h).wait_recv()
                half = self.wide // 2
                total = self.total(way, n, h).astype(BF)
                self.own_v[way, n % 3, :, h * half : (h + 1) * half] = total
            self.save(way).start()
        for way in range(2):
            for h in range(2):
                for t in range(2, n):
                    self.forward(way, t, h).wait_send()
            self.save(way).wait()


def reduce_scratch(n, rows, wide):
    dma = pltpu.SemaphoreType.DMA
    return [
        pltpu.VMEM((2, 2, n - 1, rows, wide // 2), BF),
        pltpu.VMEM((2, 3, rows, wide), BF),
        dma((2, 3)),
        dma((2,)),
        dma((2, 2, n)),
        dma((2, 2, n)),
    ]


class TeamSpread:
    def __init__(self, size, own, others, send, recv):
        self.own, self.others, self.send, self.recv = own, others, send, recv
        self.count = len(own)
        me = lax.axis_index("dp")
        self.stages = []
        held, bit = 1, size // 2
        while bit:
            partner = {"dp": me + bit - 2 * bit * ((me // bit) % 2)}
            self.stages.append((held, partner))
            held, bit = 2 * held, bit // 2

    def partners(self):
        return [partner for _, partner in self.stages]

    def copies(self, stage):
        held, partner = self.stages[stage]
        for k in range(self.count):
            for b in range(held):
                yield pltpu.make_async_remote_copy(
                    src_ref=self.own[k] if b == 0 else self.others[k][b - 1],
                    dst_ref=self.others[k][held + b - 1],
                    send_sem=self.send.at[k, held + b - 1],
                    recv_sem=self.recv.at[k, held + b - 1],
                    device_id=partner,
                    device_id_type=MESH,
                )

    def start(self, stage):
        for later in range(stage, len(self.stages) if stage == 0 else min(stage + 1, len(self.stages))):
            held = self.stages[later][0]
            for k, copy in enumerate(self.copies(later)):
                if (k % held == 0) == (stage == 0):
                    copy.start()

    def arrive(self, stage):
        if stage < len(self.stages):
            for copy in self.copies(stage):
                copy.wait_recv()

    def last(self):
        for stage in range(len(self.stages)):
            for copy in self.copies(stage):
                copy.wait_send()


def spread_scratch(count, size):
    return [pltpu.SemaphoreType.DMA((count, size)), pltpu.SemaphoreType.DMA((count, size))]


def feed_forward(sizes, xs, dys, weights, before, ring_parts, reducing, ident):
    n_dp, n_fsdp, n_ctx = sizes
    n = n_fsdp * n_ctx
    team, (span, width) = len(xs), xs[0].shape
    rows, wide = width // n, weights[0][0].shape[1]
    sub = wide // 3
    pieces = [piece for group in weights for piece in group]
    counts = [len(group) for group in weights]
    tile = min(span, 256)
    per = span // tile
    steps = team * per
    part = max(rows, 128)
    half = width // 2
    gsteps = width // part
    total = 2 * steps + gsteps
    inside = team // 2 if reducing and team > 2 else 0
    carried = [] if before is None else [b[0] for b in before] + [b[1] for b in before]
    backwards = reducing

    def kernel(*refs):
        refs = list(refs)

        def take(count):
            out = refs[:count]
            del refs[:count]
            return out

        x_refs, dy_refs, piece_refs = take(team), take(team), take(len(pieces))
        old_y, old_dn = take(len(carried) // 2), take(len(carried) // 2)
        part_refs = take(2)
        y_refs, dn_refs, grad_refs, ring_outs = take(team), take(team), take(2), take(2)
        if reducing:
            near = take(max(1, inside))
            (far,) = take(1)
        wgu, wd, xb, dyb, yb, dnb, dgu, inner, xg, dyg, gout = take(11)
        w_sems, x_sems, y_sems, g_sems, gout_sems = take(5)
        if carried:
            cb, c_sems = take(2)
        if reducing:
            swap_send, swap_recv, face_send, face_recv = take(4)
            ring = RingReduce(sizes, part_refs, ring_outs, *refs)
        else:
            ring = RingGather(sizes, own_columns(n_dp, *part_refs, SUBS // 2), ring_outs, *refs)
        me = lax.axis_index("dp")
        sibling = {"dp": me + 1 - 2 * (me % 2)}
        bit = team // 2
        facing = {"dp": me + bit - 2 * bit * ((me // bit) % 2)}

        k = 0
        w_copies = []
        for b, count in enumerate(counts):
            at = 0
            for ref in piece_refs[k : k + count]:
                high = ref.shape[0]
                w_copies += [
                    pltpu.make_async_copy(
                        ref.at[:, pl.ds(0, 2 * sub)],
                        wgu.at[pl.ds(at, high), pl.ds(b * 2 * sub, 2 * sub)],
                        w_sems.at[2 * k],
                    ),
                    pltpu.make_async_copy(
                        ref.at[:, pl.ds(2 * sub, sub)],
                        wd.at[pl.ds(at, high), pl.ds(b * sub, sub)],
                        w_sems.at[2 * k + 1],
                    ),
                ]
                at += high
                k += 1
        for copy in w_copies:
            copy.start()

        def block_of(i):
            return team - 1 - i // per if backwards else i // per

        def loads(m, i):
            rows_here = pl.ds((i % per) * tile, tile)
            return [
                pltpu.make_async_copy(x_refs[m].at[rows_here], xb.at[i % 2], x_sems.at[0, i % 2]),
                pltpu.make_async_copy(dy_refs[m].at[rows_here], dyb.at[i % 2], x_sems.at[1, i % 2]),
            ]

        def more(m, i):
            if not carried:
                return []
            rows_here = pl.ds((i % per) * tile, tile)
            out = [
                pltpu.make_async_copy(old_y[m].at[rows_here], yb, c_sems.at[0]),
                pltpu.make_async_copy(old_dn[m].at[rows_here], dnb, c_sems.at[1]),
            ]
            if m < inside:
                out.append(pltpu.make_async_copy(near[m].at[rows_here], cb, c_sems.at[2]))
            return out

        def writes(m, i):
            rows_here = pl.ds((i % per) * tile, tile)
            return [
                pltpu.make_async_copy(yb, y_refs[m].at[rows_here], y_sems.at[0]),
                pltpu.make_async_copy(dnb, dn_refs[m].at[rows_here], y_sems.at[1]),
            ]

        def on_block(i, act):
            for m in range(team):

                @pl.when(block_of(i) == m)
                def _():
                    act(m)

        def swap(m):
            return pltpu.make_async_remote_copy(
                src_ref=dn_refs[m],
                dst_ref=near[m - inside],
                send_sem=swap_send.at[m - inside],
                recv_sem=swap_recv.at[m - inside],
                device_id=sibling,
                device_id_type=MESH,
            )

        def face():
            return pltpu.make_async_remote_copy(
                src_ref=dn_refs[1],
                dst_ref=far,
                send_sem=face_send,
                recv_sem=face_recv,
                device_id=facing,
                device_id_type=MESH,
            )

        def go(copies):
            for copy in copies:
                copy.start()

        def end(copies):
            for copy in copies:
                copy.wait()

        def ticks(lo, hi):
            if reducing:
                count, base, act = 2 * (n - 2), 4, ring.step
            else:
                count, base, act = n - 2, 2, ring.tick
            lax.fori_loop(
                base + lo * count // total, base + hi * count // total, lambda t, c: (act(t), c)[1], 0
            )

        on_block(0, lambda m: go(loads(m, 0)))
        partners = list(ring.partners)
        if inside:
            partners.append(sibling)
        if reducing and team > 1:
            partners.append(facing)
        greet(partners)
        ring.first()
        for copy in w_copies:
            copy.wait()

        def forward(i, carry):
            @pl.when(i + 1 < steps)
            def _():
                on_block(i + 1, lambda m: go(loads(m, i + 1)))

            @pl.when(i == steps - 1)
            def _():
                go(sides(0))

            if inside:
                @pl.when(i % per == 0)
                def _():
                    on_block(i, lambda m: swap(m + inside).wait_recv() if m < inside else None)

            ticks(2 * i, 2 * i + 2)
            end(loads(0, i))
            here = pl.ds(pl.multiple_of(i * tile, tile), tile)
            if carried:
                drained = (i > 0) & (i % per != 0) if reducing else i > 0

                @pl.when(drained)
                def _():
                    end(writes(0, i))

                on_block(i, lambda m: go(more(m, i)))
            for b in range(2):
                gate_up = dot_nn(xb[i % 2], wgu[:, b * 2 * sub : (b + 1) * 2 * sub])
                d_inner = dot_nn(dyb[i % 2], wd[:, b * sub : (b + 1) * sub])
                gate, up = gate_up[:, :sub], gate_up[:, sub:]
                sig = 1.0 / (1.0 + jnp.exp(-gate))
                act = gate * sig
                inner[here, b * sub : (b + 1) * sub] = (act * up).astype(BF)
                dgu[here, b * 2 * sub : b * 2 * sub + sub] = (
                    d_inner * up * (sig + act * (1.0 - sig))
                ).astype(BF)
                dgu[here, b * 2 * sub + sub : (b + 1) * 2 * sub] = (d_inner * act).astype(BF)
            if not carried:

                @pl.when(i > 0)
                def _():
                    end(writes(0, i))

            else:
                on_block(i, lambda m: end(more(m, i)))
            for at in range(0, width, half):
                lanes = slice(at, at + half)
                y = dot_nt(inner[here, :], wd[lanes, :])
                if carried:
                    y = y + yb[:, lanes].astype(F32)
                yb[:, lanes] = y.astype(BF)
                dn = dot_nt(dgu[here, :], wgu[lanes, :])
                if carried:
                    dn = dn + dnb[:, lanes].astype(F32)
                if inside:
                    dn = dn + jnp.where(block_of(i) < inside, cb[:, lanes].astype(F32), 0.0)
                dnb[:, lanes] = dn.astype(BF)
            on_block(i, lambda m: go(writes(m, i)))
            if reducing and team > 1:

                @pl.when(i % per == per - 1)
                def _():
                    def sent(m):
                        if m >= 1:
                            end(writes(m, i))
                            go([swap(m)] if inside and m >= inside else [face()])

                    on_block(i, sent)

            return carry

        def sides(g):
            cols = pl.ds(g * part, part) if isinstance(g, int) else pl.ds(pl.multiple_of(g * part, part), part)
            out = []
            for k in range(team):
                m = team - 1 - k if backwards else k
                at = pl.ds(k * span, span)
                out += [
                    pltpu.make_async_copy(x_refs[m].at[:, cols], xg.at[g % 2, at], g_sems.at[0, g % 2, k]),
                    pltpu.make_async_copy(dy_refs[m].at[:, cols], dyg.at[g % 2, at], g_sems.at[1, g % 2, k]),
                ]
            return out

        def keep(g):
            at = pl.ds(pl.multiple_of(g * part, part), part)
            return [pltpu.make_async_copy(gout.at[b], grad_refs[b].at[at], gout_sems.at[b]) for b in range(2)]

        def outer(g, carry):
            @pl.when(g + 1 < gsteps)
            def _():
                go(sides(g + 1))

            ticks(2 * steps + g, 2 * steps + g + 1)
            end(sides(g))

            @pl.when(g > 0)
            def _():
                end(keep(g))

            for b in range(2):
                up_down = dot_tn(xg[g % 2], dgu[:, b * 2 * sub : (b + 1) * 2 * sub])
                gout[b, :, : 2 * sub] = up_down.astype(BF)
                down = dot_tn(dyg[g % 2], inner[:, b * sub : (b + 1) * sub])
                gout[b, :, 2 * sub :] = down.astype(BF)
            go(keep(g))
            return carry

        lax.fori_loop(0, steps, forward, 0)
        lax.fori_loop(0, gsteps, outer, 0)
        end(writes(0, 0))
        end(keep(0))
        ring.last()
        if reducing and team > 1:
            for m in range(inside, team) if inside else []:
                swap(m).wait_send()
            face().wait_recv()
            face().wait_send()

    shape = lambda a, b: jax.ShapeDtypeStruct((a, b), BF)
    outs = [shape(span, width)] * (2 * team) + [shape(width, wide)] * 2
    if reducing:
        outs += [shape(rows, wide)] * 2
        outs += [shape(span, width)] * (max(1, inside) + 1)
    else:
        outs += [shape(width, wide)] * 2
    dma = pltpu.SemaphoreType.DMA
    scratch = [
        pltpu.VMEM((width, 4 * sub), BF),
        pltpu.VMEM((width, 2 * sub), BF),
        pltpu.VMEM((2, tile, width), BF),
        pltpu.VMEM((2, tile, width), BF),
        pltpu.VMEM((tile, width), BF),
        pltpu.VMEM((tile, width), BF),
        pltpu.VMEM((team * span, 4 * sub), BF),
        pltpu.VMEM((team * span, 2 * sub), BF),
        pltpu.VMEM((2, team * span, part), BF),
        pltpu.VMEM((2, team * span, part), BF),
        pltpu.VMEM((2, part, wide), BF),
        dma((2 * len(pieces),)),
        dma((2, 2)),
        dma((2,)),
        dma((2, 2, team)),
        dma((2,)),
    ]
    if carried:
        scratch += [pltpu.VMEM((tile, width) if inside else (16, 128), BF), dma((3,))]
    if reducing:
        scratch += [dma((max(1, inside),)), dma((max(1, inside),)), dma(()), dma(())]
        scratch += reduce_scratch(n, rows, wide)
    else:
        scratch += gather_scratch(n, rows, wide)
    operands = list(xs) + list(dys) + pieces + carried + list(ring_parts)
    out = pl.pallas_call(
        kernel,
        in_specs=[ANY] * len(operands),
        out_specs=[ANY] * len(outs),
        out_shape=outs,
        scratch_shapes=scratch,
        compiler_params=pltpu.CompilerParams(
            collective_id=ident, has_side_effects=True, vmem_limit_bytes=60 * MIB
        ),
        cost_estimate=cost(18 * team * span * width * 2 * sub, 40 * MIB),
    )(*operands)
    y, dn, grads, ringed = out[:team], out[team : 2 * team], out[2 * team : 2 * team + 2], out[2 * team + 2 :]
    if reducing:
        return y, (dn[0], ringed[-1]) if team > 1 else (dn[0],), grads, ringed[:2]
    return y, dn, grads, ringed[:2]


def attend_forward(sizes, x, qkv, kv_far, seen, w_out, gains, dy, w_gate_up, w_down):
    n_dp, n_fsdp, n_ctx = sizes
    n = n_fsdp * n_ctx
    span, width = x.shape
    rows = width // n
    far = kv_far.shape[0]
    blocks = far // span
    qwidth, kvwidth = HEADS * HD, KV_HEADS * HD
    near, kvpairs = qwidth // 128, kvwidth // 128
    pairs = HEADS // 2
    tile = min(span, 256)
    wide = 3 * (w_down.shape[1] // n_dp // SUBS)
    early = max(0, 3 * (n - 2) // 7)
    paced = pairs - 2 if pairs * early // max(1, pairs - 2) == early else pairs
    others = n_dp - 1
    chunk = min(512, width)

    def kernel(seen_ref, q_ref, k_ref, v_ref, kf_ref, vf_ref, x_ref, gains_ref, *refs):
        refs = list(refs)

        def take(count):
            out = refs[:count]
            del refs[:count]
            return out

        wo_ref, dy_ref, gu_ref, down_ref = take(4)
        lse_ref, scale_ref, attn_out, hidden_out, normed_out = take(5)
        x_blocks, dy_blocks, ring_outs = take(others), take(others), take(2)
        attn_v, wo_v, hidden_v, normed_v, load_sem, save_sems = take(6)
        dy_send, dy_recv, x_send, x_recv = take(4)
        ring = RingGather(sizes, own_columns(n_dp, gu_ref, down_ref, 0), ring_outs, *refs)
        dy_spread = TeamSpread(n_dp, [dy_ref], [dy_blocks], dy_send, dy_recv)
        x_spread = TeamSpread(n_dp, [normed_v], [x_blocks], x_send, x_recv)
        group = pl.program_id(0)
        mask = causal_tile(tile)
        flags = [seen_ref[k] == 1 for k in range(blocks)]
        load = pltpu.make_async_copy(wo_ref, wo_v, load_sem)

        @pl.when(group == 0)
        def _():
            greet(ring.partners + dy_spread.partners())
            ring.first()
            dy_spread.start(0)
            load.start()

        lax.fori_loop(
            2 + group * early // paced,
            2 + (group + 1) * early // paced,
            lambda t, c: (ring.tick(t), c)[1],
            0,
        )
        key, value = head_of(k_ref[...], group), head_of(v_ref[...], group)
        key_far, value_far = head_of(kf_ref[...], group), head_of(vf_ref[...], group)
        value_t = value.astype(F32).T.astype(BF)
        value_far_t = value_far.astype(F32).T.astype(BF)
        for head in range(2):
            down = pl.ds(pl.multiple_of(group * 128 + head * HD, HD), HD)
            for at in range(0, span, tile):
                end = at + tile
                q = q_ref[at:end, head * HD : (head + 1) * HD]
                own, other = scores_of(key[:end], key_far, q, flags, mask, span)
                peak = jnp.maximum(jnp.max(own, 0, keepdims=True), jnp.max(other, 0, keepdims=True))
                own = jnp.exp(own - peak)
                other = jnp.exp(other - peak)
                total = jnp.sum(own, 0, keepdims=True) + jnp.sum(other, 0, keepdims=True)
                scale = 1.0 / total
                result = dot_nn(value_t[:, :end], (own * scale).astype(BF)) + dot_nn(
                    value_far_t, (other * scale).astype(BF)
                )
                attn_v[down, at:end] = result.astype(BF)
                lse_ref[0, head : head + 1, at:end] = peak + jnp.log(total)

        @pl.when(group == pairs - 1)
        def _():
            saves = [
                pltpu.make_async_copy(a, b, save_sems.at[k])
                for k, (a, b) in enumerate([(attn_v, attn_out), (hidden_v, hidden_out), (normed_v, normed_out)])
            ]
            saves[0].start()
            load.wait()
            square = jnp.zeros((span, 1), F32)
            for at in range(0, width, chunk):
                lanes = slice(at, at + chunk)
                hidden = x_ref[:, lanes].astype(F32) + dot_tn(attn_v[...], wo_v[:, lanes])
                hidden_v[:, lanes] = hidden
                square = square + jnp.sum(hidden * hidden, -1, keepdims=True)
            scale = lax.rsqrt(square / width + EPS)
            scale_ref[...] = jnp.broadcast_to(scale, (span, 128))
            place, device = ring_place(n_fsdp)
            for slot in range(n):
                there = device((place + n - slot) % n)
                part = slot_lanes(hidden_v, there["fsdp"] * n_ctx + there["ctx"], rows)
                normed = part * scale * gains_ref[slot, 1:2, :].astype(F32)
                normed_v[:, slot * rows : (slot + 1) * rows] = normed.astype(BF)
            x_spread.start(0)
            saves[1].start()
            saves[2].start()
            dy_spread.arrive(0)
            dy_spread.start(1)
            middle = max(2 + early, n - 2)
            for t in range(2 + early, middle):
                ring.tick(t)
            x_spread.arrive(0)
            x_spread.start(1)
            for t in range(middle, n):
                ring.tick(t)
            dy_spread.arrive(1)
            x_spread.arrive(1)
            ring.last()
            dy_spread.last()
            x_spread.last()
            for copy in saves:
                copy.wait()

    pair = lambda high, shift: pl.BlockSpec((high, 128), lambda i: (0, i // 4 + shift))
    dma = pltpu.SemaphoreType.DMA
    block = jax.ShapeDtypeStruct((span, width), BF)
    out = pl.pallas_call(
        kernel,
        grid=(pairs,),
        in_specs=[
            pl.BlockSpec(memory_space=pltpu.SMEM),
            pl.BlockSpec((span, 128), lambda i: (0, i)),
            pair(span, near),
            pair(span, near + kvpairs),
            pair(far, 0),
            pair(far, kvpairs),
            pl.BlockSpec((span, width), lambda i: (0, 0)),
            pl.BlockSpec(gains.shape, lambda i: (0, 0, 0)),
        ]
        + [ANY] * 4,
        out_specs=[pl.BlockSpec((1, 8, span), lambda i: (i, 0, 0)), pl.BlockSpec((span, 128), lambda i: (0, 0))]
        + [ANY] * (5 + 2 * others),
        out_shape=[
            jax.ShapeDtypeStruct((pairs, 8, span), F32),
            jax.ShapeDtypeStruct((span, 128), F32),
            jax.ShapeDtypeStruct((qwidth, span), BF),
            jax.ShapeDtypeStruct((span, width), F32),
        ]
        + [block] * (1 + 2 * others)
        + [jax.ShapeDtypeStruct((width, wide), BF)] * 2,
        scratch_shapes=[
            pltpu.VMEM((qwidth, span), BF),
            pltpu.VMEM((qwidth, width), BF),
            pltpu.VMEM((span, width), F32),
            pltpu.VMEM((span, width), BF),
            dma(()),
            dma((3,)),
        ]
        + spread_scratch(1, n_dp)
        + spread_scratch(1, n_dp)
        + gather_scratch(n, rows, wide),
        compiler_params=pltpu.CompilerParams(
            collective_id=5, has_side_effects=True, vmem_limit_bytes=58 * MIB
        ),
        cost_estimate=cost(pairs * 2 * span * (span + far) * 128 * 4, 30 * MIB),
    )(seen, qkv, qkv, qkv, kv_far, kv_far, x, gains, w_out, dy, w_gate_up, w_down)
    lse, scale, attn, hidden, normed = out[:5]
    blocks = out[5 : 5 + others], out[5 + others : 5 + 2 * others]
    return attn, lse, hidden, scale[:, :1], normed, *blocks, out[5 + 2 * others :]


def attend_backward(sizes, qkv, kv_far, d_attn, lse, seen, tables, attn_t, d_proj, normed, ring_parts, sums, ident):
    n_dp, n_fsdp, n_ctx = sizes
    n = n_fsdp * n_ctx
    span, far = qkv.shape[0], kv_far.shape[0]
    blocks = far // span
    qwidth, kvwidth = HEADS * HD, KV_HEADS * HD
    near, kvpairs = qwidth // 128, kvwidth // 128
    pairs = HEADS // 2
    tile = min(span, 256)
    rows, wide = ring_parts[0].shape[0] // n, ring_parts[0].shape[1]
    early = 4 + 8 * (n - 2) // 6
    width = normed.shape[1]
    qkvwidth = qwidth + 2 * kvwidth
    part = max(rows, 128)
    others = n_dp - 1

    def kernel(seen_ref, q_ref, k_ref, v_ref, kf_ref, vf_ref, d_ref, lse_ref, cos_ref, low_ref, high_ref, *refs):
        refs = list(refs)

        def take(count):
            out = refs[:count]
            del refs[:count]
            return out

        attn_ref, proj_ref, normed_ref = take(3)
        parts, own_sums = take(2), take(2)
        dqkv_out, go_out, gq_out = take(3)
        ring_outs, blocks_out = take(2), take(2 * others)
        dqkv_v, dkv, dkv_far, give, got, save_sem, kv_send, kv_recv = take(8)
        attn_v, proj_v, normed_v, stage, load_sems, stage_sems = take(6)
        spread_send, spread_recv = take(2)
        ring = RingReduce(sizes, parts, ring_outs, *refs)
        spread = TeamSpread(
            n_dp, own_sums, [blocks_out[k * others : (k + 1) * others] for k in range(2)], spread_send, spread_recv
        )
        loads = [
            pltpu.make_async_copy(a, b, load_sems.at[k])
            for k, (a, b) in enumerate([(attn_ref, attn_v), (proj_ref, proj_v), (normed_ref, normed_v)])
        ]

        def product(out, cols, make):
            def write(g):
                return pltpu.make_async_copy(
                    stage.at[g % 2, :, pl.ds(0, cols)],
                    out.at[pl.ds(pl.multiple_of(g * part, part), part)],
                    stage_sems.at[g % 2],
                )

            def body(g, carry):
                @pl.when(g >= 2)
                def _():
                    write(g - 2).wait()

                stage[g % 2, :, :cols] = make(pl.ds(pl.multiple_of(g * part, part), part)).astype(BF)
                write(g).start()
                return carry

            count = width // part
            lax.fori_loop(0, count, body, 0)
            for g in range(max(0, count - 2), count):
                write(g).wait()

        ctx = lax.axis_index("ctx")
        group = pl.program_id(0)
        mask = causal_tile(tile)
        flags = [seen_ref[k] == 1 for k in range(blocks)]
        key, value = head_of(k_ref[...], group), head_of(v_ref[...], group)
        key_far, value_far = head_of(kf_ref[...], group), head_of(vf_ref[...], group)
        key_t = key.astype(F32).T.astype(BF)
        key_far_t = key_far.astype(F32).T.astype(BF)
        odd = (group // 2) % 2 == 1
        cosine, low, high = cos_ref[...], -low_ref[...], -high_ref[...]

        @pl.when(group == 0)
        def _():
            greet(ring.partners + [{"ctx": (ctx + k) % n_ctx} for k in range(1, n_ctx)] + spread.partners())
            ring.first()
            spread.start(0)
            for copy in loads:
                copy.start()
            dkv[...] = jnp.zeros_like(dkv)
            dkv_far[...] = jnp.zeros_like(dkv_far)

        lax.fori_loop(
            4 + group * (early - 4) // pairs,
            4 + (group + 1) * (early - 4) // pairs,
            lambda u, c: (ring.step(u), c)[1],
            0,
        )

        def put(ref, size, shift, add):
            zero = jnp.zeros_like(add)
            lanes = pl.ds(pl.multiple_of(group // 4 * 128 + shift, 128), 128)
            ref[0:size, lanes] += jnp.concatenate([jnp.where(odd, zero, add), jnp.where(odd, add, zero)], 1)

        for at in range(0, span, tile):
            end = at + tile
            turned = []
            for head in range(2):
                lanes = slice(head * HD, (head + 1) * HD)
                q = q_ref[at:end, lanes]
                d = d_ref[at:end, lanes]
                own, other = scores_of(key[:end], key_far, q, flags, mask, span)
                base = lse_ref[0, head : head + 1, at:end]
                own = jnp.exp(own - base)
                other = jnp.exp(other - base)
                d_own = dot_nt(value[:end], d)
                d_other = dot_nt(value_far, d)
                delta = jnp.sum(own * d_own, 0, keepdims=True) + jnp.sum(other * d_other, 0, keepdims=True)
                ds_own = (own * (d_own - delta)).astype(BF)
                ds_other = (other * (d_other - delta)).astype(BF)
                put(dkv, end, kvwidth, dot_nn(own.astype(BF), d))
                put(dkv_far, far, kvwidth, dot_nn(other.astype(BF), d))
                put(dkv, end, 0, dot_nn(ds_own, q))
                put(dkv_far, far, 0, dot_nn(ds_other, q))
                turned.append(dot_nn(key_t[:, :end], ds_own) + dot_nn(key_far_t, ds_other))
            d_query = jnp.concatenate(turned, 0).T * HD**-0.5
            dqkv_v[at:end, pl.ds(pl.multiple_of(group * 128, 128), 128)] = turn(
                d_query, cosine[at:end], low[at:end], high[at:end]
            ).astype(BF)

        @pl.when(group == pairs - 1)
        def _():
            give[...] = dkv_far[...].astype(BF)

            def back(k):
                return pltpu.make_async_remote_copy(
                    src_ref=give.at[pl.ds((k - 1) * span, span)],
                    dst_ref=got.at[k - 1],
                    send_sem=kv_send.at[k],
                    recv_sem=kv_recv.at[k],
                    device_id={"ctx": (ctx + k) % n_ctx},
                    device_id_type=MESH,
                )

            for k in range(1, n_ctx):
                back(k).start()
            for copy in loads:
                copy.wait()
            ring.step(early)
            product(go_out, qwidth, lambda at: dot_nn(attn_v[at, :], proj_v[...]))
            ring.step(early + 1)
            for k in range(1, n_ctx):
                back(k).wait_recv()
            for at in range(0, 2 * kvwidth, 128):
                piece = dkv[:, at : at + 128]
                for k in range(1, n_ctx):
                    piece = piece + got[k - 1, :, at : at + 128].astype(F32)
                if at < kvwidth:
                    piece = turn(piece, cosine, low, high)
                dqkv_v[:, qwidth + at : qwidth + at + 128] = piece.astype(BF)
            save = pltpu.make_async_copy(dqkv_v, dqkv_out, save_sem)
            save.start()
            lax.fori_loop(early + 2, 2 * n, lambda u, c: (ring.step(u), c)[1], 0)
            spread.arrive(0)
            spread.start(1)
            product(gq_out, qkvwidth, lambda at: dot_tn(normed_v[:, at], dqkv_v[...]))
            spread.arrive(1)
            ring.last()
            spread.last()
            for k in range(1, n_ctx):
                back(k).wait_send()
            save.wait()

    pair = lambda high, shift: pl.BlockSpec((high, 128), lambda i: (0, i // 4 + shift))
    wide_block = pl.BlockSpec((span, 128), lambda i: (0, i))
    table = pl.BlockSpec((span, 128), lambda i: (0, 0))
    dma = pltpu.SemaphoreType.DMA
    out = pl.pallas_call(
        kernel,
        grid=(pairs,),
        in_specs=[
            pl.BlockSpec(memory_space=pltpu.SMEM),
            wide_block,
            pair(span, near),
            pair(span, near + kvpairs),
            pair(far, 0),
            pair(far, kvpairs),
            wide_block,
            pl.BlockSpec((1, 8, span), lambda i: (i, 0, 0)),
            table,
            table,
            table,
        ]
        + [ANY] * 7,
        out_specs=[ANY] * (5 + 2 * others),
        out_shape=[
            jax.ShapeDtypeStruct((span, qkvwidth), BF),
            jax.ShapeDtypeStruct((width, qwidth), BF),
            jax.ShapeDtypeStruct((width, qkvwidth), BF),
        ]
        + [jax.ShapeDtypeStruct((rows, wide), BF)] * (2 + 2 * others),
        scratch_shapes=[
            pltpu.VMEM((span, qwidth + 2 * kvwidth), BF),
            pltpu.VMEM((span, 2 * kvwidth), F32),
            pltpu.VMEM((far, 2 * kvwidth), F32),
            pltpu.VMEM((far, 2 * kvwidth), BF),
            pltpu.VMEM((n_ctx - 1, span, 2 * kvwidth), BF),
            dma(()),
            dma((n_ctx,)),
            dma((n_ctx,)),
            pltpu.VMEM(attn_t.shape, BF),
            pltpu.VMEM(d_proj.shape, BF),
            pltpu.VMEM(normed.shape, BF),
            pltpu.VMEM((2, part, max(qwidth, qkvwidth)), BF),
            dma((3,)),
            dma((2,)),
        ]
        + spread_scratch(2, n_dp)
        + reduce_scratch(n, rows, wide),
        compiler_params=pltpu.CompilerParams(
            collective_id=ident, has_side_effects=True, vmem_limit_bytes=58 * MIB
        ),
        cost_estimate=cost(pairs * 2 * span * (span + far) * 128 * 10, 30 * MIB),
    )(seen, qkv, qkv, qkv, kv_far, kv_far, d_attn, lse, *tables, attn_t, d_proj, normed, *ring_parts, *sums)
    return out[0], out[1], out[2], out[3:5], [out[5 + k * others : 5 + (k + 1) * others] for k in range(2)]


def opening(sizes, x, dy, w_qkv, w_out, gains, tables):
    n_dp, n_fsdp, n_ctx = sizes
    n = n_fsdp * n_ctx
    span, width = x.shape
    rows = width // n
    share, half = w_qkv.shape[1] // n_dp, w_out.shape[1] // 2
    qwidth, kvwidth = HEADS * HD, KV_HEADS * HD
    qkvwidth = qwidth + 2 * kvwidth
    chunk = share // 2 if share % 256 == 0 else share
    across_x = n_dp > 2

    def kernel(x_ref, dy_ref, wq_ref, wo_ref, g_ref, cos_ref, low_ref, high_ref, *refs):
        refs = list(refs)

        def take(count):
            out = refs[:count]
            del refs[:count]
            return out

        qkv_out, far_out, xs_out, wq_out, wo_out, gains_out, dy_out = take(7)
        qkv_v, far_v, xs_v, dy_v = take(4)
        wq_v = take(n_dp)
        om_v, oo_v, gains_v = take(3)
        load_sems, save_sems, wq_sems, wo_sems = take(4)
        send, recv, x_send, x_recv, c_send, c_recv, o_send, o_recv = take(8)
        gain_send, gain_recv, kv_send, kv_recv = take(4)
        me = lax.axis_index("dp")
        core = me % 2
        sibling = {"dp": team_place(n_dp, me, 1)}
        facing = {"dp": team_place(n_dp, me, n_dp // 2)}
        bases = [me, team_place(n_dp, me, n_dp // 2)] if across_x else [me]
        bases = [b * share for b in bases + [team_place(n_dp, b, 1) for b in bases]]
        held = n_dp // 2
        place, device = ring_place(n_fsdp)
        ahead, behind = device((place + 1) % n), device((place + n - 1) % n)
        mine = (wq_v[0], om_v)
        widths = (share, half)

        def block_of(slot):
            there = device((place + n - slot) % n)
            return there["fsdp"] * n_ctx + there["ctx"]

        loads = [
            pltpu.make_async_copy(
                ref.at[:, pl.ds(pl.multiple_of(at, 128), w)], mine[k].at[pl.ds(0, rows)], load_sems.at[k]
            )
            for k, (ref, at, w) in enumerate(((wq_ref, me * share, share), (wo_ref, core * half, half)))
        ] + [pltpu.make_async_copy(g_ref, gains_v.at[0], load_sems.at[2])]
        for copy in loads:
            copy.start()
        ctx = lax.axis_index("ctx")
        greet(
            [ahead, behind, sibling]
            + ([facing] if across_x else [])
            + [{"ctx": (ctx + k) % n_ctx} for k in range(1, n_ctx)]
        )

        def lanes(k, way):
            return pl.ds(way * (widths[k] // 2), widths[k] // 2)

        def remote(source, target, send_sem, recv_sem, partner):
            return pltpu.make_async_remote_copy(
                src_ref=source,
                dst_ref=target,
                send_sem=send_sem,
                recv_sem=recv_sem,
                device_id=partner,
                device_id_type=MESH,
            )

        def step(k, way, t):
            here = t - 1 if way == 0 else (n - t + 1) % n
            there = t if way == 0 else n - t
            return remote(
                mine[k].at[pl.ds(here * rows, rows), lanes(k, way)],
                mine[k].at[pl.ds(there * rows, rows), lanes(k, way)],
                send.at[k, way, t],
                recv.at[k, way, t],
                ahead if way == 0 else behind,
            )

        def over_x(way, slot):
            at = (pl.ds(slot * rows, rows), lanes(0, way))
            return remote(wq_v[0].at[at], wq_v[1].at[at], x_send.at[way, slot], x_recv.at[way, slot], facing)

        def over_core(b, way, slot):
            at = (pl.ds(slot * rows, rows), lanes(0, way))
            return remote(
                wq_v[b].at[at], wq_v[held + b].at[at], c_send.at[b, way, slot], c_recv.at[b, way, slot], sibling
            )

        def out_over(way, slot):
            at = (pl.ds(slot * rows, rows), lanes(1, way))
            return remote(om_v.at[at], oo_v.at[at], o_send.at[way, slot], o_recv.at[way, slot], sibling)

        def gain_step(t):
            return remote(gains_v.at[t - 1], gains_v.at[t], gain_send.at[t], gain_recv.at[t], ahead)

        def kv_step(k):
            return remote(
                qkv_v.at[:, pl.ds(qwidth, 2 * kvwidth)],
                far_v.at[pl.ds((k - 1) * span, span)],
                kv_send.at[k],
                kv_recv.at[k],
                {"ctx": (ctx + n_ctx - k) % n_ctx},
            )

        def give(way, slot):
            if across_x:
                over_x(way, slot).start()
            over_core(0, way, slot).start()

        f32 = x_ref[...].astype(F32)
        scale = lax.rsqrt(jnp.mean(f32 * f32, -1, keepdims=True) + EPS)

        def normalize(slot):
            part = slot_lanes(x_ref, block_of(slot), rows)
            xs_v[:, slot * rows : (slot + 1) * rows] = (
                part * scale * gains_v[slot, 0:1, :].astype(F32)
            ).astype(BF)
            dy_v[:, slot * rows : (slot + 1) * rows] = slot_lanes(dy_ref, block_of(slot), rows).astype(BF)

        loads[0].wait()
        loads[2].wait()
        gain_step(1).start()
        for way in range(2):
            step(0, way, 1).start()
        loads[1].wait()
        for way in range(2):
            give(way, 0)
        normalize(0)
        for t in range(1, n):
            gain_step(t).wait_recv()
            if t < n - 1:
                gain_step(t + 1).start()
            for way in range(2):
                step(0, way, t).wait_recv()
                if t < n - 1:
                    step(0, way, t + 1).start()
                give(way, t if way == 0 else n - t)
            normalize(t)

        for way in range(2):
            step(1, way, 1).start()
            out_over(way, 0).start()

        def out_tick(t):
            for way in range(2):
                step(1, way, t).wait_recv()
                if t < n - 1:
                    step(1, way, t + 1).start()
                out_over(way, t if way == 0 else n - t).start()

        order = [(way, 0) for way in range(2)]
        for t in range(1, n):
            order += [(0, t), (1, n - t)]
        cosine, low, high = cos_ref[...], low_ref[...], high_ref[...]

        def form(b, at):
            value = dot_nn(xs_v[...], wq_v[b][:, at : at + chunk])
            for part in range(0, chunk, 128):
                piece = value[:, part : part + 128]
                here = bases[b] + at + part
                piece = jnp.where(here >= qwidth + kvwidth, piece, turn(piece, cosine, low, high))
                piece = piece * jnp.where(here < qwidth, HD**-0.5, 1.0)
                qkv_v[:, pl.ds(pl.multiple_of(here, 128), 128)] = piece.astype(BF)

        def save_share(b):
            return [
                pltpu.make_async_copy(
                    wq_v[b].at[pl.ds(slot * rows, rows)],
                    wq_out.at[
                        pl.ds(pl.multiple_of(block_of(slot) * rows, rows), rows),
                        pl.ds(pl.multiple_of(bases[b], 128), share),
                    ],
                    wq_sems.at[b, slot],
                )
                for slot in range(n)
            ]

        def save_half(k):
            whose = core if k == 0 else 1 - core
            return [
                pltpu.make_async_copy(
                    (om_v, oo_v)[k].at[pl.ds(slot * rows, rows)],
                    wo_out.at[
                        pl.ds(pl.multiple_of(block_of(slot) * rows, rows), rows),
                        pl.ds(pl.multiple_of(whose * half, 128), half),
                    ],
                    wo_sems.at[k, slot],
                )
                for slot in range(n)
            ]

        def go(copies):
            for copy in copies:
                copy.start()

        jobs = [lambda at=at: form(0, at) for at in range(0, share, chunk)]
        jobs.append(lambda: go(save_share(0)))

        def core_shares(b):
            for way, slot in order:
                over_core(b, way, slot).wait_recv()
            go(save_share(held + b))

        jobs.append(lambda: core_shares(0))
        jobs += [lambda at=at: form(held, at) for at in range(0, share, chunk)]
        if across_x:

            def relay(way, slot):
                over_x(way, slot).wait_recv()
                over_core(1, way, slot).start()

            jobs += [lambda w=way, k=slot: relay(w, k) for way, slot in order]
            jobs.append(lambda: go(save_share(1)))
            jobs += [lambda at=at: form(1, at) for at in range(0, share, chunk)]
            jobs.append(lambda: core_shares(1))
            jobs += [lambda at=at: form(held + 1, at) for at in range(0, share, chunk)]
        for k, job in enumerate(jobs):
            job()
            for t in range(1 + k * (n - 1) // len(jobs), 1 + (k + 1) * (n - 1) // len(jobs)):
                out_tick(t)
        for j in range(1, n_ctx):
            kv_step(j).start()
        saves = [
            pltpu.make_async_copy(a, b, save_sems.at[k])
            for k, (a, b) in enumerate(
                [(qkv_v, qkv_out), (far_v, far_out), (xs_v, xs_out), (gains_v, gains_out), (dy_v, dy_out)]
            )
        ]
        for k in (0, 2, 3, 4):
            saves[k].start()
        go(save_half(0))
        for way, slot in order:
            out_over(way, slot).wait_recv()
        go(save_half(1))
        for j in range(1, n_ctx):
            kv_step(j).wait_recv()
        saves[1].start()
        for t in range(1, n):
            gain_step(t).wait_send()
            for way in range(2):
                for k in range(2):
                    step(k, way, t).wait_send()
        for way, slot in order:
            out_over(way, slot).wait_send()
            for b in range(held):
                over_core(b, way, slot).wait_send()
            if across_x:
                over_x(way, slot).wait_send()
        for j in range(1, n_ctx):
            kv_step(j).wait_send()
        for copies in [save_share(b) for b in range(n_dp)] + [save_half(k) for k in range(2)] + [saves]:
            for copy in copies:
                copy.wait()

    dma = pltpu.SemaphoreType.DMA
    shapes = [
        (span, qkvwidth),
        ((n_ctx - 1) * span, 2 * kvwidth),
        (span, width),
        (width, qkvwidth),
        (width, 2 * half),
        (n, 16, rows),
        (span, width),
    ]
    return pl.pallas_call(
        kernel,
        in_specs=[WHOLE, WHOLE, ANY, ANY, ANY, WHOLE, WHOLE, WHOLE],
        out_specs=[ANY] * 7,
        out_shape=[jax.ShapeDtypeStruct(shape, BF) for shape in shapes],
        scratch_shapes=[pltpu.VMEM(shape, BF) for shape in shapes[:3] + shapes[6:]]
        + [pltpu.VMEM((width, share), BF)] * n_dp
        + [pltpu.VMEM((width, half), BF)] * 2
        + [pltpu.VMEM((n, 16, rows), BF)]
        + [
            dma((3,)),
            dma((5,)),
            dma((n_dp, n)),
            dma((2, n)),
            dma((2, 2, n)),
            dma((2, 2, n)),
            dma((2, n)),
            dma((2, n)),
            dma((n_dp // 2, 2, n)),
            dma((n_dp // 2, 2, n)),
            dma((2, n)),
            dma((2, n)),
            dma((n,)),
            dma((n,)),
            dma((n_ctx,)),
            dma((n_ctx,)),
        ],
        compiler_params=pltpu.CompilerParams(
            collective_id=0, has_side_effects=True, vmem_limit_bytes=56 * MIB
        ),
        cost_estimate=cost(2 * span * width * qkvwidth, 4 * width * qkvwidth),
    )(x, dy, w_qkv, w_out, gains, *tables)


def closing(sizes, part_qkv, part_out, sums, d_qkv, w_qkv, x, gain, d_gain):
    n_dp, n_fsdp, n_ctx = sizes
    n = n_fsdp * n_ctx
    span, width = x.shape
    mine = width // n
    rows, widths, kinds = [mine, 8], [part_qkv.shape[1] // 2, max(mine, 256)], [BF, F32]
    count = 2
    outwidth = part_out.shape[1]
    split = n_dp > 2
    quarter = outwidth // n_dp
    chunk = min(512, width)
    parts = width // chunk
    bits = [1 << k for k in range(1, n_dp.bit_length() - 1)]
    others = n_dp - 1

    def kernel(*refs):
        refs = list(refs)

        def take(size):
            out = refs[:size]
            del refs[:size]
            return out

        full, (out_ref,), own_sums = take(1), take(1), take(len(sums))
        dq_ref, w_ref, x_ref, gain_ref, d_gain_ref = take(5)
        outs, (wo_out,) = take(count), take(1)
        blocks_out, (input_out,) = take(len(sums) * others), take(1)
        gain_v, both_v, d_v, w_v, dn_v, w_sem, d_sem, dn_sem = take(8)
        full = full + [gain_v]
        near, land, done, extra, back = take(count), take(count), take(count), take(count), take(count)
        own = take(count)
        (own_sems,) = take(1)
        o_own, o_near, o_x, o_land, o_done = take(5)
        o_blocks = take(others)
        o_load, o_swap_send, o_swap_recv, o_x_send, o_x_recv, o_send, o_recv, o_end_send, o_end_recv = take(9)
        send, recv, pair_send, pair_recv, x_send, x_recv, end_send, end_recv = take(8)
        spread = TeamSpread(
            n_dp, own_sums, [blocks_out[k * others : (k + 1) * others] for k in range(len(sums))], *refs
        )
        me = lax.axis_index("dp")
        core = me % 2
        sibling = {"dp": me + 1 - 2 * core}
        place, device = ring_place(n_fsdp)
        ahead, behind = device((place + 1) % n), device((place + n - 1) % n)
        facing = [{"dp": me + bit - 2 * bit * ((me // bit) % 2)} for bit in bits]
        greet([ahead, behind, sibling] + facing)

        def half(g, way):
            return pl.ds(way * (widths[g] // 2), widths[g] // 2)

        def half_of(g, way, whose):
            base = whose * widths[g] + way * (widths[g] // 2)
            return pl.ds(pl.multiple_of(base, 128), widths[g] // 2)

        def at(g, slot):
            return pl.ds(slot * rows[g], rows[g])

        def swap(g, way, slot):
            return pltpu.make_async_remote_copy(
                src_ref=full[g].at[at(g, slot), half_of(g, way, 1 - core)],
                dst_ref=near[g].at[at(g, slot), half(g, way)],
                send_sem=pair_send.at[g, way, slot],
                recv_sem=pair_recv.at[g, way, slot],
                device_id=sibling,
                device_id_type=MESH,
            )

        def step(g, way, t):
            slot = t if way == 0 else n - t
            source = near[g].at[at(g, slot), half(g, way)] if t == 1 else land[g].at[way, t - 2]
            return pltpu.make_async_remote_copy(
                src_ref=source,
                dst_ref=land[g].at[way, t - 1],
                send_sem=send.at[g, way, t],
                recv_sem=recv.at[g, way, t],
                device_id=ahead if way == 0 else behind,
                device_id_type=MESH,
            )

        def face(g, k):
            return pltpu.make_async_remote_copy(
                src_ref=done[g].at[k],
                dst_ref=extra[g].at[k],
                send_sem=x_send.at[g, k],
                recv_sem=x_recv.at[g, k],
                device_id=facing[k],
                device_id_type=MESH,
            )

        def end(g):
            return pltpu.make_async_remote_copy(
                src_ref=done[g].at[len(bits)],
                dst_ref=back[g],
                send_sem=end_send.at[g],
                recv_sem=end_recv.at[g],
                device_id=sibling,
                device_id_type=MESH,
            )

        def own_load(g, way, t):
            slot = t % n if way == 0 else n - t
            return pltpu.make_async_copy(
                full[g].at[at(g, slot), half_of(g, way, core)],
                own[g].at[way, t % 2],
                own_sems.at[g, way, t % 2],
            )

        def both(g, way, t, slot):
            own_load(g, way, t).wait()
            swap(g, way, slot).wait_recv()
            return own[g][way, t % 2].astype(F32) + near[g][at(g, slot), half(g, way)].astype(F32)

        def forward(g, t):
            for way in range(2):
                slot = t if way == 0 else n - t
                value = both(g, way, t, slot)
                if t == 1:
                    near[g][at(g, slot), half(g, way)] = value.astype(kinds[g])
                else:
                    step(g, way, t - 1).wait_recv()
                    land[g][way, t - 2] = (value + land[g][way, t - 2].astype(F32)).astype(kinds[g])
                step(g, way, t).start()
                own_load(g, way, t + 1).start()

        def finish(g):
            for way in range(2):
                value = both(g, way, n, 0)
                step(g, way, n - 1).wait_recv()
                done[g][0, :, half(g, way)] = (value + land[g][way, n - 2].astype(F32)).astype(kinds[g])
            if bits:
                face(g, 0).start()

        w_load = pltpu.make_async_copy(w_ref, w_v, w_sem)
        d_load = pltpu.make_async_copy(dq_ref, d_v, d_sem)
        dn_save = pltpu.make_async_copy(dn_v, input_out, dn_sem)

        def begin(g):
            for way in range(2):
                own_load(g, way, 1).start()

        def swaps(g, t):
            swap(g, 0, t % n).start()
            swap(g, 1, n - t).start()

        def product(k):
            lanes = slice(k * chunk, (k + 1) * chunk)
            dn_v[:, lanes] = dot_nt(d_v[...], w_v[lanes, :])

        def norm():
            square = jnp.zeros((span, 1), F32)
            for k in range(parts):
                value = x_ref[:, k * chunk : (k + 1) * chunk].astype(F32)
                square = square + jnp.sum(value * value, -1, keepdims=True)
            scale = lax.rsqrt(square / width + EPS)
            inner = jnp.zeros((span, 1), F32)
            for k in range(parts):
                lanes = slice(k * chunk, (k + 1) * chunk)
                unit = x_ref[:, lanes].astype(F32) * scale
                product = dn_v[:, lanes] * unit
                both_v[1:2, lanes] = jnp.sum(product, 0, keepdims=True)
                inner = inner + jnp.sum(product * gain_ref[0:1, lanes], -1, keepdims=True)
            inner = inner / width
            for k in range(parts):
                lanes = slice(k * chunk, (k + 1) * chunk)
                unit = x_ref[:, lanes].astype(F32) * scale
                dn_v[:, lanes] = scale * (dn_v[:, lanes] * gain_ref[0:1, lanes] - unit * inner)
            dn_save.start()
            gain_v[...] = jnp.zeros_like(gain_v)
            both_v[0:1, :] = d_gain_ref[0:1, :]
            both_v[2:8, :] = jnp.zeros((6, width), F32)
            for slot in range(n):
                there = device((place + n - slot) % n)
                pair = slot_lanes(both_v, there["fsdp"] * n_ctx + there["ctx"], mine)
                gain_v[slot * 8 : slot * 8 + 1, :mine] = pair[1:2]
                gain_v[slot * 8 : slot * 8 + 1, widths[-1] : widths[-1] + mine] = pair[0:1]

        side = me // 2 if split else 0
        across = {"dp": team_place(n_dp, me, n_dp // 2)}
        ends = TeamSpread(n_dp, [o_done], [o_blocks], o_end_send, o_end_recv)

        def natural(slot):
            there = device((place + n - slot) % n)
            return pl.ds(pl.multiple_of((there["fsdp"] * n_ctx + there["ctx"]) * mine, mine), mine)

        def quarter_of(whose, which):
            return pl.ds(pl.multiple_of(whose * (outwidth // 2) + which * quarter, 128), quarter)

        def piece(which):
            return pl.ds(pl.multiple_of(which * quarter, 128), quarter)

        def o_half(way):
            return pl.ds(way * (quarter // 2), quarter // 2)

        def out_load(slot):
            return pltpu.make_async_copy(
                out_ref.at[natural(slot), pl.ds(pl.multiple_of(core * (outwidth // 2), 128), outwidth // 2)],
                o_own.at[slot],
                o_load.at[slot],
            )

        def out_swap(slot, which):
            return pltpu.make_async_remote_copy(
                src_ref=out_ref.at[natural(slot), quarter_of(1 - core, which)],
                dst_ref=o_near.at[slot, :, piece(which)],
                send_sem=o_swap_send.at[slot, which],
                recv_sem=o_swap_recv.at[slot, which],
                device_id=sibling,
                device_id_type=MESH,
            )

        def out_across(slot):
            return pltpu.make_async_remote_copy(
                src_ref=o_near.at[slot, :, piece(1 - side)],
                dst_ref=o_x.at[slot],
                send_sem=o_x_send.at[slot],
                recv_sem=o_x_recv.at[slot],
                device_id=across,
                device_id_type=MESH,
            )

        def out_step(way, t):
            slot = t if way == 0 else n - t
            return pltpu.make_async_remote_copy(
                src_ref=o_x.at[slot, :, o_half(way)] if t == 1 else o_land.at[way, t - 2],
                dst_ref=o_land.at[way, t - 1],
                send_sem=o_send.at[way, t],
                recv_sem=o_recv.at[way, t],
                device_id=ahead if way == 0 else behind,
                device_id_type=MESH,
            )

        def out_pair(slot):
            out_load(slot).wait()
            for which in range(2 if split else 1):
                out_swap(slot, which).wait_recv()
            total = o_own[slot].astype(F32) + o_near[slot].astype(F32)
            o_near[slot] = total.astype(BF)
            if split:
                out_across(slot).start()

        def out_quarter(slot):
            here = o_near[slot, :, piece(side)].astype(F32)
            if split:
                out_across(slot).wait_recv()
                here = here + o_x[slot].astype(F32)
            o_x[slot] = here.astype(BF)

        def out_forward(t):
            for slot in sorted({t, n - t}):
                if min(slot, n - slot) == t:
                    out_quarter(slot)
            for way in range(2):
                slot = t if way == 0 else n - t
                if t > 1:
                    out_step(way, t - 1).wait_recv()
                    value = o_x[slot, :, o_half(way)].astype(F32) + o_land[way, t - 2].astype(F32)
                    o_land[way, t - 2] = value.astype(BF)
                out_step(way, t).start()

        def out_finish():
            out_quarter(0)
            for way in range(2):
                out_step(way, n - 1).wait_recv()
                value = o_x[0, :, o_half(way)].astype(F32) + o_land[way, n - 2].astype(F32)
                o_done[:, o_half(way)] = value.astype(BF)
            ends.start(0)

        gains = 1
        d_load.start()
        w_load.start()
        begin(0)
        slots = []
        for t in range(1, n // 2 + 1):
            slots += [t] if 2 * t == n else [t, n - t]
        slots.append(0)
        for slot in slots:
            out_load(slot).start()
        for t in range(1, n + 1):
            swaps(0, t)
            for slot in slots[t - 1 : t]:
                for which in range(2 if split else 1):
                    out_swap(slot, which).start()
        jobs = [lambda k=k: product(k) for k in range(parts)] + [norm]

        def open_gains():
            begin(gains)
            for t in range(1, n + 1):
                swaps(gains, t)

        jobs.append(open_gains)
        half_way = n // 2
        small = []
        for t in range(1, n):
            small.append(lambda t=t: forward(gains, t))
            if t % 2 == 0 or n <= 4:
                small.append(lambda t=t: out_forward(t // 2 if n > 4 else t))
        for t in range(1, n):
            forward(0, t)
            if t == 1:
                d_load.wait()
                w_load.wait()
            if t <= half_way:
                for slot in slots[(t - 1) * n // half_way : t * n // half_way]:
                    out_pair(slot)
                for job in jobs[(t - 1) * len(jobs) // half_way : t * len(jobs) // half_way]:
                    job()
                if t == half_way:
                    spread.start(0)
            else:
                left, k = n - 1 - half_way, t - half_way - 1
                for job in small[k * len(small) // left : (k + 1) * len(small) // left]:
                    job()
        finish(0)
        for t in range((n - 1) // 2 + 1 if n > 4 else n, n):
            out_forward(t)
        finish(gains)
        out_finish()
        spread.arrive(0)
        spread.start(1)
        ends.arrive(0)
        ends.start(1)
        for k in range(len(bits)):
            for g in range(count):
                face(g, k).wait_recv()
                done[g][k + 1] = (done[g][k].astype(F32) + extra[g][k].astype(F32)).astype(kinds[g])
                if k + 1 < len(bits):
                    face(g, k + 1).start()
        for g in range(count):
            end(g).start()
            here = pl.ds(pl.multiple_of(core * widths[g], 128), widths[g])
            outs[g][:, here] = done[g][len(bits)].astype(F32)
        for g in range(count):
            end(g).wait_recv()
            here = pl.ds(pl.multiple_of((1 - core) * widths[g], 128), widths[g])
            outs[g][:, here] = back[g][...].astype(F32)
        ends.arrive(1)
        bases = [core * (outwidth // 2) + side * quarter]
        if split:
            bases.append(core * (outwidth // 2) + (1 - side) * quarter)
        bases += [b + (1 - 2 * core) * (outwidth // 2) for b in bases]
        for base, ref in zip(bases, [o_done] + list(o_blocks)):
            wo_out[:, pl.ds(pl.multiple_of(base, 128), quarter)] = ref[...].astype(F32)
        ends.last()
        for slot in range(n):
            for which in range(2 if split else 1):
                out_swap(slot, which).wait_send()
            if split:
                out_across(slot).wait_send()
        for way in range(2):
            for t in range(1, n):
                out_step(way, t).wait_send()
        spread.arrive(1)
        spread.last()
        dn_save.wait()
        for g in range(count):
            end(g).wait_send()
            for k in range(len(bits)):
                face(g, k).wait_send()
            for way in range(2):
                for t in range(1, n):
                    step(g, way, t).wait_send()
                for slot in range(n):
                    swap(g, way, slot).wait_send()

    dma = pltpu.SemaphoreType.DMA
    groups = list(zip(rows, widths, kinds))
    out = pl.pallas_call(
        kernel,
        in_specs=[ANY] * (2 + len(sums) + 2) + [WHOLE] * 3,
        out_specs=[WHOLE] * (count + 1) + [ANY] * (len(sums) * others + 1),
        out_shape=[jax.ShapeDtypeStruct((r, 2 * w), F32) for r, w, _ in groups]
        + [jax.ShapeDtypeStruct((mine, outwidth), F32)]
        + [jax.ShapeDtypeStruct(a.shape, BF) for a in sums for _ in range(others)]
        + [jax.ShapeDtypeStruct((span, width), F32)],
        scratch_shapes=[
            pltpu.VMEM((n * 8, 2 * widths[-1]), F32),
            pltpu.VMEM((8, width), F32),
            pltpu.VMEM(d_qkv.shape, BF),
            pltpu.VMEM(w_qkv.shape, BF),
            pltpu.VMEM((span, width), F32),
            dma(()),
            dma(()),
            dma(()),
        ]
        + [pltpu.VMEM((n * r, w), kind) for r, w, kind in groups]
        + [pltpu.VMEM((2, n - 1, r, w // 2), kind) for r, w, kind in groups]
        + [pltpu.VMEM((len(bits) + 1, r, w), kind) for r, w, kind in groups]
        + [pltpu.VMEM((max(1, len(bits)), r, w), kind) for r, w, kind in groups]
        + [pltpu.VMEM((r, w), kind) for r, w, kind in groups]
        + [pltpu.VMEM((2, 2, r, w // 2), kind) for r, w, kind in groups]
        + [
            dma((count, 2, 2)),
            pltpu.VMEM((n, mine, outwidth // 2), BF),
            pltpu.VMEM((n, mine, outwidth // 2), BF),
            pltpu.VMEM((n, mine, quarter), BF),
            pltpu.VMEM((2, n - 1, mine, quarter // 2), BF),
            pltpu.VMEM((mine, quarter), BF),
        ]
        + [pltpu.VMEM((mine, quarter), BF)] * others
        + [
            dma((n,)),
            dma((n, 2)),
            dma((n, 2)),
            dma((n,)),
            dma((n,)),
            dma((2, n)),
            dma((2, n)),
        ]
        + spread_scratch(1, n_dp)
        + [
            dma((count, 2, n)),
            dma((count, 2, n)),
            dma((count, 2, n)),
            dma((count, 2, n)),
            dma((count, max(1, len(bits)))),
            dma((count, max(1, len(bits)))),
            dma((count,)),
            dma((count,)),
        ]
        + spread_scratch(len(sums), n_dp),
        compiler_params=pltpu.CompilerParams(
            collective_id=1, has_side_effects=True, vmem_limit_bytes=58 * MIB
        ),
        cost_estimate=cost(0, sum(12 * n * r * w for r, w, _ in groups)),
    )(part_qkv, part_out, *sums, d_qkv, w_qkv, x, gain, d_gain)
    blocks = [out[3 + k * others : 3 + (k + 1) * others] for k in range(len(sums))]
    return out[0], out[2], out[1], blocks, out[-1]


class Ring:
    def __init__(self, n_fsdp, n_ctx):
        order = []
        for c in range(n_ctx):
            rows = range(n_fsdp) if c % 2 == 0 else reversed(range(n_fsdp))
            order += [f * n_ctx + c for f in rows]
        self.order = order
        self.size = n = len(order)
        place = [0] * n
        for k, block in enumerate(order):
            place[block] = k
        self.place = place
        self.block = lax.axis_index(GRID)
        self.rank = jnp.array(place, jnp.int32)[self.block]

    def slot_blocks(self):
        slots = jnp.arange(self.size, dtype=jnp.int32)
        return jnp.array(self.order, jnp.int32)[(self.rank - slots) % self.size]

    def to_slots(self, array, axis=1, deps=()):
        return reorder(array, self.slot_blocks(), axis, deps)

    def from_slots(self, array, axis=1):
        return reorder(array, (self.rank - jnp.array(self.place, jnp.int32)) % self.size, axis)


class Team:
    def __init__(self, size):
        self.size = size
        self.rank = lax.axis_index("dp")
        self.bits = [1 << k for k in range(size.bit_length() - 1)]
        self.order = [0]
        for bit in reversed(self.bits):
            self.order = self.order + [m ^ bit for m in self.order]

    def swap(self, value, bit):
        return lax.ppermute(value, "dp", [(k, k ^ bit) for k in range(self.size)])

    def scatter(self, parts):
        for bit in self.bits:
            half = len(parts) // 2
            got = [self.swap(part.astype(BF), bit) for part in parts[half:]]
            parts = [kept + part.astype(F32) for kept, part in zip(parts[:half], got)]
        return parts[0]


def shards(sizes, x_in, span_order, attn_gain, w_qkv, w_out, ffn_gain, w_gate_up, w_down, cotangent):
    n_dp, n_fsdp, n_ctx = sizes
    ring = Ring(n_fsdp, n_ctx)
    team = Team(n_dp)
    n = ring.size
    width = x_in.shape[-1]
    rows = width // n
    tokens = x_in.reshape(-1, width)
    span = tokens.shape[0]
    rank = lax.axis_index("ctx")
    qwidth = HEADS * HD
    kvwidth = KV_HEADS * HD
    ffwidth = w_down.shape[1]
    order = span_order.reshape(-1)
    near = [(rank + k) % n_ctx for k in range(n_ctx)]
    offsets = jnp.arange(span, dtype=jnp.int32)
    query_pos = order[rank] * span + offsets
    seen = jnp.stack([order[c] < order[rank] for c in near[1:]]).astype(jnp.int32)
    tables = rope_tables(query_pos.astype(F32))

    ffq = ffwidth // n_dp
    sub = ffq // SUBS
    grad_y = cotangent.reshape(span, width)
    gains = jnp.concatenate([attn_gain[None], ffn_gain[None], jnp.zeros((14, rows), BF)], 0)
    qkv, kv_far, normed_one, wqkv, wout, gains, dy = opening(
        sizes, tokens, grad_y, w_qkv, w_out, gains, tables
    )
    attn_t, lse, hidden_one, scale_two, normed_two, x_others, dy_others, weights_a = attend_forward(
        sizes, tokens, qkv, kv_far, seen, wout, gains, dy, w_gate_up, w_down
    )
    xs = [normed_two] + list(x_others)
    dys = [dy] + list(dy_others)
    gains = gains[:, :2][(ring.rank - jnp.array(ring.place, jnp.int32)) % n]
    gain_one = gains[:, 0].reshape(-1).astype(F32)
    gain_two = gains[:, 1].reshape(-1).astype(F32)

    y, dn, grads_a, weights_b = feed_forward(
        sizes, xs, dys, [[w] for w in weights_a], None, (w_gate_up, w_down), False, 2
    )
    y, dn, grads_b, sums_a = feed_forward(
        sizes, xs, dys, [[w] for w in weights_b], list(zip(y, dn)), grads_a, True, 3
    )

    d_normed_two = ring.from_slots(sum(part.astype(F32) for part in dn))
    d_hidden_norm, d_gain_two = norm_back(hidden_one, scale_two, gain_two, d_normed_two)
    d_hidden = grad_y.astype(F32) + d_hidden_norm
    d_proj = d_hidden.astype(BF)

    d_attn = matmul_rows(d_proj, wout).astype(BF)
    d_qkv, part_out, part_qkv, sums_b, others_a = attend_backward(
        sizes, qkv, kv_far, d_attn, lse, seen, tables, attn_t, d_proj, normed_one, grads_b, sums_a, 4
    )
    room = max(rows, 256)
    grad_qkv, grad_out, grad_gain, others_b, d_input_norm = closing(
        sizes,
        part_qkv,
        part_out,
        sums_b,
        d_qkv,
        wqkv,
        tokens,
        jnp.broadcast_to(gain_one[None], (8, width)),
        jnp.broadcast_to(d_gain_two[None], (8, width)),
    )
    grad_input = d_hidden + d_input_norm

    placed, columns = [], []
    for q in range(SUBS):
        blocks = [sums_a[q]] + list(others_a[q]) if q < 2 else [sums_b[q - 2]] + list(others_b[q - 2])
        for m, block in zip(team.order, blocks):
            placed.append(block)
            columns.append((team.rank ^ m) * ffq + q * sub)
    grad_gate_up, grad_down = place_grads(placed, jnp.stack(columns).astype(jnp.int32), sub, ffwidth)

    y_out = hidden_one + ring.from_slots(team.scatter(y))
    return (
        y_out.astype(BF).reshape(x_in.shape),
        grad_input.reshape(x_in.shape),
        grad_gain[0, :rows],
        grad_qkv,
        grad_out,
        grad_gain[0, room : room + rows],
        grad_gate_up,
        grad_down,
    )


def solution(mesh):
    sizes = (mesh.shape["dp"], mesh.shape["fsdp"], mesh.shape["ctx"])
    tokens = P(("dp", "fsdp"), "ctx", None)
    weight = P(("fsdp", "ctx"), None)
    gain = P(("fsdp", "ctx"))

    def body(*args):
        return shards(sizes, *args)

    return jax.shard_map(
        body,
        mesh=mesh,
        in_specs=(tokens, P(("dp", "fsdp"), None), gain, weight, weight, gain, weight, weight, tokens),
        out_specs=(tokens, tokens, gain, weight, weight, gain, weight, weight),
        check_vma=False,
    )
```
